32 devices in a mesh: img: 8 (over z, y), ch: 4 (over x, core).
Axes of the slice: x: 2, y: 2, z: 4, core: 2. Of those that a mesh axis runs over, the one named last changes fastest.
Arguments:
- x_big: bfloat16 [64, 14, 14, 1024], P('img', None, None, 'ch'), may hold values from -6 to 6
- x_small: bfloat16 [64, 10, 10, 1024], P('img', None, None, 'ch'), may hold values from -6 to 6
- cot_big: bfloat16 [64, 7, 7, 2048], P('img', None, None, 'ch'), may hold values from -6 to 6
- cot_small: bfloat16 [64, 5, 5, 2048], P('img', None, None, 'ch'), may hold values from -6 to 6
- counts: int32 [8, 2], replicated, may hold values from 1 to 8, as said below
- w_reduce: bfloat16 [1024, 256], P(None, 'ch'), may hold values from -0.1875 to 0.1875
- w_mix: bfloat16 [3, 3, 256, 256], P(None, None, None, 'ch'), may hold values from -0.125 to 0.125
- w_expand: bfloat16 [256, 1024], P(None, 'ch'), may hold values from -0.375 to 0.375
- w_narrow: bfloat16 [1024, 512], P(None, 'ch'), may hold values from -0.1875 to 0.1875
- w_stride: bfloat16 [3, 3, 512, 512], P(None, None, None, 'ch'), may hold values from -0.09375 to 0.09375
- w_widen: bfloat16 [512, 2048], P(None, 'ch'), may hold values from -0.25 to 0.25
- w_short: bfloat16 [1024, 2048], P(None, 'ch'), may hold values from -0.1875 to 0.1875
- gain_mid3: float32 [2, 256], P(None, 'ch'), may hold values from 0.1 to 1.9
- shift_mid3: float32 [2, 256], P(None, 'ch'), may hold values from -3 to 3
- gain_out3: float32 [1024], P('ch'), may hold values from 0.1 to 1.9
- shift_out3: float32 [1024], P('ch'), may hold values from -3 to 3
- gain_mid4: float32 [2, 512], P(None, 'ch'), may hold values from 0.1 to 1.9
- shift_mid4: float32 [2, 512], P(None, 'ch'), may hold values from -3 to 3
- gain_out4: float32 [2, 2048], P(None, 'ch'), may hold values from 0.1 to 1.9
- shift_out4: float32 [2, 2048], P(None, 'ch'), may hold values from -3 to 3
Outputs:
- out_big: float32 [64, 7, 7, 2048], P('img', None, None, 'ch')
- out_small: float32 [64, 5, 5, 2048], P('img', None, None, 'ch')
- grad_x_big: float32 [64, 14, 14, 1024], P('img', None, None, 'ch')
- grad_x_small: float32 [64, 10, 10, 1024], P('img', None, None, 'ch')
- grad_w_reduce: float32 [1024, 256], P(None, 'ch')
- grad_w_mix: float32 [3, 3, 256, 256], P(None, None, None, 'ch')
- grad_w_expand: float32 [256, 1024], P(None, 'ch')
- grad_w_narrow: float32 [1024, 512], P(None, 'ch')
- grad_w_stride: float32 [3, 3, 512, 512], P(None, None, None, 'ch')
- grad_w_widen: float32 [512, 2048], P(None, 'ch')
- grad_w_short: float32 [1024, 2048], P(None, 'ch')
- grad_gain_mid3: float32 [2, 256], P(None, 'ch')
- grad_shift_mid3: float32 [2, 256], P(None, 'ch')
- grad_gain_out3: float32 [1024], P('ch')
- grad_shift_out3: float32 [1024], P('ch')
- grad_gain_mid4: float32 [2, 512], P(None, 'ch')
- grad_shift_mid4: float32 [2, 512], P(None, 'ch')
- grad_gain_out4: float32 [2, 2048], P(None, 'ch')
- grad_shift_out4: float32 [2, 2048], P(None, 'ch')
The draws below stay inside these ranges and needn't reach their ends.
Inputs may be any that keep to these rules, and one draw needn't show every extreme that they name: `counts`: column 0 lies between 1 and 8, column 1 between 1 and 8; in every draw some index is full in column 0 and some in column 1. The live views of a device are its first slots.
All inputs are finite; a program needn't handle non-finite values.
Results may differ from the reference program's by a relative error of at most 0.03.
Values may be sent and summed in bfloat16 or wider, within the bound.
No kernel may reach another device: no remote copies, remote signals or barrier semaphores. Data moves between devices by JAX's collectives and lax.ppermute only.
A program may use at most 192 MiB of HBM per device.

```python
import jax
import jax.numpy as jnp
from jax import lax

C3 = 1024
M3 = 256
M4 = 512
C4 = 2048
HB = 14
HS = 10
SB = 8
SS = 8
VB = 64
VS = 64
N_IMG = 8


def draw_counts(key, part):
    key = jax.random.fold_in(key, 11)
    keys = jax.random.split(key, 4)
    larger = jax.random.randint(keys[0], (N_IMG,), 1, SB + 1)
    smaller = jax.random.randint(keys[1], (N_IMG,), 1, SS + 1)
    full_large = jax.random.randint(keys[2], (), 0, N_IMG)
    full_small = jax.random.randint(keys[3], (), 0, N_IMG)
    indices = jnp.arange(N_IMG)
    larger = jnp.where(indices == full_large, SB, larger)
    smaller = jnp.where(indices == full_small, SS, smaller)
    return jnp.stack([larger, smaller], axis=1).astype(jnp.int32)


def levels(key, dims, cuts, low, high):
    def one(axis_at, parts):
        steps = jax.random.uniform(jax.random.fold_in(jax.random.fold_in(key, 6), axis_at), (parts,), jnp.float32, low / len(cuts), high / len(cuts))
        return jnp.repeat(jnp.exp(steps), dims[axis_at] // parts).reshape((-1,) + (1,) * (len(dims) - axis_at - 1))

    level = one(*cuts[0])
    for cut in cuts[1:]:
        level = level * one(*cut)
    return level


def scatter_about(rng, shape, scale, limit, cuts=(), held_as=jnp.bfloat16):
    loudness = levels(rng, shape, cuts, -0.22, 0.18) if cuts else 1.0
    array = jax.random.normal(rng, shape, jnp.float32) * scale * loudness
    return jnp.minimum(jnp.maximum(array, -limit), limit).astype(held_as)


def setup_inputs(seed: int = 0) -> dict:
    arg_keys = jax.random.split(jax.random.key(seed), 21)
    return {
        "x_big": scatter_about(arg_keys[0], (VB, HB, HB, C3), 1.0, 6.0, ((0, 8), (3, 4))),
        "x_small": scatter_about(arg_keys[1], (VS, HS, HS, C3), 1.0, 6.0, ((0, 8), (3, 4))),
        "cot_big": scatter_about(arg_keys[2], (VB, HB // 2, HB // 2, C4), 1.0, 6.0, ((0, 8), (3, 4))),
        "cot_small": scatter_about(arg_keys[3], (VS, HS // 2, HS // 2, C4), 1.0, 6.0, ((0, 8), (3, 4))),
        "counts": draw_counts(jax.random.fold_in(arg_keys[20], 71), 0),
        "w_reduce": scatter_about(arg_keys[5], (C3, M3), C3 ** -0.5, 0.1875, ((1, 4),)),
        "w_mix": scatter_about(arg_keys[6], (3, 3, M3, M3), (9 * M3) ** -0.5, 0.125, ((3, 4),)),
        "w_expand": scatter_about(arg_keys[7], (M3, C3), M3 ** -0.5, 0.375, ((1, 4),)),
        "w_narrow": scatter_about(arg_keys[8], (C3, M4), C3 ** -0.5, 0.1875, ((1, 4),)),
        "w_stride": scatter_about(arg_keys[9], (3, 3, M4, M4), (9 * M4) ** -0.5, 0.09375, ((3, 4),)),
        "w_widen": scatter_about(arg_keys[10], (M4, C4), M4 ** -0.5, 0.25, ((1, 4),)),
        "w_short": scatter_about(arg_keys[11], (C3, C4), C3 ** -0.5, 0.1875, ((1, 4),)),
        "gain_mid3": jnp.clip(1.0 + 0.18 * jax.random.normal(arg_keys[12], (2, M3), jnp.float32), 0.1, 1.9),
        "shift_mid3": scatter_about(arg_keys[13], (2, M3), 0.5, 3.0, ((1, 4),), jnp.float32),
        "gain_out3": jnp.clip(1.0 + 0.18 * jax.random.normal(arg_keys[14], (C3,), jnp.float32), 0.1, 1.9),
        "shift_out3": scatter_about(arg_keys[15], (C3,), 0.5, 3.0, ((0, 4),), jnp.float32),
        "gain_mid4": jnp.clip(1.0 + 0.18 * jax.random.normal(arg_keys[16], (2, M4), jnp.float32), 0.1, 1.9),
        "shift_mid4": scatter_about(arg_keys[17], (2, M4), 0.5, 3.0, ((1, 4),), jnp.float32),
        "gain_out4": jnp.clip(1.0 + 0.18 * jax.random.normal(arg_keys[18], (2, C4), jnp.float32), 0.1, 1.9),
        "shift_out4": scatter_about(arg_keys[19], (2, C4), 0.5, 3.0, ((1, 4),), jnp.float32),
    }


@jax.custom_vjp
def low(v):
    return lax.optimization_barrier(v.astype(jnp.bfloat16)).astype(jnp.float32)

@jax.custom_vjp
def low_back(v):
    return v

def low_keep(v):
    return (low(v), None)

def low_pass(kept, grad):
    return (grad,)

def back_keep(v):
    return (v, None)

def back_low(kept, grad):
    return (low(grad),)
low.defvjp(low_keep, low_pass)
low_back.defvjp(back_keep, back_low)
highest = lax.Precision.HIGHEST
epsilon = 1e-05

def project(inputs, weight):
    return jnp.einsum('bhwc,cd->bhwd', inputs, weight, precision=highest)

def conv_taps(inputs, weight, stride):
    padded = jnp.pad(inputs, ((0, 0), (1, 1), (1, 1), (0, 0)))
    height = (inputs.shape[1] - 1) // stride + 1
    width = (inputs.shape[2] - 1) // stride + 1
    result = jnp.zeros((inputs.shape[0], height, width, weight.shape[3]), jnp.float32)
    for row_tap in range(3):
        for col_tap in range(3):
            window = padded[:, row_tap:row_tap + stride * (height - 1) + 1:stride, col_tap:col_tap + stride * (width - 1) + 1:stride, :]
            result = result + jnp.einsum('bhwc,cd->bhwd', window, weight[row_tap, col_tap], precision=highest)
    return result

def normalize(pre, gain_vec, shift_vec, lives, count):
    center = (lax.optimization_barrier(jnp.sum(pre[0] * lives[0], axis=(0, 1, 2))) + lax.optimization_barrier(jnp.sum(pre[1] * lives[1], axis=(0, 1, 2)))) / count
    devs = [value - center for value in pre]
    variance = (lax.optimization_barrier(jnp.sum(devs[0] * devs[0] * lives[0], axis=(0, 1, 2))) + lax.optimization_barrier(jnp.sum(devs[1] * devs[1] * lives[1], axis=(0, 1, 2)))) / count
    inv_std = lax.rsqrt(variance + epsilon)
    return [dev * inv_std * gain_vec + shift_vec for dev in devs]

def reference(x_big, x_small, cot_big, cot_small, counts, w_reduce, w_mix, w_expand, w_narrow, w_stride, w_widen, w_short, gain_mid3, shift_mid3, gain_out3, shift_out3, gain_mid4, shift_mid4, gain_out4, shift_out4):
    slot_big = jnp.arange(VB, dtype=jnp.int32)
    slot_small = jnp.arange(VS, dtype=jnp.int32)
    live_big = (slot_big % SB < counts[slot_big // SB, 0]).astype(jnp.float32)
    live_small = (slot_small % SS < counts[slot_small // SS, 1]).astype(jnp.float32)
    lives = [live_big[:, None, None, None], live_small[:, None, None, None]]
    views_big = jnp.sum(counts[:, 0]).astype(jnp.float32)
    views_small = jnp.sum(counts[:, 1]).astype(jnp.float32)
    count3 = views_big * (HB * HB) + views_small * (HS * HS)
    count4 = views_big * (HB // 2 * (HB // 2)) + views_small * (HS // 2 * (HS // 2))
    floats = [value.astype(jnp.float32) for value in (x_big, x_small, w_reduce, w_mix, w_expand, w_narrow, w_stride, w_widen, w_short)]
    floats = floats + [gain_mid3, shift_mid3, gain_out3, shift_out3, gain_mid4, shift_mid4, gain_out4, shift_out4]

    def forward(inp_big, inp_small, wr, wm, we, wn, wst, wwi, wsh, gm3, sm3, go3, so3, gm4, sm4, go4, so4):
        inputs = [inp_big, inp_small]
        pre = [low_back(project(value, wr)) for value in inputs]
        acts = [low(jax.nn.gelu(value)) for value in normalize(pre, gm3[0], sm3[0], lives, count3)]
        pre = [low_back(conv_taps(value, wm, 1)) for value in acts]
        acts = [low(jax.nn.gelu(value)) for value in normalize(pre, gm3[1], sm3[1], lives, count3)]
        pre = [low_back(project(value, we)) for value in acts]
        normed = normalize(pre, go3, so3, lives, count3)
        mids = [low(jax.nn.gelu(normed[index] + inputs[index])) for index in range(2)]
        pre = [low_back(project(value, wn)) for value in mids]
        acts = [low(jax.nn.gelu(value)) for value in normalize(pre, gm4[0], sm4[0], lives, count3)]
        pre = [low_back(conv_taps(value, wst, 2)) for value in acts]
        acts = [low(jax.nn.gelu(value)) for value in normalize(pre, gm4[1], sm4[1], lives, count4)]
        main = [low_back(project(value, wwi)) for value in acts]
        side = [low_back(project(value[:, ::2, ::2, :], wsh)) for value in mids]
        main_n = normalize(main, go4[0], so4[0], lives, count4)
        side_n = normalize(side, go4[1], so4[1], lives, count4)
        return tuple((jax.nn.gelu(main_n[index] + side_n[index]) * lives[index] for index in range(2)))
    outputs, pullback = jax.vjp(forward, *floats)
    grads = pullback((cot_big.astype(jnp.float32), cot_small.astype(jnp.float32)))
    return (outputs[0], outputs[1], grads[0], grads[1], grads[2], grads[3], grads[4], grads[5], grads[6], grads[7], grads[8], grads[9], grads[10], grads[11], grads[12], grads[13], grads[14], grads[15], grads[16])
```

```python
import functools

import jax
import jax.numpy as jnp
from jax import lax
from jax.experimental import pallas as pl
from jax.experimental.pallas import tpu as pltpu
from jax.sharding import PartitionSpec as P

EPS = 1e-05
G0 = 0.7978845608028654
G1 = G0 * 0.044715
F32 = jnp.float32
BF16 = jnp.bfloat16
VIEWS = 8

ANY = pl.BlockSpec(memory_space=pl.ANY)
VMEM = pl.BlockSpec(memory_space=pltpu.VMEM)
SMEM = pl.BlockSpec(memory_space=pltpu.SMEM)


def sds(shape, dtype=F32):
    return jax.ShapeDtypeStruct(tuple(shape), dtype)


def call(name, kernel, ins, outs, scratch=(), limit=48, cost=None):
    outs = [o if isinstance(o, tuple) else (o, VMEM) for o in outs]
    result = pl.pallas_call(
        kernel,
        out_shape=[o[0] for o in outs],
        in_specs=[spec for _, spec in ins],
        out_specs=[o[1] for o in outs],
        scratch_shapes=list(scratch),
        compiler_params=pltpu.CompilerParams(vmem_limit_bytes=limit << 20),
        cost_estimate=cost,
        name=name,
    )(*[array for array, _ in ins])
    return result


def vm(*arrays):
    return [(a, VMEM) for a in arrays]


def nn(a, b):
    return lax.dot_general(a, b, (((1,), (0,)), ((), ())), preferred_element_type=F32)


def nt(a, b):
    return lax.dot_general(a, b, (((1,), (1,)), ((), ())), preferred_element_type=F32)


def tn(a, b):
    return lax.dot_general(a, b, (((0,), (0,)), ((), ())), preferred_element_type=F32)


def gelu(t):
    half = 0.5 * t
    return half + half * jnp.tanh(t * (G0 + G1 * (t * t)))


def gelu_slope(t):
    sq = t * t
    th = jnp.tanh(t * (G0 + G1 * sq))
    return 0.5 * (1.0 + th) + (0.5 * t) * (1.0 - th * th) * (G0 + (3.0 * G1) * sq)


def live_rows(count, chans):
    return (lax.broadcasted_iota(jnp.int32, (VIEWS, chans), 0) < count).astype(F32)


def rows_sum(v):
    return jnp.sum(v, axis=0, keepdims=True)


def merged(sa, sb, na, nb):
    total = na + nb
    mean = (na * sa[0:1] + nb * sb[0:1]) / total
    diff = sb[0:1] - sa[0:1]
    square = sa[1:2] + sb[1:2] + diff * diff * (na * nb / total)
    return mean, lax.rsqrt(square / total + EPS)


def as_rows(v):
    return v.reshape(v.shape[0] * v.shape[1], v.shape[2])


def as_pix(v):
    return v.reshape(v.shape[0] // VIEWS, VIEWS, v.shape[1])


class Geo:
    def __init__(self, hb, hs):
        self.hb, self.hs = hb, hs
        self.pb, self.ps = hb * hb, hs * hs
        self.px = self.pb + self.ps
        self.rows = self.px * VIEWS
        self.qb, self.qs = self.pb // 4, self.ps // 4
        self.px4 = self.qb + self.qs
        self.rows4 = self.px4 * VIEWS
        self.parts = ((hb, 0), (hs, self.pb))

    def loop(self, body, carries):
        out = []
        for part, (side, start) in enumerate(self.parts):
            step = 2 * side

            def run(i, carry, part=part, start=start, step=step):
                pix = start + i * step
                row = pl.multiple_of(start * VIEWS + i * (step * VIEWS), 16)
                return body(part, i, pix, step, row, step * VIEWS, carry)

            out.append(lax.fori_loop(0, side // 2, run, carries[part]))
        return out


def finish_stats(geo, ref, sums, lives, count, out, quarter=None):
    mean = (rows_sum(sums[0] * lives[0]) + rows_sum(sums[1] * lives[1])) / count

    def body(part, i, pix, npx, row, nrows, carry):
        dev = ref[pl.ds(pix, npx)] - mean
        return carry + jnp.sum(dev * dev, axis=0)

    zero = jnp.zeros(sums[0].shape, F32)
    sq = geo.loop(body, [zero, zero])
    out[0:1] = mean
    out[1:2] = rows_sum(sq[0] * lives[0]) + rows_sum(sq[1] * lives[1])


def block_stats(geo, value, lives, count):
    big, small = value[: geo.qb], value[geo.qb :]
    mean = (
        rows_sum(jnp.sum(big, axis=0) * lives[0]) + rows_sum(jnp.sum(small, axis=0) * lives[1])
    ) / count
    db, ds = big - mean, small - mean
    square = rows_sum(jnp.sum(db * db, axis=0) * lives[0]) + rows_sum(
        jnp.sum(ds * ds, axis=0) * lives[1]
    )
    return mean, square


def k_assemble(plan, me, *refs):
    n = len(plan)
    pieces, outs, sem = refs[: 4 * n], refs[4 * n : 5 * n], refs[5 * n]
    copies = []
    for w, (kind, size) in enumerate(plan):
        for p in range(4):
            src = pieces[4 * w + p]
            at = pl.ds(pl.multiple_of((me[0] ^ p) * size, size), size)
            if kind == "cols":
                dsts = [(src, outs[w].at[:, at])]
            elif kind == "rows":
                dsts = [(src, outs[w].at[at, :])]
            elif kind == "taps_nt":
                dsts = [
                    (src.at[t], outs[w].at[t // 3, at, pl.ds((t % 3) * 256, 256)])
                    for t in range(9)
                ]
            else:
                dsts = [(src.at[t], outs[w].at[t, at, :]) for t in range(9)]
            for a, b in dsts:
                copies.append(pltpu.make_async_copy(a, b, sem.at[len(copies)]))
                copies[-1].start()
    for c in copies:
        c.wait()


def assemble(name, me, items):
    plan = [(kind, size) for _, kind, size, _ in items]
    ncopies = sum(36 if k.startswith("taps") else 4 for k, _ in plan)
    ins = [(me, SMEM)] + [(p, ANY) for pieces, _, _, _ in items for p in pieces]
    return call(
        name,
        functools.partial(k_assemble, plan),
        ins,
        [(sds(shape, BF16), ANY) for _, _, _, shape in items],
        [pltpu.SemaphoreType.DMA((ncopies,))],
        limit=4,
    )


def k_reduce(geo, me, nf, x0b, x1b, x2b, x3b, x0s, x1s, x2s, x3s, wt, pre, xs, stats, wx):
    xb, xsm = (x0b, x1b, x2b, x3b), (x0s, x1s, x2s, x3s)
    q = me[0]
    for p in range(4):
        wx[p] = wt[:, pl.ds(pl.multiple_of((q ^ p) * 256, 256), 256)]
    chans = wt.shape[0]
    lives = [live_rows(me[1], chans), live_rows(me[2], chans)]

    def body(part, i, pix, npx, row, nrows, carry):
        src = (xb, xsm)[part]
        local = pl.multiple_of(i * nrows, 16)
        acc = None
        for p in range(4):
            v = src[p][pl.ds(local, nrows), :]
            xs[q ^ p, pl.ds(row, nrows), :] = v
            d = nt(v, wx[p])
            acc = d if acc is None else acc + d
        z = as_pix(acc)
        pre[pl.ds(pix, npx)] = z
        return carry + jnp.sum(z, axis=0)

    zero = jnp.zeros((VIEWS, chans), F32)
    sums = geo.loop(body, [zero, zero])
    finish_stats(geo, pre, sums, lives, nf[0], stats)


def side_shift(v, by):
    zero = jnp.zeros((v.shape[0], 1) + v.shape[2:], v.dtype)
    if by > 0:
        return jnp.concatenate([zero, v[:, :-1]], axis=1)
    return jnp.concatenate([v[:, 1:], zero], axis=1)


def store_shifted(buf, row, nrows, side, v, order):
    img = v.reshape(2, side, VIEWS, v.shape[-1])
    chans = v.shape[-1]
    forms = [side_shift(img, 1), img, side_shift(img, -1)]
    for lane, k in enumerate(order):
        flat = forms[k].reshape(nrows, chans).astype(BF16)
        buf[pl.ds(row, nrows), lane * chans : (lane + 1) * chans] = flat


def put_phases(ref, i, v):
    for k in range(4):
        ref[k // 2, k % 2, i] = v[k // 2, :, k % 2]


def get_phases(ref, i):
    rows = [jnp.stack([ref[r, 0, i], ref[r, 1, i]], axis=1) for r in range(2)]
    return jnp.stack(rows)


def zero_edges(buf, edge):
    total = buf.shape[0]
    buf[0:edge, :] = jnp.zeros((edge, buf.shape[1]), BF16)
    buf[total - edge : total, :] = jnp.zeros((edge, buf.shape[1]), BF16)


def k_mix(geo, me, nf, pre1, sa, sb, gs, w, pre2, wb, ws, stats):
    chans = pre1.shape[-1]
    lives = [live_rows(me[1], chans), live_rows(me[2], chans)]
    mean, inv = merged(sa[...], sb[...], nf[1], nf[2])
    scale, shift = gs[0:1] * inv, gs[1:2]
    bufs = (wb, ws)
    for part, (side, _) in enumerate(geo.parts):
        zero_edges(bufs[part], side * VIEWS)

    def act(part, i, pix, npx, row, nrows, carry):
        a = gelu((pre1[pl.ds(pix, npx)] - mean) * scale + shift)
        side = geo.parts[part][0]
        at = pl.multiple_of(side * VIEWS + i * nrows, 16)
        store_shifted(bufs[part], at, nrows, side, a, (0, 1, 2))
        return carry

    geo.loop(act, [0, 0])

    def dots(part, i, pix, npx, row, nrows, carry):
        acc = None
        for r in range(3):
            at = pl.multiple_of(i * nrows + r * (nrows // 2), 16)
            d = nt(bufs[part][pl.ds(at, nrows), :], w[r])
            acc = d if acc is None else acc + d
        z = as_pix(acc)
        pre2[pl.ds(pix, npx)] = z
        return carry + jnp.sum(z, axis=0)

    zero = jnp.zeros((VIEWS, chans), F32)
    sums = geo.loop(dots, [zero, zero])
    finish_stats(geo, pre2, sums, lives, nf[0], stats)


def k_expand(geo, me, nf, pre2, sa, sb, gs, w, pre3, act2, stats):
    chans = w.shape[1]
    lives = [live_rows(me[1], chans), live_rows(me[2], chans)]
    mean, inv = merged(sa[...], sb[...], nf[1], nf[2])
    scale, shift = gs[0:1] * inv, gs[1:2]

    def body(part, i, pix, npx, row, nrows, carry):
        a = as_rows(gelu((pre2[pl.ds(pix, npx)] - mean) * scale + shift)).astype(BF16)
        act2[pl.ds(row, nrows), :] = a
        z = as_pix(nn(a, w[...]))
        pre3[pl.ds(pix, npx)] = z
        return carry + jnp.sum(z, axis=0)

    zero = jnp.zeros((VIEWS, chans), F32)
    sums = geo.loop(body, [zero, zero])
    finish_stats(geo, pre3, sums, lives, nf[0], stats)


def k_narrow(geo, me, nf, pre3, xs, sa, sb, gs, w, pre4b, pre4s, mid, mids, stats, mid_even):
    chans = w.shape[1]
    lives = [live_rows(me[1], chans), live_rows(me[2], chans)]
    mean, inv = merged(sa[...], sb[...], nf[1], nf[2])
    scale, shift = gs[0:1] * inv, gs[1:2]
    pre4 = (pre4b, pre4s)

    def body(part, i, pix, npx, row, nrows, carry):
        side = geo.parts[part][0]
        half = side // 2
        for j in range(4):
            at = slice(256 * j, 256 * j + 256)
            dev = pre3[pl.ds(pix, npx), :, at] - mean[:, at]
            x = as_pix(xs[j, pl.ds(row, nrows), :].astype(F32))
            a = gelu(dev * scale[:, at] + shift[:, at] + x)
            mid[pl.ds(row, nrows), at] = as_rows(a).astype(BF16)
            even = a.reshape(2, half, 2, VIEWS, 256)[0, :, 0]
            mid_even[pl.ds((0, geo.qb)[part] + half * i, half), :, at] = even
        z = nn(mid[pl.ds(row, nrows), :], w[...])
        put_phases(pre4[part], i, z.reshape(2, half, 2, VIEWS, chans))
        return carry + jnp.sum(as_pix(z), axis=0)

    zero = jnp.zeros((VIEWS, chans), F32)
    sums = geo.loop(body, [zero, zero])
    mean4 = (rows_sum(sums[0] * lives[0]) + rows_sum(sums[1] * lives[1])) / nf[0]
    mids[...] = as_rows(mid_even[...]).astype(BF16)
    sq = []
    for part in range(2):

        def dev2(i, carry, part=part):
            for k in range(4):
                d = pre4[part][k // 2, k % 2, i] - mean4
                carry = carry + jnp.sum(d * d, axis=0)
            return carry

        sq.append(lax.fori_loop(0, geo.parts[part][0] // 2, dev2, zero))
    stats[0:1] = mean4
    stats[1:2] = rows_sum(sq[0] * lives[0]) + rows_sum(sq[1] * lives[1])


def k_short(geo, me, nf, mids, w0, w1, w2, w3, side, stats):
    chans = w0.shape[1]
    lives = [live_rows(me[1], chans), live_rows(me[2], chans)]
    for p, w in enumerate((w0, w1, w2, w3)):
        j = me[0] ^ p
        z = as_pix(nn(mids[...], w[...]))
        side[j] = z
        mean, square = block_stats(geo, z, lives, nf[0])
        stats[j] = jnp.concatenate([mean, square], axis=0)


def k_stride(geo, me, nf, n4, pre4b, pre4s, sa, sb, gs, w, pre5, cols, stats, sb_act, ss_act):
    chans = pre4b.shape[-1]
    lives = [live_rows(me[1], chans), live_rows(me[2], chans)]
    mean, inv = merged(sa[...], sb[...], n4[1], n4[2])
    scale, shift = gs[0:1] * inv, gs[1:2]
    srcs, dsts = (pre4b, pre4s), (sb_act, ss_act)
    for part in range(2):

        def act(i, carry, part=part):
            for k in range(4):
                at = (k // 2, k % 2, i)
                dsts[part][at] = gelu((srcs[part][at] - mean) * scale + shift)
            return carry

        lax.fori_loop(0, geo.parts[part][0] // 2, act, 0)
    for r in range(3):
        for c in range(3):
            flats = []
            for part in range(2):
                half = geo.parts[part][0] // 2
                v = dsts[part][(r + 1) % 2, (c + 1) % 2]
                if c == 0:
                    v = side_shift(v, 1)
                if r == 0:
                    v = jnp.concatenate([jnp.zeros((1,) + v.shape[1:], F32), v[:-1]], axis=0)
                flats.append(v.reshape(half * half * VIEWS, chans))
            t = 3 * r + c
            cols[:, t * chans : (t + 1) * chans] = jnp.concatenate(flats, axis=0).astype(BF16)
    z = as_pix(nn(cols[...], w[...]))
    pre5[...] = z
    m5, s5 = block_stats(geo, z, lives, nf[0])
    stats[0:1] = m5
    stats[1:2] = s5


def k_widen(geo, me, nf, pre5, sa, sb, gs, w0, w1, w2, w3, pre6, act5, stats):
    chans = w0.shape[1]
    lives = [live_rows(me[1], chans), live_rows(me[2], chans)]
    mean, inv = merged(sa[...], sb[...], nf[1], nf[2])
    scale, shift = gs[0:1] * inv, gs[1:2]
    act5[...] = as_rows(gelu((pre5[...] - mean) * scale + shift)).astype(BF16)
    for p, w in enumerate((w0, w1, w2, w3)):
        j = me[0] ^ p
        z = as_pix(nn(act5[...], w[...]))
        pre6[j] = z
        m6, s6 = block_stats(geo, z, lives, nf[0])
        stats[j] = jnp.concatenate([m6, s6], axis=0)


def k_total(geo, me, nf, pre6, side, sa, sb, gs, cb0, cb1, cb2, cb3, cs0, cs1, cs2, cs3, out_b, out_s, dt, sums):
    chans = pre6.shape[-1]
    lives = [live_rows(me[1], chans), live_rows(me[2], chans)]
    cots = ((cb0, cb1, cb2, cb3), (cs0, cs1, cs2, cs3))
    spans = ((0, geo.qb), (geo.qb, geo.px4))
    outs = (out_b, out_s)
    for p in range(4):
        j = me[0] ^ p
        a, b, g = sa[j], sb[j], gs[j]
        m6, r6 = merged(a[0:2], b[0:2], nf[1], nf[2])
        ms, rs = merged(a[2:4], b[2:4], nf[1], nf[2])
        acc = [None, None, None]
        for part, (lo, hi) in enumerate(spans):
            d6 = pre6[j, lo:hi] - m6
            dd = side[j, lo:hi] - ms
            total = d6 * (g[0:1] * r6) + g[1:2] + (dd * (g[2:3] * rs) + g[3:4])
            live = lives[part]
            if p == 0:
                outs[part][...] = gelu(total) * live
            grad = gelu_slope(total) * (as_pix(cots[part][p][...].astype(F32)) * live)
            dt[j, lo:hi] = grad
            terms = [jnp.sum(v, axis=0) for v in (grad, grad * d6, grad * dd)]
            acc = [t if s is None else s + t for s, t in zip(acc, terms)]
        sums[j] = jnp.concatenate(
            [rows_sum(acc[0]), rows_sum(acc[1]) * r6, rows_sum(acc[2]) * rs], axis=0
        )


def back_coefs(lives, s1, s2, inv, gain, count):
    c1 = gain * inv
    c2 = [live * (c1 * s1 / count) for live in lives]
    c3 = [live * (c1 * inv * s2 / count) for live in lives]
    return c1, c2, c3


def k_back_wide(geo, me, nf, dt, pre6, side, sa, sb, gs, ga, gb, pre5, sa5, sb5, gs5, w0, w1, w2, w3, dt5, dz6, dzs, sums5):
    chans = pre6.shape[-1]
    lives = [live_rows(me[1], chans), live_rows(me[2], chans)]
    total = nf[1] + nf[2]
    spans = ((0, geo.qb), (geo.qb, geo.px4))
    acc = None
    for p, w in enumerate((w0, w1, w2, w3)):
        j = me[0] ^ p
        a, b, g = sa[j], sb[j], gs[j]
        s = ga[j] + gb[j]
        m6, r6 = merged(a[0:2], b[0:2], nf[1], nf[2])
        ms, rs = merged(a[2:4], b[2:4], nf[1], nf[2])
        k1, k2, k3 = back_coefs(lives, s[0:1], s[1:2], r6, g[0:1], total)
        h1, h2, h3 = back_coefs(lives, s[0:1], s[2:3], rs, g[2:3], total)
        main, short = [], []
        for part, (lo, hi) in enumerate(spans):
            grad = dt[j, lo:hi]
            main.append(grad * k1 - k2[part] - (pre6[j, lo:hi] - m6) * k3[part])
            short.append(grad * h1 - h2[part] - (side[j, lo:hi] - ms) * h3[part])
        z6 = as_rows(jnp.concatenate(main, axis=0)).astype(BF16)
        dzs[j] = as_rows(jnp.concatenate(short, axis=0)).astype(BF16)
        if p == 0:
            dz6[...] = z6
        d = nt(z6, w[...])
        acc = d if acc is None else acc + d
    m5, r5 = merged(sa5[...], sb5[...], nf[1], nf[2])
    dev = pre5[...] - m5
    grad = gelu_slope(dev * (gs5[0:1] * r5) + gs5[1:2]) * as_pix(acc)
    dt5[...] = grad
    sums5[0:1] = rows_sum(jnp.sum(grad, axis=0))
    sums5[1:2] = rows_sum(jnp.sum(grad * dev, axis=0)) * r5


def k_back_short(geo, me, dzs, w0, w1, w2, w3, dms):
    acc = None
    for p, w in enumerate((w0, w1, w2, w3)):
        d = nt(dzs[me[0] ^ p], w[...])
        acc = d if acc is None else acc + d
    dms[...] = as_pix(acc)


def k_back_stride(geo, me, nf, dt5, pre5, sa5, sb5, gs5, ga, gb, pre4b, pre4s, sa4, sb4, gs4, n4, w, dt4b, dt4s, dz5, sums4, shifts):
    chans = pre5.shape[-1]
    lives = [live_rows(me[1], chans), live_rows(me[2], chans)]
    s = ga[...] + gb[...]
    m5, r5 = merged(sa5[...], sb5[...], nf[1], nf[2])
    c1, c2, c3 = back_coefs(lives, s[0:1], s[1:2], r5, gs5[0:1], nf[1] + nf[2])
    spans = ((0, geo.qb), (geo.qb, geo.px4))
    imgs = []
    for part, (lo, hi) in enumerate(spans):
        half = geo.parts[part][0] // 2
        z = dt5[lo:hi] * c1 - c2[part] - (pre5[lo:hi] - m5) * c3[part]
        imgs.append(z.reshape(half, half, VIEWS, chans))

    def flat(moved):
        return jnp.concatenate([v.reshape(-1, chans) for v in moved], axis=0).astype(BF16)

    def up(v):
        return jnp.concatenate([v[1:], jnp.zeros((1,) + v.shape[1:], F32)], axis=0)

    shifts[0] = flat(imgs)
    dz5[...] = shifts[0]
    shifts[1] = flat([side_shift(v, -1) for v in imgs])
    shifts[2] = flat([up(v) for v in imgs])
    shifts[3] = flat([up(side_shift(v, -1)) for v in imgs])
    m4, r4 = merged(sa4[...], sb4[...], n4[1], n4[2])
    scale, off = gs4[0:1] * r4, gs4[1:2]
    plan = {
        (0, 0): ((0, 4),),
        (0, 1): ((0, 5), (1, 3)),
        (1, 0): ((0, 7), (2, 1)),
        (1, 1): ((0, 8), (1, 6), (2, 2), (3, 0)),
    }
    t1, t2 = jnp.zeros((VIEWS, chans), F32), jnp.zeros((VIEWS, chans), F32)
    for (rp, cp), terms in plan.items():
        acc = None
        for k, t in terms:
            d = nt(shifts[k], w[t * chans : (t + 1) * chans, :])
            acc = d if acc is None else acc + d
        for part, (lo, hi) in enumerate(spans):
            half = geo.parts[part][0] // 2
            d = acc[lo * VIEWS : hi * VIEWS].reshape(half, half, VIEWS, chans)
            dev = (pre4b, pre4s)[part][rp, cp] - m4
            grad = gelu_slope(dev * scale + off) * d
            (dt4b, dt4s)[part][rp, cp] = grad
            t1 = t1 + jnp.sum(grad, axis=(0, 1))
            t2 = t2 + jnp.sum(grad * dev, axis=(0, 1))
    sums4[0:1] = rows_sum(t1)
    sums4[1:2] = rows_sum(t2) * r4


def k_back_narrow(geo, me, nf, dt4b, dt4s, pre4b, pre4s, sa4, sb4, gs4, ga, gb, pre3, xs, sa3, sb3, gs3, dms, w, dt3, dz4, sums3, db, ds):
    chans = w.shape[1]
    wide = w.shape[0]
    lives = [live_rows(me[1], chans), live_rows(me[2], chans)]
    s = ga[...] + gb[...]
    m4, r4 = merged(sa4[...], sb4[...], nf[1], nf[2])
    c1, c2, c3 = back_coefs(lives, s[0:1], s[1:2], r4, gs4[0:1], nf[1] + nf[2])
    m3, r3 = merged(sa3[...], sb3[...], nf[1], nf[2])
    scale, off = gs3[0:1] * r3, gs3[1:2]
    dts, pres, bufs = (dt4b, dt4s), (pre4b, pre4s), (db, ds)

    def body(part, i, pix, npx, row, nrows, carry):
        half = geo.parts[part][0] // 2
        dev4 = get_phases(pres[part], i) - m4
        z = get_phases(dts[part], i) * c1 - c2[part] - dev4 * c3[part]
        z = z.reshape(nrows, chans).astype(BF16)
        dz4[pl.ds(row, nrows), :] = z
        buf = bufs[part]
        buf[...] = nt(z, w[...]).reshape(buf.shape)
        buf[0, :, 0] += dms[pl.ds((0, geo.qb)[part] + half * i, half)]
        t1, t2 = [], []
        for j in range(4):
            at = slice(256 * j, 256 * j + 256)
            dev = pre3[pl.ds(pix, npx), :, at] - m3[:, at]
            x = as_pix(xs[j, pl.ds(row, nrows), :].astype(F32))
            d = buf[:, :, :, :, at].reshape(npx, VIEWS, 256)
            grad = gelu_slope(dev * scale[:, at] + off[:, at] + x) * d
            dt3[pl.ds(pix, npx), :, at] = grad
            t1.append(jnp.sum(grad, axis=0))
            t2.append(jnp.sum(grad * dev, axis=0))
        return carry[0] + jnp.concatenate(t1, axis=1), carry[1] + jnp.concatenate(t2, axis=1)

    zero = jnp.zeros((VIEWS, wide), F32)
    (a1, a2), (b1, b2) = geo.loop(body, [(zero, zero), (zero, zero)])
    sums3[0:1] = rows_sum(a1 + b1)
    sums3[1:2] = rows_sum(a2 + b2) * r3


def k_back_expand(geo, me, nf, dt3, pre3, sa3, sb3, gs3, ga, gb, pre2, sa2, sb2, gs2, w, dt2, dz3, sums2, zbuf_b, zbuf_s):
    wide, chans = w.shape[1], w.shape[0]
    lives = [live_rows(me[1], wide), live_rows(me[2], wide)]
    s = ga[...] + gb[...]
    m3, r3 = merged(sa3[...], sb3[...], nf[1], nf[2])
    c1, c2, c3 = back_coefs(lives, s[0:1], s[1:2], r3, gs3[0:1], nf[1] + nf[2])
    m2, r2 = merged(sa2[...], sb2[...], nf[1], nf[2])
    scale, off = gs2[0:1] * r2, gs2[1:2]
    mine = pl.ds(pl.multiple_of(me[0] * 256, 256), 256)

    def body(part, i, pix, npx, row, nrows, carry):
        zbuf = (zbuf_b, zbuf_s)[part]
        for j in range(4):
            at = slice(256 * j, 256 * j + 256)
            z = (
                dt3[pl.ds(pix, npx), :, at] * c1[:, at]
                - c2[part][:, at]
                - (pre3[pl.ds(pix, npx), :, at] - m3[:, at]) * c3[part][:, at]
            )
            zbuf[:, at] = as_rows(z).astype(BF16)
        dz3[pl.ds(row, nrows), :] = zbuf[:, mine]
        d = as_pix(nt(zbuf[...], w[...]))
        dev = pre2[pl.ds(pix, npx)] - m2
        grad = gelu_slope(dev * scale + off) * d
        dt2[pl.ds(pix, npx)] = grad
        return carry[0] + jnp.sum(grad, axis=0), carry[1] + jnp.sum(grad * dev, axis=0)

    zero = jnp.zeros((VIEWS, chans), F32)
    (a1, a2), (b1, b2) = geo.loop(body, [(zero, zero), (zero, zero)])
    sums2[0:1] = rows_sum(a1 + b1)
    sums2[1:2] = rows_sum(a2 + b2) * r2


def k_back_mix(geo, me, nf, dt2, pre2, sa2, sb2, gs2, ga, gb, pre1, sa1, sb1, gs1, w, dt1, dz2, sums1, zb, zs):
    chans = pre2.shape[-1]
    lives = [live_rows(me[1], chans), live_rows(me[2], chans)]
    s = ga[...] + gb[...]
    m2, r2 = merged(sa2[...], sb2[...], nf[1], nf[2])
    c1, c2, c3 = back_coefs(lives, s[0:1], s[1:2], r2, gs2[0:1], nf[1] + nf[2])
    m1, r1 = merged(sa1[...], sb1[...], nf[1], nf[2])
    scale, off = gs1[0:1] * r1, gs1[1:2]
    bufs = (zb, zs)
    for part, (side, _) in enumerate(geo.parts):
        zero_edges(bufs[part], side * VIEWS)

    def back(part, i, pix, npx, row, nrows, carry):
        z = dt2[pl.ds(pix, npx)] * c1 - c2[part] - (pre2[pl.ds(pix, npx)] - m2) * c3[part]
        dz2[pl.ds(row, nrows), :] = as_rows(z).astype(BF16)
        side = geo.parts[part][0]
        at = pl.multiple_of(side * VIEWS + i * nrows, 16)
        store_shifted(bufs[part], at, nrows, side, z, (2, 1, 0))
        return carry

    geo.loop(back, [0, 0])

    def dots(part, i, pix, npx, row, nrows, carry):
        acc = None
        for r in range(3):
            at = pl.multiple_of(i * nrows + (2 - r) * (nrows // 2), 16)
            d = nn(bufs[part][pl.ds(at, nrows), :], w[r])
            acc = d if acc is None else acc + d
        dev = pre1[pl.ds(pix, npx)] - m1
        grad = gelu_slope(dev * scale + off) * as_pix(acc)
        dt1[pl.ds(pix, npx)] = grad
        return carry[0] + jnp.sum(grad, axis=0), carry[1] + jnp.sum(grad * dev, axis=0)

    zero = jnp.zeros((VIEWS, chans), F32)
    (a1, a2), (b1, b2) = geo.loop(dots, [(zero, zero), (zero, zero)])
    sums1[0:1] = rows_sum(a1 + b1)
    sums1[1:2] = rows_sum(a2 + b2) * r1


def k_back_reduce(geo, me, nf, dt1, pre1, sa1, sb1, gs1, ga, gb, dt3, wt, gxb, gxs, dz1, wq):
    chans = pre1.shape[-1]
    lives = [live_rows(me[1], chans), live_rows(me[2], chans)]
    s = ga[...] + gb[...]
    m1, r1 = merged(sa1[...], sb1[...], nf[1], nf[2])
    c1, c2, c3 = back_coefs(lives, s[0:1], s[1:2], r1, gs1[0:1], nf[1] + nf[2])
    mine = pl.ds(pl.multiple_of(me[0] * 256, 256), 256)
    wq[...] = wt[:, mine]

    def body(part, i, pix, npx, row, nrows, carry):
        z = dt1[pl.ds(pix, npx)] * c1 - c2[part] - (pre1[pl.ds(pix, npx)] - m1) * c3[part]
        z = as_rows(z).astype(BF16)
        dz1[pl.ds(row, nrows), :] = z
        g = as_pix(nn(z, wq[...])) + dt3[pl.ds(pix, npx), :, mine]
        (gxb, gxs)[part][pl.ds(pix - (0, geo.pb)[part], npx)] = g
        return carry

    geo.loop(body, [0, 0])


def k_dw_wide(act5, dz6, mids, me, dzs, dwide, dshort):
    dwide[...] = tn(act5[...], dz6[...])
    dshort[...] = tn(mids[...], dzs[me[0]])


def k_dw_stride(me, cols, dz5, dw):
    mine = pl.ds(pl.multiple_of(me[0] * 128, 128), 128)
    z = dz5[:, mine]
    for t in range(9):
        dw[t] = tn(cols[:, t * 512 : (t + 1) * 512], z)


def k_dw_cols(me, size, act, dz, dw):
    mine = pl.ds(pl.multiple_of(me[0] * size, size), size)
    dw[...] = tn(act[...], dz[:, mine])


def k_dw_narrow(me, mid, dz4, dw):
    k_dw_cols(me, 128, mid, dz4, dw)


def k_dw_expand(act2, dz3, dw):
    dw[...] = tn(act2[...], dz3[...])


def k_dw_mix(geo, me, wb, ws, dz2, dw, full):
    mine = pl.ds(pl.multiple_of(me[0] * 64, 64), 64)
    nb, ns = geo.pb * VIEWS, geo.ps * VIEWS
    for r in range(3):
        ob, os = r * geo.hb * VIEWS, r * geo.hs * VIEWS
        full[...] = tn(dz2[0:nb, :], wb[ob : ob + nb, :]) + tn(
            dz2[nb : nb + ns, :], ws[os : os + ns, :]
        )
        dw[r] = full[mine, :]


def k_dw_reduce(me, xs, dz1, dw, full):
    mine = pl.ds(pl.multiple_of(me[0] * 64, 64), 64)
    for j in range(4):
        full[...] = tn(dz1[...], xs[j])
        dw[:, 256 * j : 256 * j + 256] = full[mine, :]


def per_device(
    ni,
    nc,
    x_big,
    x_small,
    cot_big,
    cot_small,
    counts,
    w_reduce,
    w_mix,
    w_expand,
    w_narrow,
    w_stride,
    w_widen,
    w_short,
    gain_mid3,
    shift_mid3,
    gain_out3,
    shift_out3,
    gain_mid4,
    shift_mid4,
    gain_out4,
    shift_out4,
):
    assert nc == 4 and x_big.shape[0] == VIEWS and x_small.shape[0] == VIEWS
    geo = Geo(x_big.shape[1], x_small.shape[1])
    img = lax.axis_index("img")
    q = lax.axis_index("ch").astype(jnp.int32)
    levels = ni.bit_length() - 1
    mine = lax.dynamic_slice_in_dim(counts, img, 1, 0)[0]
    me = jnp.stack([q, mine[0], mine[1]]).astype(jnp.int32)
    per3 = counts[:, 0] * geo.pb + counts[:, 1] * geo.ps
    per4 = counts[:, 0] * geo.qb + counts[:, 1] * geo.qs

    def group_counts(per):
        at = jnp.arange(ni, dtype=jnp.int32)
        out = []
        for k in range(levels):
            own = jnp.sum(jnp.where((at >> k) == (img >> k), per, 0))
            other = jnp.sum(jnp.where((at >> k) == ((img >> k) ^ 1), per, 0))
            out.append((own.astype(F32), other.astype(F32)))
        return out

    cnt3, cnt4 = group_counts(per3), group_counts(per4)
    nf3 = jnp.stack([cnt3[0][0], cnt3[-1][0], cnt3[-1][1]])
    nf4 = jnp.stack([cnt4[0][0], cnt4[-1][0], cnt4[-1][1]])

    def over_img(v, k):
        return lax.ppermute(v, "img", [(i, i ^ (1 << k)) for i in range(ni)])

    def over_ch(v, k):
        return lax.ppermute(v, "ch", [(i, i ^ k) for i in range(nc)])

    def sync_stats(stats, cnt):
        for k in range(levels):
            other = over_img(stats, k)
            if k == levels - 1:
                return stats, other
            na, nb = cnt[k]
            shape = stats.shape
            a = stats.reshape(shape[:-2] + (shape[-2] // 2, 2, shape[-1]))
            b = other.reshape(a.shape)
            ma, mb = a[..., 0, :], b[..., 0, :]
            diff = mb - ma
            mean = (na * ma + nb * mb) / (na + nb)
            square = a[..., 1, :] + b[..., 1, :] + diff * diff * (na * nb / (na + nb))
            stats = jnp.stack([mean, square], axis=-2).reshape(shape)

    def sync_sums(sums):
        for k in range(levels):
            other = over_img(sums, k)
            if k == levels - 1:
                return sums, other
            sums = sums + other

    def quarters(v):
        p1 = over_ch(v, 1)
        p2 = over_ch(v, 2)
        return [v, p1, p2, over_ch(p2, 1)]

    def in_order(pieces):
        full = jnp.stack(pieces)
        return jnp.take(full, jnp.arange(4, dtype=jnp.int32) ^ q, axis=0)

    params = jnp.concatenate(
        [
            v.reshape(-1)
            for v in (
                gain_mid3,
                shift_mid3,
                gain_out3,
                shift_out3,
                gain_mid4,
                shift_mid4,
                gain_out4,
                shift_out4,
            )
        ]
    ).reshape(-1, 128)
    params = in_order(quarters(params)).reshape(4, -1)
    cuts, at = [], 0
    for v in (gain_mid3, shift_mid3, gain_out3, shift_out3, gain_mid4, shift_mid4, gain_out4, shift_out4):
        cuts.append(params[:, at : at + v.size].reshape((4,) + v.shape))
        at += v.size
    gm3, sm3, go3, so3, gm4, sm4, go4, so4 = cuts

    def pair(g, s):
        return jnp.stack([g.reshape(-1), s.reshape(-1)])

    gs1, gs2 = pair(gm3[:, 0], sm3[:, 0]), pair(gm3[:, 1], sm3[:, 1])
    gs3 = pair(go3, so3)
    gs4, gs5 = pair(gm4[:, 0], sm4[:, 0]), pair(gm4[:, 1], sm4[:, 1])
    gs6 = jnp.stack([go4[:, 0], so4[:, 0], go4[:, 1], so4[:, 1]], axis=1)

    def rows_of(v):
        return jnp.transpose(v, (1, 2, 0, 3)).reshape(-1, v.shape[3])

    wr = quarters(w_reduce.T)
    xb, xsm = quarters(rows_of(x_big)), quarters(rows_of(x_small))
    wm = quarters(jnp.transpose(w_mix, (0, 1, 3, 2)).reshape(9, w_mix.shape[3], w_mix.shape[2]))
    we = quarters(w_expand)
    wn = quarters(w_narrow)
    wst = quarters(w_stride.reshape(-1, w_stride.shape[3]))
    wsh = quarters(w_short)
    wwi = quarters(w_widen)
    cb, cs = quarters(rows_of(cot_big)), quarters(rows_of(cot_small))

    m3 = 4 * w_reduce.shape[1]
    c3 = w_reduce.shape[0]
    m4 = w_widen.shape[0]
    c4q = w_widen.shape[1]
    (wt,) = assemble("asm_reduce", me, [(wr, "rows", m3 // 4, (m3, c3))])
    wmix_f, wmix_b = assemble(
        "asm_mix",
        me,
        [
            (wm, "taps_nt", m3 // 4, (3, m3, 3 * m3)),
            (wm, "taps_nn", m3 // 4, (9, m3, m3)),
        ],
    )
    wexp, wnar = assemble(
        "asm_mid",
        me,
        [(we, "cols", c3 // 4, (m3, c3)), (wn, "cols", m4 // 4, (c3, m4))],
    )
    (wstr,) = assemble("asm_stride", me, [(wst, "cols", m4 // 4, (9 * m4, m4))])
    wmix_b = wmix_b.reshape(3, 3 * m3, m3)

    smem = [(me, SMEM)]
    n3, n4 = [(nf3, SMEM)], [(nf4, SMEM)]

    def k(fn):
        return functools.partial(fn, geo)

    hb, hs = geo.hb, geo.hs
    sb4, ss4 = (2, 2, hb // 2, hb // 2, VIEWS, m4), (2, 2, hs // 2, hs // 2, VIEWS, m4)
    wb_shape, ws_shape = ((hb + 2) * hb * VIEWS, 3 * m3), ((hs + 2) * hs * VIEWS, 3 * m3)

    pre1, xs, st = call(
        "reduce",
        k(k_reduce),
        smem + n3 + vm(*xb, *xsm, wt),
        [sds((geo.px, VIEWS, m3)), sds((4, geo.rows, c3 // 4), BF16), sds((2, m3))],
        [pltpu.VMEM((4, m3, c3 // 4), BF16)],
    )
    a1, b1 = sync_stats(st, cnt3)
    pre2, winb, wins, st = call(
        "mix",
        k(k_mix),
        smem + n3 + vm(pre1, a1, b1, gs1, wmix_f),
        [sds((geo.px, VIEWS, m3)), sds(wb_shape, BF16), sds(ws_shape, BF16), sds((2, m3))],
    )
    a2, b2 = sync_stats(st, cnt3)
    pre3, act2, st = call(
        "expand",
        k(k_expand),
        smem + n3 + vm(pre2, a2, b2, gs2, wexp),
        [sds((geo.px, VIEWS, c3)), sds((geo.rows, m3), BF16), sds((2, c3))],
    )
    a3, b3 = sync_stats(st, cnt3)
    pre4b, pre4s, mid, mids, st = call(
        "narrow",
        k(k_narrow),
        smem + n3 + vm(pre3, xs, a3, b3, gs3, wnar),
        [sds(sb4), sds(ss4), sds((geo.rows, c3), BF16), sds((geo.rows4, c3), BF16), sds((2, m4))],
        [pltpu.VMEM((geo.px4, VIEWS, c3), F32)],
    )
    a4, b4 = sync_stats(st, cnt3)
    side, st_side = call(
        "short",
        k(k_short),
        smem + n4 + vm(mids, *wsh),
        [sds((4, geo.px4, VIEWS, c4q)), sds((4, 2, c4q))],
    )
    pre5, cols, st = call(
        "stride",
        k(k_stride),
        smem + n4 + n3 + vm(pre4b, pre4s, a4, b4, gs4, wstr),
        [sds((geo.px4, VIEWS, m4)), sds((geo.rows4, 9 * m4), BF16), sds((2, m4))],
        [pltpu.VMEM(sb4, F32), pltpu.VMEM(ss4, F32)],
    )
    a5, b5 = sync_stats(st, cnt4)
    pre6, act5, st = call(
        "widen",
        k(k_widen),
        smem + n4 + vm(pre5, a5, b5, gs5, *wwi),
        [sds((4, geo.px4, VIEWS, c4q)), sds((geo.rows4, m4), BF16), sds((4, 2, c4q))],
    )
    a6, b6 = sync_stats(jnp.concatenate([st, st_side], axis=1), cnt4)
    out_b, out_s, dt6, sums = call(
        "total",
        k(k_total),
        smem + n4 + vm(pre6, side, a6, b6, gs6, *cb, *cs),
        [
            sds((geo.qb, VIEWS, c4q)),
            sds((geo.qs, VIEWS, c4q)),
            sds((4, geo.px4, VIEWS, c4q)),
            sds((4, 3, c4q)),
        ],
    )
    ga6, gb6 = sync_sums(sums)
    dt5, dz6, dzs, sums = call(
        "back_wide",
        k(k_back_wide),
        smem + n4 + vm(dt6, pre6, side, a6, b6, gs6, ga6, gb6, pre5, a5, b5, gs5, *wwi),
        [
            sds((geo.px4, VIEWS, m4)),
            sds((geo.rows4, c4q), BF16),
            sds((4, geo.rows4, c4q), BF16),
            sds((2, m4)),
        ],
    )
    ga5, gb5 = sync_sums(sums)
    (dms,) = call(
        "back_short", k(k_back_short), smem + vm(dzs, *wsh), [sds((geo.px4, VIEWS, c3))]
    )
    dwide, dshort = call(
        "dw_wide",
        k_dw_wide,
        vm(act5, dz6, mids) + smem + vm(dzs),
        [sds((m4, c4q)), sds((c3, c4q))],
    )
    dt4b, dt4s, dz5, sums = call(
        "back_stride",
        k(k_back_stride),
        smem
        + n4
        + vm(dt5, pre5, a5, b5, gs5, ga5, gb5, pre4b, pre4s, a4, b4, gs4)
        + n3
        + vm(wstr),
        [sds(sb4), sds(ss4), sds((geo.rows4, m4), BF16), sds((2, m4))],
        [pltpu.VMEM((4, geo.rows4, m4), BF16)],
    )
    ga4, gb4 = sync_sums(sums)
    (dstride,) = call("dw_stride", k_dw_stride, smem + vm(cols, dz5), [sds((9, m4, m4 // 4))])
    dt3, dz4, sums = call(
        "back_narrow",
        k(k_back_narrow),
        smem
        + n3
        + vm(dt4b, dt4s, pre4b, pre4s, a4, b4, gs4, ga4, gb4, pre3, xs, a3, b3, gs3, dms, wnar),
        [sds((geo.px, VIEWS, c3)), sds((geo.rows, m4), BF16), sds((2, c3))],
        [pltpu.VMEM((2, hb // 2, 2, VIEWS, c3), F32), pltpu.VMEM((2, hs // 2, 2, VIEWS, c3), F32)],
        limit=56,
    )
    ga3, gb3 = sync_sums(sums)
    (dnarrow,) = call("dw_narrow", k_dw_narrow, smem + vm(mid, dz4), [sds((c3, m4 // 4))])
    dt2, dz3, sums = call(
        "back_expand",
        k(k_back_expand),
        smem + n3 + vm(dt3, pre3, a3, b3, gs3, ga3, gb3, pre2, a2, b2, gs2, wexp),
        [sds((geo.px, VIEWS, m3)), sds((geo.rows, c3 // 4), BF16), sds((2, m3))],
        [
            pltpu.VMEM((2 * hb * VIEWS, c3), BF16),
            pltpu.VMEM((2 * hs * VIEWS, c3), BF16),
        ],
    )
    ga2, gb2 = sync_sums(sums)
    (dexpand,) = call("dw_expand", k_dw_expand, vm(act2, dz3), [sds((m3, c3 // 4))])
    dt1, dz2, sums = call(
        "back_mix",
        k(k_back_mix),
        smem + n3 + vm(dt2, pre2, a2, b2, gs2, ga2, gb2, pre1, a1, b1, gs1, wmix_b),
        [sds((geo.px, VIEWS, m3)), sds((geo.rows, m3), BF16), sds((2, m3))],
        [pltpu.VMEM(wb_shape, BF16), pltpu.VMEM(ws_shape, BF16)],
    )
    ga1, gb1 = sync_sums(sums)
    (dmix,) = call(
        "dw_mix",
        k(k_dw_mix),
        smem + vm(winb, wins, dz2),
        [sds((3, m3 // 4, 3 * m3))],
        [pltpu.VMEM((m3, 3 * m3), F32)],
    )
    gxb, gxs, dz1 = call(
        "back_reduce",
        k(k_back_reduce),
        smem + n3 + vm(dt1, pre1, a1, b1, gs1, ga1, gb1, dt3, wt),
        [
            sds((geo.pb, VIEWS, c3 // 4)),
            sds((geo.ps, VIEWS, c3 // 4)),
            sds((geo.rows, m3), BF16),
        ],
        [pltpu.VMEM((m3, c3 // 4), BF16)],
    )
    (dreduce,) = call(
        "dw_reduce",
        k_dw_reduce,
        smem + vm(xs, dz1),
        [sds((m3 // 4, c3))],
        [pltpu.VMEM((m3, c3 // 4), F32)],
    )
    dwide, dshort = lax.psum((dwide, dshort), "img")
    dstride = lax.psum(dstride, "img")
    dnarrow, dexpand, dmix, dreduce = lax.psum((dnarrow, dexpand, dmix, dreduce), "img")

    def views_first(v, side):
        return jnp.transpose(v.reshape(side, side, VIEWS, v.shape[2]), (2, 0, 1, 3))

    def own(v):
        n = v.shape[0] // 4
        return lax.dynamic_slice_in_dim(v, q * n, n, 0)

    t1, t2, t3 = ga1 + gb1, ga2 + gb2, ga3 + gb3
    t4, t5 = ga4 + gb4, ga5 + gb5
    t6 = lax.dynamic_index_in_dim(ga6 + gb6, q, 0, keepdims=False)
    return (
        views_first(out_b, hb // 2),
        views_first(out_s, hs // 2),
        views_first(gxb, hb),
        views_first(gxs, hs),
        dreduce.T,
        jnp.transpose(dmix.reshape(3, m3 // 4, 3, m3), (0, 2, 3, 1)),
        dexpand,
        dnarrow,
        dstride.reshape(3, 3, m4, m4 // 4),
        dwide,
        dshort,
        jnp.stack([own(t1[1]), own(t2[1])]),
        jnp.stack([own(t1[0]), own(t2[0])]),
        own(t3[1]),
        own(t3[0]),
        jnp.stack([own(t4[1]), own(t5[1])]),
        jnp.stack([own(t4[0]), own(t5[0])]),
        jnp.stack([t6[1], t6[2]]),
        jnp.stack([t6[0], t6[0]]),
    )


def solution(mesh):
    act = P("img", None, None, "ch")
    flat, taps, vec = P(None, "ch"), P(None, None, None, "ch"), P("ch")
    in_specs = (act,) * 4 + (P(), flat, taps, flat, flat, taps, flat, flat)
    in_specs += (flat, flat, vec, vec, flat, flat, flat, flat)
    out_specs = (act,) * 4 + (flat, taps, flat, flat, taps, flat, flat)
    out_specs += (flat, flat, vec, vec, flat, flat, flat, flat)
    return jax.shard_map(
        functools.partial(per_device, mesh.shape["img"], mesh.shape["ch"]),
        mesh=mesh,
        in_specs=in_specs,
        out_specs=out_specs,
        check_vma=False,
    )
```

```python
import functools
import math

import jax
import jax.numpy as jnp
from jax import lax
from jax.experimental import pallas as pl
from jax.experimental.pallas import tpu as pltpu
from jax.sharding import PartitionSpec as P

EPS = 1e-05
G0 = 0.7978845608028654
G1 = G0 * 0.044715
F32 = jnp.float32
BF16 = jnp.bfloat16
VIEWS = 8
AHEAD = 3

ANY = pl.BlockSpec(memory_space=pl.ANY)
HBM = pl.BlockSpec(memory_space=pltpu.HBM)
VMEM = pl.BlockSpec(memory_space=pltpu.VMEM)
SMEM = pl.BlockSpec(memory_space=pltpu.SMEM)


def sds(shape, dtype=F32):
    return jax.ShapeDtypeStruct(tuple(shape), dtype)


class Flow:
    WHOLE = ("w", "all", "part", "w_in", "w_ahead", "w_back")

    def __init__(self, kind, base=0, shape=None):
        self.kind, self.base, self.shape = kind, base, shape

    def keys(self, geo, shape):
        parts = (0, 1)
        if self.kind in ("big", "big_px"):
            parts = (0,)
        if self.kind in ("small", "small_px"):
            parts = (1,)
        if self.kind not in ("lead",) + self.WHOLE:
            return [(part, n) for part in parts for n in range(len(geo.groups[part]))]
        if self.kind == "lead":
            return list(range(shape[0]))
        return [None]

    def buffer(self, geo, shapes, dtype):
        if self.kind == "x":
            return pltpu.VMEM((4, geo.rows, shapes[0][1]), dtype)
        if self.kind == "w":
            return pltpu.VMEM(self.shape, dtype)
        if self.kind == "part":
            return pltpu.VMEM(self.shape, dtype)
        c = shapes[0][-1]
        if self.kind.startswith("w_"):
            return pltpu.VMEM({"w_in": (4, c, c), "w_ahead": (3, c, 3 * c), "w_back": (9, c, c)}[self.kind], dtype)
        return pltpu.VMEM(tuple(shapes[0]), dtype)

    def pairs(self, geo, q, hbm, buf, key):
        if self.kind == "w":
            rows, n = buf.shape[0], buf.shape[1] // 4
            found = []
            for p in range(4):
                for b in range(n // 128):
                    at = pl.ds(pl.multiple_of((q ^ p) * n + 128 * b, 128), 128)
                    found.append((hbm[p].at[pl.ds(self.base + rows * b, rows)], buf.at[:, at]))
            return found
        if self.kind.startswith("w_"):
            c = buf.shape[1]
            n = c // 4
            found = []
            for p in range(4):
                at = pl.ds(pl.multiple_of((q ^ p) * n, n), n)
                for t in range(4 if self.kind == "w_in" else 9):
                    src = hbm[p].at[pl.ds(self.base + n * t, n)]
                    if self.kind == "w_ahead":
                        found.append((src, buf.at[t // 3, at, pl.ds(t % 3 * c, c)]))
                    else:
                        found.append((src, buf.at[t, at]))
            return found
        if self.kind == "part":
            return [(hbm[0].at[pl.ds(self.base, buf.shape[0])], buf)]
        if key is None:
            return [(hbm[0], buf)]
        if self.kind == "lead":
            return [(hbm[0].at[key], buf.at[key])]
        part, group = key
        i, end = geo.groups[part][group]
        pix, npx, row, nrows = geo.step(part, i)
        npx, nrows, first = npx * (end - i), nrows * (end - i), pix - geo.parts[part][1]
        if self.kind == "px":
            at = pl.ds(pix, npx)
        elif self.kind == "rows":
            at = pl.ds(row, nrows)
        elif self.kind in ("big_px", "small_px"):
            at = pl.ds(first, npx)
        elif self.kind == "x":
            local = pl.ds(first * VIEWS, nrows)
            return [
                (hbm[4 * part + p].at[local], buf.at[q ^ p, pl.ds(row, nrows)]) for p in range(4)
            ]
        else:
            at = pl.ds(i, end - i)
            return [(hbm[0].at[:, :, at], buf.at[:, :, at])]
        return [(hbm[0].at[at], buf.at[at])]


class Moves:
    def __init__(self, geo, q):
        self.geo, self.q, self.flows, self.kept = geo, q, [], []

    def add(self, flow, hbm, buf, sem, inward):
        self.flows.append((flow, hbm, buf, sem, inward))

    def copies(self, entry, key):
        flow, hbm, buf, sem, inward = entry
        if flow.kind in flow.WHOLE:
            at = 0
        elif flow.kind == "lead":
            at = key
        elif flow.kind in ("px", "rows", "x"):
            at = (0, len(self.geo.groups[0]))[key[0]] + key[1]
        else:
            at = key[1]
        pairs = flow.pairs(self.geo, self.q, hbm, buf, key)
        return [
            pltpu.make_async_copy(*((a, b) if inward else (b, a)), sem.at[n, at])
            for n, (a, b) in enumerate(pairs)
        ]

    def entries(self, inward, key):
        for entry in self.flows:
            flow = entry[0]
            if entry[4] != inward:
                continue
            if key is None:
                fits = flow.kind in flow.WHOLE
            elif isinstance(key, int):
                fits = flow.kind == "lead"
            else:
                kinds = ("px", "rows", "x") + (("big", "big_px"), ("small", "small_px"))[key[0]]
                fits = flow.kind in kinds
            if fits:
                yield entry

    def start(self, inward, key):
        for entry in self.entries(inward, key):
            for c in self.copies(entry, key):
                c.start()

    def wait(self, inward, key):
        for entry in self.entries(inward, key):
            for c in self.copies(entry, key):
                c.wait()

    def begin(self):
        self.order = [(part, n) for part in range(2) for n in range(len(self.geo.groups[part]))]
        self.start(True, self.order[0])
        self.start(True, None)
        for key in self.order[1:AHEAD]:
            self.start(True, key)
        leads = [e[1][0].shape[0] for e in self.flows if e[4] and e[0].kind == "lead"]
        for n in range(max(leads, default=0)):
            self.start(True, n)
        streams = any(e[4] and e[0].kind not in ("lead",) + Flow.WHOLE for e in self.flows)
        if not streams:
            for c in self.kept:
                c.start()

    def ready(self):
        self.wait(True, None)

    def arrive(self, *key):
        if len(key) == 1:
            self.wait(True, key[0])
            return
        self.wait(True, key)
        at = self.order.index(key)
        if at + AHEAD < len(self.order):
            self.start(True, self.order[at + AHEAD])
        streams = any(e[4] and e[0].kind not in ("lead",) + Flow.WHOLE for e in self.flows)
        if at == 0 and streams:
            for c in self.kept:
                c.start()

    def leave(self, *key):
        self.start(False, key if len(key) > 1 else key[0])

    def send(self, *refs):
        for entry in self.entries(False, None):
            if any(entry[2] is r for r in refs):
                for c in self.copies(entry, None):
                    c.start()

    def finish(self):
        for entry in self.flows:
            if not entry[4]:
                shape = entry[1][0].shape
                for key in entry[0].keys(self.geo, shape):
                    for c in self.copies(entry, key):
                        c.wait()
        for c in self.kept:
            c.wait()


class Keep:
    kind = "keep"

    def __init__(self, source):
        self.source = source


def fast(shape, dtype=F32):
    return pltpu.VMEM(tuple(shape), dtype)


def scoped_bytes(v):
    return math.prod(v.shape) * jnp.dtype(v.dtype).itemsize


def in_hbm(v):
    return pltpu.with_memory_space_constraint(v, pltpu.HBM)


def call(name, kernel, ins, outs, scratch=(), cost=None, order=False, geo=None, slack=14):
    if order:
        inner, n_in, n_out = kernel, len(ins), len(outs)

        def kernel(*refs):
            rest = refs[n_in:]
            return inner(*refs[:n_in], *rest[n_out:], *rest[:n_out])

    outs = [o if isinstance(o, tuple) else (o, VMEM) for o in outs]
    arrays, specs, moved = [], [], []
    for a, spec in ins:
        group = a if isinstance(a, list) else [a]
        flow = isinstance(spec, Flow)
        arrays += [in_hbm(v) for v in group] if flow else group
        specs += [HBM if flow else spec] * len(group)
        moved.append((spec if flow else None, len(group), [v.shape for v in group], group[0].dtype))
    out_shapes, out_specs = [], []
    for shape, spec in outs:
        flow = isinstance(spec, (Flow, Keep))
        out_shapes.append(pltpu.HBM(shape.shape, shape.dtype) if flow else shape)
        out_specs.append(HBM if flow else spec)
        moved.append((spec if flow else None, 1, [shape.shape], shape.dtype))
    extra = []
    for flow, _, shapes, dtype in moved:
        if isinstance(flow, Keep):
            extra += [pltpu.SemaphoreType.DMA((1,))]
        elif flow:
            keys = len(flow.keys(geo, shapes[0]))
            copies = {"x": 4, "w": 4, "w_in": 16, "w_ahead": 36, "w_back": 36}.get(flow.kind, 1)
            if flow.kind == "w":
                copies = flow.shape[1] // 128
            extra += [flow.buffer(geo, shapes, dtype), pltpu.SemaphoreType.DMA((copies, keys))]
    body = kernel
    if extra:

        def body(*refs):
            n_io = sum(n for _, n, _, _ in moved)
            given, own, rest = list(refs[:n_io]), refs[n_io : n_io + len(scratch)], refs[n_io + len(scratch) :]
            rest = list(rest)
            moves = Moves(geo, given[0][0])
            args = []
            for n, (flow, count, _, _) in enumerate(moved):
                group, given = given[:count], given[count:]
                if not flow:
                    args += group
                    continue
                if isinstance(flow, Keep):
                    moves.kept.append(pltpu.make_async_copy(args[flow.source], group[0], rest[0].at[0]))
                    rest = rest[1:]
                    continue
                buf, sem = rest[:2]
                rest = rest[2:]
                moves.add(flow, group, buf, sem, n < len(ins))
                args.append(buf)
            moves.begin()
            kernel(moves, *args, *own)
            moves.finish()

    scratch = list(scratch)
    def held(v):
        pinned = "vmem" in str(getattr(v, "memory_space", "")).lower()
        return 0 if pinned else scoped_bytes(v)

    need = sum(held(jax.typeof(a)) for a, spec in zip(arrays, specs) if spec is VMEM)
    need += sum(held(o) for o, spec in zip(out_shapes, out_specs) if spec is VMEM)
    need += sum(
        scoped_bytes(v)
        for v in scratch + extra
        if getattr(v, "memory_space", None) == pltpu.VMEM
    )
    result = pl.pallas_call(
        body,
        out_shape=out_shapes,
        in_specs=specs,
        out_specs=out_specs,
        scratch_shapes=scratch + extra,
        compiler_params=pltpu.CompilerParams(vmem_limit_bytes=need + need // 16 + (slack << 20)),
        cost_estimate=cost,
        name=name,
    )(*arrays)
    return list(result)


def vm(*arrays):
    return [(a, VMEM) for a in arrays]


def nn(a, b):
    return lax.dot_general(a, b, (((1,), (0,)), ((), ())), preferred_element_type=F32)


def nt(a, b):
    return lax.dot_general(a, b, (((1,), (1,)), ((), ())), preferred_element_type=F32)


def tn(a, b):
    return lax.dot_general(a, b, (((0,), (0,)), ((), ())), preferred_element_type=F32)


def gelu(t):
    half = 0.5 * t
    return half + half * jnp.tanh(t * (G0 + G1 * (t * t)))


def gelu_slope(t):
    sq = t * t
    th = jnp.tanh(t * (G0 + G1 * sq))
    return 0.5 * (1.0 + th) + (0.5 * t) * (1.0 - th * th) * (G0 + (3.0 * G1) * sq)


def live_rows(count, chans):
    return (lax.broadcasted_iota(jnp.int32, (VIEWS, chans), 0) < count).astype(F32)


def rows_sum(v):
    return jnp.sum(v, axis=0, keepdims=True)


def merged(sa, sb, na, nb):
    total = na + nb
    mean = (na * sa[0:1] + nb * sb[0:1]) / total
    diff = sb[0:1] - sa[0:1]
    square = sa[1:2] + sb[1:2] + diff * diff * (na * nb / total)
    return mean, lax.rsqrt(square / total + EPS)


def as_rows(v):
    return v.reshape(v.shape[0] * v.shape[1], v.shape[2])


def as_pix_rows(v):
    return v.reshape(v.shape[0] * v.shape[1], VIEWS, v.shape[3])


def as_pix(v):
    return v.reshape(v.shape[0] // VIEWS, VIEWS, v.shape[1])


class Geo:
    def __init__(self, hb, hs):
        self.hb, self.hs = hb, hs
        self.pb, self.ps = hb * hb, hs * hs
        self.px = self.pb + self.ps
        self.rows = self.px * VIEWS
        self.qb, self.qs = self.pb // 4, self.ps // 4
        self.px4 = self.qb + self.qs
        self.rows4 = self.px4 * VIEWS
        self.parts = ((hb, 0), (hs, self.pb))
        self.groups = [self.cuts(hb // 2, 1), self.cuts(hs // 2, 2)]

    @staticmethod
    def cuts(steps, first):
        at = sorted({0, steps} | set(range(first, steps, 2)))
        return list(zip(at[:-1], at[1:]))

    @staticmethod
    def aligned(n):
        return n if isinstance(n, int) else pl.multiple_of(n, 16)

    def step(self, part, i):
        side, start = self.parts[part]
        npx = 2 * side
        return start + i * npx, npx, self.aligned((start + i * npx) * VIEWS), npx * VIEWS

    def loop(self, body, carries, arrive=None, leave=None):
        out = []
        for part in range(2):

            def run(i, carry, part=part):
                for n, (lo, hi) in enumerate(self.groups[part]):
                    if arrive:
                        pl.when(i == lo)(functools.partial(arrive.arrive, part, n))
                carry = body(part, i, *self.step(part, i), carry)
                for n, (lo, hi) in enumerate(self.groups[part]):
                    if leave:
                        pl.when(i == hi - 1)(functools.partial(leave.leave, part, n))
                return carry

            out.append(lax.fori_loop(0, self.groups[part][-1][1], run, carries[part]))
        return out


def finish_stats(geo, ref, sums, lives, count, out, quarter=None):
    mean = (rows_sum(sums[0] * lives[0]) + rows_sum(sums[1] * lives[1])) / count

    def body(part, i, pix, npx, row, nrows, carry):
        dev = ref[pl.ds(pix, npx)] - mean
        return carry + jnp.sum(dev * dev, axis=0)

    zero = jnp.zeros(sums[0].shape, F32)
    sq = geo.loop(body, [zero, zero])
    out[0:1] = mean
    out[1:2] = rows_sum(sq[0] * lives[0]) + rows_sum(sq[1] * lives[1])


def block_stats(geo, value, lives, count):
    big, small = value[: geo.qb], value[geo.qb :]
    mean = (
        rows_sum(jnp.sum(big, axis=0) * lives[0]) + rows_sum(jnp.sum(small, axis=0) * lives[1])
    ) / count
    db, ds = big - mean, small - mean
    square = rows_sum(jnp.sum(db * db, axis=0) * lives[0]) + rows_sum(
        jnp.sum(ds * ds, axis=0) * lives[1]
    )
    return mean, square


def k_reduce(geo, io, me, nf, xs, wt, pre, stats):
    io.ready()
    chans = wt.shape[1]
    lives = [live_rows(me[1], chans), live_rows(me[2], chans)]

    def body(part, i, pix, npx, row, nrows, carry):
        acc = None
        for j in range(4):
            d = nt(xs[j, pl.ds(row, nrows), :], wt[j])
            acc = d if acc is None else acc + d
        z = as_pix(acc)
        pre[pl.ds(pix, npx)] = z
        return carry + jnp.sum(z, axis=0)

    zero = jnp.zeros((VIEWS, chans), F32)
    sums = geo.loop(body, [zero, zero], io, io)
    finish_stats(geo, pre, sums, lives, nf[0], stats)


def k_counts(ni, sizes, counts, me, nf3, cnt3, nf4, cnt4):
    img = lax.axis_index("img")
    levels = ni.bit_length() - 1
    me[0] = lax.axis_index("ch").astype(jnp.int32)
    me[1] = counts[img, 0]
    me[2] = counts[img, 1]
    me[3] = img
    for (big, small), nf, cnt in zip(sizes, (nf3, nf4), (cnt3, cnt4)):

        def group(shift, index):
            def add(i, total):
                at = index * (1 << shift) + i
                return total + counts[at, 0] * big + counts[at, 1] * small

            return lax.fori_loop(0, 1 << shift, add, jnp.int32(0)).astype(F32)

        nf[0] = group(0, img)
        for m in range(2):
            nf[1 + m] = group(levels - 1, (img >> (levels - 1)) ^ m)
        row, k = 0, 0
        while k < levels - 1:
            bits = 2 if k == 0 else 1
            for m in range(8):
                cnt[row + m] = group(k, (img >> k) ^ m) if m < 1 << bits else jnp.float32(0.0)
            row, k = row + 8, k + bits


def k_merge(first, n, cnt, *refs):
    arrays, out = refs[:n], refs[n]
    for at in range(0, out.shape[-2], 2):
        mean_at, sq_at = (..., slice(at, at + 1), slice(None)), (..., slice(at + 1, at + 2), slice(None))
        groups = [(cnt[first + m], a[mean_at], a[sq_at]) for m, a in enumerate(arrays)]
        while len(groups) > 1:
            pairs = []
            for (na, ma, qa), (nb, mb, qb) in zip(groups[::2], groups[1::2]):
                total = na + nb
                diff = mb - ma
                pairs.append(
                    (total, (na * ma + nb * mb) / total, qa + qb + diff * diff * (na * nb / total))
                )
            groups = pairs
        out[mean_at], out[sq_at] = groups[0][1], groups[0][2]


def k_add(n, *refs):
    values = [r[...] for r in refs[:n]]
    while len(values) > 1:
        values = [a + b for a, b in zip(values[::2], values[1::2])]
    refs[n][...] = values[0]


def side_shift(v, by):
    zero = jnp.zeros((v.shape[0], 1) + v.shape[2:], v.dtype)
    if by > 0:
        return jnp.concatenate([zero, v[:, :-1]], axis=1)
    return jnp.concatenate([v[:, 1:], zero], axis=1)


def store_shifted(buf, row, nrows, side, v, order):
    img = v.reshape(2, side, VIEWS, v.shape[-1])
    chans = v.shape[-1]
    forms = [side_shift(img, 1), img, side_shift(img, -1)]
    for lane, k in enumerate(order):
        flat = forms[k].reshape(nrows, chans).astype(BF16)
        buf[pl.ds(row, nrows), lane * chans : (lane + 1) * chans] = flat


def put_phases(ref, i, v):
    for k in range(4):
        ref[k // 2, k % 2, i] = v[k // 2, :, k % 2]


def get_phases(ref, i):
    rows = [jnp.stack([ref[r, 0, i], ref[r, 1, i]], axis=1) for r in range(2)]
    return jnp.stack(rows)


def zero_edges(buf, edge):
    total = buf.shape[0]
    buf[0:edge, :] = jnp.zeros((edge, buf.shape[1]), BF16)
    buf[total - edge : total, :] = jnp.zeros((edge, buf.shape[1]), BF16)


def k_mix(geo, io, me, nf, pre1, sa, sb, gs, w, pre2, wb, ws, stats):
    chans = pre1.shape[-1]
    lives = [live_rows(me[1], chans), live_rows(me[2], chans)]
    mean, inv = merged(sa[...], sb[...], nf[1], nf[2])
    scale, shift = gs[0:1] * inv, gs[1:2]
    bufs = (wb, ws)
    for part, (side, _) in enumerate(geo.parts):
        zero_edges(bufs[part], side * VIEWS)

    def act(part, i, pix, npx, row, nrows, carry):
        a = gelu((pre1[pl.ds(pix, npx)] - mean) * scale + shift)
        side = geo.parts[part][0]
        at = pl.multiple_of(side * VIEWS + i * nrows, 16)
        store_shifted(bufs[part], at, nrows, side, a, (0, 1, 2))
        return carry

    geo.loop(act, [0, 0], io)
    io.send(wb, ws)
    io.ready()

    def dots(part, i, pix, npx, row, nrows, carry):
        acc = None
        for r in range(3):
            at = pl.multiple_of(i * nrows + r * (nrows // 2), 16)
            d = nt(bufs[part][pl.ds(at, nrows), :], w[r])
            acc = d if acc is None else acc + d
        z = as_pix(acc)
        pre2[pl.ds(pix, npx)] = z
        return carry + jnp.sum(z, axis=0)

    zero = jnp.zeros((VIEWS, chans), F32)
    sums = geo.loop(dots, [zero, zero], None, io)
    finish_stats(geo, pre2, sums, lives, nf[0], stats)


def k_expand(geo, io, me, nf, pre2, sa, sb, gs, w, pre3, act2, stats):
    chans = w.shape[1]
    lives = [live_rows(me[1], chans), live_rows(me[2], chans)]
    mean, inv = merged(sa[...], sb[...], nf[1], nf[2])
    scale, shift = gs[0:1] * inv, gs[1:2]

    def body(part, i, pix, npx, row, nrows, carry):
        a = as_rows(gelu((pre2[pl.ds(pix, npx)] - mean) * scale + shift)).astype(BF16)
        act2[pl.ds(row, nrows), :] = a
        z = as_pix(nn(a, w[...]))
        pre3[pl.ds(pix, npx)] = z
        return carry + jnp.sum(z, axis=0)

    io.ready()
    zero = jnp.zeros((VIEWS, chans), F32)
    sums = geo.loop(body, [zero, zero], io, io)
    finish_stats(geo, pre3, sums, lives, nf[0], stats)


def k_narrow(geo, io, me, nf, pre3, xs, sa, sb, gs, w, pre4b, pre4s, mid, mids, stats, mid_even):
    chans = w.shape[1]
    lives = [live_rows(me[1], chans), live_rows(me[2], chans)]
    mean, inv = merged(sa[...], sb[...], nf[1], nf[2])
    scale, shift = gs[0:1] * inv, gs[1:2]
    pre4 = (pre4b, pre4s)

    def body(part, i, pix, npx, row, nrows, carry):
        side = geo.parts[part][0]
        half = side // 2
        for j in range(4):
            at = slice(256 * j, 256 * j + 256)
            dev = pre3[pl.ds(pix, npx), :, at] - mean[:, at]
            x = as_pix(xs[j, pl.ds(row, nrows), :].astype(F32))
            a = gelu(dev * scale[:, at] + shift[:, at] + x)
            mid[pl.ds(row, nrows), at] = as_rows(a).astype(BF16)
            even = a.reshape(2, half, 2, VIEWS, 256)[0, :, 0]
            mid_even[pl.ds((0, geo.qb)[part] + half * i, half), :, at] = even
        z = nn(mid[pl.ds(row, nrows), :], w[...])
        put_phases(pre4[part], i, z.reshape(2, half, 2, VIEWS, chans))
        return carry + jnp.sum(as_pix(z), axis=0)

    io.ready()
    zero = jnp.zeros((VIEWS, chans), F32)
    sums = geo.loop(body, [zero, zero], io, io)
    mean4 = (rows_sum(sums[0] * lives[0]) + rows_sum(sums[1] * lives[1])) / nf[0]
    mids[...] = as_rows(mid_even[...]).astype(BF16)
    io.send(mids)
    sq = []
    for part in range(2):

        def dev2(i, carry, part=part):
            for k in range(4):
                d = pre4[part][k // 2, k % 2, i] - mean4
                carry = carry + jnp.sum(d * d, axis=0)
            return carry

        sq.append(lax.fori_loop(0, geo.parts[part][0] // 2, dev2, zero))
    stats[0:1] = mean4
    stats[1:2] = rows_sum(sq[0] * lives[0]) + rows_sum(sq[1] * lives[1])


def k_short(geo, io, me, nf, mids, w0, w1, side, stats):
    io.ready()
    chans = w0.shape[1]
    lives = [live_rows(me[1], chans), live_rows(me[2], chans)]
    for j, w in enumerate((w0, w1)):
        z = as_pix(nn(mids[...], w[...]))
        side[j] = z
        io.leave(j)
        mean, square = block_stats(geo, z, lives, nf[0])
        stats[j] = jnp.concatenate([mean, square], axis=0)


def k_stride(geo, io, me, nf, n4, pre4b, pre4s, sa, sb, gs, w, pre5, cols, stats, sb_act, ss_act):
    chans = pre4b.shape[-1]
    lives = [live_rows(me[1], chans), live_rows(me[2], chans)]
    mean, inv = merged(sa[...], sb[...], n4[1], n4[2])
    scale, shift = gs[0:1] * inv, gs[1:2]
    srcs, dsts = (pre4b, pre4s), (sb_act, ss_act)
    for part in range(2):

        def act(i, carry, part=part):
            for k in range(4):
                at = (k // 2, k % 2, i)
                dsts[part][at] = gelu((srcs[part][at] - mean) * scale + shift)
            return carry

        lax.fori_loop(0, geo.parts[part][0] // 2, act, 0)
    for r in range(3):
        for c in range(3):
            flats = []
            for part in range(2):
                half = geo.parts[part][0] // 2
                v = dsts[part][(r + 1) % 2, (c + 1) % 2]
                if c == 0:
                    v = side_shift(v, 1)
                if r == 0:
                    v = jnp.concatenate([jnp.zeros((1,) + v.shape[1:], F32), v[:-1]], axis=0)
                flats.append(v.reshape(half * half * VIEWS, chans))
            t = 3 * r + c
            cols[:, t * chans : (t + 1) * chans] = jnp.concatenate(flats, axis=0).astype(BF16)
    io.send(cols)
    io.ready()
    z = as_pix(nn(cols[...], w[...]))
    pre5[...] = z
    m5, s5 = block_stats(geo, z, lives, nf[0])
    stats[0:1] = m5
    stats[1:2] = s5


def k_widen(geo, io, me, nf, pre5, sa, sb, gs, w0, w1, st_side, pre6, act5, stats):
    chans = w0.shape[1]
    lives = [live_rows(me[1], chans), live_rows(me[2], chans)]
    mean, inv = merged(sa[...], sb[...], nf[1], nf[2])
    scale, shift = gs[0:1] * inv, gs[1:2]
    act5[...] = as_rows(gelu((pre5[...] - mean) * scale + shift)).astype(BF16)
    io.ready()
    for j, w in enumerate((w0, w1)):
        z = as_pix(nn(act5[...], w[...]))
        pre6[j] = z
        io.leave(j)
        m6, s6 = block_stats(geo, z, lives, nf[0])
        stats[j] = jnp.concatenate([m6, s6, st_side[j]], axis=0)


def k_total(geo, io, me, nf, pre6, side, sa, sb, gs, cb0, cb1, cs0, cs1, out_b, out_s, dt, sums):
    chans = pre6.shape[-1]
    lives = [live_rows(me[1], chans), live_rows(me[2], chans)]
    cots = ((cb0, cb1), (cs0, cs1))
    spans = ((0, geo.qb), (geo.qb, geo.px4))
    outs = (out_b, out_s)
    io.ready()
    for j in range(2):
        io.arrive(j)
        a, b, g = sa[j], sb[j], gs[j]
        m6, r6 = merged(a[0:2], b[0:2], nf[1], nf[2])
        ms, rs = merged(a[2:4], b[2:4], nf[1], nf[2])
        acc = [None, None, None]
        for part, (lo, hi) in enumerate(spans):
            d6 = pre6[j, lo:hi] - m6
            dd = side[j, lo:hi] - ms
            total = d6 * (g[0:1] * r6) + g[1:2] + (dd * (g[2:3] * rs) + g[3:4])
            live = lives[part]
            if j == 0:
                outs[part][...] = gelu(total) * live
            grad = gelu_slope(total) * (as_pix(cots[part][j][...].astype(F32)) * live)
            dt[j, lo:hi] = grad
            terms = [jnp.sum(v, axis=0) for v in (grad, grad * d6, grad * dd)]
            acc = [t if s is None else s + t for s, t in zip(acc, terms)]
        io.leave(j)
        if j == 0:
            io.send(out_b, out_s)
        sums[j] = jnp.concatenate(
            [rows_sum(acc[0]), rows_sum(acc[1]) * r6, rows_sum(acc[2]) * rs], axis=0
        )


def back_coefs(lives, s1, s2, inv, gain, count):
    c1 = gain * inv
    c2 = [live * (c1 * s1 / count) for live in lives]
    c3 = [live * (c1 * inv * s2 / count) for live in lives]
    return c1, c2, c3


def k_back_wide(geo, io, me, nf, dt, pre6, side, sa, sb, gs, ga, gb, w0, w1, part5, dz6, dzs, tot):
    chans = pre6.shape[-1]
    lives = [live_rows(me[1], chans), live_rows(me[2], chans)]
    total = nf[1] + nf[2]
    spans = ((0, geo.qb), (geo.qb, geo.px4))
    acc = None
    io.ready()
    for j, w in enumerate((w0, w1)):
        io.arrive(j)
        a, b, g = sa[j], sb[j], gs[j]
        s = ga[j] + gb[j]
        tot[j] = s
        m6, r6 = merged(a[0:2], b[0:2], nf[1], nf[2])
        ms, rs = merged(a[2:4], b[2:4], nf[1], nf[2])
        k1, k2, k3 = back_coefs(lives, s[0:1], s[1:2], r6, g[0:1], total)
        h1, h2, h3 = back_coefs(lives, s[0:1], s[2:3], rs, g[2:3], total)
        main, short = [], []
        for part, (lo, hi) in enumerate(spans):
            grad = dt[j, lo:hi]
            main.append(grad * k1 - k2[part] - (pre6[j, lo:hi] - m6) * k3[part])
            short.append(grad * h1 - h2[part] - (side[j, lo:hi] - ms) * h3[part])
        z6 = as_rows(jnp.concatenate(main, axis=0)).astype(BF16)
        dzs[j] = as_rows(jnp.concatenate(short, axis=0)).astype(BF16)
        io.leave(j)
        if j == 0:
            dz6[...] = z6
        d = nt(z6, w[...])
        acc = d if acc is None else acc + d
    part5[...] = as_pix(acc)


def k_back_act5(nf, mine, other, pre5, sa5, sb5, gs5, dt5, sums5):
    m5, r5 = merged(sa5[...], sb5[...], nf[1], nf[2])
    dev = pre5[...] - m5
    grad = gelu_slope(dev * (gs5[0:1] * r5) + gs5[1:2]) * (mine[...] + other[...])
    dt5[...] = grad
    sums5[0:1] = rows_sum(jnp.sum(grad, axis=0))
    sums5[1:2] = rows_sum(jnp.sum(grad * dev, axis=0)) * r5


def k_back_short(io, me, dzs, w0, w1, dms):
    io.ready()
    acc = None
    for j, w in enumerate((w0, w1)):
        d = nt(dzs[j], w[...])
        acc = d if acc is None else acc + d
    dms[...] = as_pix(acc).astype(BF16)


def k_back_stride(geo, io, me, nf, dt5, pre5, sa5, sb5, gs5, ga, gb, pre4b, pre4s, sa4, sb4, gs4, n4, w, dt4b, dt4s, dz5, sums4, tot, shifts):
    chans = pre5.shape[-1]
    lives = [live_rows(me[1], chans), live_rows(me[2], chans)]
    s = ga[...] + gb[...]
    tot[...] = s
    m5, r5 = merged(sa5[...], sb5[...], nf[1], nf[2])
    c1, c2, c3 = back_coefs(lives, s[0:1], s[1:2], r5, gs5[0:1], nf[1] + nf[2])
    spans = ((0, geo.qb), (geo.qb, geo.px4))
    imgs = []
    for part, (lo, hi) in enumerate(spans):
        half = geo.parts[part][0] // 2
        z = dt5[lo:hi] * c1 - c2[part] - (pre5[lo:hi] - m5) * c3[part]
        imgs.append(z.reshape(half, half, VIEWS, chans))

    def flat(moved):
        return jnp.concatenate([v.reshape(-1, chans) for v in moved], axis=0).astype(BF16)

    def up(v):
        return jnp.concatenate([v[1:], jnp.zeros((1,) + v.shape[1:], F32)], axis=0)

    shifts[0] = flat(imgs)
    dz5[...] = shifts[0]
    shifts[1] = flat([side_shift(v, -1) for v in imgs])
    shifts[2] = flat([up(v) for v in imgs])
    shifts[3] = flat([up(side_shift(v, -1)) for v in imgs])
    m4, r4 = merged(sa4[...], sb4[...], n4[1], n4[2])
    scale, off = gs4[0:1] * r4, gs4[1:2]
    io.ready()
    plan = {
        (0, 0): ((0, 4),),
        (0, 1): ((0, 5), (1, 3)),
        (1, 0): ((0, 7), (2, 1)),
        (1, 1): ((0, 8), (1, 6), (2, 2), (3, 0)),
    }
    t1, t2 = jnp.zeros((VIEWS, chans), F32), jnp.zeros((VIEWS, chans), F32)
    for (rp, cp), terms in plan.items():
        acc = None
        for k, t in terms:
            d = nt(shifts[k], w[t * chans : (t + 1) * chans, :])
            acc = d if acc is None else acc + d
        for part, (lo, hi) in enumerate(spans):
            half = geo.parts[part][0] // 2
            d = acc[lo * VIEWS : hi * VIEWS].reshape(half, half, VIEWS, chans)
            dev = (pre4b, pre4s)[part][rp, cp] - m4
            grad = gelu_slope(dev * scale + off) * d
            (dt4b, dt4s)[part][rp, cp] = grad
            t1 = t1 + jnp.sum(grad, axis=(0, 1))
            t2 = t2 + jnp.sum(grad * dev, axis=(0, 1))
    io.send(dt4b, dt4s)
    sums4[0:1] = rows_sum(t1)
    sums4[1:2] = rows_sum(t2) * r4


def k_back_narrow(geo, io, me, nf, dt4b, dt4s, pre4b, pre4s, sa4, sb4, gs4, ga, gb, pre3, xs, sa3, sb3, gs3, dms, dmo, w, dt3, dz4, sums3, tot):
    chans = w.shape[1]
    wide = w.shape[0]
    lives = [live_rows(me[1], chans), live_rows(me[2], chans)]
    s = ga[...] + gb[...]
    tot[...] = s
    m4, r4 = merged(sa4[...], sb4[...], nf[1], nf[2])
    c1, c2, c3 = back_coefs(lives, s[0:1], s[1:2], r4, gs4[0:1], nf[1] + nf[2])
    m3, r3 = merged(sa3[...], sb3[...], nf[1], nf[2])
    scale, off = gs3[0:1] * r3, gs3[1:2]
    dts, pres = (dt4b, dt4s), (pre4b, pre4s)

    def body(part, i, pix, npx, row, nrows, carry):
        half = geo.parts[part][0] // 2
        dev4 = get_phases(pres[part], i) - m4
        z = get_phases(dts[part], i) * c1 - c2[part] - dev4 * c3[part]
        z = z.reshape(nrows, chans).astype(BF16)
        dz4[pl.ds(row, nrows), :] = z
        at = pl.ds((0, geo.qb)[part] + half * i, half)
        t1, t2 = [], []
        for j in range(4):
            at_j = slice(256 * j, 256 * j + 256)
            d = nt(z, w[at_j, :]).reshape(2, half, 2, VIEWS, 256)
            even = d[0, :, 0] + (dms[at, :, at_j].astype(F32) + dmo[at, :, at_j].astype(F32))
            top = jnp.stack([even, d[0, :, 1]], axis=1)
            d = jnp.concatenate([as_pix_rows(top), as_pix_rows(d[1])], axis=0)
            dev = pre3[pl.ds(pix, npx), :, at_j] - m3[:, at_j]
            x = as_pix(xs[j, pl.ds(row, nrows), :].astype(F32))
            grad = gelu_slope(dev * scale[:, at_j] + off[:, at_j] + x) * d
            dt3[pl.ds(row, nrows), at_j] = as_rows(grad).astype(BF16)
            t1.append(jnp.sum(grad, axis=0))
            t2.append(jnp.sum(grad * dev, axis=0))
        return carry[0] + jnp.concatenate(t1, axis=1), carry[1] + jnp.concatenate(t2, axis=1)

    io.ready()
    zero = jnp.zeros((VIEWS, wide), F32)
    (a1, a2), (b1, b2) = geo.loop(body, [(zero, zero), (zero, zero)], io, io)
    sums3[0:1] = rows_sum(a1 + b1)
    sums3[1:2] = rows_sum(a2 + b2) * r3


def k_back_expand(geo, io, me, nf, dt3, pre3, sa3, sb3, gs3, ga, gb, pre2, sa2, sb2, gs2, w, dt2, dz3, dt3q, sums2, tot, zbuf_b, zbuf_s):
    wide, chans = w.shape[1], w.shape[0]
    lives = [live_rows(me[1], wide), live_rows(me[2], wide)]
    s = ga[...] + gb[...]
    tot[...] = s
    m3, r3 = merged(sa3[...], sb3[...], nf[1], nf[2])
    c1, c2, c3 = back_coefs(lives, s[0:1], s[1:2], r3, gs3[0:1], nf[1] + nf[2])
    m2, r2 = merged(sa2[...], sb2[...], nf[1], nf[2])
    scale, off = gs2[0:1] * r2, gs2[1:2]
    mine = pl.ds(pl.multiple_of(me[0] * 256, 256), 256)

    def body(part, i, pix, npx, row, nrows, carry):
        zbuf = (zbuf_b, zbuf_s)[part]
        dt3q[pl.ds(row, nrows), :] = dt3[pl.ds(row, nrows), mine]
        for j in range(4):
            at = slice(256 * j, 256 * j + 256)
            z = (
                as_pix(dt3[pl.ds(row, nrows), at].astype(F32)) * c1[:, at]
                - c2[part][:, at]
                - (pre3[pl.ds(pix, npx), :, at] - m3[:, at]) * c3[part][:, at]
            )
            zbuf[:, at] = as_rows(z).astype(BF16)
        dz3[pl.ds(row, nrows), :] = zbuf[:, mine]
        d = as_pix(nt(zbuf[...], w[...]))
        dev = pre2[pl.ds(pix, npx)] - m2
        grad = gelu_slope(dev * scale + off) * d
        dt2[pl.ds(pix, npx)] = grad
        return carry[0] + jnp.sum(grad, axis=0), carry[1] + jnp.sum(grad * dev, axis=0)

    io.ready()
    zero = jnp.zeros((VIEWS, chans), F32)
    (a1, a2), (b1, b2) = geo.loop(body, [(zero, zero), (zero, zero)], io, io)
    sums2[0:1] = rows_sum(a1 + b1)
    sums2[1:2] = rows_sum(a2 + b2) * r2


def k_back_mix(geo, io, me, nf, dt2, pre2, sa2, sb2, gs2, ga, gb, pre1, sa1, sb1, gs1, w, dt1, dz2, sums1, tot, zb, zs):
    chans = pre2.shape[-1]
    lives = [live_rows(me[1], chans), live_rows(me[2], chans)]
    s = ga[...] + gb[...]
    tot[...] = s
    m2, r2 = merged(sa2[...], sb2[...], nf[1], nf[2])
    c1, c2, c3 = back_coefs(lives, s[0:1], s[1:2], r2, gs2[0:1], nf[1] + nf[2])
    m1, r1 = merged(sa1[...], sb1[...], nf[1], nf[2])
    scale, off = gs1[0:1] * r1, gs1[1:2]
    bufs = (zb, zs)
    for part, (side, _) in enumerate(geo.parts):
        zero_edges(bufs[part], side * VIEWS)

    def back(part, i, pix, npx, row, nrows, carry):
        z = dt2[pl.ds(pix, npx)] * c1 - c2[part] - (pre2[pl.ds(pix, npx)] - m2) * c3[part]
        dz2[pl.ds(row, nrows), :] = as_rows(z).astype(BF16)
        side = geo.parts[part][0]
        at = pl.multiple_of(side * VIEWS + i * nrows, 16)
        store_shifted(bufs[part], at, nrows, side, z, (2, 1, 0))
        return carry

    geo.loop(back, [0, 0], io)
    io.send(dz2)
    io.ready()

    def dots(part, i, pix, npx, row, nrows, carry):
        acc = None
        for r in range(3):
            at = pl.multiple_of(i * nrows + (2 - r) * (nrows // 2), 16)
            taps = w[3 * r : 3 * r + 3].reshape(3 * chans, chans)
            d = nn(bufs[part][pl.ds(at, nrows), :], taps)
            acc = d if acc is None else acc + d
        dev = pre1[pl.ds(pix, npx)] - m1
        grad = gelu_slope(dev * scale + off) * as_pix(acc)
        dt1[pl.ds(pix, npx)] = grad
        return carry[0] + jnp.sum(grad, axis=0), carry[1] + jnp.sum(grad * dev, axis=0)

    zero = jnp.zeros((VIEWS, chans), F32)
    (a1, a2), (b1, b2) = geo.loop(dots, [(zero, zero), (zero, zero)], None, io)
    sums1[0:1] = rows_sum(a1 + b1)
    sums1[1:2] = rows_sum(a2 + b2) * r1


def k_back_reduce(geo, io, me, nf, dt1, pre1, sa1, sb1, gs1, ga, gb, dt3q, wt, gxb, gxs, dz1, tot):
    chans = pre1.shape[-1]
    lives = [live_rows(me[1], chans), live_rows(me[2], chans)]
    s = ga[...] + gb[...]
    tot[...] = s
    m1, r1 = merged(sa1[...], sb1[...], nf[1], nf[2])
    c1, c2, c3 = back_coefs(lives, s[0:1], s[1:2], r1, gs1[0:1], nf[1] + nf[2])
    io.ready()

    def body(part, i, pix, npx, row, nrows, carry):
        z = dt1[pl.ds(pix, npx)] * c1 - c2[part] - (pre1[pl.ds(pix, npx)] - m1) * c3[part]
        z = as_rows(z).astype(BF16)
        dz1[pl.ds(row, nrows), :] = z
        g = as_pix(nn(z, wt[me[0]])) + as_pix(dt3q[pl.ds(row, nrows), :].astype(F32))
        (gxb, gxs)[part][pl.ds(pix - (0, geo.pb)[part], npx)] = g
        return carry

    geo.loop(body, [0, 0], io, io)


def k_dw_wide(act5, dz6, mids, dzs, dwide, dshort):
    dwide[...] = tn(act5[...], dz6[...]).astype(BF16)
    dshort[...] = tn(mids[...], dzs[0]).astype(BF16)


def lane_blocks(v):
    return [v[:, 128 * b : 128 * b + 128] for b in range(v.shape[1] // 128)]


def put_halves(me, full, keep, send):
    bit = me[3] & 1
    keep[...] = full[bit].astype(BF16)
    send[...] = full[1 - bit].astype(BF16)


def k_dw_stride(me, cols, dz5, keep, send, full):
    mine = pl.ds(pl.multiple_of(me[0] * 128, 128), 128)
    z = dz5[:, mine]
    rows = full.shape[1]
    for t in range(9):
        dw = tn(cols[:, t * 512 : (t + 1) * 512], z)
        lo = 0
        while lo < 512:
            half, at = divmod(t * 512 + lo, rows)
            n = min(512 - lo, rows - at)
            full[half, at : at + n] = dw[lo : lo + n]
            lo += n
    put_halves(me, full, keep, send)


def k_dw_mid(me, mid, dz4, act2, dz3, keep, send, full):
    mine = pl.ds(pl.multiple_of(me[0] * 128, 128), 128)
    blocks = [tn(mid[...], dz4[:, mine])] + lane_blocks(tn(act2[...], dz3[...]))
    flat = jnp.concatenate(blocks, axis=0)
    full[...] = flat.reshape(full.shape)
    put_halves(me, full, keep, send)


def k_dw_mix(geo, me, wb, ws, dz2, out, full):
    mine = pl.ds(pl.multiple_of(me[0] * 64, 64), 64)
    nb, ns = geo.pb * VIEWS, geo.ps * VIEWS
    at = 0
    for r in range(3):
        ob, os = r * geo.hb * VIEWS, r * geo.hs * VIEWS
        full[...] = tn(dz2[0:nb, :], wb[ob : ob + nb, :]) + tn(
            dz2[nb : nb + ns, :], ws[os : os + ns, :]
        )
        for block in lane_blocks(full[mine, :]):
            out[at : at + 64] = block
            at += 64


def k_dw_reduce(geo, me, x0b, x1b, x2b, x3b, x0s, x1s, x2s, x3s, dz1, dmix, keep, send, part, flat):
    mine = pl.ds(pl.multiple_of(me[0] * 64, 64), 64)
    nb = geo.pb * VIEWS
    base = dmix.shape[0]
    flat[0:base] = dmix[...]
    for p, (b, s) in enumerate(((x0b, x0s), (x1b, x1s), (x2b, x2s), (x3b, x3s))):
        part[...] = tn(dz1[0:nb, :], b[...]) + tn(dz1[nb:, :], s[0 : geo.ps * VIEWS, :])
        for n, block in enumerate(lane_blocks(part[mine, :])):
            flat[pl.ds(pl.multiple_of(base + (me[0] ^ p) * 128 + 64 * n, 64), 64)] = block
    half = keep.shape[0]
    bit = me[3] & 1
    keep[...] = flat[pl.ds(pl.multiple_of(bit * half, 8), half)].astype(BF16)
    send[...] = flat[pl.ds(pl.multiple_of((1 - bit) * half, 8), half)].astype(BF16)


def k_sum_split(shift, size, n_in, me, *refs):
    total = refs[n_in]
    acc = refs[0][...].astype(F32)
    for r in refs[1:n_in]:
        acc = acc + r[...].astype(F32)
    total[...] = acc
    where = (me[3] >> shift) & (size - 1)
    for m, out in enumerate(refs[n_in + 1 :]):
        out[...] = total[where ^ m].astype(BF16)


def k_sum(n_in, *refs):
    acc = refs[0][...].astype(F32)
    for r in refs[1:n_in]:
        acc = acc + r[...].astype(F32)
    refs[n_in][...] = acc.astype(BF16)


def k_join(shift, size, me, *refs):
    where = (me[3] >> shift) & (size - 1)
    for m in range(size):
        refs[size][where ^ m] = refs[m][...]


def k_unpack(plan, me, a, b, *refs):
    full = refs[-1]
    bit = me[3] & 1
    full[bit] = a[...].reshape(full.shape[1:]).astype(F32)
    full[1 - bit] = b[...].reshape(full.shape[1:]).astype(F32)
    flat = full[...].reshape(2 * full.shape[1], 128)
    at = 0
    for out, (lead, rows, cols) in zip(refs, plan):
        for t in range(lead):
            for block in range(cols // 128):
                v = flat[at : at + rows]
                lanes = slice(128 * block, 128 * block + 128)
                if lead > 1:
                    out[t, :, lanes] = v
                else:
                    out[:, lanes] = v
                at += rows


def per_device(
    ni,
    nc,
    x_big,
    x_small,
    cot_big,
    cot_small,
    counts,
    w_reduce,
    w_mix,
    w_expand,
    w_narrow,
    w_stride,
    w_widen,
    w_short,
    gain_mid3,
    shift_mid3,
    gain_out3,
    shift_out3,
    gain_mid4,
    shift_mid4,
    gain_out4,
    shift_out4,
):
    assert nc == 4 and ni >= 8 and x_big.shape[0] == VIEWS and x_small.shape[0] == VIEWS
    geo = Geo(x_big.shape[1], x_small.shape[1])
    img = lax.axis_index("img")
    q = lax.axis_index("ch").astype(jnp.int32)
    levels = ni.bit_length() - 1
    me, nf3, cnt3, nf4, cnt4 = call(
        "counts",
        functools.partial(k_counts, ni, ((geo.pb, geo.ps), (geo.qb, geo.qs))),
        [(counts, SMEM)],
        [(sds((4,), jnp.int32), SMEM)]
        + [(sds((n,)), SMEM) for n in (3, 8 * (levels - 2)) * 2],
        slack=1,
    )

    smem = [(me, SMEM)]

    def over_img(v, k):
        return lax.ppermute(v, "img", [(i, i ^ (1 << k)) for i in range(ni)])

    def over_ch(v, k):
        return lax.ppermute(v, "ch", [(i, i ^ k) for i in range(nc)])

    rounds, at = [], 0
    while at < levels:
        rounds.append((at, min(2, levels - at) if at == 0 else 1))
        at += rounds[-1][1]

    def peers(v, shift, bits):
        out = []
        for m in range(1, 1 << bits):
            out.append(lax.ppermute(v, "img", [(i, i ^ (m << shift)) for i in range(ni)]))
        return out

    def sync(v, combine, wait=(), free=()):
        wait, free = dict(wait), dict(free)
        freed = []
        for k, (shift, bits) in enumerate(rounds):
            if k in wait:
                v = lax.optimization_barrier((v,) + tuple(wait[k]))[0]
            others = peers(v, shift, bits)
            if k in free:
                held = lax.optimization_barrier(tuple(others) + tuple(free[k]))
                others = list(held[: len(others)])
                freed += held[len(others) :]
            if k == len(rounds) - 1:
                return (v, others[0]) + ((freed,) if free else ())
            v = combine(k, [v] + others)

    def sync_stats(stats, cnt):
        def combine(k, arrays):
            (v,) = call(
                "merge",
                functools.partial(k_merge, 8 * k, len(arrays)),
                [(cnt, SMEM)] + vm(*arrays),
                [sds(stats.shape)],
                slack=1,
            )
            return v

        return sync(stats, combine)

    def sync_sums(sums, wait=(), free=()):
        def combine(k, arrays):
            (v,) = call("add", functools.partial(k_add, len(arrays)), vm(*arrays), [sds(sums.shape)], slack=1)
            return v

        return sync(sums, combine, wait, free)

    groups = [(0, 1)]
    while groups[-1][0] + groups[-1][1] < levels:
        done = groups[-1][0] + groups[-1][1]
        groups.append((done, min(2, levels - done)))

    def to_peers(parts, group):
        shift, bits = group
        out = []
        for m in range(1, 1 << bits):
            perm = [(i, i ^ (m << shift)) for i in range(ni)]
            out.append(lax.ppermute(parts[m if len(parts) > 1 else 0], "img", perm))
        return out

    def sum_split(name, arrays, group):
        shift, bits = group
        size = 1 << bits
        shape = arrays[0].shape
        view = (size, shape[0] // size) + shape[1:]
        return call(
            name,
            functools.partial(k_sum_split, shift, size, len(arrays)),
            smem + vm(*[a.reshape(view) for a in arrays]),
            [sds(view[1:], BF16)] * size,
            [pltpu.VMEM(view, F32)],
            order=True,
        )

    def join(name, parts, group):
        shift, bits = group
        size = 1 << bits
        (full,) = call(
            name,
            functools.partial(k_join, shift, size),
            smem + vm(*parts),
            [sds((size,) + parts[0].shape, BF16)],
        )
        return full.reshape((-1,) + parts[0].shape[1:])

    def reduce_parts(name, parts):
        arrays = [parts[0]] + to_peers(parts, groups[1])
        for at, group in enumerate(groups[2:]):
            parts = sum_split(name + "_split%d" % at, arrays, group)
            arrays = [parts[0]] + to_peers(parts, group)
        return arrays

    def sum_parts(name, arrays):
        (part,) = call(
            name + "_sum",
            functools.partial(k_sum, len(arrays)),
            vm(*arrays),
            [sds(arrays[0].shape, BF16)],
        )
        return part

    def gather_parts(name, part, received):
        full = join(name + "_join", [part] + received, groups[-1])
        for at, group in reversed(list(enumerate(groups[1:-1]))):
            full = join(name + "_join%d" % at, [full] + to_peers([full], group), group)
        return full

    def quarters(v):
        p1 = over_ch(v, 1)
        p2 = over_ch(v, 2)
        return [v, p1, p2, over_ch(p2, 1)]

    def after(marker, *arrays):
        return list(lax.optimization_barrier((marker,) + arrays))

    def sent(v):
        return [v, over_ch(v, 1), over_ch(v, 2)]

    def passed_on(g):
        return g + [over_ch(g[2], 1)]

    def in_order(pieces):
        full = jnp.stack(pieces)
        return jnp.take(full, jnp.arange(4, dtype=jnp.int32) ^ q, axis=0)

    def rows_of(v):
        return jnp.transpose(v, (1, 2, 0, 3)).reshape(-1, v.shape[3])

    def chips(v):
        return [v, over_ch(v, 2)]

    def tie(first, *later):
        return list(lax.optimization_barrier(tuple(first) + tuple(later))[len(first) :])

    m3, c3 = 4 * w_reduce.shape[1], w_reduce.shape[0]
    m4, c4q = w_widen.shape
    first = [rows_of(x_small)]
    first.append(jnp.transpose(w_mix, (0, 1, 3, 2)).reshape(-1, m3))
    first += [w_reduce.T[:, j * m3 : (j + 1) * m3] for j in range(c3 // m3)]
    mix_at, reduce_at = first[0].shape[0], first[0].shape[0] + first[1].shape[0]
    xb, xsm = quarters(rows_of(x_big)), quarters(jnp.concatenate(first))
    held = (gain_mid3, shift_mid3, gain_out3, shift_out3, gain_mid4, shift_mid4, gain_out4, shift_out4)
    params = quarters(jnp.concatenate([v.reshape(-1) for v in held]).reshape(-1, 128))

    def split(flat):
        cuts, at = [], 0
        for v in held:
            cuts.append(flat[..., at : at + v.size].reshape(flat.shape[:-1] + v.shape))
            at += v.size
        return cuts

    gm3, sm3, go3, so3, gm4, sm4, _, _ = split(in_order(params).reshape(4, -1))

    def pair(g, s):
        return jnp.stack([g.reshape(-1), s.reshape(-1)])

    gs1, gs2 = pair(gm3[:, 0], sm3[:, 0]), pair(gm3[:, 1], sm3[:, 1])
    gs3 = pair(go3, so3)
    gs4, gs5 = pair(gm4[:, 0], sm4[:, 0]), pair(gm4[:, 1], sm4[:, 1])
    wide = [split(v.reshape(-1))[6:] for v in (params[0], params[2])]
    gs6 = jnp.stack([jnp.stack([g[0], h[0], g[1], h[1]]) for g, h in wide])

    n3, n4 = [(nf3, SMEM)], [(nf4, SMEM)]

    def k(fn):
        return functools.partial(fn, geo)

    hb, hs = geo.hb, geo.hs
    sb4, ss4 = (2, 2, hb // 2, hb // 2, VIEWS, m4), (2, 2, hs // 2, hs // 2, VIEWS, m4)
    wb_shape, ws_shape = ((hb + 2) * hb * VIEWS, 3 * m3), ((hs + 2) * hs * VIEWS, 3 * m3)

    def flow(kind, *arrays):
        return [(a, Flow(kind)) for a in arrays]

    def out(kind, shape, dtype=F32):
        return (sds(shape, dtype), Flow(kind))

    x_all = [(xb + xsm, Flow("x"))]
    w_in, w_ahead, w_back = [
        [(xsm, Flow(kind, base))]
        for kind, base in (("w_in", reduce_at), ("w_ahead", mix_at), ("w_back", mix_at))
    ]
    run = functools.partial(call, geo=geo)
    px1, px3, px4 = (geo.px, VIEWS, m3), (geo.px, VIEWS, c3), (geo.px4, VIEWS, m4)

    pre1, st = run(
        "reduce",
        k(k_reduce),
        smem + n3 + x_all + w_in,
        [fast(px1), sds((2, m3))],
    )
    def blocks128(v):
        return [v[:, 128 * b : 128 * b + 128] for b in range(v.shape[1] // 128)]

    st, w_mid = after(st, jnp.concatenate(blocks128(w_expand) + blocks128(w_narrow)))
    w_mid = sent(w_mid)
    a1, b1 = sync_stats(st, cnt3)
    pre2, winb, wins, st, keep1 = run(
        "mix",
        k(k_mix),
        smem + n3 + vm(pre1, a1, b1, gs1) + w_ahead,
        [
            fast(px1),
            out("all", wb_shape, BF16),
            out("all", ws_shape, BF16),
            sds((2, m3)),
            (sds(px1), Keep(2)),
        ],
    )
    st, w_mid[2], wst = after(st, w_mid[2], w_stride.reshape(-1, w_stride.shape[3]))
    w_mid, wst = passed_on(w_mid), sent(wst)
    w_expand_all = [(w_mid, Flow("w", 0, (m3, c3)))]
    w_narrow_all = [(w_mid, Flow("w", m3 * (c3 // 4 // 128), (c3, m4)))]
    a2, b2 = sync_stats(st, cnt3)
    pre3, act2, st, keep2 = run(
        "expand",
        k(k_expand),
        smem + n3 + vm(pre2, a2, b2, gs2) + w_expand_all,
        [
            fast(px3),
            out("rows", (geo.rows, m3), BF16),
            sds((2, c3)),
            (sds(px1), Keep(2)),
        ],
    )
    last_in = jnp.concatenate([w_short, w_widen, rows_of(cot_big), rows_of(cot_small)])
    st, wst[2], last_in = after(st, wst[2], last_in)
    wst, last_in = passed_on(wst), chips(last_in)
    a3, b3 = sync_stats(st, cnt3)
    pre4b, pre4s, mid, mids, st, keep3 = run(
        "narrow",
        k(k_narrow),
        smem + n3 + vm(pre3) + x_all + vm(a3, b3, gs3) + w_narrow_all,
        [
            fast(sb4),
            fast(ss4),
            out("rows", (geo.rows, c3), BF16),
            fast((geo.rows4, c3), BF16),
            sds((2, m4)),
            (sds(px3), Keep(2)),
        ],
        [pltpu.VMEM((geo.px4, VIEWS, c3), F32)],
    )
    a4, b4 = sync_stats(st, cnt3)
    w_stride_all = [(wst, Flow("w", 0, (9 * m4, m4)))]
    pre5, cols, st, keep4b, keep4s = run(
        "stride",
        k(k_stride),
        smem + n4 + n3 + vm(pre4b, pre4s, a4, b4, gs4) + w_stride_all,
        [
            sds(px4),
            out("all", (geo.rows4, 9 * m4), BF16),
            sds((2, m4)),
            (sds(sb4), Keep(3)),
            (sds(ss4), Keep(4)),
        ],
        [pltpu.VMEM(sb4, F32), pltpu.VMEM(ss4, F32)],
    )
    st, last_in[1], mids = after(st, last_in[1], mids)
    at_w, at_b, at_s = c3, c3 + m4, c3 + m4 + geo.qb * VIEWS
    wsh = [(v, Flow("part", 0, (c3, c4q))) for v in last_in]
    wwi = [(v, Flow("part", at_w, (m4, c4q))) for v in last_in]
    cots = [(v, Flow("part", at_b, (geo.qb * VIEWS, c4q))) for v in last_in]
    cots += [(v, Flow("part", at_s, (geo.qs * VIEWS, c4q))) for v in last_in]
    a5, b5 = sync_stats(st, cnt4)
    side, st_side = run(
        "short",
        k(k_short),
        smem + n4 + vm(mids) + wsh,
        [fast((2, geo.px4, VIEWS, c4q)), sds((2, 2, c4q))],
    )
    pre6, act5, st = run(
        "widen",
        k(k_widen),
        smem + n4 + vm(pre5, a5, b5, gs5) + wwi + vm(st_side),
        [
            fast((2, geo.px4, VIEWS, c4q)),
            sds((geo.rows4, m4), BF16),
            sds((2, 4, c4q)),
        ],
    )
    a6, b6 = sync_stats(st, cnt4)
    out_b, out_s, dt6, sums = run(
        "total",
        k(k_total),
        smem + n4 + vm(pre6, side, a6, b6, gs6) + cots,
        [
            out("all", (geo.qb, VIEWS, c4q)),
            out("all", (geo.qs, VIEWS, c4q)),
            fast((2, geo.px4, VIEWS, c4q)),
            sds((2, 3, c4q)),
        ],
    )
    ga6, gb6 = sync_sums(sums)
    part5, dz6, dzs, t6 = run(
        "back_wide",
        k(k_back_wide),
        smem
        + n4
        + vm(dt6, pre6, side, a6, b6, gs6, ga6, gb6)
        + wwi,
        [
            sds(px4),
            sds((geo.rows4, c4q), BF16),
            sds((2, geo.rows4, c4q), BF16),
            sds((2, 3, c4q)),
        ],
    )
    other5 = over_ch(part5, 1)
    dt5, sums = call(
        "back_act5",
        k_back_act5,
        n4 + vm(part5, other5, pre5, a5, b5, gs5),
        [sds(px4), sds((2, m4))],
    )
    (dms,) = run(
        "back_short", k_back_short, smem + vm(dzs) + wsh, [sds((geo.px4, VIEWS, c3), BF16)]
    )
    dmo = over_ch(dms, 1)
    dwide, dshort = call(
        "dw_wide",
        k_dw_wide,
        vm(act5, dz6, mids, dzs),
        [sds((m4, c4q), BF16), sds((c3, c4q), BF16)],
    )
    ga5, gb5, (dwide, dshort) = sync_sums(sums, free={0: [dwide, dshort]})
    dt4b, dt4s, dz5, sums, t5 = run(
        "back_stride",
        k(k_back_stride),
        smem
        + n4
        + vm(dt5, pre5, a5, b5, gs5, ga5, gb5)
        + flow("all", keep4b, keep4s)
        + vm(a4, b4, gs4)
        + n3
        + w_stride_all,
        [fast(sb4), fast(ss4), sds((geo.rows4, m4), BF16), sds((2, m4)), sds((2, m4))],
        [pltpu.VMEM((4, geo.rows4, m4), BF16)],
    )
    last = len(rounds) - 1

    def halves(rows):
        return [sds((rows // 2, 128), BF16)] * 2, pltpu.VMEM((2, rows // 2, 128), F32)

    outs, full = halves(9 * m4)
    own2, send2 = call("dw_stride", k_dw_stride, smem + vm(cols, dz5), outs, [full])
    ga4, gb4, (send2,) = sync_sums(sums, free={0: [send2]})
    recv2 = over_img(send2, 0)
    dt3, dz4, sums, t4 = run(
        "back_narrow",
        k(k_back_narrow),
        smem
        + n3
        + vm(dt4b, dt4s)
        + flow("big", keep4b)
        + flow("small", keep4s)
        + vm(a4, b4, gs4, ga4, gb4)
        + flow("px", keep3)
        + x_all
        + vm(a3, b3, gs3, dms, dmo)
        + w_narrow_all,
        [
            fast((geo.rows, c3), BF16),
            out("rows", (geo.rows, m4), BF16),
            sds((2, c3)),
            sds((2, m4)),
        ],
    )
    parts2 = sum_split("stride_split", [own2, recv2], groups[1])
    ga3, gb3, parts = sync_sums(sums, wait={0: [recv2]}, free={last: parts2[1:]})
    arrays2 = reduce_parts("stride", parts2[:1] + parts)
    dt2, dz3, dt3q, sums, t3 = run(
        "back_expand",
        k(k_back_expand),
        smem
        + n3
        + vm(dt3)
        + flow("px", keep3)
        + vm(a3, b3, gs3, ga3, gb3)
        + flow("px", keep2)
        + vm(a2, b2, gs2)
        + w_expand_all,
        [
            fast(px1),
            out("rows", (geo.rows, c3 // 4), BF16),
            out("rows", (geo.rows, c3 // 4), BF16),
            sds((2, m3)),
            sds((2, c3)),
        ],
        [
            pltpu.VMEM((2 * hb * VIEWS, c3), BF16),
            pltpu.VMEM((2 * hs * VIEWS, c3), BF16),
        ],
    )
    part2 = sum_parts("stride", arrays2)
    rows_mid = c3 + (c3 // 4 // 128) * m3
    outs, full = halves(rows_mid)
    own3, send3 = call("dw_mid", k_dw_mid, smem + vm(mid, dz4, act2, dz3), outs, [full])
    ga2, gb2, (send3, part2) = sync_sums(
        sums, wait={0: arrays2[1:]}, free={0: [send3], last: [part2]}
    )
    recv3 = over_img(send3, 0)
    back2 = to_peers([part2], groups[-1])
    dt1, dz2, sums, t2 = run(
        "back_mix",
        k(k_back_mix),
        smem
        + n3
        + vm(dt2)
        + flow("px", keep2)
        + vm(a2, b2, gs2, ga2, gb2)
        + flow("px", keep1)
        + vm(a1, b1, gs1)
        + w_back,
        [fast(px1), out("all", (geo.rows, m3), BF16), sds((2, m3)), sds((2, m3))],
        [pltpu.VMEM(wb_shape, BF16), pltpu.VMEM(ws_shape, BF16)],
    )
    join2 = gather_parts("stride", part2, back2)
    parts3 = sum_split("mid_split", [own3, recv3], groups[1])
    mix_rows = 9 * m3 // 128 * (m3 // 4)
    (dmix,) = call(
        "dw_mix",
        k(k_dw_mix),
        smem + vm(winb, wins, dz2),
        [sds((mix_rows, 128))],
        [pltpu.VMEM((m3, 3 * m3), F32)],
    )
    ga1, gb1, (join2, *parts) = sync_sums(
        sums, wait={0: back2 + [recv3]}, free={0: [join2], last: parts3[1:]}
    )
    other2 = over_img(join2, 0)
    arrays3 = reduce_parts("mid", parts3[:1] + parts)
    gxb, gxs, dz1, t1 = run(
        "back_reduce",
        k(k_back_reduce),
        smem
        + n3
        + vm(dt1)
        + flow("px", keep1)
        + vm(a1, b1, gs1, ga1, gb1)
        + flow("rows", dt3q)
        + w_in,
        [
            out("big_px", (geo.pb, VIEWS, c3 // 4)),
            out("small_px", (geo.ps, VIEWS, c3 // 4)),
            sds((geo.rows, m3), BF16),
            sds((2, m3)),
        ],
    )
    rows_last = mix_rows + c3 // 128 * (m3 // 4)
    outs, _ = halves(rows_last)
    dmix_late, *arrays3[1:] = after(dmix, *arrays3[1:])
    own4, send4 = call(
        "dw_reduce",
        k(k_dw_reduce),
        smem + vm(*xb, *xsm, dz1, dmix_late),
        outs,
        [pltpu.VMEM((m3, c3 // 4), F32), pltpu.VMEM((rows_last, 128), F32)],
    )
    recv4 = over_img(send4, 0)
    part3 = sum_parts("mid", arrays3)
    parts4 = sum_split("last_split", [own4, recv4], groups[1])
    join3 = gather_parts("mid", part3, to_peers([part3], groups[-1]))
    other3 = over_img(join3, 0)
    arrays4 = reduce_parts("last", parts4)
    part4 = sum_parts("last", arrays4)
    join4 = gather_parts("last", part4, to_peers([part4], groups[-1]))
    other4 = over_img(join4, 0)

    def unpack(name, a, b, plan):
        shapes = [((lead,) if lead > 1 else ()) + (rows, cols) for lead, rows, cols in plan]
        return call(
            name,
            functools.partial(k_unpack, plan),
            smem + vm(a, b),
            [sds(shape) for shape in shapes],
            [pltpu.VMEM((2,) + a.shape, F32)],
        )

    (dstride,) = unpack("out_stride", join2, other2, [(1, 9 * m4, 128)])
    dnarrow, dexpand = unpack("out_mid", join3, other3, [(1, c3, m4 // 4), (1, m3, c3 // 4)])
    dmix, dreduce = unpack(
        "out_last", join4, other4, [(3, m3 // 4, 3 * m3), (1, m3 // 4, c3)]
    )
    dwide, dshort = [v.astype(F32) for v in lax.psum((dwide, dshort), "img")]

    def views_first(v, side):
        return jnp.transpose(v.reshape(side, side, VIEWS, v.shape[2]), (2, 0, 1, 3))

    def own(v):
        n = v.shape[0] // 4
        return lax.dynamic_slice_in_dim(v, q * n, n, 0)

    t6 = t6[0]
    return (
        views_first(out_b, hb // 2),
        views_first(out_s, hs // 2),
        views_first(gxb, hb),
        views_first(gxs, hs),
        dreduce.T,
        jnp.transpose(dmix.reshape(3, m3 // 4, 3, m3), (0, 2, 3, 1)),
        dexpand,
        dnarrow,
        dstride.reshape(3, 3, m4, m4 // 4),
        dwide,
        dshort,
        jnp.stack([own(t1[1]), own(t2[1])]),
        jnp.stack([own(t1[0]), own(t2[0])]),
        own(t3[1]),
        own(t3[0]),
        jnp.stack([own(t4[1]), own(t5[1])]),
        jnp.stack([own(t4[0]), own(t5[0])]),
        jnp.stack([t6[1], t6[2]]),
        jnp.stack([t6[0], t6[0]]),
    )


def solution(mesh):
    act = P("img", None, None, "ch")
    flat, taps, vec = P(None, "ch"), P(None, None, None, "ch"), P("ch")
    in_specs = (act,) * 4 + (P(), flat, taps, flat, flat, taps, flat, flat)
    in_specs += (flat, flat, vec, vec, flat, flat, flat, flat)
    out_specs = (act,) * 4 + (flat, taps, flat, flat, taps, flat, flat)
    out_specs += (flat, flat, vec, vec, flat, flat, flat, flat)
    return jax.shard_map(
        functools.partial(per_device, mesh.shape["img"], mesh.shape["ch"]),
        mesh=mesh,
        in_specs=in_specs,
        out_specs=out_specs,
        check_vma=False,
    )
```

```python
import functools
import math

import jax
import jax.numpy as jnp
from jax import lax
from jax.experimental import pallas as pl
from jax.experimental.pallas import tpu as pltpu
from jax.sharding import PartitionSpec as P

EPS = 1e-05
G0 = 0.7978845608028654
G1 = G0 * 0.044715
F32 = jnp.float32
BF16 = jnp.bfloat16
VIEWS = 8

ANY = pl.BlockSpec(memory_space=pl.ANY)
HBM = pl.BlockSpec(memory_space=pltpu.HBM)
VMEM = pl.BlockSpec(memory_space=pltpu.VMEM)
SMEM = pl.BlockSpec(memory_space=pltpu.SMEM)


def sds(shape, dtype=F32):
    return jax.ShapeDtypeStruct(tuple(shape), dtype)


class Flow:
    WHOLE = ("w", "w4", "all", "chip", "w_in", "w_ahead", "w_back")

    def __init__(self, kind, base=0, shape=None, which=0):
        self.kind, self.base, self.shape, self.which = kind, base, shape, which

    def keys(self, geo, shape):
        parts = (0, 1)
        if self.kind in ("big", "big_px"):
            parts = (0,)
        if self.kind in ("small", "small_px"):
            parts = (1,)
        if self.kind not in ("lead",) + self.WHOLE:
            return [(part, n) for part in parts for n in range(len(geo.groups[part]))]
        if self.kind == "lead":
            return list(range(shape[0]))
        return [None]

    def buffer(self, geo, shapes, dtype):
        if self.kind == "x":
            return pltpu.VMEM((4, geo.rows, shapes[0][1]), dtype)
        if self.kind == "w":
            return pltpu.VMEM(self.shape, dtype)
        if self.kind in ("chip", "w4"):
            return pltpu.VMEM(self.shape, dtype)
        c = shapes[0][-1]
        if self.kind.startswith("w_"):
            return pltpu.VMEM({"w_in": (4, c, c), "w_ahead": (3, c, 3 * c), "w_back": (9, c, c)}[self.kind], dtype)
        return pltpu.VMEM(tuple(shapes[0]), dtype)

    def pairs(self, geo, q, hbm, buf, key):
        if self.kind == "w":
            rows, n = buf.shape[0], buf.shape[1] // 4
            found = []
            for p in range(4):
                for b in range(n // 128):
                    at = pl.ds(pl.multiple_of((q ^ p) * n + 128 * b, 128), 128)
                    found.append((hbm[p].at[pl.ds(self.base + rows * b, rows)], buf.at[:, at]))
            return found
        if self.kind.startswith("w_"):
            c = buf.shape[1]
            n = c // 4
            found = []
            for p in range(4):
                at = pl.ds(pl.multiple_of((q ^ p) * n, n), n)
                for t in range(4 if self.kind == "w_in" else 9):
                    src = hbm[p].at[pl.ds(self.base + n * t, n)]
                    if self.kind == "w_ahead":
                        found.append((src, buf.at[t // 3, at, pl.ds(t % 3 * c, c)]))
                    else:
                        found.append((src, buf.at[t, at]))
            return found
        if self.kind == "chip":
            return [(hbm[0].at[(q >> 1) ^ self.which, pl.ds(self.base, buf.shape[0])], buf)]
        if self.kind == "w4":
            n = buf.shape[1] // 4
            found = []
            for chip in range(2):
                for other in range(2):
                    at = pl.multiple_of((2 * chip + ((q & 1) ^ other)) * n, n)
                    found.append((hbm[other].at[chip], buf.at[:, pl.ds(at, n)]))
            return found
        if key is None:
            return [(hbm[0], buf)]
        if self.kind == "lead":
            return [(hbm[0].at[key], buf.at[key])]
        part, group = key
        i, end = geo.groups[part][group]
        pix, npx, row, nrows = geo.step(part, i)
        npx, nrows, first = npx * (end - i), nrows * (end - i), pix - geo.parts[part][1]
        if self.kind == "px":
            at = pl.ds(pix, npx)
        elif self.kind == "rows":
            at = pl.ds(row, nrows)
        elif self.kind in ("big_px", "small_px"):
            at = pl.ds(first, npx)
        elif self.kind == "x":
            local = pl.ds(first * VIEWS, nrows)
            return [
                (hbm[4 * part + p].at[local], buf.at[q ^ p, pl.ds(row, nrows)]) for p in range(4)
            ]
        else:
            at = pl.ds(i, end - i)
            return [(hbm[0].at[:, :, at], buf.at[:, :, at])]
        return [(hbm[0].at[at], buf.at[at])]


class Moves:
    def __init__(self, geo, q, ahead):
        self.geo, self.q, self.flows, self.kept, self.ahead = geo, q, [], [], ahead

    def add(self, flow, hbm, buf, sem, inward):
        self.flows.append((flow, hbm, buf, sem, inward))

    def copies(self, entry, key):
        flow, hbm, buf, sem, inward = entry
        if flow.kind in flow.WHOLE:
            at = 0
        elif flow.kind == "lead":
            at = key
        elif flow.kind in ("px", "rows", "x"):
            at = (0, len(self.geo.groups[0]))[key[0]] + key[1]
        else:
            at = key[1]
        pairs = flow.pairs(self.geo, self.q, hbm, buf, key)
        return [
            pltpu.make_async_copy(*((a, b) if inward else (b, a)), sem.at[n, at])
            for n, (a, b) in enumerate(pairs)
        ]

    def entries(self, inward, key):
        for entry in self.flows:
            flow = entry[0]
            if entry[4] != inward:
                continue
            if key is None:
                fits = flow.kind in flow.WHOLE
            elif isinstance(key, int):
                fits = flow.kind == "lead"
            else:
                kinds = ("px", "rows", "x") + (("big", "big_px"), ("small", "small_px"))[key[0]]
                fits = flow.kind in kinds
            if fits:
                yield entry

    def start(self, inward, key):
        for entry in self.entries(inward, key):
            for c in self.copies(entry, key):
                c.start()

    def wait(self, inward, key):
        for entry in self.entries(inward, key):
            for c in self.copies(entry, key):
                c.wait()

    def begin(self):
        self.order = [(part, n) for part in range(2) for n in range(len(self.geo.groups[part]))]
        self.start(True, self.order[0])
        self.start(True, None)
        for key in self.order[1:self.ahead]:
            self.start(True, key)
        for n in range(self.ahead):
            self.start_lead(n)
        streams = any(e[4] and e[0].kind not in ("lead",) + Flow.WHOLE for e in self.flows)
        if not streams:
            for c in self.kept:
                c.start()

    def start_lead(self, n):
        for entry in self.flows:
            if entry[4] and entry[0].kind == "lead" and n < entry[1][0].shape[0]:
                for c in self.copies(entry, n):
                    c.start()

    def ready(self):
        self.wait(True, None)

    def arrive(self, *key):
        if len(key) == 1:
            self.wait(True, key[0])
            self.start_lead(key[0] + self.ahead)
            return
        self.wait(True, key)
        at = self.order.index(key)
        if at + self.ahead < len(self.order):
            self.start(True, self.order[at + self.ahead])
        streams = any(e[4] and e[0].kind not in ("lead",) + Flow.WHOLE for e in self.flows)
        if at == 0 and streams:
            for c in self.kept:
                c.start()

    def leave(self, *key):
        self.start(False, key if len(key) > 1 else key[0])

    def send(self, *refs):
        for entry in self.entries(False, None):
            if any(entry[2] is r for r in refs):
                for c in self.copies(entry, None):
                    c.start()

    def finish(self):
        for entry in self.flows:
            if not entry[4]:
                shape = entry[1][0].shape
                for key in entry[0].keys(self.geo, shape):
                    for c in self.copies(entry, key):
                        c.wait()
        for c in self.kept:
            c.wait()


class Keep:
    kind = "keep"

    def __init__(self, source):
        self.source = source


def fast(shape, dtype=F32):
    return pltpu.VMEM(tuple(shape), dtype)


def scoped_bytes(v):
    return math.prod(v.shape) * jnp.dtype(v.dtype).itemsize


def in_hbm(v):
    return pltpu.with_memory_space_constraint(v, pltpu.HBM)


def call(name, kernel, ins, outs, scratch=(), cost=None, order=False, geo=None, slack=14, ahead=3):
    if order:
        inner, n_in, n_out = kernel, len(ins), len(outs)

        def kernel(*refs):
            rest = refs[n_in:]
            return inner(*refs[:n_in], *rest[n_out:], *rest[:n_out])

    outs = [o if isinstance(o, tuple) else (o, VMEM) for o in outs]
    arrays, specs, moved = [], [], []
    for a, spec in ins:
        group = a if isinstance(a, list) else [a]
        flow = isinstance(spec, Flow)
        arrays += [in_hbm(v) for v in group] if flow else group
        specs += [HBM if flow else spec] * len(group)
        moved.append((spec if flow else None, len(group), [v.shape for v in group], group[0].dtype))
    out_shapes, out_specs = [], []
    for shape, spec in outs:
        flow = isinstance(spec, (Flow, Keep))
        out_shapes.append(pltpu.HBM(shape.shape, shape.dtype) if flow else shape)
        out_specs.append(HBM if flow else spec)
        moved.append((spec if flow else None, 1, [shape.shape], shape.dtype))
    extra = []
    for flow, _, shapes, dtype in moved:
        if isinstance(flow, Keep):
            extra += [pltpu.SemaphoreType.DMA((1,))]
        elif flow:
            keys = len(flow.keys(geo, shapes[0]))
            copies = {"x": 4, "w": 4, "w4": 4, "w_in": 16, "w_ahead": 36, "w_back": 36}.get(flow.kind, 1)
            if flow.kind == "w":
                copies = flow.shape[1] // 128
            extra += [flow.buffer(geo, shapes, dtype), pltpu.SemaphoreType.DMA((copies, keys))]
    body = kernel
    if extra:

        def body(*refs):
            n_io = sum(n for _, n, _, _ in moved)
            given, own, rest = list(refs[:n_io]), refs[n_io : n_io + len(scratch)], refs[n_io + len(scratch) :]
            rest = list(rest)
            moves = Moves(geo, given[0][0], ahead)
            args = []
            for n, (flow, count, _, _) in enumerate(moved):
                group, given = given[:count], given[count:]
                if not flow:
                    args += group
                    continue
                if isinstance(flow, Keep):
                    moves.kept.append(pltpu.make_async_copy(args[flow.source], group[0], rest[0].at[0]))
                    rest = rest[1:]
                    continue
                buf, sem = rest[:2]
                rest = rest[2:]
                moves.add(flow, group, buf, sem, n < len(ins))
                args.append(buf)
            moves.begin()
            kernel(moves, *args, *own)
            moves.finish()

    scratch = list(scratch)
    def held(v):
        pinned = "vmem" in str(getattr(v, "memory_space", "")).lower()
        return 0 if pinned else scoped_bytes(v)

    need = sum(held(jax.typeof(a)) for a, spec in zip(arrays, specs) if spec is VMEM)
    need += sum(held(o) for o, spec in zip(out_shapes, out_specs) if spec is VMEM)
    need += sum(
        scoped_bytes(v)
        for v in scratch + extra
        if getattr(v, "memory_space", None) == pltpu.VMEM
    )
    result = pl.pallas_call(
        body,
        out_shape=out_shapes,
        in_specs=specs,
        out_specs=out_specs,
        scratch_shapes=scratch + extra,
        compiler_params=pltpu.CompilerParams(vmem_limit_bytes=need + need // 16 + (slack << 20)),
        cost_estimate=cost,
        name=name,
    )(*arrays)
    return list(result)


def vm(*arrays):
    return [(a, VMEM) for a in arrays]


def nn(a, b):
    return lax.dot_general(a, b, (((1,), (0,)), ((), ())), preferred_element_type=F32)


def nt(a, b):
    return lax.dot_general(a, b, (((1,), (1,)), ((), ())), preferred_element_type=F32)


def tn(a, b):
    return lax.dot_general(a, b, (((0,), (0,)), ((), ())), preferred_element_type=F32)


def gelu(t):
    half = 0.5 * t
    return half + half * jnp.tanh(t * (G0 + G1 * (t * t)))


def gelu_slope(t):
    sq = t * t
    th = jnp.tanh(t * (G0 + G1 * sq))
    return 0.5 * (1.0 + th) + (0.5 * t) * (1.0 - th * th) * (G0 + (3.0 * G1) * sq)


def live_rows(count, chans):
    return (lax.broadcasted_iota(jnp.int32, (VIEWS, chans), 0) < count).astype(F32)


def rows_sum(v):
    return jnp.sum(v, axis=0, keepdims=True)


def merged(sa, sb, na, nb):
    total = na + nb
    mean = (na * sa[0:1] + nb * sb[0:1]) / total
    diff = sb[0:1] - sa[0:1]
    square = sa[1:2] + sb[1:2] + diff * diff * (na * nb / total)
    return mean, lax.rsqrt(square / total + EPS)


def as_rows(v):
    return v.reshape(v.shape[0] * v.shape[1], v.shape[2])


def as_pix_rows(v):
    return v.reshape(v.shape[0] * v.shape[1], VIEWS, v.shape[3])


def as_pix(v):
    return v.reshape(v.shape[0] // VIEWS, VIEWS, v.shape[1])


class Geo:
    def __init__(self, hb, hs):
        self.hb, self.hs = hb, hs
        self.pb, self.ps = hb * hb, hs * hs
        self.px = self.pb + self.ps
        self.rows = self.px * VIEWS
        self.qb, self.qs = self.pb // 4, self.ps // 4
        self.px4 = self.qb + self.qs
        self.rows4 = self.px4 * VIEWS
        self.parts = ((hb, 0), (hs, self.pb))
        self.groups = [self.cuts(hb // 2, 1), self.cuts(hs // 2, 2)]

    @staticmethod
    def cuts(steps, first):
        at = sorted({0, steps} | set(range(first, steps, 2)))
        return list(zip(at[:-1], at[1:]))

    @staticmethod
    def aligned(n):
        return n if isinstance(n, int) else pl.multiple_of(n, 16)

    def step(self, part, i):
        side, start = self.parts[part]
        npx = 2 * side
        return start + i * npx, npx, self.aligned((start + i * npx) * VIEWS), npx * VIEWS

    def loop(self, body, carries, arrive=None, leave=None):
        out = []
        for part in range(2):

            def run(i, carry, part=part):
                for n, (lo, hi) in enumerate(self.groups[part]):
                    if arrive:
                        pl.when(i == lo)(functools.partial(arrive.arrive, part, n))
                carry = body(part, i, *self.step(part, i), carry)
                for n, (lo, hi) in enumerate(self.groups[part]):
                    if leave:
                        pl.when(i == hi - 1)(functools.partial(leave.leave, part, n))
                return carry

            out.append(lax.fori_loop(0, self.groups[part][-1][1], run, carries[part]))
        return out


def finish_stats(geo, ref, sums, lives, count, out, quarter=None):
    mean = (rows_sum(sums[0] * lives[0]) + rows_sum(sums[1] * lives[1])) / count

    def body(part, i, pix, npx, row, nrows, carry):
        dev = ref[pl.ds(pix, npx)] - mean
        return carry + jnp.sum(dev * dev, axis=0)

    zero = jnp.zeros(sums[0].shape, F32)
    sq = geo.loop(body, [zero, zero])
    out[0:1] = mean
    out[1:2] = rows_sum(sq[0] * lives[0]) + rows_sum(sq[1] * lives[1])


def block_stats(geo, value, lives, count):
    big, small = value[: geo.qb], value[geo.qb :]
    mean = (
        rows_sum(jnp.sum(big, axis=0) * lives[0]) + rows_sum(jnp.sum(small, axis=0) * lives[1])
    ) / count
    db, ds = big - mean, small - mean
    square = rows_sum(jnp.sum(db * db, axis=0) * lives[0]) + rows_sum(
        jnp.sum(ds * ds, axis=0) * lives[1]
    )
    return mean, square


def k_reduce(geo, io, me, nf, xs, wt, pre, stats):
    io.ready()
    chans = wt.shape[1]
    lives = [live_rows(me[1], chans), live_rows(me[2], chans)]

    def body(part, i, pix, npx, row, nrows, carry):
        acc = None
        for j in range(4):
            d = nt(xs[j, pl.ds(row, nrows), :], wt[j])
            acc = d if acc is None else acc + d
        z = as_pix(acc)
        pre[pl.ds(pix, npx)] = z
        return carry + jnp.sum(z, axis=0)

    zero = jnp.zeros((VIEWS, chans), F32)
    sums = geo.loop(body, [zero, zero], io, io)
    finish_stats(geo, pre, sums, lives, nf[0], stats)


def k_counts(ni, sizes, counts, me, nf3, cnt3, nf4, cnt4):
    img = lax.axis_index("img")
    levels = ni.bit_length() - 1
    me[0] = lax.axis_index("ch").astype(jnp.int32)
    me[1] = counts[img, 0]
    me[2] = counts[img, 1]
    me[3] = img
    for (big, small), nf, cnt in zip(sizes, (nf3, nf4), (cnt3, cnt4)):

        def group(shift, index):
            def add(i, total):
                at = index * (1 << shift) + i
                return total + counts[at, 0] * big + counts[at, 1] * small

            return lax.fori_loop(0, 1 << shift, add, jnp.int32(0)).astype(F32)

        nf[0] = group(0, img)
        for m in range(2):
            nf[1 + m] = group(levels - 1, (img >> (levels - 1)) ^ m)
        row, k = 0, 0
        while k < levels - 1:
            bits = 2 if k == 0 else 1
            for m in range(8):
                cnt[row + m] = group(k, (img >> k) ^ m) if m < 1 << bits else jnp.float32(0.0)
            row, k = row + 8, k + bits


def k_pack_params(gm3, sm3, go3, so3, gm4, sm4, go4, so4, out, rows):
    rows[...] = jnp.zeros(rows.shape, F32)
    rows[0:2, 0:64] = gm3[...]
    rows[2:4, 0:64] = sm3[...]
    for b in range(2):
        lanes = slice(128 * b, 128 * b + 128)
        rows[4 + b : 5 + b] = go3[:, lanes]
        rows[6 + b : 7 + b] = so3[:, lanes]
    rows[8:10] = gm4[...]
    rows[10:12] = sm4[...]
    for n in range(2):
        for b in range(4):
            lanes = slice(128 * b, 128 * b + 128)
            rows[12 + 4 * n + b : 13 + 4 * n + b] = go4[n : n + 1, lanes]
            rows[20 + 4 * n + b : 21 + 4 * n + b] = so4[n : n + 1, lanes]
    v = rows[...]
    high = v.astype(BF16)
    rest = v - high.astype(F32)
    mid = rest.astype(BF16)
    low = (rest - mid.astype(F32)).astype(BF16)
    out[0:32, 0:128] = high
    out[0:32, 128:256] = mid
    out[32:64, 0:128] = low
    out[32:64, 128:256] = jnp.zeros_like(low)


def k_unpack_params(base, me, p0, p1, p2, p3, gs1, gs2, gs3, gs4, gs5, gs6, buf, sem):
    copies = [
        pltpu.make_async_copy(p.at[pl.ds(base, 64)], buf.at[n], sem.at[n])
        for n, p in enumerate((p0, p1, p2, p3))
    ]
    for c in copies:
        c.start()
    for c in copies:
        c.wait()
    rows = []
    for n in range(4):
        v = buf[n].astype(F32)
        rows.append(v[0:32, 0:128] + v[0:32, 128:256] + v[32:64, 0:128])
    odd = me[0] & 1
    for chip in range(2):
        mine, other = rows[2 * chip][:, 0:64], rows[2 * chip + 1][:, 0:64]
        both = jnp.where(
            odd == 0,
            jnp.concatenate([mine, other], axis=1),
            jnp.concatenate([other, mine], axis=1),
        )
        at = pl.ds(pl.multiple_of(((me[0] >> 1) ^ chip) * 128, 128), 128)
        for n, gs in enumerate((gs1, gs2)):
            gs[0:1, at] = both[n : n + 1]
            gs[1:2, at] = both[2 + n : 3 + n]
    for p, v in enumerate(rows):
        for b in range(2):
            at = pl.ds(pl.multiple_of((me[0] ^ p) * 256 + 128 * b, 128), 128)
            gs3[0:1, at] = v[4 + b : 5 + b]
            gs3[1:2, at] = v[6 + b : 7 + b]
        at = pl.ds(pl.multiple_of((me[0] ^ p) * 128, 128), 128)
        for n, gs in enumerate((gs4, gs5)):
            gs[0:1, at] = v[8 + n : 9 + n]
            gs[1:2, at] = v[10 + n : 11 + n]
    for chip in range(2):
        v = rows[2 * chip]
        for n in range(2):
            for b in range(4):
                lanes = slice(128 * b, 128 * b + 128)
                gs6[chip, 2 * n : 2 * n + 1, lanes] = v[12 + 4 * n + b : 13 + 4 * n + b]
                gs6[chip, 2 * n + 1 : 2 * n + 2, lanes] = v[20 + 4 * n + b : 21 + 4 * n + b]


def k_merge(first, n, cnt, *refs):
    arrays, out = refs[:n], refs[n]
    for at in range(0, out.shape[-2], 2):
        mean_at, sq_at = (..., slice(at, at + 1), slice(None)), (..., slice(at + 1, at + 2), slice(None))
        groups = [(cnt[first + m], a[mean_at], a[sq_at]) for m, a in enumerate(arrays)]
        while len(groups) > 1:
            pairs = []
            for (na, ma, qa), (nb, mb, qb) in zip(groups[::2], groups[1::2]):
                total = na + nb
                diff = mb - ma
                pairs.append(
                    (total, (na * ma + nb * mb) / total, qa + qb + diff * diff * (na * nb / total))
                )
            groups = pairs
        out[mean_at], out[sq_at] = groups[0][1], groups[0][2]


def k_add(n, *refs):
    values = [r[...] for r in refs[:n]]
    while len(values) > 1:
        values = [a + b for a, b in zip(values[::2], values[1::2])]
    refs[n][...] = values[0]


def side_shift(v, by):
    zero = jnp.zeros((v.shape[0], 1) + v.shape[2:], v.dtype)
    if by > 0:
        return jnp.concatenate([zero, v[:, :-1]], axis=1)
    return jnp.concatenate([v[:, 1:], zero], axis=1)


def store_shifted(buf, row, nrows, side, v, order):
    img = v.reshape(2, side, VIEWS, v.shape[-1])
    chans = v.shape[-1]
    forms = [side_shift(img, 1), img, side_shift(img, -1)]
    for lane, k in enumerate(order):
        flat = forms[k].reshape(nrows, chans).astype(BF16)
        buf[pl.ds(row, nrows), lane * chans : (lane + 1) * chans] = flat


def put_phases(ref, i, v):
    for k in range(4):
        ref[k // 2, k % 2, i] = v[k // 2, :, k % 2]


def get_phases(ref, i):
    rows = [jnp.stack([ref[r, 0, i], ref[r, 1, i]], axis=1) for r in range(2)]
    return jnp.stack(rows)


def zero_edges(buf, edge):
    total = buf.shape[0]
    buf[0:edge, :] = jnp.zeros((edge, buf.shape[1]), BF16)
    buf[total - edge : total, :] = jnp.zeros((edge, buf.shape[1]), BF16)


def k_mix(geo, io, me, nf, pre1, sa, sb, gs, w, pre2, wb, ws, stats, dev, center):
    chans = pre1.shape[-1]
    lives = [live_rows(me[1], chans), live_rows(me[2], chans)]
    mean, inv = merged(sa[...], sb[...], nf[1], nf[2])
    scale, shift = gs[0:1] * inv, gs[1:2]
    bufs = (wb, ws)
    for part, (side, _) in enumerate(geo.parts):
        zero_edges(bufs[part], side * VIEWS)

    def act(part, i, pix, npx, row, nrows, carry):
        a = gelu((pre1[pl.ds(pix, npx)] - mean) * scale + shift)
        own = (pre1[pl.ds(pix, npx), :, lanes] - center[:, lanes]) * lives[part][:, 0:128]
        dev[pl.ds(row, nrows), :] = as_rows(own).astype(BF16)
        side = geo.parts[part][0]
        at = pl.multiple_of(side * VIEWS + i * nrows, 16)
        store_shifted(bufs[part], at, nrows, side, a, (0, 1, 2))
        return carry

    lanes, _ = own_block(me)
    center[...] = mean
    geo.loop(act, [0, 0], io)
    io.send(wb, ws, dev)
    io.ready()

    def dots(part, i, pix, npx, row, nrows, carry):
        acc = None
        for r in range(3):
            at = pl.multiple_of(i * nrows + r * (nrows // 2), 16)
            d = nt(bufs[part][pl.ds(at, nrows), :], w[r])
            acc = d if acc is None else acc + d
        z = as_pix(acc)
        pre2[pl.ds(pix, npx)] = z
        return carry + jnp.sum(z, axis=0)

    zero = jnp.zeros((VIEWS, chans), F32)
    sums = geo.loop(dots, [zero, zero], None, io)
    finish_stats(geo, pre2, sums, lives, nf[0], stats)


def k_expand(geo, io, me, nf, pre2, sa, sb, gs, w, pre3, act2, stats):
    chans = w.shape[1]
    lives = [live_rows(me[1], chans), live_rows(me[2], chans)]
    mean, inv = merged(sa[...], sb[...], nf[1], nf[2])
    scale, shift = gs[0:1] * inv, gs[1:2]

    def body(part, i, pix, npx, row, nrows, carry):
        a = as_rows(gelu((pre2[pl.ds(pix, npx)] - mean) * scale + shift)).astype(BF16)
        act2[pl.ds(row, nrows), :] = a
        z = as_pix(nn(a, w[...]))
        pre3[pl.ds(pix, npx)] = z
        return carry + jnp.sum(z, axis=0)

    io.ready()
    zero = jnp.zeros((VIEWS, chans), F32)
    sums = geo.loop(body, [zero, zero], io, io)
    finish_stats(geo, pre3, sums, lives, nf[0], stats)


def k_narrow(geo, io, me, nf, pre3, xs, sa, sb, gs, w, pre4b, pre4s, mid, mids, stats, mid_even):
    chans = w.shape[1]
    lives = [live_rows(me[1], chans), live_rows(me[2], chans)]
    mean, inv = merged(sa[...], sb[...], nf[1], nf[2])
    scale, shift = gs[0:1] * inv, gs[1:2]
    pre4 = (pre4b, pre4s)

    def body(part, i, pix, npx, row, nrows, carry):
        side = geo.parts[part][0]
        half = side // 2
        for j in range(4):
            at = slice(256 * j, 256 * j + 256)
            dev = pre3[pl.ds(pix, npx), :, at] - mean[:, at]
            x = as_pix(xs[j, pl.ds(row, nrows), :].astype(F32))
            a = gelu(dev * scale[:, at] + shift[:, at] + x)
            mid[pl.ds(row, nrows), at] = as_rows(a).astype(BF16)
            even = a.reshape(2, half, 2, VIEWS, 256)[0, :, 0]
            mid_even[pl.ds((0, geo.qb)[part] + half * i, half), :, at] = even
        z = nn(mid[pl.ds(row, nrows), :], w[...])
        put_phases(pre4[part], i, z.reshape(2, half, 2, VIEWS, chans))
        return carry + jnp.sum(as_pix(z), axis=0)

    io.ready()
    zero = jnp.zeros((VIEWS, chans), F32)
    sums = geo.loop(body, [zero, zero], io, io)
    mean4 = (rows_sum(sums[0] * lives[0]) + rows_sum(sums[1] * lives[1])) / nf[0]
    mids[...] = as_rows(mid_even[...]).astype(BF16)
    io.send(mids)
    sq = []
    for part in range(2):

        def dev2(i, carry, part=part):
            for k in range(4):
                d = pre4[part][k // 2, k % 2, i] - mean4
                carry = carry + jnp.sum(d * d, axis=0)
            return carry

        sq.append(lax.fori_loop(0, geo.parts[part][0] // 2, dev2, zero))
    stats[0:1] = mean4
    stats[1:2] = rows_sum(sq[0] * lives[0]) + rows_sum(sq[1] * lives[1])


def k_short(geo, io, me, nf, mids, w0, w1, side, stats):
    io.ready()
    chans = w0.shape[1]
    lives = [live_rows(me[1], chans), live_rows(me[2], chans)]
    for j, w in enumerate((w0, w1)):
        z = as_pix(nn(mids[...], w[...]))
        side[j] = z
        io.leave(j)
        mean, square = block_stats(geo, z, lives, nf[0])
        stats[j] = jnp.concatenate([mean, square], axis=0)


def k_stride(geo, io, me, nf, n4, pre4b, pre4s, sa, sb, gs, w, pre5, cols, stats, sb_act, ss_act):
    chans = pre4b.shape[-1]
    lives = [live_rows(me[1], chans), live_rows(me[2], chans)]
    mean, inv = merged(sa[...], sb[...], n4[1], n4[2])
    scale, shift = gs[0:1] * inv, gs[1:2]
    srcs, dsts = (pre4b, pre4s), (sb_act, ss_act)

    def act(part, i, pix, npx, row, nrows, carry):
        for k in range(4):
            at = (k // 2, k % 2, i)
            dsts[part][at] = gelu((srcs[part][at] - mean) * scale + shift)
        return carry

    geo.loop(act, [0, 0], io)
    for r in range(3):
        for c in range(3):
            flats = []
            for part in range(2):
                half = geo.parts[part][0] // 2
                v = dsts[part][(r + 1) % 2, (c + 1) % 2]
                if c == 0:
                    v = side_shift(v, 1)
                if r == 0:
                    v = jnp.concatenate([jnp.zeros((1,) + v.shape[1:], F32), v[:-1]], axis=0)
                flats.append(v.reshape(half * half * VIEWS, chans))
            t = 3 * r + c
            cols[t] = jnp.concatenate(flats, axis=0).astype(BF16)
            io.leave(t)
    io.ready()
    acc = None
    for t in range(9):
        d = nn(cols[t], w[t * chans : (t + 1) * chans, :])
        acc = d if acc is None else acc + d
    z = as_pix(acc)
    pre5[...] = z
    m5, s5 = block_stats(geo, z, lives, nf[0])
    stats[0:1] = m5
    stats[1:2] = s5


def k_widen(geo, io, me, nf, pre5, sa, sb, gs, w0, w1, st_side, pre6, act5, stats):
    chans = w0.shape[1]
    lives = [live_rows(me[1], chans), live_rows(me[2], chans)]
    mean, inv = merged(sa[...], sb[...], nf[1], nf[2])
    scale, shift = gs[0:1] * inv, gs[1:2]
    act5[...] = as_rows(gelu((pre5[...] - mean) * scale + shift)).astype(BF16)
    io.ready()
    for j, w in enumerate((w0, w1)):
        z = as_pix(nn(act5[...], w[...]))
        pre6[j] = z
        io.leave(j)
        m6, s6 = block_stats(geo, z, lives, nf[0])
        stats[j] = jnp.concatenate([m6, s6, st_side[j]], axis=0)


def k_total(geo, io, me, nf, pre6, side, sa, sb, gs, cb0, cb1, cs0, cs1, out_b, out_s, dt, sums):
    chans = pre6.shape[-1]
    lives = [live_rows(me[1], chans), live_rows(me[2], chans)]
    cots = ((cb0, cb1), (cs0, cs1))
    spans = ((0, geo.qb), (geo.qb, geo.px4))
    outs = (out_b, out_s)
    io.ready()
    for j in range(2):
        io.arrive(j)
        a, b, g = sa[j], sb[j], gs[j]
        m6, r6 = merged(a[0:2], b[0:2], nf[1], nf[2])
        ms, rs = merged(a[2:4], b[2:4], nf[1], nf[2])
        acc = [None, None, None]
        for part, (lo, hi) in enumerate(spans):
            d6 = pre6[j, lo:hi] - m6
            dd = side[j, lo:hi] - ms
            total = d6 * (g[0:1] * r6) + g[1:2] + (dd * (g[2:3] * rs) + g[3:4])
            live = lives[part]
            if j == 0:
                outs[part][...] = gelu(total) * live
            grad = gelu_slope(total) * (as_pix(cots[part][j][...].astype(F32)) * live)
            dt[j, lo:hi] = grad
            terms = [jnp.sum(v, axis=0) for v in (grad, grad * d6, grad * dd)]
            acc = [t if s is None else s + t for s, t in zip(acc, terms)]
        io.leave(j)
        if j == 0:
            io.send(out_b, out_s)
        sums[j] = jnp.concatenate(
            [rows_sum(acc[0]), rows_sum(acc[1]) * r6, rows_sum(acc[2]) * rs], axis=0
        )


def back_coefs(lives, s1, s2, inv, gain, count):
    c1 = gain * inv
    c2 = [live * (c1 * s1 / count) for live in lives]
    c3 = [live * (c1 * inv * s2 / count) for live in lives]
    return c1, c2, c3


def k_back_wide(geo, io, me, nf, dt, pre6, side, sa, sb, gs, ga, gb, w0, w1, part5, dz6, dzs, tot):
    chans = pre6.shape[-1]
    lives = [live_rows(me[1], chans), live_rows(me[2], chans)]
    total = nf[1] + nf[2]
    spans = ((0, geo.qb), (geo.qb, geo.px4))
    acc = None
    io.ready()
    for j, w in enumerate((w0, w1)):
        io.arrive(j)
        a, b, g = sa[j], sb[j], gs[j]
        s = ga[j] + gb[j]
        tot[j] = s
        m6, r6 = merged(a[0:2], b[0:2], nf[1], nf[2])
        ms, rs = merged(a[2:4], b[2:4], nf[1], nf[2])
        k1, k2, k3 = back_coefs(lives, s[0:1], s[1:2], r6, g[0:1], total)
        h1, h2, h3 = back_coefs(lives, s[0:1], s[2:3], rs, g[2:3], total)
        main, short = [], []
        for part, (lo, hi) in enumerate(spans):
            grad = dt[j, lo:hi]
            main.append(grad * k1 - k2[part] - (pre6[j, lo:hi] - m6) * k3[part])
            short.append(grad * h1 - h2[part] - (side[j, lo:hi] - ms) * h3[part])
        z6 = as_rows(jnp.concatenate(main, axis=0)).astype(BF16)
        dzs[j] = as_rows(jnp.concatenate(short, axis=0)).astype(BF16)
        io.leave(j)
        if j == 0:
            dz6[...] = z6
        d = nt(z6, w[...])
        acc = d if acc is None else acc + d
    part5[...] = as_pix(acc)


def k_back_act5(nf, mine, other, pre5, sa5, sb5, gs5, dt5, sums5):
    m5, r5 = merged(sa5[...], sb5[...], nf[1], nf[2])
    dev = pre5[...] - m5
    grad = gelu_slope(dev * (gs5[0:1] * r5) + gs5[1:2]) * (mine[...] + other[...])
    dt5[...] = grad
    sums5[0:1] = rows_sum(jnp.sum(grad, axis=0))
    sums5[1:2] = rows_sum(jnp.sum(grad * dev, axis=0)) * r5


def k_back_short(io, me, dzs, w0, w1, dms):
    io.ready()
    acc = None
    for j, w in enumerate((w0, w1)):
        d = nt(dzs[j], w[...])
        acc = d if acc is None else acc + d
    dms[...] = as_pix(acc).astype(BF16)


def k_back_stride(geo, io, me, nf, dt5, pre5, sa5, sb5, gs5, ga, gb, pre4b, pre4s, sa4, sb4, gs4, n4, w, dt4b, dt4s, dz5, sums4, tot, shifts):
    chans = pre5.shape[-1]
    lives = [live_rows(me[1], chans), live_rows(me[2], chans)]
    s = ga[...] + gb[...]
    tot[...] = s
    m5, r5 = merged(sa5[...], sb5[...], nf[1], nf[2])
    c1, c2, c3 = back_coefs(lives, s[0:1], s[1:2], r5, gs5[0:1], nf[1] + nf[2])
    spans = ((0, geo.qb), (geo.qb, geo.px4))
    imgs = []
    for part, (lo, hi) in enumerate(spans):
        half = geo.parts[part][0] // 2
        z = dt5[lo:hi] * c1 - c2[part] - (pre5[lo:hi] - m5) * c3[part]
        imgs.append(z.reshape(half, half, VIEWS, chans))

    def flat(moved):
        return jnp.concatenate([v.reshape(-1, chans) for v in moved], axis=0).astype(BF16)

    def up(v):
        return jnp.concatenate([v[1:], jnp.zeros((1,) + v.shape[1:], F32)], axis=0)

    shifts[0] = flat(imgs)
    dz5[...] = shifts[0]
    shifts[1] = flat([side_shift(v, -1) for v in imgs])
    shifts[2] = flat([up(v) for v in imgs])
    shifts[3] = flat([up(side_shift(v, -1)) for v in imgs])
    m4, r4 = merged(sa4[...], sb4[...], n4[1], n4[2])
    scale, off = gs4[0:1] * r4, gs4[1:2]
    io.ready()
    plan = {
        (0, 0): ((0, 4),),
        (0, 1): ((0, 5), (1, 3)),
        (1, 0): ((0, 7), (2, 1)),
        (1, 1): ((0, 8), (1, 6), (2, 2), (3, 0)),
    }
    t1, t2 = jnp.zeros((VIEWS, chans), F32), jnp.zeros((VIEWS, chans), F32)
    for (rp, cp), terms in plan.items():
        acc = None
        for k, t in terms:
            d = nt(shifts[k], w[t * chans : (t + 1) * chans, :])
            acc = d if acc is None else acc + d
        for part, (lo, hi) in enumerate(spans):
            half = geo.parts[part][0] // 2
            d = acc[lo * VIEWS : hi * VIEWS].reshape(half, half, VIEWS, chans)
            dev = (pre4b, pre4s)[part][rp, cp] - m4
            grad = gelu_slope(dev * scale + off) * d
            (dt4b, dt4s)[part][rp, cp] = grad
            t1 = t1 + jnp.sum(grad, axis=(0, 1))
            t2 = t2 + jnp.sum(grad * dev, axis=(0, 1))
    io.send(dt4b, dt4s)
    sums4[0:1] = rows_sum(t1)
    sums4[1:2] = rows_sum(t2) * r4


def k_back_narrow(geo, io, me, nf, dt4b, dt4s, pre4b, pre4s, sa4, sb4, gs4, ga, gb, pre3, xs, sa3, sb3, gs3, dms, dmo, w, dt3, dz4, sums3, tot):
    chans = w.shape[1]
    wide = w.shape[0]
    lives = [live_rows(me[1], chans), live_rows(me[2], chans)]
    s = ga[...] + gb[...]
    tot[...] = s
    m4, r4 = merged(sa4[...], sb4[...], nf[1], nf[2])
    c1, c2, c3 = back_coefs(lives, s[0:1], s[1:2], r4, gs4[0:1], nf[1] + nf[2])
    m3, r3 = merged(sa3[...], sb3[...], nf[1], nf[2])
    scale, off = gs3[0:1] * r3, gs3[1:2]
    dts, pres = (dt4b, dt4s), (pre4b, pre4s)

    def body(part, i, pix, npx, row, nrows, carry):
        half = geo.parts[part][0] // 2
        dev4 = get_phases(pres[part], i) - m4
        z = get_phases(dts[part], i) * c1 - c2[part] - dev4 * c3[part]
        z = z.reshape(nrows, chans).astype(BF16)
        dz4[pl.ds(row, nrows), :] = z
        at = pl.ds((0, geo.qb)[part] + half * i, half)
        t1, t2 = [], []
        for j in range(4):
            at_j = slice(256 * j, 256 * j + 256)
            d = nt(z, w[at_j, :]).reshape(2, half, 2, VIEWS, 256)
            even = d[0, :, 0] + (dms[at, :, at_j].astype(F32) + dmo[at, :, at_j].astype(F32))
            top = jnp.stack([even, d[0, :, 1]], axis=1)
            d = jnp.concatenate([as_pix_rows(top), as_pix_rows(d[1])], axis=0)
            dev = pre3[pl.ds(pix, npx), :, at_j] - m3[:, at_j]
            x = as_pix(xs[j, pl.ds(row, nrows), :].astype(F32))
            grad = gelu_slope(dev * scale[:, at_j] + off[:, at_j] + x) * d
            dt3[pl.ds(row, nrows), at_j] = as_rows(grad).astype(BF16)
            t1.append(jnp.sum(grad, axis=0))
            t2.append(jnp.sum(grad * dev, axis=0))
        return carry[0] + jnp.concatenate(t1, axis=1), carry[1] + jnp.concatenate(t2, axis=1)

    io.ready()
    zero = jnp.zeros((VIEWS, wide), F32)
    (a1, a2), (b1, b2) = geo.loop(body, [(zero, zero), (zero, zero)], io, io)
    sums3[0:1] = rows_sum(a1 + b1)
    sums3[1:2] = rows_sum(a2 + b2) * r3


def k_back_expand(geo, io, me, nf, dt3, pre3, sa3, sb3, gs3, ga, gb, pre2, sa2, sb2, gs2, w, dt2, dz3, dt3q, sums2, tot, zbuf_b, zbuf_s):
    wide, chans = w.shape[1], w.shape[0]
    lives = [live_rows(me[1], wide), live_rows(me[2], wide)]
    s = ga[...] + gb[...]
    tot[...] = s
    m3, r3 = merged(sa3[...], sb3[...], nf[1], nf[2])
    c1, c2, c3 = back_coefs(lives, s[0:1], s[1:2], r3, gs3[0:1], nf[1] + nf[2])
    m2, r2 = merged(sa2[...], sb2[...], nf[1], nf[2])
    scale, off = gs2[0:1] * r2, gs2[1:2]
    mine = pl.ds(pl.multiple_of(me[0] * 256, 256), 256)

    def body(part, i, pix, npx, row, nrows, carry):
        zbuf = (zbuf_b, zbuf_s)[part]
        dt3q[pl.ds(row, nrows), :] = dt3[pl.ds(row, nrows), mine]
        for j in range(4):
            at = slice(256 * j, 256 * j + 256)
            z = (
                as_pix(dt3[pl.ds(row, nrows), at].astype(F32)) * c1[:, at]
                - c2[part][:, at]
                - (pre3[pl.ds(pix, npx), :, at] - m3[:, at]) * c3[part][:, at]
            )
            zbuf[:, at] = as_rows(z).astype(BF16)
        dz3[pl.ds(row, nrows), :] = zbuf[:, mine]
        d = as_pix(nt(zbuf[...], w[...]))
        dev = pre2[pl.ds(pix, npx)] - m2
        grad = gelu_slope(dev * scale + off) * d
        dt2[pl.ds(pix, npx)] = grad
        return carry[0] + jnp.sum(grad, axis=0), carry[1] + jnp.sum(grad * dev, axis=0)

    io.ready()
    zero = jnp.zeros((VIEWS, chans), F32)
    (a1, a2), (b1, b2) = geo.loop(body, [(zero, zero), (zero, zero)], io, io)
    sums2[0:1] = rows_sum(a1 + b1)
    sums2[1:2] = rows_sum(a2 + b2) * r2


def k_back_mix(geo, io, me, nf, dt2, pre2, sa2, sb2, gs2, ga, gb, pre1, sa1, sb1, gs1, w, dt1, dz2, sums1, tot, dt1q, zb, zs):
    chans = pre2.shape[-1]
    lives = [live_rows(me[1], chans), live_rows(me[2], chans)]
    s = ga[...] + gb[...]
    tot[...] = s
    m2, r2 = merged(sa2[...], sb2[...], nf[1], nf[2])
    c1, c2, c3 = back_coefs(lives, s[0:1], s[1:2], r2, gs2[0:1], nf[1] + nf[2])
    m1, r1 = merged(sa1[...], sb1[...], nf[1], nf[2])
    scale, off = gs1[0:1] * r1, gs1[1:2]
    bufs = (zb, zs)
    for part, (side, _) in enumerate(geo.parts):
        zero_edges(bufs[part], side * VIEWS)

    def back(part, i, pix, npx, row, nrows, carry):
        z = dt2[pl.ds(pix, npx)] * c1 - c2[part] - (pre2[pl.ds(pix, npx)] - m2) * c3[part]
        dz2[pl.ds(row, nrows), :] = as_rows(z).astype(BF16)
        side = geo.parts[part][0]
        at = pl.multiple_of(side * VIEWS + i * nrows, 16)
        store_shifted(bufs[part], at, nrows, side, z, (2, 1, 0))
        return carry

    lanes, _ = own_block(me)
    geo.loop(back, [0, 0], io)
    io.send(dz2)
    io.ready()

    def dots(part, i, pix, npx, row, nrows, carry):
        acc = None
        for r in range(3):
            at = pl.multiple_of(i * nrows + (2 - r) * (nrows // 2), 16)
            taps = w[3 * r : 3 * r + 3].reshape(3 * chans, chans)
            d = nn(bufs[part][pl.ds(at, nrows), :], taps)
            acc = d if acc is None else acc + d
        dev = pre1[pl.ds(pix, npx)] - m1
        grad = gelu_slope(dev * scale + off) * as_pix(acc)
        dt1[pl.ds(pix, npx)] = grad
        dt1q[pl.ds(row, nrows), :] = as_rows(dt1[pl.ds(pix, npx), :, lanes]).astype(BF16)
        return carry[0] + jnp.sum(grad, axis=0), carry[1] + jnp.sum(grad * dev, axis=0)

    zero = jnp.zeros((VIEWS, chans), F32)
    (a1, a2), (b1, b2) = geo.loop(dots, [(zero, zero), (zero, zero)], None, io)
    sums1[0:1] = rows_sum(a1 + b1)
    sums1[1:2] = rows_sum(a2 + b2) * r1


def k_back_reduce(geo, io, me, nf, dt1, pre1, sa1, sb1, gs1, ga, gb, dt3q, wt, gxb, gxs, tot, coef):
    chans = pre1.shape[-1]
    lives = [live_rows(me[1], chans), live_rows(me[2], chans)]
    s = ga[...] + gb[...]
    tot[...] = s
    m1, r1 = merged(sa1[...], sb1[...], nf[1], nf[2])
    c1, c2, c3 = back_coefs(lives, s[0:1], s[1:2], r1, gs1[0:1], nf[1] + nf[2])
    io.ready()
    total = nf[1] + nf[2]
    coef[0:1] = c1
    coef[1:2] = c1 * s[0:1] / total
    coef[2:3] = c1 * r1 * s[1:2] / total

    def body(part, i, pix, npx, row, nrows, carry):
        z = dt1[pl.ds(pix, npx)] * c1 - c2[part] - (pre1[pl.ds(pix, npx)] - m1) * c3[part]
        z = as_rows(z).astype(BF16)
        g = as_pix(nn(z, wt[me[0]])) + as_pix(dt3q[pl.ds(row, nrows), :].astype(F32))
        (gxb, gxs)[part][pl.ds(pix - (0, geo.pb)[part], npx)] = g
        return carry

    geo.loop(body, [0, 0], io, io)


def k_dw_wide(act5, dz6, mids, dzs, dwide, dshort):
    dwide[...] = tn(act5[...], dz6[...]).astype(BF16)
    dshort[...] = tn(mids[...], dzs[0]).astype(BF16)


def lane_blocks(v):
    return [v[:, 128 * b : 128 * b + 128] for b in range(v.shape[1] // 128)]


def put_halves(me, full, keep, send):
    bit = me[3] & 1
    keep[...] = full[bit].astype(BF16)
    send[...] = full[1 - bit].astype(BF16)


def k_dw_stride(io, me, cols, dz5, keep, send, full):
    mine = pl.ds(pl.multiple_of(me[0] * 128, 128), 128)
    z = dz5[:, mine]
    rows = full.shape[1]
    for t in range(9):
        io.arrive(t)
        dw = tn(cols[t], z)
        lo = 0
        while lo < 512:
            half, at = divmod(t * 512 + lo, rows)
            n = min(512 - lo, rows - at)
            full[half, at : at + n] = dw[lo : lo + n]
            lo += n
    put_halves(me, full, keep, send)


def k_dw_mid(me, mid, dz4, act2, dz3, keep, send, full):
    mine = pl.ds(pl.multiple_of(me[0] * 128, 128), 128)
    blocks = [tn(mid[...], dz4[:, mine])] + lane_blocks(tn(act2[...], dz3[...]))
    full[...] = jnp.concatenate(blocks, axis=0).reshape(full.shape)
    put_halves(me, full, keep, send)


def own_block(me):
    lanes = pl.ds(pl.multiple_of((me[0] >> 1) * 128, 128), 128)
    return lanes, pl.ds(pl.multiple_of((me[0] & 1) * 64, 64), 64)


def k_dw_mix(geo, me, wb, ws, dz2, out, full):
    lanes, mine = own_block(me)
    nb, ns = geo.pb * VIEWS, geo.ps * VIEWS
    at = 0
    for r in range(3):
        ob, os = r * geo.hb * VIEWS, r * geo.hs * VIEWS
        full[...] = tn(dz2[0:nb, lanes], wb[ob : ob + nb, :]) + tn(
            dz2[nb : nb + ns, lanes], ws[os : os + ns, :]
        )
        for block in lane_blocks(full[mine, :]):
            out[at : at + 64] = block
            at += 64


def k_dev_products(geo, io, me, devq, xs, out, lhs, part):
    lives = [live_rows(me[1], 128), live_rows(me[2], 128)]
    _, mine = own_block(me)
    io.ready()

    def body(step, i, pix, npx, row, nrows, carry):
        live = jnp.broadcast_to(lives[step][None], (npx, VIEWS, 128))
        lhs[pl.ds(row, nrows), 0:128] = devq[pl.ds(row, nrows), :]
        lhs[pl.ds(row, nrows), 128:256] = as_rows(live).astype(BF16)
        return carry

    geo.loop(body, [0, 0], io)
    for j in range(4):
        part[:, 256 * j : 256 * j + 256] = tn(lhs[...], xs[j])
    out[...] = jnp.concatenate([part[mine, :], part[128:136, :]], axis=0).astype(BF16)


def k_dw_last(geo, io, me, xs, dt1q, dmix, keep, send, part, flat):
    _, mine = own_block(me)
    io.ready()
    base = dmix.shape[0]
    flat[0:base] = dmix[...]
    geo.loop(lambda step, i, pix, npx, row, nrows, carry: carry, [0, 0], io)
    for j in range(4):
        part[:, 256 * j : 256 * j + 256] = tn(dt1q[...], xs[j])
    flat[base:] = jnp.concatenate(lane_blocks(part[mine, :]), axis=0)
    half = keep.shape[0]
    bit = me[3] & 1
    keep[...] = flat[pl.ds(pl.multiple_of(bit * half, 8), half)].astype(BF16)
    send[...] = flat[pl.ds(pl.multiple_of((1 - bit) * half, 8), half)].astype(BF16)


def k_small_outputs(me, t1, t2, t3, t4, t5, t6, late, gm3, sm3, go3, so3, gm4, sm4, go4, so4):
    lanes, _ = own_block(me)
    half = me[0] & 1
    for n, t in enumerate((t1, t2)):
        block = t[:, lanes]
        mine = jnp.where(half == 0, block[:, 0:64], block[:, 64:128])
        gm3[n : n + 1] = mine[1:2]
        sm3[n : n + 1] = mine[0:1]
    wide = pl.ds(pl.multiple_of(me[0] * 256, 256), 256)
    go3[...] = t3[1:2, wide]
    so3[...] = t3[0:1, wide]
    mid = pl.ds(pl.multiple_of(me[0] * 128, 128), 128)
    for n, t in enumerate((t4, t5)):
        gm4[n : n + 1] = t[1:2, mid]
        sm4[n : n + 1] = t[0:1, mid]
    go4[...] = t6[1:3]
    so4[0:1] = t6[0:1]
    so4[1:2] = t6[0:1]


def k_sum_split(shift, size, n_in, me, *refs):
    total = refs[n_in]
    acc = refs[0][...].astype(F32)
    for r in refs[1:n_in]:
        acc = acc + r[...].astype(F32)
    total[...] = acc
    where = (me[3] >> shift) & (size - 1)
    for m, out in enumerate(refs[n_in + 1 :]):
        out[...] = total[where ^ m].astype(BF16)


def k_sum(n_in, *refs):
    acc = refs[0][...].astype(F32)
    for r in refs[1:n_in]:
        acc = acc + r[...].astype(F32)
    refs[n_in][...] = acc.astype(BF16)


def k_join(shift, size, me, *refs):
    where = (me[3] >> shift) & (size - 1)
    for m in range(size):
        refs[size][where ^ m] = refs[m][...]


def k_unpack(plan, me, a, b, *refs):
    full = refs[-1]
    bit = me[3] & 1
    full[bit] = a[...].reshape(full.shape[1:]).astype(F32)
    full[1 - bit] = b[...].reshape(full.shape[1:]).astype(F32)
    flat = full[...].reshape(2 * full.shape[1], 128)
    at = 0
    for out, (lead, rows, cols) in zip(refs, plan):
        for t in range(lead):
            for block in range(cols // 128):
                v = flat[at : at + rows]
                lanes = slice(128 * block, 128 * block + 128)
                if lead > 1:
                    out[t, :, lanes] = v
                else:
                    out[:, lanes] = v
                at += rows


def k_out_last(me, a, b, dev, coef, dmix, dreduce, full):
    bit = me[3] & 1
    full[bit] = a[...].reshape(full.shape[1:]).astype(F32)
    full[1 - bit] = b[...].reshape(full.shape[1:]).astype(F32)
    flat = full[...].reshape(2 * full.shape[1], 128)
    at = 0
    for t in range(9):
        for block in range(2):
            dmix[t, :, 128 * block : 128 * block + 128] = flat[at : at + 64]
            at += 64
    fix = dev[64:65].astype(F32) * coef[1] + dev[0:64].astype(F32) * coef[2]
    for block in range(8):
        lanes = slice(128 * block, 128 * block + 128)
        dreduce[:, lanes] = flat[at : at + 64] * coef[0] - fix[:, lanes]
        at += 64


def per_device(
    ni,
    nc,
    x_big,
    x_small,
    cot_big,
    cot_small,
    counts,
    w_reduce,
    w_mix,
    w_expand,
    w_narrow,
    w_stride,
    w_widen,
    w_short,
    gain_mid3,
    shift_mid3,
    gain_out3,
    shift_out3,
    gain_mid4,
    shift_mid4,
    gain_out4,
    shift_out4,
):
    assert nc == 4 and ni >= 8 and x_big.shape[0] == VIEWS and x_small.shape[0] == VIEWS
    geo = Geo(x_big.shape[1], x_small.shape[1])
    img = lax.axis_index("img")
    q = lax.axis_index("ch").astype(jnp.int32)
    levels = ni.bit_length() - 1
    me, nf3, cnt3, nf4, cnt4 = call(
        "counts",
        functools.partial(k_counts, ni, ((geo.pb, geo.ps), (geo.qb, geo.qs))),
        [(counts, SMEM)],
        [(sds((4,), jnp.int32), SMEM)]
        + [(sds((n,)), SMEM) for n in (3, 8 * (levels - 2)) * 2],
        slack=1,
    )

    smem = [(me, SMEM)]

    def over_img(v, k):
        return lax.ppermute(v, "img", [(i, i ^ (1 << k)) for i in range(ni)])

    def over_ch(v, k):
        return lax.ppermute(v, "ch", [(i, i ^ k) for i in range(nc)])

    rounds, at = [], 0
    while at < levels:
        rounds.append((at, min(2, levels - at) if at == 0 else 1))
        at += rounds[-1][1]

    def peers(v, shift, bits):
        out = []
        for m in range(1, 1 << bits):
            out.append(lax.ppermute(v, "img", [(i, i ^ (m << shift)) for i in range(ni)]))
        return out

    def sync(v, combine, wait=(), free=()):
        wait, free = dict(wait), dict(free)
        freed = []
        for k, (shift, bits) in enumerate(rounds):
            if k in wait:
                v = lax.optimization_barrier((v,) + tuple(wait[k]))[0]
            others = peers(v, shift, bits)
            if k in free:
                held = lax.optimization_barrier(tuple(others) + tuple(free[k]))
                others = list(held[: len(others)])
                freed += held[len(others) :]
            if k == len(rounds) - 1:
                return (v, others[0]) + ((freed,) if free else ())
            v = combine(k, [v] + others)

    last = len(rounds) - 1

    def sync_stats(stats, cnt, wait=(), free=()):
        def combine(k, arrays):
            (v,) = call(
                "merge",
                functools.partial(k_merge, 8 * k, len(arrays)),
                [(cnt, SMEM)] + vm(*arrays),
                [sds(stats.shape)],
                slack=1,
            )
            return v

        return sync(stats, combine, wait, free)

    def sync_sums(sums, wait=(), free=()):
        def combine(k, arrays):
            (v,) = call("add", functools.partial(k_add, len(arrays)), vm(*arrays), [sds(sums.shape)], slack=1)
            return v

        return sync(sums, combine, wait, free)

    pairs = [(at, 1) for at in range(levels)]
    fours = [(0, 1)]
    while fours[-1][0] + fours[-1][1] < levels:
        done = fours[-1][0] + fours[-1][1]
        fours.append((done, min(2, levels - done)))

    def to_peers(parts, group):
        shift, bits = group
        out = []
        for m in range(1, 1 << bits):
            perm = [(i, i ^ (m << shift)) for i in range(ni)]
            out.append(lax.ppermute(parts[m if len(parts) > 1 else 0], "img", perm))
        return out

    def sum_split(name, arrays, group):
        shift, bits = group
        size = 1 << bits
        shape = arrays[0].shape
        view = (size, shape[0] // size) + shape[1:]
        return call(
            name,
            functools.partial(k_sum_split, shift, size, len(arrays)),
            smem + vm(*[a.reshape(view) for a in arrays]),
            [sds(view[1:], BF16)] * size,
            [pltpu.VMEM(view, F32)],
            order=True,
        )

    def join(name, parts, group):
        shift, bits = group
        size = 1 << bits
        (full,) = call(
            name,
            functools.partial(k_join, shift, size),
            smem + vm(*parts),
            [sds((size,) + parts[0].shape, BF16)],
        )
        return full.reshape((-1,) + parts[0].shape[1:])

    class Train:
        def __init__(self, name, groups, parts):
            self.name, self.groups, self.parts, self.at, self.summing = name, groups, parts, 0, True

        def sends(self):
            return self.parts[1:] if self.summing else self.parts

        def launch(self, sends):
            parts = self.parts[:1] + list(sends) if self.summing else list(sends)
            self.received = to_peers(parts, self.groups[self.at])

        def advance(self):
            name = "%s_%d" % (self.name, self.at)
            arrays = self.parts[:1] + self.received
            if self.summing and self.at + 1 < len(self.groups):
                self.at += 1
                self.parts = sum_split(name, arrays, self.groups[self.at])
            elif self.summing:
                self.summing = False
                self.parts = call(
                    name + "s",
                    functools.partial(k_sum, len(arrays)),
                    vm(*arrays),
                    [sds(arrays[0].shape, BF16)],
                    slack=2,
                )
            else:
                self.parts = [join(name + "j", arrays, self.groups[self.at])]
                self.at -= 1

        def to_last(self):
            while self.summing or self.at > 0:
                self.advance()
                self.launch(self.sends())

        def finish(self):
            self.to_last()
            return self.parts[0], self.received[0]

    def quarters(v):
        p1 = over_ch(v, 1)
        p2 = over_ch(v, 2)
        return [v, p1, p2, over_ch(p2, 1)]

    def after(marker, *arrays):
        return list(lax.optimization_barrier((marker,) + arrays))

    def sent(v):
        return [v, over_ch(v, 1), over_ch(v, 2)]

    def passed_on(g):
        return g + [over_ch(g[2], 1)]

    def rows_of(v):
        return jnp.transpose(v, (1, 2, 0, 3)).reshape(-1, v.shape[3])

    m3, c3 = 4 * w_reduce.shape[1], w_reduce.shape[0]
    m4, c4q = w_widen.shape
    first = [rows_of(x_small)]
    first.append(jnp.transpose(w_mix, (0, 1, 3, 2)).reshape(-1, m3))
    first += [w_reduce.T[:, j * m3 : (j + 1) * m3] for j in range(c3 // m3)]
    mix_at, reduce_at = first[0].shape[0], first[0].shape[0] + first[1].shape[0]
    held = (gain_mid3, shift_mid3, gain_out3[None], shift_out3[None], gain_mid4, shift_mid4, gain_out4, shift_out4)
    first += call(
        "pack_params",
        k_pack_params,
        vm(*held),
        [sds((64, 256), BF16)],
        [pltpu.VMEM((32, 128), F32)],
        slack=2,
    )
    params_at = sum(v.shape[0] for v in first[:-1])
    xb = quarters(rows_of(x_big))
    xb[1], me, *first = lax.optimization_barrier((xb[1], me, *first))
    smem = [(me, SMEM)]
    xsm = sent(jnp.concatenate(first))
    xb[3], xsm[2] = after(xb[3], xsm[2])
    xsm = passed_on(xsm)
    gs1, gs2, gs3, gs4, gs5, gs6 = call(
        "unpack_params",
        functools.partial(k_unpack_params, params_at),
        smem + [(in_hbm(v), HBM) for v in xsm],
        [sds((2, n)) for n in (m3, m3, c3, m4, m4)] + [sds((2, 4, c4q))],
        [pltpu.VMEM((4, 64, 256), BF16), pltpu.SemaphoreType.DMA((4,))],
        slack=2,
    )

    def blocks128(v):
        return [v[:, 128 * b : 128 * b + 128] for b in range(v.shape[1] // 128)]

    w_mid = jnp.concatenate(blocks128(w_expand) + blocks128(w_narrow))
    last_in = jnp.concatenate([w_short, w_widen, rows_of(cot_big), rows_of(cot_small)])
    wst = w_stride.reshape(-1, w_stride.shape[3])
    xsm[3], w_mid, last_in, wst = after(xsm[3], w_mid, last_in, wst)
    chip_pairs = [[0, 2], [1, 3]]
    wst = lax.all_gather(wst, "ch", axis_index_groups=chip_pairs)
    last_in = lax.all_gather(last_in, "ch", axis_index_groups=chip_pairs)

    n3, n4 = [(nf3, SMEM)], [(nf4, SMEM)]

    def k(fn):
        return functools.partial(fn, geo)

    hb, hs = geo.hb, geo.hs
    sb4, ss4 = (2, 2, hb // 2, hb // 2, VIEWS, m4), (2, 2, hs // 2, hs // 2, VIEWS, m4)
    wb_shape, ws_shape = ((hb + 2) * hb * VIEWS, 3 * m3), ((hs + 2) * hs * VIEWS, 3 * m3)

    def flow(kind, *arrays):
        return [(a, Flow(kind)) for a in arrays]

    def out(kind, shape, dtype=F32):
        return (sds(shape, dtype), Flow(kind))

    x_all = [(xb + xsm, Flow("x"))]
    w_in, w_ahead, w_back = [
        [(xsm, Flow(kind, base))]
        for kind, base in (("w_in", reduce_at), ("w_ahead", mix_at), ("w_back", mix_at))
    ]
    run = functools.partial(call, geo=geo)
    px1, px3, px4 = (geo.px, VIEWS, m3), (geo.px, VIEWS, c3), (geo.px4, VIEWS, m4)

    pre1, st = run(
        "reduce",
        k(k_reduce),
        smem + n3 + x_all + w_in,
        [fast(px1), sds((2, m3))],
    )
    st, w_mid = after(st, w_mid)
    w_mid = sent(w_mid)
    a1, b1 = sync_stats(st, cnt3)
    pre2, winb, wins, st, devq, keep1 = run(
        "mix",
        k(k_mix),
        smem + n3 + vm(pre1, a1, b1, gs1) + w_ahead,
        [
            fast(px1),
            out("all", wb_shape, BF16),
            out("all", ws_shape, BF16),
            sds((2, m3)),
            out("all", (geo.rows, 128), BF16),
            (sds(px1), Keep(2)),
        ],
        [pltpu.VMEM((1, m3), F32)],
    )
    st, w_mid[2] = after(st, w_mid[2])
    w_mid = passed_on(w_mid)
    w_expand_all = [(w_mid, Flow("w", 0, (m3, c3)))]
    w_narrow_all = [(w_mid, Flow("w", m3 * (c3 // 4 // 128), (c3, m4)))]
    a2, b2 = sync_stats(st, cnt3)
    pre3, act2, st, keep2 = run(
        "expand",
        k(k_expand),
        smem + n3 + vm(pre2, a2, b2, gs2) + w_expand_all,
        [
            fast(px3),
            out("rows", (geo.rows, m3), BF16),
            sds((2, c3)),
            (sds(px1), Keep(2)),
        ],
    )
    a3, b3 = sync_stats(st, cnt3)
    pre4b, pre4s, mid, mids, st, keep3 = run(
        "narrow",
        k(k_narrow),
        smem + n3 + vm(pre3) + x_all + vm(a3, b3, gs3) + w_narrow_all,
        [
            out("big", sb4),
            out("small", ss4),
            out("rows", (geo.rows, c3), BF16),
            fast((geo.rows4, c3), BF16),
            sds((2, m4)),
            (sds(px3), Keep(2)),
        ],
        [pltpu.VMEM((geo.px4, VIEWS, c3), F32)],
    )
    st, wst = after(st, wst)
    wst = [wst, over_ch(wst, 1)]
    a4, b4 = sync_stats(st, cnt3)
    w_stride_all = [(wst, Flow("w4", 0, (9 * m4, m4)))]
    pre5, cols, st = run(
        "stride",
        k(k_stride),
        smem
        + n4
        + n3
        + flow("big", pre4b)
        + flow("small", pre4s)
        + vm(a4, b4, gs4)
        + w_stride_all,
        [
            sds(px4),
            out("lead", (9, geo.rows4, m4), BF16),
            sds((2, m4)),
        ],
        [pltpu.VMEM(sb4, F32), pltpu.VMEM(ss4, F32)],
    )
    (dev,) = run(
        "dev_products",
        k(k_dev_products),
        smem + flow("all", devq) + x_all,
        [sds((m3 // 4 + 8, c3), BF16)],
        [pltpu.VMEM((geo.rows, 256), BF16), pltpu.VMEM((256, c3), F32)],
        ahead=8,
    )
    a5, b5, (dev,) = sync_stats(st, cnt4, free={last: [dev]})
    a5, last_in, mids = after(a5, last_in, mids)
    at_w, at_b, at_s = c3, c3 + m4, c3 + m4 + geo.qb * VIEWS

    def from_chips(base, rows):
        return [(last_in, Flow("chip", base, (rows, c4q), j)) for j in range(2)]

    wsh, wwi = from_chips(0, c3), from_chips(at_w, m4)
    cots = from_chips(at_b, geo.qb * VIEWS) + from_chips(at_s, geo.qs * VIEWS)
    side, st_side = run(
        "short",
        k(k_short),
        smem + n4 + vm(mids) + wsh,
        [fast((2, geo.px4, VIEWS, c4q)), sds((2, 2, c4q))],
    )
    pre6, act5, st = run(
        "widen",
        k(k_widen),
        smem + n4 + vm(pre5, a5, b5, gs5) + wwi + vm(st_side),
        [
            fast((2, geo.px4, VIEWS, c4q)),
            sds((geo.rows4, m4), BF16),
            sds((2, 4, c4q)),
        ],
    )
    a6, b6 = sync_stats(st, cnt4)
    out_b, out_s, dt6, sums = run(
        "total",
        k(k_total),
        smem + n4 + vm(pre6, side, a6, b6, gs6) + cots,
        [
            out("all", (geo.qb, VIEWS, c4q)),
            out("all", (geo.qs, VIEWS, c4q)),
            fast((2, geo.px4, VIEWS, c4q)),
            sds((2, 3, c4q)),
        ],
    )
    ga6, gb6 = sync_sums(sums)
    part5, dz6, dzs, t6 = run(
        "back_wide",
        k(k_back_wide),
        smem
        + n4
        + vm(dt6, pre6, side, a6, b6, gs6, ga6, gb6)
        + wwi,
        [
            sds(px4),
            sds((geo.rows4, c4q), BF16),
            sds((2, geo.rows4, c4q), BF16),
            sds((2, 3, c4q)),
        ],
    )
    other5 = over_ch(part5, 1)
    dt5, sums = call(
        "back_act5",
        k_back_act5,
        n4 + vm(part5, other5, pre5, a5, b5, gs5),
        [sds(px4), sds((2, m4))],
    )
    (dms,) = run(
        "back_short", k_back_short, smem + vm(dzs) + wsh, [sds((geo.px4, VIEWS, c3), BF16)]
    )
    dmo = over_ch(dms, 1)
    dwide, dshort = call(
        "dw_wide",
        k_dw_wide,
        vm(act5, dz6, mids, dzs),
        [sds((m4, c4q), BF16), sds((c3, c4q), BF16)],
    )
    ga5, gb5, (dwide, dshort) = sync_sums(sums, free={0: [dwide, dshort]})
    dt4b, dt4s, dz5, sums, t5 = run(
        "back_stride",
        k(k_back_stride),
        smem
        + n4
        + vm(dt5, pre5, a5, b5, gs5, ga5, gb5)
        + flow("all", pre4b, pre4s)
        + vm(a4, b4, gs4)
        + n3
        + w_stride_all,
        [fast(sb4), fast(ss4), sds((geo.rows4, m4), BF16), sds((2, m4)), sds((2, m4))],
        [pltpu.VMEM((4, geo.rows4, m4), BF16)],
    )

    def halves(rows):
        return [sds((rows // 2, 128), BF16)] * 2, pltpu.VMEM((2, rows // 2, 128), F32)

    outs, full = halves(9 * m4)
    parts = run("dw_stride", k_dw_stride, smem + flow("lead", cols) + vm(dz5), outs, [full])
    stride_train = Train("stride", pairs, parts)
    ga4, gb4, sends = sync_sums(sums, free={0: stride_train.sends()})
    stride_train.launch(sends)
    dt3, dz4, sums, t4 = run(
        "back_narrow",
        k(k_back_narrow),
        smem
        + n3
        + vm(dt4b, dt4s)
        + flow("big", pre4b)
        + flow("small", pre4s)
        + vm(a4, b4, gs4, ga4, gb4)
        + flow("px", keep3)
        + x_all
        + vm(a3, b3, gs3, dms, dmo)
        + w_narrow_all,
        [
            fast((geo.rows, c3), BF16),
            out("rows", (geo.rows, m4), BF16),
            sds((2, c3)),
            sds((2, m4)),
        ],
    )
    came = stride_train.received
    stride_train.advance()
    ga3, gb3, sends = sync_sums(sums, wait={0: came}, free={last: stride_train.sends()})
    stride_train.launch(sends)
    dt2, dz3, dt3q, sums, t3 = run(
        "back_expand",
        k(k_back_expand),
        smem
        + n3
        + vm(dt3)
        + flow("px", keep3)
        + vm(a3, b3, gs3, ga3, gb3)
        + flow("px", keep2)
        + vm(a2, b2, gs2)
        + w_expand_all,
        [
            fast(px1),
            out("rows", (geo.rows, c3 // 4), BF16),
            out("rows", (geo.rows, c3 // 4), BF16),
            sds((2, m3)),
            sds((2, c3)),
        ],
        [
            pltpu.VMEM((2 * hb * VIEWS, c3), BF16),
            pltpu.VMEM((2 * hs * VIEWS, c3), BF16),
        ],
    )
    came = stride_train.received
    stride_train.advance()
    outs, full = halves(c3 + (c3 // 4 // 128) * m3)
    parts = call("dw_mid", k_dw_mid, smem + vm(mid, dz4, act2, dz3), outs, [full])
    mid_train = Train("mid", pairs, parts)
    ga2, gb2, (mid_send, *sends) = sync_sums(
        sums, wait={0: came}, free={0: mid_train.sends(), last: stride_train.sends()}
    )
    mid_train.launch([mid_send])
    stride_train.launch(sends)
    dt1, dz2, sums, t2, dt1q = run(
        "back_mix",
        k(k_back_mix),
        smem
        + n3
        + vm(dt2)
        + flow("px", keep2)
        + vm(a2, b2, gs2, ga2, gb2)
        + flow("px", keep1)
        + vm(a1, b1, gs1)
        + w_back,
        [
            out("px", px1),
            out("all", (geo.rows, m3), BF16),
            sds((2, m3)),
            sds((2, m3)),
            out("rows", (geo.rows, 128), BF16),
        ],
        [pltpu.VMEM(wb_shape, BF16), pltpu.VMEM(ws_shape, BF16)],
    )
    came = stride_train.received + mid_train.received
    stride_train.advance()
    mid_train.advance()
    mix_rows = 9 * m3 // 128 * (m3 // 4)
    (dmix,) = call(
        "dw_mix",
        k(k_dw_mix),
        smem + vm(winb, wins, dz2),
        [sds((mix_rows, 128))],
        [pltpu.VMEM((128, 3 * m3), F32)],
    )
    rows_last = mix_rows + c3 // 128 * (m3 // 4)
    outs, _ = halves(rows_last)
    parts = run(
        "dw_last",
        k(k_dw_last),
        smem + x_all + flow("all", dt1q) + vm(dmix),
        outs,
        [pltpu.VMEM((128, c3), F32), pltpu.VMEM((rows_last, 128), F32)],
        ahead=8,
    )
    last_train = Train("last", fours, parts)
    dwide, dshort, dev = lax.psum((dwide, dshort, dev), "img")
    wide = [dwide, dshort, dev]
    ga1, gb1, (last_send, mid_send, *sends) = sync_sums(
        sums,
        wait={0: came + wide},
        free={last: last_train.sends() + mid_train.sends() + stride_train.sends()},
    )
    last_train.launch([last_send])
    mid_train.launch([mid_send])
    stride_train.launch(sends)
    dwide, dshort, dev = wide
    gxb, gxs, t1, coef = run(
        "back_reduce",
        k(k_back_reduce),
        smem
        + n3
        + flow("px", dt1, keep1)
        + vm(a1, b1, gs1, ga1, gb1)
        + flow("rows", dt3q)
        + w_in,
        [
            out("big_px", (geo.pb, VIEWS, c3 // 4)),
            out("small_px", (geo.ps, VIEWS, c3 // 4)),
            sds((2, m3)),
            sds((3, m3)),
        ],
    )
    def unpack(name, a, b, plan):
        shapes = [((lead,) if lead > 1 else ()) + (rows, cols) for lead, rows, cols in plan]
        return call(
            name,
            functools.partial(k_unpack, plan),
            smem + vm(a, b),
            [sds(shape) for shape in shapes],
            [pltpu.VMEM((2,) + a.shape, F32)],
        )

    trains = (last_train, mid_train, stride_train)
    gxb, dwide, dshort, dev, coef, *came = after(
        gxb, dwide, dshort, dev, coef, *[train.received[0] for train in trains]
    )
    for train, first in zip(trains, came):
        train.received[0] = first
    (dstride,) = unpack("out_stride", *stride_train.finish(), [(1, 9 * m4, 128)])
    dnarrow, dexpand = unpack(
        "out_mid", *mid_train.finish(), [(1, c3, m4 // 4), (1, m3, c3 // 4)]
    )
    last_train.to_last()
    dwide, dshort = [v.astype(F32) for v in (dwide, dshort)]
    coef = lax.dynamic_slice_in_dim(coef, q * (m3 // 4), m3 // 4, 1)[:, :, None]
    dstride, dwide, dshort, *last_train.received = lax.optimization_barrier(
        (dstride, dwide, dshort, *last_train.received)
    )
    mine, other = last_train.finish()
    dmix, dreduce = call(
        "out_last",
        k_out_last,
        smem + vm(mine, other, dev, coef),
        [sds((9, m3 // 4, m3)), sds((m3 // 4, c3))],
        [pltpu.VMEM((2,) + mine.shape, F32)],
    )

    def views_first(v, side):
        return jnp.transpose(v.reshape(side, side, VIEWS, v.shape[2]), (2, 0, 1, 3))

    small = call(
        "small_outputs",
        k_small_outputs,
        smem + vm(t1, t2, t3, t4, t5, t6[0], gxs[0]),
        [sds((2, m3 // 4))] * 2
        + [sds((1, c3 // 4))] * 2
        + [sds((2, m4 // 4))] * 2
        + [sds((2, c4q))] * 2,
        slack=4,
    )
    small[2], small[3] = small[2][0], small[3][0]
    return (
        views_first(out_b, hb // 2),
        views_first(out_s, hs // 2),
        views_first(gxb, hb),
        views_first(gxs, hs),
        dreduce.T,
        jnp.transpose(dmix.reshape(3, 3, m3 // 4, m3), (0, 1, 3, 2)),
        dexpand,
        dnarrow,
        dstride.reshape(3, 3, m4, m4 // 4),
        dwide,
        dshort,
        *small,
    )


def solution(mesh):
    act = P("img", None, None, "ch")
    flat, taps, vec = P(None, "ch"), P(None, None, None, "ch"), P("ch")
    in_specs = (act,) * 4 + (P(), flat, taps, flat, flat, taps, flat, flat)
    in_specs += (flat, flat, vec, vec, flat, flat, flat, flat)
    out_specs = (act,) * 4 + (flat, taps, flat, flat, taps, flat, flat)
    out_specs += (flat, flat, vec, vec, flat, flat, flat, flat)
    return jax.shard_map(
        functools.partial(per_device, mesh.shape["img"], mesh.shape["ch"]),
        mesh=mesh,
        in_specs=in_specs,
        out_specs=out_specs,
        check_vma=False,
    )
```

```python
import functools
import math

import jax
import jax.numpy as jnp
from jax import lax
from jax.experimental import pallas as pl
from jax.experimental.pallas import tpu as pltpu
from jax.sharding import PartitionSpec as P

EPS = 1e-05
G0 = 0.7978845608028654
G1 = G0 * 0.044715
F32 = jnp.float32
BF16 = jnp.bfloat16
VIEWS = 8

ANY = pl.BlockSpec(memory_space=pl.ANY)
HBM = pl.BlockSpec(memory_space=pltpu.HBM)
VMEM = pl.BlockSpec(memory_space=pltpu.VMEM)
SMEM = pl.BlockSpec(memory_space=pltpu.SMEM)


def sds(shape, dtype=F32):
    return jax.ShapeDtypeStruct(tuple(shape), dtype)


class Flow:
    WHOLE = ("w", "w4", "all", "chip", "w_in", "w_ahead", "w_back")

    def __init__(self, kind, base=0, shape=None, which=0):
        self.kind, self.base, self.shape, self.which = kind, base, shape, which

    def keys(self, geo, shape):
        parts = (0, 1)
        if self.kind in ("big", "big_px"):
            parts = (0,)
        if self.kind in ("small", "small_px"):
            parts = (1,)
        if self.kind not in ("lead",) + self.WHOLE:
            return [(part, n) for part in parts for n in range(len(geo.groups[part]))]
        if self.kind == "lead":
            return list(range(shape[0]))
        return [None]

    def buffer(self, geo, shapes, dtype):
        if self.kind == "x":
            return pltpu.VMEM((4, geo.rows, shapes[0][1]), dtype)
        if self.kind == "w":
            return pltpu.VMEM(self.shape, dtype)
        if self.kind in ("chip", "w4"):
            return pltpu.VMEM(self.shape, dtype)
        c = shapes[0][-1]
        if self.kind.startswith("w_"):
            return pltpu.VMEM({"w_in": (4, c, c), "w_ahead": (3, c, 3 * c), "w_back": (9, c, c)}[self.kind], dtype)
        return pltpu.VMEM(tuple(shapes[0]), dtype)

    def pairs(self, geo, q, hbm, buf, key):
        if self.kind == "w":
            rows, n = buf.shape[0], buf.shape[1] // 4
            found = []
            for p in range(4):
                for b in range(n // 128):
                    at = pl.ds(pl.multiple_of((q ^ p) * n + 128 * b, 128), 128)
                    found.append((hbm[p].at[pl.ds(self.base + rows * b, rows)], buf.at[:, at]))
            return found
        if self.kind.startswith("w_"):
            c = buf.shape[1]
            n = c // 4
            found = []
            for p in range(4):
                at = pl.ds(pl.multiple_of((q ^ p) * n, n), n)
                for t in range(4 if self.kind == "w_in" else 9):
                    src = hbm[p].at[pl.ds(self.base + n * t, n)]
                    if self.kind == "w_ahead":
                        found.append((src, buf.at[t // 3, at, pl.ds(t % 3 * c, c)]))
                    else:
                        found.append((src, buf.at[t, at]))
            return found
        if self.kind == "chip":
            return [(hbm[0].at[(q >> 1) ^ self.which, pl.ds(self.base, buf.shape[0])], buf)]
        if self.kind == "w4":
            n = buf.shape[1] // 4
            found = []
            for chip in range(2):
                for other in range(2):
                    at = pl.multiple_of((2 * chip + ((q & 1) ^ other)) * n, n)
                    found.append((hbm[other].at[chip], buf.at[:, pl.ds(at, n)]))
            return found
        if key is None:
            return [(hbm[0], buf)]
        if self.kind == "lead":
            return [(hbm[0].at[key], buf.at[key])]
        part, group = key
        i, end = geo.groups[part][group]
        pix, npx, row, nrows = geo.step(part, i)
        npx, nrows, first = npx * (end - i), nrows * (end - i), pix - geo.parts[part][1]
        if self.kind == "px":
            at = pl.ds(pix, npx)
        elif self.kind == "rows":
            at = pl.ds(row, nrows)
        elif self.kind in ("big_px", "small_px"):
            at = pl.ds(first, npx)
        elif self.kind == "x":
            local = pl.ds(first * VIEWS, nrows)
            return [
                (hbm[4 * part + p].at[local], buf.at[q ^ p, pl.ds(row, nrows)]) for p in range(4)
            ]
        else:
            at = pl.ds(i, end - i)
            return [(hbm[0].at[:, :, at], buf.at[:, :, at])]
        return [(hbm[0].at[at], buf.at[at])]


class Moves:
    def __init__(self, geo, q, ahead):
        self.geo, self.q, self.flows, self.kept, self.ahead = geo, q, [], [], ahead

    def add(self, flow, hbm, buf, sem, inward):
        self.flows.append((flow, hbm, buf, sem, inward))

    def copies(self, entry, key):
        flow, hbm, buf, sem, inward = entry
        if flow.kind in flow.WHOLE:
            at = 0
        elif flow.kind == "lead":
            at = key
        elif flow.kind in ("px", "rows", "x"):
            at = (0, len(self.geo.groups[0]))[key[0]] + key[1]
        else:
            at = key[1]
        pairs = flow.pairs(self.geo, self.q, hbm, buf, key)
        return [
            pltpu.make_async_copy(*((a, b) if inward else (b, a)), sem.at[n, at])
            for n, (a, b) in enumerate(pairs)
        ]

    def entries(self, inward, key):
        for entry in self.flows:
            flow = entry[0]
            if entry[4] != inward:
                continue
            if key is None:
                fits = flow.kind in flow.WHOLE
            elif isinstance(key, int):
                fits = flow.kind == "lead" and key < entry[1][0].shape[0]
            else:
                kinds = ("px", "rows", "x") + (("big", "big_px"), ("small", "small_px"))[key[0]]
                fits = flow.kind in kinds
            if fits:
                yield entry

    def start(self, inward, key):
        for entry in self.entries(inward, key):
            for c in self.copies(entry, key):
                c.start()

    def wait(self, inward, key):
        for entry in self.entries(inward, key):
            for c in self.copies(entry, key):
                c.wait()

    def begin(self, hold):
        self.order = [(part, n) for part in range(2) for n in range(len(self.geo.groups[part]))]
        if hold:
            self.start(True, None)
            return
        self.start(True, self.order[0])
        self.start(True, None)
        for key in self.order[1 : self.ahead]:
            self.start(True, key)
        for n in range(self.ahead):
            self.start_lead(n)
        streams = any(e[4] and e[0].kind not in ("lead",) + Flow.WHOLE for e in self.flows)
        if not streams:
            for c in self.kept:
                c.start()

    def start_steps(self):
        for key in self.order:
            self.start(True, key)

    def start_lead(self, n):
        for entry in self.flows:
            if entry[4] and entry[0].kind == "lead" and n < entry[1][0].shape[0]:
                for c in self.copies(entry, n):
                    c.start()

    def ready(self):
        self.wait(True, None)

    def arrive(self, *key):
        if len(key) == 1:
            self.wait(True, key[0])
            self.start_lead(key[0] + self.ahead)
            return
        self.wait(True, key)
        at = self.order.index(key)
        if at + self.ahead < len(self.order):
            self.start(True, self.order[at + self.ahead])
        streams = any(e[4] and e[0].kind not in ("lead",) + Flow.WHOLE for e in self.flows)
        if at == 0 and streams:
            for c in self.kept:
                c.start()

    def leave(self, *key):
        self.start(False, key if len(key) > 1 else key[0])

    def send(self, *refs):
        for entry in self.entries(False, None):
            if any(entry[2] is r for r in refs):
                for c in self.copies(entry, None):
                    c.start()

    def finish(self):
        for entry in self.flows:
            if not entry[4]:
                shape = entry[1][0].shape
                for key in entry[0].keys(self.geo, shape):
                    for c in self.copies(entry, key):
                        c.wait()
        for c in self.kept:
            c.wait()


class Keep:
    kind = "keep"

    def __init__(self, source):
        self.source = source


def fast(shape, dtype=F32):
    return pltpu.VMEM(tuple(shape), dtype)


def scoped_bytes(v):
    return math.prod(v.shape) * jnp.dtype(v.dtype).itemsize


def in_hbm(v):
    return pltpu.with_memory_space_constraint(v, pltpu.HBM)


def call(name, kernel, ins, outs, scratch=(), cost=None, order=False, geo=None, slack=14, ahead=3, hold=False, staying=0):
    if order:
        inner, n_in, n_out = kernel, len(ins), len(outs)

        def kernel(*refs):
            rest = refs[n_in:]
            return inner(*refs[:n_in], *rest[n_out:], *rest[:n_out])

    outs = [o if isinstance(o, tuple) else (o, VMEM) for o in outs]
    arrays, specs, moved = [], [], []
    for a, spec in ins:
        group = a if isinstance(a, list) else [a]
        flow = isinstance(spec, Flow)
        arrays += [in_hbm(v) for v in group] if flow else group
        specs += [HBM if flow else spec] * len(group)
        moved.append((spec if flow else None, len(group), [v.shape for v in group], group[0].dtype))
    out_shapes, out_specs = [], []
    for shape, spec in outs:
        flow = isinstance(spec, (Flow, Keep))
        out_shapes.append(pltpu.HBM(shape.shape, shape.dtype) if flow else shape)
        out_specs.append(HBM if flow else spec)
        moved.append((spec if flow else None, 1, [shape.shape], shape.dtype))
    extra = []
    for flow, _, shapes, dtype in moved:
        if isinstance(flow, Keep):
            extra += [pltpu.SemaphoreType.DMA((1,))]
        elif flow:
            keys = len(flow.keys(geo, shapes[0]))
            copies = {"x": 4, "w": 4, "w4": 4, "w_in": 16, "w_ahead": 36, "w_back": 36}.get(flow.kind, 1)
            if flow.kind == "w":
                copies = flow.shape[1] // 128
            extra += [flow.buffer(geo, shapes, dtype), pltpu.SemaphoreType.DMA((copies, keys))]
    body = kernel
    if extra:

        def body(*refs):
            n_io = sum(n for _, n, _, _ in moved)
            given, own, rest = list(refs[:n_io]), refs[n_io : n_io + len(scratch)], refs[n_io + len(scratch) :]
            rest = list(rest)
            moves = Moves(geo, given[0][0], ahead)
            args = []
            for n, (flow, count, _, _) in enumerate(moved):
                group, given = given[:count], given[count:]
                if not flow:
                    args += group
                    continue
                if isinstance(flow, Keep):
                    moves.kept.append(pltpu.make_async_copy(args[flow.source], group[0], rest[0].at[0]))
                    rest = rest[1:]
                    continue
                buf, sem = rest[:2]
                rest = rest[2:]
                moves.add(flow, group, buf, sem, n < len(ins))
                args.append(buf)
            moves.begin(hold)
            kernel(moves, *args, *own)
            moves.finish()

    scratch = list(scratch)
    def held(v):
        pinned = "vmem" in str(getattr(v, "memory_space", "")).lower()
        return 0 if pinned else scoped_bytes(v)

    need = sum(held(jax.typeof(a)) for a, spec in zip(arrays, specs) if spec is VMEM)
    need += sum(held(o) for o, spec in zip(out_shapes, out_specs) if spec is VMEM)
    need += sum(
        scoped_bytes(v)
        for v in scratch + extra
        if getattr(v, "memory_space", None) == pltpu.VMEM
    )
    need -= staying
    result = pl.pallas_call(
        body,
        out_shape=out_shapes,
        in_specs=specs,
        out_specs=out_specs,
        scratch_shapes=scratch + extra,
        compiler_params=pltpu.CompilerParams(vmem_limit_bytes=need + need // 16 + (slack << 20)),
        cost_estimate=cost,
        name=name,
    )(*arrays)
    return list(result)


def vm(*arrays):
    return [(a, VMEM) for a in arrays]


def nn(a, b):
    return lax.dot_general(a, b, (((1,), (0,)), ((), ())), preferred_element_type=F32)


def nt(a, b):
    return lax.dot_general(a, b, (((1,), (1,)), ((), ())), preferred_element_type=F32)


def tn(a, b):
    return lax.dot_general(a, b, (((0,), (0,)), ((), ())), preferred_element_type=F32)


def gelu(t):
    half = 0.5 * t
    return half + half * jnp.tanh(t * (G0 + G1 * (t * t)))


def gelu_both(t):
    sq = t * t
    half = 0.5 * t
    th = jnp.tanh(t * (G0 + G1 * sq))
    return half + half * th, 0.5 + 0.5 * th + half * (1.0 - th * th) * (G0 + (3.0 * G1) * sq)


def gelu_slope(t):
    sq = t * t
    th = jnp.tanh(t * (G0 + G1 * sq))
    return 0.5 * (1.0 + th) + (0.5 * t) * (1.0 - th * th) * (G0 + (3.0 * G1) * sq)


def live_rows(count, chans):
    return (lax.broadcasted_iota(jnp.int32, (VIEWS, chans), 0) < count).astype(F32)


def rows_sum(v):
    return jnp.sum(v, axis=0, keepdims=True)


def merged(sa, sb, na, nb):
    total = na + nb
    mean = (na * sa[0:1] + nb * sb[0:1]) / total
    diff = sb[0:1] - sa[0:1]
    square = sa[1:2] + sb[1:2] + diff * diff * (na * nb / total)
    return mean, lax.rsqrt(square / total + EPS)


def as_rows(v):
    return v.reshape(v.shape[0] * v.shape[1], v.shape[2])


def as_pix_rows(v):
    return v.reshape(v.shape[0] * v.shape[1], VIEWS, v.shape[3])


def as_pix(v):
    return v.reshape(v.shape[0] // VIEWS, VIEWS, v.shape[1])


class Geo:
    def __init__(self, hb, hs):
        self.hb, self.hs = hb, hs
        self.pb, self.ps = hb * hb, hs * hs
        self.px = self.pb + self.ps
        self.rows = self.px * VIEWS
        self.qb, self.qs = self.pb // 4, self.ps // 4
        self.px4 = self.qb + self.qs
        self.rows4 = self.px4 * VIEWS
        self.parts = ((hb, 0), (hs, self.pb))
        self.groups = [self.cuts(hb // 2, 1), self.cuts(hs // 2, 2)]
        self.spans = [[list(range(n))[: n // 2], list(range(n))[n // 2 :]] for n in map(len, self.groups)]
        self.bands = [[(0, hb // 2), (hb // 2, hb)], [(0, hs)]]

    @staticmethod
    def cuts(steps, first):
        at = sorted({0, steps} | set(range(first, steps, 2)))
        return list(zip(at[:-1], at[1:]))

    @staticmethod
    def aligned(n):
        return n if isinstance(n, int) else pl.multiple_of(n, 16)

    def step(self, part, i):
        side, start = self.parts[part]
        npx = 2 * side
        return start + i * npx, npx, self.aligned((start + i * npx) * VIEWS), npx * VIEWS

    def staged(self, io, before, product, carries):
        out = []
        for part in range(2):
            carry = carries[part]
            for span in self.spans[part]:
                lo, hi = self.groups[part][span[0]][0], self.groups[part][span[-1]][1]
                for n in span:
                    io.arrive(part, n)
                pix, npx, row, nrows = self.step(part, lo)
                if before:

                    def early(i, c, part=part):
                        before(part, i, *self.step(part, i))
                        return c

                    lax.fori_loop(lo, hi, early, 0)
                carry = product(part, pix, npx * (hi - lo), row, nrows * (hi - lo), carry)
                for n in span:
                    io.leave(part, n)
            out.append(carry)
        return out

    def loop(self, body, carries, arrive=None, leave=None):
        out = []
        for part in range(2):

            def run(i, carry, part=part):
                for n, (lo, hi) in enumerate(self.groups[part]):
                    if arrive:
                        pl.when(i == lo)(functools.partial(arrive.arrive, part, n))
                carry = body(part, i, *self.step(part, i), carry)
                for n, (lo, hi) in enumerate(self.groups[part]):
                    if leave:
                        pl.when(i == hi - 1)(functools.partial(leave.leave, part, n))
                return carry

            out.append(lax.fori_loop(0, self.groups[part][-1][1], run, carries[part]))
        return out


def finish_stats(geo, ref, sums, lives, count, out, quarter=None):
    mean = (rows_sum(sums[0] * lives[0]) + rows_sum(sums[1] * lives[1])) / count

    def body(part, i, pix, npx, row, nrows, carry):
        dev = ref[pl.ds(pix, npx)] - mean
        return carry + jnp.sum(dev * dev, axis=0)

    zero = jnp.zeros(sums[0].shape, F32)
    sq = geo.loop(body, [zero, zero])
    out[0:1] = mean
    out[1:2] = rows_sum(sq[0] * lives[0]) + rows_sum(sq[1] * lives[1])


def block_stats(geo, value, lives, count):
    big, small = value[: geo.qb], value[geo.qb :]
    mean = (
        rows_sum(jnp.sum(big, axis=0) * lives[0]) + rows_sum(jnp.sum(small, axis=0) * lives[1])
    ) / count
    db, ds = big - mean, small - mean
    square = rows_sum(jnp.sum(db * db, axis=0) * lives[0]) + rows_sum(
        jnp.sum(ds * ds, axis=0) * lives[1]
    )
    return mean, square


def k_reduce(geo, io, me, nf, xs, wt, pre, stats):
    io.ready()
    chans = wt.shape[1]
    lives = [live_rows(me[1], chans), live_rows(me[2], chans)]

    def product(part, pix, npx, row, nrows, carry):
        acc = None
        for j in range(4):
            d = nt(xs[j, row : row + nrows, :], wt[j])
            acc = d if acc is None else acc + d
        z = as_pix(acc)
        pre[pix : pix + npx] = z
        return carry + jnp.sum(z, axis=0)

    zero = jnp.zeros((VIEWS, chans), F32)
    sums = geo.staged(io, None, product, [zero, zero])
    finish_stats(geo, pre, sums, lives, nf[0], stats)


def k_counts(ni, sizes, counts, me, nf3, cnt3, nf4, cnt4):
    img = lax.axis_index("img")
    levels = ni.bit_length() - 1
    me[0] = lax.axis_index("ch").astype(jnp.int32)
    me[1] = counts[img, 0]
    me[2] = counts[img, 1]
    me[3] = img
    for (big, small), nf, cnt in zip(sizes, (nf3, nf4), (cnt3, cnt4)):

        def group(shift, index):
            def add(i, total):
                at = index * (1 << shift) + i
                return total + counts[at, 0] * big + counts[at, 1] * small

            return lax.fori_loop(0, 1 << shift, add, jnp.int32(0)).astype(F32)

        nf[0] = group(0, img)
        for m in range(2):
            nf[1 + m] = group(levels - 1, (img >> (levels - 1)) ^ m)
        row, k = 0, 0
        while k < levels - 1:
            bits = 2 if k == 0 else 1
            for m in range(8):
                cnt[row + m] = group(k, (img >> k) ^ m) if m < 1 << bits else jnp.float32(0.0)
            row, k = row + 8, k + bits


def k_pack_params(gm3, sm3, go3, so3, gm4, sm4, go4, so4, out, rows):
    rows[...] = jnp.zeros(rows.shape, F32)
    rows[0:2, 0:64] = gm3[...]
    rows[2:4, 0:64] = sm3[...]
    for b in range(2):
        lanes = slice(128 * b, 128 * b + 128)
        rows[4 + b : 5 + b] = go3[:, lanes]
        rows[6 + b : 7 + b] = so3[:, lanes]
    rows[8:10] = gm4[...]
    rows[10:12] = sm4[...]
    for n in range(2):
        for b in range(4):
            lanes = slice(128 * b, 128 * b + 128)
            rows[12 + 4 * n + b : 13 + 4 * n + b] = go4[n : n + 1, lanes]
            rows[20 + 4 * n + b : 21 + 4 * n + b] = so4[n : n + 1, lanes]
    v = rows[...]
    high = v.astype(BF16)
    rest = v - high.astype(F32)
    mid = rest.astype(BF16)
    low = (rest - mid.astype(F32)).astype(BF16)
    out[0:32, 0:128] = high
    out[0:32, 128:256] = mid
    out[32:64, 0:128] = low
    out[32:64, 128:256] = jnp.zeros_like(low)


def k_unpack_params(base, me, p0, p1, p2, p3, gs1, gs2, gs3, gs4, gs5, gs6, buf, sem):
    copies = [
        pltpu.make_async_copy(p.at[pl.ds(base, 64)], buf.at[n], sem.at[n])
        for n, p in enumerate((p0, p1, p2, p3))
    ]
    for c in copies:
        c.start()
    for c in copies:
        c.wait()
    rows = []
    for n in range(4):
        v = buf[n].astype(F32)
        rows.append(v[0:32, 0:128] + v[0:32, 128:256] + v[32:64, 0:128])
    odd = me[0] & 1
    for chip in range(2):
        mine, other = rows[2 * chip][:, 0:64], rows[2 * chip + 1][:, 0:64]
        both = jnp.where(
            odd == 0,
            jnp.concatenate([mine, other], axis=1),
            jnp.concatenate([other, mine], axis=1),
        )
        at = pl.ds(pl.multiple_of(((me[0] >> 1) ^ chip) * 128, 128), 128)
        for n, gs in enumerate((gs1, gs2)):
            gs[0:1, at] = both[n : n + 1]
            gs[1:2, at] = both[2 + n : 3 + n]
    for p, v in enumerate(rows):
        for b in range(2):
            at = pl.ds(pl.multiple_of((me[0] ^ p) * 256 + 128 * b, 128), 128)
            gs3[0:1, at] = v[4 + b : 5 + b]
            gs3[1:2, at] = v[6 + b : 7 + b]
        at = pl.ds(pl.multiple_of((me[0] ^ p) * 128, 128), 128)
        for n, gs in enumerate((gs4, gs5)):
            gs[0:1, at] = v[8 + n : 9 + n]
            gs[1:2, at] = v[10 + n : 11 + n]
    for chip in range(2):
        v = rows[2 * chip]
        for n in range(2):
            for b in range(4):
                lanes = slice(128 * b, 128 * b + 128)
                gs6[chip, 2 * n : 2 * n + 1, lanes] = v[12 + 4 * n + b : 13 + 4 * n + b]
                gs6[chip, 2 * n + 1 : 2 * n + 2, lanes] = v[20 + 4 * n + b : 21 + 4 * n + b]


def k_merge(first, n, cnt, *refs):
    arrays, out = refs[:n], refs[n]
    for at in range(0, out.shape[-2], 2):
        mean_at, sq_at = (..., slice(at, at + 1), slice(None)), (..., slice(at + 1, at + 2), slice(None))
        groups = [(cnt[first + m], a[mean_at], a[sq_at]) for m, a in enumerate(arrays)]
        while len(groups) > 1:
            pairs = []
            for (na, ma, qa), (nb, mb, qb) in zip(groups[::2], groups[1::2]):
                total = na + nb
                diff = mb - ma
                pairs.append(
                    (total, (na * ma + nb * mb) / total, qa + qb + diff * diff * (na * nb / total))
                )
            groups = pairs
        out[mean_at], out[sq_at] = groups[0][1], groups[0][2]


def k_add(n, *refs):
    values = [r[...] for r in refs[:n]]
    while len(values) > 1:
        values = [a + b for a, b in zip(values[::2], values[1::2])]
    refs[n][...] = values[0]


def side_shift(v, by):
    zero = jnp.zeros((v.shape[0], 1) + v.shape[2:], v.dtype)
    if by > 0:
        return jnp.concatenate([zero, v[:, :-1]], axis=1)
    return jnp.concatenate([v[:, 1:], zero], axis=1)


def store_shifted(buf, row, nrows, side, v, order):
    img = v.reshape(2, side, VIEWS, v.shape[-1])
    chans = v.shape[-1]
    forms = [side_shift(img, 1), img, side_shift(img, -1)]
    for lane, k in enumerate(order):
        flat = forms[k].reshape(nrows, chans).astype(BF16)
        buf[pl.ds(row, nrows), lane * chans : (lane + 1) * chans] = flat


def put_phases(ref, i, v):
    for k in range(4):
        ref[k // 2, k % 2, i] = v[k // 2, :, k % 2]


def get_phases(ref, i):
    rows = [jnp.stack([ref[r, 0, i], ref[r, 1, i]], axis=1) for r in range(2)]
    return jnp.stack(rows)


def zero_edges(buf, edge):
    total = buf.shape[0]
    buf[0:edge, :] = jnp.zeros((edge, buf.shape[1]), BF16)
    buf[total - edge : total, :] = jnp.zeros((edge, buf.shape[1]), BF16)


def k_mix(geo, io, me, nf, pre1, sa, sb, gs, w, pre2, wb, ws, stats, dev, center):
    chans = pre1.shape[-1]
    lives = [live_rows(me[1], chans), live_rows(me[2], chans)]
    mean, inv = merged(sa[...], sb[...], nf[1], nf[2])
    scale, shift = gs[0:1] * inv, gs[1:2]
    bufs = (wb, ws)
    for part, (side, _) in enumerate(geo.parts):
        zero_edges(bufs[part], side * VIEWS)

    def act(part, i, pix, npx, row, nrows, carry):
        a = gelu((pre1[pl.ds(pix, npx)] - mean) * scale + shift)
        own = (pre1[pl.ds(pix, npx), :, lanes] - center[:, lanes]) * lives[part][:, 0:128]
        dev[pl.ds(row, nrows), :] = as_rows(own).astype(BF16)
        side = geo.parts[part][0]
        at = pl.multiple_of(side * VIEWS + i * nrows, 16)
        store_shifted(bufs[part], at, nrows, side, a, (0, 1, 2))
        return carry

    lanes, _ = own_block(me)
    center[...] = mean
    geo.loop(act, [0, 0], io)
    io.send(wb, ws, dev)
    io.ready()

    sums = [jnp.zeros((VIEWS, chans), F32)] * 2
    for part, (side, start) in enumerate(geo.parts):
        for lo, hi in geo.bands[part]:
            acc = None
            for r in range(3):
                at = (lo + r) * side * VIEWS
                d = nt(bufs[part][at : at + (hi - lo) * side * VIEWS, :], w[r])
                acc = d if acc is None else acc + d
            z = as_pix(acc)
            pre2[start + lo * side : start + hi * side] = z
            sums[part] = sums[part] + jnp.sum(z, axis=0)
    finish_stats(geo, pre2, sums, lives, nf[0], stats)


def k_expand(geo, io, me, nf, pre2, sa, sb, gs, w, pre3, act2, stats):
    chans = w.shape[1]
    lives = [live_rows(me[1], chans), live_rows(me[2], chans)]
    mean, inv = merged(sa[...], sb[...], nf[1], nf[2])
    scale, shift = gs[0:1] * inv, gs[1:2]

    def before(part, i, pix, npx, row, nrows):
        a = as_rows(gelu((pre2[pl.ds(pix, npx)] - mean) * scale + shift)).astype(BF16)
        act2[pl.ds(row, nrows), :] = a

    def product(part, pix, npx, row, nrows, carry):
        total = []
        for j in range(4):
            at = slice(256 * j, 256 * j + 256)
            z = as_pix(nn(act2[row : row + nrows, :], w[:, at]))
            pre3[pix : pix + npx, :, at] = z
            total.append(jnp.sum(z, axis=0))
        return carry + jnp.concatenate(total, axis=1)

    io.ready()
    zero = jnp.zeros((VIEWS, chans), F32)
    sums = geo.staged(io, before, product, [zero, zero])
    finish_stats(geo, pre3, sums, lives, nf[0], stats)


def k_narrow(geo, io, me, nf, pre3, xs, sa, sb, gs, w, pre4b, pre4s, mid, mids, stats, dev3, slope3, mid_even):
    chans = w.shape[1]
    lives = [live_rows(me[1], chans), live_rows(me[2], chans)]
    mean, inv = merged(sa[...], sb[...], nf[1], nf[2])
    scale, shift = gs[0:1] * inv, gs[1:2]
    pre4 = (pre4b, pre4s)

    def body(part, i, pix, npx, row, nrows, carry):
        side = geo.parts[part][0]
        half = side // 2
        for j in range(4):
            at = slice(256 * j, 256 * j + 256)
            dev = pre3[pl.ds(pix, npx), :, at] - mean[:, at]
            x = as_pix(xs[j, pl.ds(row, nrows), :].astype(F32))
            a, slope = gelu_both(dev * scale[:, at] + shift[:, at] + x)
            mid[pl.ds(row, nrows), at] = as_rows(a).astype(BF16)
            dev3[pl.ds(row, nrows), at] = as_rows(dev).astype(BF16)
            slope3[pl.ds(row, nrows), at] = as_rows(slope).astype(BF16)
            even = a.reshape(2, half, 2, VIEWS, 256)[0, :, 0]
            mid_even[pl.ds((0, geo.qb)[part] + half * i, half), :, at] = even
        z = nn(mid[pl.ds(row, nrows), :], w[...])
        put_phases(pre4[part], i, z.reshape(2, half, 2, VIEWS, chans))
        return carry + jnp.sum(as_pix(z), axis=0)

    io.ready()
    zero = jnp.zeros((VIEWS, chans), F32)
    sums = geo.loop(body, [zero, zero], io, io)
    mean4 = (rows_sum(sums[0] * lives[0]) + rows_sum(sums[1] * lives[1])) / nf[0]
    mids[...] = as_rows(mid_even[...]).astype(BF16)
    io.send(mids)
    sq = []
    for part in range(2):

        def dev2(i, carry, part=part):
            for k in range(4):
                d = pre4[part][k // 2, k % 2, i] - mean4
                carry = carry + jnp.sum(d * d, axis=0)
            return carry

        sq.append(lax.fori_loop(0, geo.parts[part][0] // 2, dev2, zero))
    stats[0:1] = mean4
    stats[1:2] = rows_sum(sq[0] * lives[0]) + rows_sum(sq[1] * lives[1])


def k_short(geo, io, me, nf, mids, w0, w1, side, stats):
    io.ready()
    chans = w0.shape[1]
    lives = [live_rows(me[1], chans), live_rows(me[2], chans)]
    for j, w in enumerate((w0, w1)):
        z = as_pix(nn(mids[...], w[...]))
        side[j] = z
        io.leave(j)
        mean, square = block_stats(geo, z, lives, nf[0])
        stats[j] = jnp.concatenate([mean, square], axis=0)


def k_stride(geo, io, me, nf, n4, pre4b, pre4s, sa, sb, gs, w, pre5, cols, stats, sb_act, ss_act):
    chans = pre4b.shape[-1]
    lives = [live_rows(me[1], chans), live_rows(me[2], chans)]
    mean, inv = merged(sa[...], sb[...], n4[1], n4[2])
    scale, shift = gs[0:1] * inv, gs[1:2]
    srcs, dsts = (pre4b, pre4s), (sb_act, ss_act)

    def act(part, i, pix, npx, row, nrows, carry):
        for k in range(4):
            at = (k // 2, k % 2, i)
            dsts[part][at] = gelu((srcs[part][at] - mean) * scale + shift)
        return carry

    geo.loop(act, [0, 0], io)
    for r in range(3):
        for c in range(3):
            flats = []
            for part in range(2):
                half = geo.parts[part][0] // 2
                v = dsts[part][(r + 1) % 2, (c + 1) % 2]
                if c == 0:
                    v = side_shift(v, 1)
                if r == 0:
                    v = jnp.concatenate([jnp.zeros((1,) + v.shape[1:], F32), v[:-1]], axis=0)
                flats.append(v.reshape(half * half * VIEWS, chans))
            t = 3 * r + c
            cols[t] = jnp.concatenate(flats, axis=0).astype(BF16)
            io.leave(t)
    io.ready()
    acc = None
    for t in range(9):
        d = nn(cols[t], w[t * chans : (t + 1) * chans, :])
        acc = d if acc is None else acc + d
    z = as_pix(acc)
    pre5[...] = z
    m5, s5 = block_stats(geo, z, lives, nf[0])
    stats[0:1] = m5
    stats[1:2] = s5


def k_widen(geo, io, me, nf, pre5, sa, sb, gs, w0, w1, st_side, pre6, act5, stats):
    chans = w0.shape[1]
    lives = [live_rows(me[1], chans), live_rows(me[2], chans)]
    mean, inv = merged(sa[...], sb[...], nf[1], nf[2])
    scale, shift = gs[0:1] * inv, gs[1:2]
    act5[...] = as_rows(gelu((pre5[...] - mean) * scale + shift)).astype(BF16)
    io.ready()
    for j, w in enumerate((w0, w1)):
        z = as_pix(nn(act5[...], w[...]))
        pre6[j] = z
        io.leave(j)
        m6, s6 = block_stats(geo, z, lives, nf[0])
        stats[j] = jnp.concatenate([m6, s6, st_side[j]], axis=0)


def k_total(geo, io, me, nf, pre6, side, sa, sb, gs, cb0, cb1, cs0, cs1, out_b, out_s, dt, sums):
    chans = pre6.shape[-1]
    lives = [live_rows(me[1], chans), live_rows(me[2], chans)]
    cots = ((cb0, cb1), (cs0, cs1))
    spans = ((0, geo.qb), (geo.qb, geo.px4))
    outs = (out_b, out_s)
    io.ready()
    for j in range(2):
        io.arrive(j)
        a, b, g = sa[j], sb[j], gs[j]
        m6, r6 = merged(a[0:2], b[0:2], nf[1], nf[2])
        ms, rs = merged(a[2:4], b[2:4], nf[1], nf[2])
        acc = [None, None, None]
        for part, (lo, hi) in enumerate(spans):
            d6 = pre6[j, lo:hi] - m6
            dd = side[j, lo:hi] - ms
            total = d6 * (g[0:1] * r6) + g[1:2] + (dd * (g[2:3] * rs) + g[3:4])
            live = lives[part]
            if j == 0:
                outs[part][...] = gelu(total) * live
            grad = gelu_slope(total) * (as_pix(cots[part][j][...].astype(F32)) * live)
            dt[j, lo:hi] = grad
            terms = [jnp.sum(v, axis=0) for v in (grad, grad * d6, grad * dd)]
            acc = [t if s is None else s + t for s, t in zip(acc, terms)]
        io.leave(j)
        if j == 0:
            io.send(out_b, out_s)
        sums[j] = jnp.concatenate(
            [rows_sum(acc[0]), rows_sum(acc[1]) * r6, rows_sum(acc[2]) * rs], axis=0
        )


def back_coefs(lives, s1, s2, inv, gain, count):
    c1 = gain * inv
    c2 = [live * (c1 * s1 / count) for live in lives]
    c3 = [live * (c1 * inv * s2 / count) for live in lives]
    return c1, c2, c3


def k_back_wide(geo, io, me, nf, dt, pre6, side, sa, sb, gs, ga, gb, w0, w1, part5, dz6, dzs, tot):
    chans = pre6.shape[-1]
    lives = [live_rows(me[1], chans), live_rows(me[2], chans)]
    total = nf[1] + nf[2]
    spans = ((0, geo.qb), (geo.qb, geo.px4))
    acc = None
    io.ready()
    for j, w in enumerate((w0, w1)):
        io.arrive(j)
        a, b, g = sa[j], sb[j], gs[j]
        s = ga[j] + gb[j]
        tot[j] = s
        m6, r6 = merged(a[0:2], b[0:2], nf[1], nf[2])
        ms, rs = merged(a[2:4], b[2:4], nf[1], nf[2])
        k1, k2, k3 = back_coefs(lives, s[0:1], s[1:2], r6, g[0:1], total)
        h1, h2, h3 = back_coefs(lives, s[0:1], s[2:3], rs, g[2:3], total)
        main, short = [], []
        for part, (lo, hi) in enumerate(spans):
            grad = dt[j, lo:hi]
            main.append(grad * k1 - k2[part] - (pre6[j, lo:hi] - m6) * k3[part])
            short.append(grad * h1 - h2[part] - (side[j, lo:hi] - ms) * h3[part])
        z6 = as_rows(jnp.concatenate(main, axis=0)).astype(BF16)
        dzs[j] = as_rows(jnp.concatenate(short, axis=0)).astype(BF16)
        io.leave(j)
        if j == 0:
            dz6[...] = z6
        d = nt(z6, w[...])
        acc = d if acc is None else acc + d
    part5[...] = as_pix(acc)


def k_back_act5(nf, mine, other, pre5, sa5, sb5, gs5, dt5, sums5):
    m5, r5 = merged(sa5[...], sb5[...], nf[1], nf[2])
    dev = pre5[...] - m5
    grad = gelu_slope(dev * (gs5[0:1] * r5) + gs5[1:2]) * (mine[...] + other[...])
    dt5[...] = grad
    sums5[0:1] = rows_sum(jnp.sum(grad, axis=0))
    sums5[1:2] = rows_sum(jnp.sum(grad * dev, axis=0)) * r5


def k_back_short(io, me, dzs, w0, w1, dms):
    io.ready()
    acc = None
    for j, w in enumerate((w0, w1)):
        d = nt(dzs[j], w[...])
        acc = d if acc is None else acc + d
    dms[...] = as_pix(acc).astype(BF16)


def k_back_stride(geo, io, me, nf, dt5, pre5, sa5, sb5, gs5, ga, gb, pre4b, pre4s, sa4, sb4, gs4, n4, w, dt4b, dt4s, dz5, sums4, tot, shifts):
    chans = pre5.shape[-1]
    lives = [live_rows(me[1], chans), live_rows(me[2], chans)]
    s = ga[...] + gb[...]
    tot[...] = s
    m5, r5 = merged(sa5[...], sb5[...], nf[1], nf[2])
    c1, c2, c3 = back_coefs(lives, s[0:1], s[1:2], r5, gs5[0:1], nf[1] + nf[2])
    spans = ((0, geo.qb), (geo.qb, geo.px4))
    imgs = []
    for part, (lo, hi) in enumerate(spans):
        half = geo.parts[part][0] // 2
        z = dt5[lo:hi] * c1 - c2[part] - (pre5[lo:hi] - m5) * c3[part]
        imgs.append(z.reshape(half, half, VIEWS, chans))

    def flat(moved):
        return jnp.concatenate([v.reshape(-1, chans) for v in moved], axis=0).astype(BF16)

    def up(v):
        return jnp.concatenate([v[1:], jnp.zeros((1,) + v.shape[1:], F32)], axis=0)

    shifts[0] = flat(imgs)
    dz5[...] = shifts[0]
    shifts[1] = flat([side_shift(v, -1) for v in imgs])
    shifts[2] = flat([up(v) for v in imgs])
    shifts[3] = flat([up(side_shift(v, -1)) for v in imgs])
    m4, r4 = merged(sa4[...], sb4[...], n4[1], n4[2])
    scale, off = gs4[0:1] * r4, gs4[1:2]
    io.ready()
    plan = {
        (0, 0): ((0, 4),),
        (0, 1): ((0, 5), (1, 3)),
        (1, 0): ((0, 7), (2, 1)),
        (1, 1): ((0, 8), (1, 6), (2, 2), (3, 0)),
    }
    t1, t2 = jnp.zeros((VIEWS, chans), F32), jnp.zeros((VIEWS, chans), F32)
    for (rp, cp), terms in plan.items():
        acc = None
        for k, t in terms:
            d = nt(shifts[k], w[t * chans : (t + 1) * chans, :])
            acc = d if acc is None else acc + d
        for part, (lo, hi) in enumerate(spans):
            half = geo.parts[part][0] // 2
            d = acc[lo * VIEWS : hi * VIEWS].reshape(half, half, VIEWS, chans)
            dev = (pre4b, pre4s)[part][rp, cp] - m4
            grad = gelu_slope(dev * scale + off) * d
            (dt4b, dt4s)[part][rp, cp] = grad
            t1 = t1 + jnp.sum(grad, axis=(0, 1))
            t2 = t2 + jnp.sum(grad * dev, axis=(0, 1))
    io.send(dt4b, dt4s)
    sums4[0:1] = rows_sum(t1)
    sums4[1:2] = rows_sum(t2) * r4


def k_back_narrow(geo, io, me, nf, dt4b, dt4s, pre4b, pre4s, sa4, sb4, gs4, ga, gb, dev3, slope3, sa3, sb3, dms, dmo, w, dt3, dz4, sums3, tot):
    chans = w.shape[1]
    wide = w.shape[0]
    lives = [live_rows(me[1], chans), live_rows(me[2], chans)]
    s = ga[...] + gb[...]
    tot[...] = s
    m4, r4 = merged(sa4[...], sb4[...], nf[1], nf[2])
    c1, c2, c3 = back_coefs(lives, s[0:1], s[1:2], r4, gs4[0:1], nf[1] + nf[2])
    _, r3 = merged(sa3[...], sb3[...], nf[1], nf[2])
    dts, pres = (dt4b, dt4s), (pre4b, pre4s)

    def body(part, i, pix, npx, row, nrows, carry):
        half = geo.parts[part][0] // 2
        dev4 = get_phases(pres[part], i) - m4
        z = get_phases(dts[part], i) * c1 - c2[part] - dev4 * c3[part]
        z = z.reshape(nrows, chans).astype(BF16)
        dz4[pl.ds(row, nrows), :] = z
        at = pl.ds((0, geo.qb)[part] + half * i, half)
        t1, t2 = [], []
        for j in range(4):
            at_j = slice(256 * j, 256 * j + 256)
            d = nt(z, w[at_j, :]).reshape(2, half, 2, VIEWS, 256)
            even = d[0, :, 0] + (dms[at, :, at_j].astype(F32) + dmo[at, :, at_j].astype(F32))
            top = jnp.stack([even, d[0, :, 1]], axis=1)
            d = jnp.concatenate([as_pix_rows(top), as_pix_rows(d[1])], axis=0)
            dev = as_pix(dev3[pl.ds(row, nrows), at_j].astype(F32))
            grad = as_pix(slope3[pl.ds(row, nrows), at_j].astype(F32)) * d
            dt3[pl.ds(row, nrows), at_j] = as_rows(grad).astype(BF16)
            t1.append(jnp.sum(grad, axis=0))
            t2.append(jnp.sum(grad * dev, axis=0))
        return carry[0] + jnp.concatenate(t1, axis=1), carry[1] + jnp.concatenate(t2, axis=1)

    io.ready()
    zero = jnp.zeros((VIEWS, wide), F32)
    (a1, a2), (b1, b2) = geo.loop(body, [(zero, zero), (zero, zero)], io, io)
    sums3[0:1] = rows_sum(a1 + b1)
    sums3[1:2] = rows_sum(a2 + b2) * r3


def k_back_expand(geo, io, me, nf, dt3, dev3, sa3, sb3, gs3, ga, gb, pre2, sa2, sb2, gs2, w, dt2, dz3, dt3q, sums2, tot, zbuf_b, zbuf_s):
    wide, chans = w.shape[1], w.shape[0]
    lives = [live_rows(me[1], wide), live_rows(me[2], wide)]
    s = ga[...] + gb[...]
    tot[...] = s
    _, r3 = merged(sa3[...], sb3[...], nf[1], nf[2])
    c1, c2, c3 = back_coefs(lives, s[0:1], s[1:2], r3, gs3[0:1], nf[1] + nf[2])
    m2, r2 = merged(sa2[...], sb2[...], nf[1], nf[2])
    scale, off = gs2[0:1] * r2, gs2[1:2]
    mine = pl.ds(pl.multiple_of(me[0] * 256, 256), 256)

    def body(part, i, pix, npx, row, nrows, carry):
        zbuf = (zbuf_b, zbuf_s)[part]
        dt3q[pl.ds(row, nrows), :] = dt3[pl.ds(row, nrows), mine]
        for j in range(4):
            at = slice(256 * j, 256 * j + 256)
            z = (
                as_pix(dt3[pl.ds(row, nrows), at].astype(F32)) * c1[:, at]
                - c2[part][:, at]
                - as_pix(dev3[pl.ds(row, nrows), at].astype(F32)) * c3[part][:, at]
            )
            zbuf[:, at] = as_rows(z).astype(BF16)
        dz3[pl.ds(row, nrows), :] = zbuf[:, mine]
        d = as_pix(nt(zbuf[...], w[...]))
        dev = pre2[pl.ds(pix, npx)] - m2
        grad = gelu_slope(dev * scale + off) * d
        dt2[pl.ds(pix, npx)] = grad
        return carry[0] + jnp.sum(grad, axis=0), carry[1] + jnp.sum(grad * dev, axis=0)

    io.ready()
    zero = jnp.zeros((VIEWS, chans), F32)
    (a1, a2), (b1, b2) = geo.loop(body, [(zero, zero), (zero, zero)], io, io)
    sums2[0:1] = rows_sum(a1 + b1)
    sums2[1:2] = rows_sum(a2 + b2) * r2


def k_back_mix(geo, io, me, nf, dt2, pre2, sa2, sb2, gs2, ga, gb, pre1, sa1, sb1, gs1, w, dt1, dz2, sums1, tot, dt1q, zb, zs):
    chans = pre2.shape[-1]
    lives = [live_rows(me[1], chans), live_rows(me[2], chans)]
    s = ga[...] + gb[...]
    tot[...] = s
    m2, r2 = merged(sa2[...], sb2[...], nf[1], nf[2])
    c1, c2, c3 = back_coefs(lives, s[0:1], s[1:2], r2, gs2[0:1], nf[1] + nf[2])
    m1, r1 = merged(sa1[...], sb1[...], nf[1], nf[2])
    scale, off = gs1[0:1] * r1, gs1[1:2]
    bufs = (zb, zs)
    for part, (side, _) in enumerate(geo.parts):
        zero_edges(bufs[part], side * VIEWS)

    def back(part, i, pix, npx, row, nrows, carry):
        z = dt2[pl.ds(pix, npx)] * c1 - c2[part] - (pre2[pl.ds(pix, npx)] - m2) * c3[part]
        dz2[pl.ds(row, nrows), :] = as_rows(z).astype(BF16)
        side = geo.parts[part][0]
        at = pl.multiple_of(side * VIEWS + i * nrows, 16)
        store_shifted(bufs[part], at, nrows, side, z, (2, 1, 0))
        return carry

    lanes, _ = own_block(me)
    geo.loop(back, [0, 0], io)
    io.send(dz2)
    io.ready()

    for part, (side, start) in enumerate(geo.parts):
        for lo, hi in geo.bands[part]:
            acc = None
            for r in range(3):
                at = (lo + 2 - r) * side * VIEWS
                taps = w[3 * r : 3 * r + 3].reshape(3 * chans, chans)
                d = nn(bufs[part][at : at + (hi - lo) * side * VIEWS, :], taps)
                acc = d if acc is None else acc + d
            dt1[start + lo * side : start + hi * side] = as_pix(acc)

    def finish(part, i, pix, npx, row, nrows, carry):
        dev = pre1[pl.ds(pix, npx)] - m1
        grad = gelu_slope(dev * scale + off) * dt1[pl.ds(pix, npx)]
        dt1[pl.ds(pix, npx)] = grad
        dt1q[pl.ds(row, nrows), :] = as_rows(dt1[pl.ds(pix, npx), :, lanes]).astype(BF16)
        return carry[0] + jnp.sum(grad, axis=0), carry[1] + jnp.sum(grad * dev, axis=0)

    zero = jnp.zeros((VIEWS, chans), F32)
    (a1, a2), (b1, b2) = geo.loop(finish, [(zero, zero), (zero, zero)], None, io)
    sums1[0:1] = rows_sum(a1 + b1)
    sums1[1:2] = rows_sum(a2 + b2) * r1


def k_back_reduce(geo, io, me, nf, dt1, pre1, sa1, sb1, gs1, ga, gb, dt3q, wt, gxb, gxs, tot, coef):
    chans = pre1.shape[-1]
    lives = [live_rows(me[1], chans), live_rows(me[2], chans)]
    s = ga[...] + gb[...]
    tot[...] = s
    m1, r1 = merged(sa1[...], sb1[...], nf[1], nf[2])
    c1, c2, c3 = back_coefs(lives, s[0:1], s[1:2], r1, gs1[0:1], nf[1] + nf[2])
    io.ready()
    total = nf[1] + nf[2]
    coef[0:1] = c1
    coef[1:2] = c1 * s[0:1] / total
    coef[2:3] = c1 * r1 * s[1:2] / total

    def body(part, i, pix, npx, row, nrows, carry):
        z = dt1[pl.ds(pix, npx)] * c1 - c2[part] - (pre1[pl.ds(pix, npx)] - m1) * c3[part]
        z = as_rows(z).astype(BF16)
        g = as_pix(nn(z, wt[me[0]])) + as_pix(dt3q[pl.ds(row, nrows), :].astype(F32))
        (gxb, gxs)[part][pl.ds(pix - (0, geo.pb)[part], npx)] = g
        return carry

    geo.loop(body, [0, 0], io, io)


def k_dw_wide(act5, dz6, mids, dzs, dwide, dshort):
    dwide[...] = tn(act5[...], dz6[...]).astype(BF16)
    dshort[...] = tn(mids[...], dzs[0]).astype(BF16)


def lane_blocks(v):
    return [v[:, 128 * b : 128 * b + 128] for b in range(v.shape[1] // 128)]


def put_halves(me, full, keep, send):
    bit = me[3] & 1
    keep[...] = full[bit].astype(BF16)
    send[...] = full[1 - bit].astype(BF16)


def k_dw_stride(io, me, cols, dz5, keep, send, full):
    mine = pl.ds(pl.multiple_of(me[0] * 128, 128), 128)
    z = dz5[:, mine]
    rows = full.shape[1]
    for t in range(9):
        io.arrive(t)
        dw = tn(cols[t], z)
        lo = 0
        while lo < 512:
            half, at = divmod(t * 512 + lo, rows)
            n = min(512 - lo, rows - at)
            full[half, at : at + n] = dw[lo : lo + n]
            lo += n
    put_halves(me, full, keep, send)


def k_dw_mid(me, mid, dz4, act2, dz3, keep, send, full):
    mine = pl.ds(pl.multiple_of(me[0] * 128, 128), 128)
    blocks = [tn(mid[...], dz4[:, mine])] + lane_blocks(tn(act2[...], dz3[...]))
    full[...] = jnp.concatenate(blocks, axis=0).reshape(full.shape)
    put_halves(me, full, keep, send)


def own_block(me):
    lanes = pl.ds(pl.multiple_of((me[0] >> 1) * 128, 128), 128)
    return lanes, pl.ds(pl.multiple_of((me[0] & 1) * 64, 64), 64)


def k_dev_products(geo, io, me, devq, xs, out, part):
    lives = [live_rows(me[1], 256), live_rows(me[2], 256)]
    _, mine = own_block(me)
    io.ready()

    def body(step, i, pix, npx, row, nrows, carry):
        return [
            carry[j] + jnp.sum(as_pix(xs[j, pl.ds(row, nrows), :].astype(F32)), axis=0) for j in range(4)
        ]

    zero = [jnp.zeros((VIEWS, 256), F32)] * 4
    big, small = geo.loop(body, [zero, zero], io)
    sums = [jnp.broadcast_to(rows_sum(b * lives[0] + s * lives[1]), (8, 256)) for b, s in zip(big, small)]
    for j in range(4):
        part[...] = tn(devq[...], xs[j])
        out[:, 256 * j : 256 * j + 256] = jnp.concatenate([part[mine, :], sums[j]], axis=0).astype(BF16)


def k_dw_last(geo, io, me, wb, ws, dz2, xs, dt1q, keep, send, full, part, flat):
    lanes, mine = own_block(me)
    io.ready()
    io.start_steps()
    nb, ns = geo.pb * VIEWS, geo.ps * VIEWS
    at = 0
    for r in range(3):
        ob, os = r * geo.hb * VIEWS, r * geo.hs * VIEWS
        full[...] = tn(dz2[0:nb, lanes], wb[ob : ob + nb, :]) + tn(
            dz2[nb : nb + ns, lanes], ws[os : os + ns, :]
        )
        for block in lane_blocks(full[mine, :]):
            flat[at : at + 64] = block
            at += 64
    geo.loop(lambda step, i, pix, npx, row, nrows, carry: carry, [0, 0], io)
    for j in range(4):
        part[:, 256 * j : 256 * j + 256] = tn(dt1q[...], xs[j])
    flat[at:] = jnp.concatenate(lane_blocks(part[mine, :]), axis=0)
    half = keep.shape[0]
    bit = me[3] & 1
    keep[...] = flat[pl.ds(pl.multiple_of(bit * half, 8), half)].astype(BF16)
    send[...] = flat[pl.ds(pl.multiple_of((1 - bit) * half, 8), half)].astype(BF16)


def k_out_first(io, me, wide, short, a, b, dwide, dshort, dstride):
    bit = me[3] & 1
    for n in range(4):
        io.arrive(n)
        if n < 2:
            dwide[n] = wide[n].astype(F32)
        dshort[n] = short[n].astype(F32)
        io.leave(n)
    io.ready()
    dstride[bit] = a[0].astype(F32)
    dstride[1 - bit] = b[0].astype(F32)
    io.send(dstride)


def k_small_outputs(me, t1, t2, t3, t4, t5, t6, late, gm3, sm3, go3, so3, gm4, sm4, go4, so4):
    lanes, _ = own_block(me)
    half = me[0] & 1
    for n, t in enumerate((t1, t2)):
        block = t[:, lanes]
        mine = jnp.where(half == 0, block[:, 0:64], block[:, 64:128])
        gm3[n : n + 1] = mine[1:2]
        sm3[n : n + 1] = mine[0:1]
    wide = pl.ds(pl.multiple_of(me[0] * 256, 256), 256)
    go3[...] = t3[1:2, wide]
    so3[...] = t3[0:1, wide]
    mid = pl.ds(pl.multiple_of(me[0] * 128, 128), 128)
    for n, t in enumerate((t4, t5)):
        gm4[n : n + 1] = t[1:2, mid]
        sm4[n : n + 1] = t[0:1, mid]
    go4[...] = t6[1:3]
    so4[0:1] = t6[0:1]
    so4[1:2] = t6[0:1]


def k_sum_split(shift, size, n_in, me, *refs):
    total = refs[n_in]
    acc = refs[0][...].astype(F32)
    for r in refs[1:n_in]:
        acc = acc + r[...].astype(F32)
    total[...] = acc
    where = (me[3] >> shift) & (size - 1)
    for m, out in enumerate(refs[n_in + 1 :]):
        out[...] = total[where ^ m].astype(BF16)


def k_sum(n_in, *refs):
    acc = refs[0][...].astype(F32)
    for r in refs[1:n_in]:
        acc = acc + r[...].astype(F32)
    refs[n_in][...] = acc.astype(BF16)


def k_join(shift, size, me, *refs):
    where = (me[3] >> shift) & (size - 1)
    for m in range(size):
        refs[size][where ^ m] = refs[m][...]


def k_unpack(plan, me, a, b, *refs):
    full = refs[-1]
    bit = me[3] & 1
    full[bit] = a[...].reshape(full.shape[1:]).astype(F32)
    full[1 - bit] = b[...].reshape(full.shape[1:]).astype(F32)
    flat = full[...].reshape(2 * full.shape[1], 128)
    at = 0
    for out, (lead, rows, cols) in zip(refs, plan):
        for t in range(lead):
            for block in range(cols // 128):
                v = flat[at : at + rows]
                lanes = slice(128 * block, 128 * block + 128)
                if lead > 1:
                    out[t, :, lanes] = v
                else:
                    out[:, lanes] = v
                at += rows


def k_out_last(me, a, b, dev, coef, dmix, dreduce, full):
    bit = me[3] & 1
    full[bit] = a[...].reshape(full.shape[1:]).astype(F32)
    full[1 - bit] = b[...].reshape(full.shape[1:]).astype(F32)
    flat = full[...].reshape(2 * full.shape[1], 128)
    at = 0
    for t in range(9):
        for block in range(2):
            dmix[t, :, 128 * block : 128 * block + 128] = flat[at : at + 64]
            at += 64
    fix = dev[64:65].astype(F32) * coef[1] + dev[0:64].astype(F32) * coef[2]
    for block in range(8):
        lanes = slice(128 * block, 128 * block + 128)
        dreduce[:, lanes] = flat[at : at + 64] * coef[0] - fix[:, lanes]
        at += 64


def per_device(
    ni,
    nc,
    x_big,
    x_small,
    cot_big,
    cot_small,
    counts,
    w_reduce,
    w_mix,
    w_expand,
    w_narrow,
    w_stride,
    w_widen,
    w_short,
    gain_mid3,
    shift_mid3,
    gain_out3,
    shift_out3,
    gain_mid4,
    shift_mid4,
    gain_out4,
    shift_out4,
):
    assert nc == 4 and ni >= 8 and x_big.shape[0] == VIEWS and x_small.shape[0] == VIEWS
    geo = Geo(x_big.shape[1], x_small.shape[1])
    img = lax.axis_index("img")
    q = lax.axis_index("ch").astype(jnp.int32)
    levels = ni.bit_length() - 1
    me, nf3, cnt3, nf4, cnt4 = call(
        "counts",
        functools.partial(k_counts, ni, ((geo.pb, geo.ps), (geo.qb, geo.qs))),
        [(counts, SMEM)],
        [(sds((4,), jnp.int32), SMEM)]
        + [(sds((n,)), SMEM) for n in (3, 8 * (levels - 2)) * 2],
        slack=1,
    )

    smem = [(me, SMEM)]

    def over_img(v, k):
        return lax.ppermute(v, "img", [(i, i ^ (1 << k)) for i in range(ni)])

    def over_ch(v, k):
        return lax.ppermute(v, "ch", [(i, i ^ k) for i in range(nc)])

    rounds, at = [], 0
    while at < levels:
        rounds.append((at, min(2, levels - at) if at == 0 else 1))
        at += rounds[-1][1]

    def peers(v, shift, bits):
        out = []
        for m in range(1, 1 << bits):
            out.append(lax.ppermute(v, "img", [(i, i ^ (m << shift)) for i in range(ni)]))
        return out

    def sync(v, combine, wait=(), free=()):
        wait, free = dict(wait), dict(free)
        freed = []
        for k, (shift, bits) in enumerate(rounds):
            if k in wait:
                v = lax.optimization_barrier((v,) + tuple(wait[k]))[0]
            others = peers(v, shift, bits)
            if k in free:
                held = lax.optimization_barrier(tuple(others) + tuple(free[k]))
                others = list(held[: len(others)])
                freed += held[len(others) :]
            if k == len(rounds) - 1:
                return (v, others[0]) + ((freed,) if free else ())
            v = combine(k, [v] + others)

    last = len(rounds) - 1

    def sync_stats(stats, cnt, wait=(), free=()):
        def combine(k, arrays):
            (v,) = call(
                "merge",
                functools.partial(k_merge, 8 * k, len(arrays)),
                [(cnt, SMEM)] + vm(*arrays),
                [sds(stats.shape)],
                slack=1,
            )
            return v

        return sync(stats, combine, wait, free)

    def sync_sums(sums, wait=(), free=()):
        def combine(k, arrays):
            (v,) = call("add", functools.partial(k_add, len(arrays)), vm(*arrays), [sds(sums.shape)], slack=1)
            return v

        return sync(sums, combine, wait, free)

    pairs = [(at, 1) for at in range(levels)]
    fours = [(0, 1)]
    while fours[-1][0] + fours[-1][1] < levels:
        done = fours[-1][0] + fours[-1][1]
        fours.append((done, min(2, levels - done)))

    def to_peers(parts, group):
        shift, bits = group
        out = []
        for m in range(1, 1 << bits):
            perm = [(i, i ^ (m << shift)) for i in range(ni)]
            out.append(lax.ppermute(parts[m if len(parts) > 1 else 0], "img", perm))
        return out

    def sum_split(name, arrays, group):
        shift, bits = group
        size = 1 << bits
        shape = arrays[0].shape
        view = (size, shape[0] // size) + shape[1:]
        return call(
            name,
            functools.partial(k_sum_split, shift, size, len(arrays)),
            smem + vm(*[a.reshape(view) for a in arrays]),
            [sds(view[1:], BF16)] * size,
            [pltpu.VMEM(view, F32)],
            order=True,
        )

    def join(name, parts, group):
        shift, bits = group
        size = 1 << bits
        (full,) = call(
            name,
            functools.partial(k_join, shift, size),
            smem + vm(*parts),
            [sds((size,) + parts[0].shape, BF16)],
        )
        return full.reshape((-1,) + parts[0].shape[1:])

    class Train:
        def __init__(self, name, groups, parts):
            self.name, self.groups, self.parts, self.at, self.summing = name, groups, parts, 0, True

        def sends(self):
            return self.parts[1:] if self.summing else self.parts

        def launch(self, sends):
            parts = self.parts[:1] + list(sends) if self.summing else list(sends)
            self.received = to_peers(parts, self.groups[self.at])

        def advance(self):
            name = "%s_%d" % (self.name, self.at)
            arrays = self.parts[:1] + self.received
            if self.summing and self.at + 1 < len(self.groups):
                self.at += 1
                self.parts = sum_split(name, arrays, self.groups[self.at])
            elif self.summing:
                self.summing = False
                self.parts = call(
                    name + "s",
                    functools.partial(k_sum, len(arrays)),
                    vm(*arrays),
                    [sds(arrays[0].shape, BF16)],
                    slack=2,
                )
            else:
                self.parts = [join(name + "j", arrays, self.groups[self.at])]
                self.at -= 1

        def to_last(self):
            while self.summing or self.at > 0:
                self.advance()
                self.launch(self.sends())

        def finish(self):
            self.to_last()
            return self.parts[0], self.received[0]

    def quarters(v):
        p1 = over_ch(v, 1)
        p2 = over_ch(v, 2)
        return [v, p1, p2, over_ch(p2, 1)]

    def after(marker, *arrays):
        return list(lax.optimization_barrier((marker,) + arrays))

    def sent(v):
        return [v, over_ch(v, 1), over_ch(v, 2)]

    def passed_on(g):
        return g + [over_ch(g[2], 1)]

    def rows_of(v):
        return jnp.transpose(v, (1, 2, 0, 3)).reshape(-1, v.shape[3])

    m3, c3 = 4 * w_reduce.shape[1], w_reduce.shape[0]
    m4, c4q = w_widen.shape
    first = [rows_of(x_small)]
    first.append(jnp.transpose(w_mix, (0, 1, 3, 2)).reshape(-1, m3))
    first += [w_reduce.T[:, j * m3 : (j + 1) * m3] for j in range(c3 // m3)]
    mix_at, reduce_at = first[0].shape[0], first[0].shape[0] + first[1].shape[0]
    held = (gain_mid3, shift_mid3, gain_out3[None], shift_out3[None], gain_mid4, shift_mid4, gain_out4, shift_out4)
    first += call(
        "pack_params",
        k_pack_params,
        vm(*held),
        [sds((64, 256), BF16)],
        [pltpu.VMEM((32, 128), F32)],
        slack=2,
    )
    params_at = sum(v.shape[0] for v in first[:-1])
    xb = quarters(rows_of(x_big))
    xb[1], me, *first = lax.optimization_barrier((xb[1], me, *first))
    smem = [(me, SMEM)]
    xsm = sent(jnp.concatenate(first))
    xb[3], xsm[2] = after(xb[3], xsm[2])
    xsm = passed_on(xsm)
    gs1, gs2, gs3, gs4, gs5, gs6 = call(
        "unpack_params",
        functools.partial(k_unpack_params, params_at),
        smem + [(in_hbm(v), HBM) for v in xsm],
        [sds((2, n)) for n in (m3, m3, c3, m4, m4)] + [sds((2, 4, c4q))],
        [pltpu.VMEM((4, 64, 256), BF16), pltpu.SemaphoreType.DMA((4,))],
        slack=2,
    )

    def blocks128(v):
        return [v[:, 128 * b : 128 * b + 128] for b in range(v.shape[1] // 128)]

    w_mid = jnp.concatenate(blocks128(w_expand) + blocks128(w_narrow))
    last_in = jnp.concatenate([w_short, w_widen, rows_of(cot_big), rows_of(cot_small)])
    wst = w_stride.reshape(-1, w_stride.shape[3])
    xsm[3], w_mid, last_in, wst = after(xsm[3], w_mid, last_in, wst)
    chip_pairs = [[0, 2], [1, 3]]
    wst = lax.all_gather(wst, "ch", axis_index_groups=chip_pairs)
    last_in = lax.all_gather(last_in, "ch", axis_index_groups=chip_pairs)

    n3, n4 = [(nf3, SMEM)], [(nf4, SMEM)]

    def k(fn):
        return functools.partial(fn, geo)

    hb, hs = geo.hb, geo.hs
    sb4, ss4 = (2, 2, hb // 2, hb // 2, VIEWS, m4), (2, 2, hs // 2, hs // 2, VIEWS, m4)
    wb_shape, ws_shape = ((hb + 2) * hb * VIEWS, 3 * m3), ((hs + 2) * hs * VIEWS, 3 * m3)

    def flow(kind, *arrays):
        return [(a, Flow(kind)) for a in arrays]

    def out(kind, shape, dtype=F32):
        return (sds(shape, dtype), Flow(kind))

    x_all = [(xb + xsm, Flow("x"))]
    w_in, w_ahead, w_back = [
        [(xsm, Flow(kind, base))]
        for kind, base in (("w_in", reduce_at), ("w_ahead", mix_at), ("w_back", mix_at))
    ]
    run = functools.partial(call, geo=geo)
    px1, px3, px4 = (geo.px, VIEWS, m3), (geo.px, VIEWS, c3), (geo.px4, VIEWS, m4)

    pre1, st = run(
        "reduce",
        k(k_reduce),
        smem + n3 + x_all + w_in,
        [fast(px1), sds((2, m3))],
    )
    st, w_mid = after(st, w_mid)
    w_mid = sent(w_mid)
    a1, b1 = sync_stats(st, cnt3)
    pre2, winb, wins, st, devq, keep1 = run(
        "mix",
        k(k_mix),
        smem + n3 + vm(pre1, a1, b1, gs1) + w_ahead,
        [
            fast(px1),
            out("all", wb_shape, BF16),
            out("all", ws_shape, BF16),
            sds((2, m3)),
            out("all", (geo.rows, 128), BF16),
            (sds(px1), Keep(2)),
        ],
        [pltpu.VMEM((1, m3), F32)],
    )
    st, w_mid[2] = after(st, w_mid[2])
    w_mid = passed_on(w_mid)
    w_expand_all = [(w_mid, Flow("w", 0, (m3, c3)))]
    w_narrow_all = [(w_mid, Flow("w", m3 * (c3 // 4 // 128), (c3, m4)))]
    a2, b2 = sync_stats(st, cnt3)
    pre3, act2, st, keep2 = run(
        "expand",
        k(k_expand),
        smem + n3 + vm(pre2, a2, b2, gs2) + w_expand_all,
        [
            fast(px3),
            out("rows", (geo.rows, m3), BF16),
            sds((2, c3)),
            (sds(px1), Keep(2)),
        ],
    )
    a3, b3 = sync_stats(st, cnt3)
    pre4b, pre4s, mid, mids, st, dev3, slope3 = run(
        "narrow",
        k(k_narrow),
        smem + n3 + vm(pre3) + x_all + vm(a3, b3, gs3) + w_narrow_all,
        [
            out("big", sb4),
            out("small", ss4),
            out("rows", (geo.rows, c3), BF16),
            fast((geo.rows4, c3), BF16),
            sds((2, m4)),
            out("rows", (geo.rows, c3), BF16),
            out("rows", (geo.rows, c3), BF16),
        ],
        [pltpu.VMEM((geo.px4, VIEWS, c3), F32)],
        slack=6,
        staying=4 * math.prod(px3),
    )
    st, wst = after(st, wst)
    wst = [wst, over_ch(wst, 1)]
    a4, b4 = sync_stats(st, cnt3)
    w_stride_all = [(wst, Flow("w4", 0, (9 * m4, m4)))]
    pre5, cols, st = run(
        "stride",
        k(k_stride),
        smem
        + n4
        + n3
        + flow("big", pre4b)
        + flow("small", pre4s)
        + vm(a4, b4, gs4)
        + w_stride_all,
        [
            sds(px4),
            out("lead", (9, geo.rows4, m4), BF16),
            sds((2, m4)),
        ],
        [pltpu.VMEM(sb4, F32), pltpu.VMEM(ss4, F32)],
    )
    (dev,) = run(
        "dev_products",
        k(k_dev_products),
        smem + flow("all", devq) + x_all,
        [sds((m3 // 4 + 8, c3), BF16)],
        [pltpu.VMEM((128, c3 // 4), F32)],
        ahead=8,
    )
    a5, b5, (dev,) = sync_stats(st, cnt4, free={last: [dev]})
    a5, last_in, mids = after(a5, last_in, mids)
    at_w, at_b, at_s = c3, c3 + m4, c3 + m4 + geo.qb * VIEWS

    def from_chips(base, rows):
        return [(last_in, Flow("chip", base, (rows, c4q), j)) for j in range(2)]

    wsh, wwi = from_chips(0, c3), from_chips(at_w, m4)
    cots = from_chips(at_b, geo.qb * VIEWS) + from_chips(at_s, geo.qs * VIEWS)
    side, st_side = run(
        "short",
        k(k_short),
        smem + n4 + vm(mids) + wsh,
        [fast((2, geo.px4, VIEWS, c4q)), sds((2, 2, c4q))],
    )
    pre6, act5, st = run(
        "widen",
        k(k_widen),
        smem + n4 + vm(pre5, a5, b5, gs5) + wwi + vm(st_side),
        [
            fast((2, geo.px4, VIEWS, c4q)),
            sds((geo.rows4, m4), BF16),
            sds((2, 4, c4q)),
        ],
    )
    a6, b6 = sync_stats(st, cnt4)
    out_b, out_s, dt6, sums = run(
        "total",
        k(k_total),
        smem + n4 + vm(pre6, side, a6, b6, gs6) + cots,
        [
            out("all", (geo.qb, VIEWS, c4q)),
            out("all", (geo.qs, VIEWS, c4q)),
            fast((2, geo.px4, VIEWS, c4q)),
            sds((2, 3, c4q)),
        ],
    )
    ga6, gb6 = sync_sums(sums)
    part5, dz6, dzs, t6 = run(
        "back_wide",
        k(k_back_wide),
        smem
        + n4
        + vm(dt6, pre6, side, a6, b6, gs6, ga6, gb6)
        + wwi,
        [
            sds(px4),
            sds((geo.rows4, c4q), BF16),
            sds((2, geo.rows4, c4q), BF16),
            sds((2, 3, c4q)),
        ],
    )
    other5 = over_ch(part5, 1)
    dt5, sums = call(
        "back_act5",
        k_back_act5,
        n4 + vm(part5, other5, pre5, a5, b5, gs5),
        [sds(px4), sds((2, m4))],
    )
    (dms,) = run(
        "back_short", k_back_short, smem + vm(dzs) + wsh, [sds((geo.px4, VIEWS, c3), BF16)]
    )
    dmo = over_ch(dms, 1)
    dwide, dshort = call(
        "dw_wide",
        k_dw_wide,
        vm(act5, dz6, mids, dzs),
        [sds((m4, c4q), BF16), sds((c3, c4q), BF16)],
    )
    ga5, gb5, (dwide, dshort) = sync_sums(sums, free={0: [dwide, dshort]})
    dt4b, dt4s, dz5, sums, t5 = run(
        "back_stride",
        k(k_back_stride),
        smem
        + n4
        + vm(dt5, pre5, a5, b5, gs5, ga5, gb5)
        + flow("all", pre4b, pre4s)
        + vm(a4, b4, gs4)
        + n3
        + w_stride_all,
        [fast(sb4), fast(ss4), sds((geo.rows4, m4), BF16), sds((2, m4)), sds((2, m4))],
        [pltpu.VMEM((4, geo.rows4, m4), BF16)],
    )

    def halves(rows):
        return [sds((rows // 2, 128), BF16)] * 2, pltpu.VMEM((2, rows // 2, 128), F32)

    outs, full = halves(9 * m4)
    parts = run("dw_stride", k_dw_stride, smem + flow("lead", cols) + vm(dz5), outs, [full])
    stride_train = Train("stride", pairs, parts)
    ga4, gb4, sends = sync_sums(sums, free={0: stride_train.sends()})
    stride_train.launch(sends)
    dt3, dz4, sums, t4 = run(
        "back_narrow",
        k(k_back_narrow),
        smem
        + n3
        + vm(dt4b, dt4s)
        + flow("big", pre4b)
        + flow("small", pre4s)
        + vm(a4, b4, gs4, ga4, gb4)
        + flow("rows", dev3, slope3)
        + vm(a3, b3, dms, dmo)
        + w_narrow_all,
        [
            fast((geo.rows, c3), BF16),
            out("rows", (geo.rows, m4), BF16),
            sds((2, c3)),
            sds((2, m4)),
        ],
    )
    came = stride_train.received
    stride_train.advance()
    ga3, gb3, sends = sync_sums(sums, wait={0: came}, free={last: stride_train.sends()})
    stride_train.launch(sends)
    dt2, dz3, dt3q, sums, t3 = run(
        "back_expand",
        k(k_back_expand),
        smem
        + n3
        + vm(dt3)
        + flow("rows", dev3)
        + vm(a3, b3, gs3, ga3, gb3)
        + flow("px", keep2)
        + vm(a2, b2, gs2)
        + w_expand_all,
        [
            fast(px1),
            out("rows", (geo.rows, c3 // 4), BF16),
            out("rows", (geo.rows, c3 // 4), BF16),
            sds((2, m3)),
            sds((2, c3)),
        ],
        [
            pltpu.VMEM((2 * hb * VIEWS, c3), BF16),
            pltpu.VMEM((2 * hs * VIEWS, c3), BF16),
        ],
    )
    came = stride_train.received
    stride_train.advance()
    outs, full = halves(c3 + (c3 // 4 // 128) * m3)
    parts = call("dw_mid", k_dw_mid, smem + vm(mid, dz4, act2, dz3), outs, [full])
    mid_train = Train("mid", pairs, parts)
    ga2, gb2, (mid_send, *sends) = sync_sums(
        sums, wait={0: came}, free={0: mid_train.sends(), last: stride_train.sends()}
    )
    mid_train.launch([mid_send])
    stride_train.launch(sends)
    dt1, dz2, sums, t2, dt1q = run(
        "back_mix",
        k(k_back_mix),
        smem
        + n3
        + vm(dt2)
        + flow("px", keep2)
        + vm(a2, b2, gs2, ga2, gb2)
        + flow("px", keep1)
        + vm(a1, b1, gs1)
        + w_back,
        [
            out("px", px1),
            out("all", (geo.rows, m3), BF16),
            sds((2, m3)),
            sds((2, m3)),
            out("rows", (geo.rows, 128), BF16),
        ],
        [pltpu.VMEM(wb_shape, BF16), pltpu.VMEM(ws_shape, BF16)],
    )
    came = stride_train.received + mid_train.received
    stride_train.advance()
    mid_train.advance()
    mix_rows = 9 * m3 // 128 * (m3 // 4)
    rows_last = mix_rows + c3 // 128 * (m3 // 4)
    outs, _ = halves(rows_last)
    parts = run(
        "dw_last",
        k(k_dw_last),
        smem + flow("all", winb, wins, dz2) + x_all + flow("all", dt1q),
        outs,
        [
            pltpu.VMEM((128, 3 * m3), F32),
            pltpu.VMEM((128, c3), F32),
            pltpu.VMEM((rows_last, 128), F32),
        ],
        ahead=8,
        hold=True,
    )
    last_train = Train("last", fours, parts)
    dwide, dshort, dev = lax.psum((dwide, dshort, dev), "img")
    wide = [dwide, dshort, dev]
    ga1, gb1, (last_send, mid_send, *sends) = sync_sums(
        sums,
        wait={last: came + wide},
        free={last: last_train.sends() + mid_train.sends() + stride_train.sends()},
    )
    last_train.launch([last_send])
    mid_train.launch([mid_send])
    stride_train.launch(sends)
    dwide, dshort, dev = wide
    gxb, gxs, t1, coef = run(
        "back_reduce",
        k(k_back_reduce),
        smem
        + n3
        + flow("px", dt1, keep1)
        + vm(a1, b1, gs1, ga1, gb1)
        + flow("rows", dt3q)
        + w_in,
        [
            out("big_px", (geo.pb, VIEWS, c3 // 4)),
            out("small_px", (geo.ps, VIEWS, c3 // 4)),
            sds((2, m3)),
            sds((3, m3)),
        ],
    )
    def unpack(name, a, b, plan):
        shapes = [((lead,) if lead > 1 else ()) + (rows, cols) for lead, rows, cols in plan]
        return call(
            name,
            functools.partial(k_unpack, plan),
            smem + vm(a, b),
            [sds(shape) for shape in shapes],
            [pltpu.VMEM((2,) + a.shape, F32)],
        )

    trains = (last_train, mid_train, stride_train)
    gxb, dwide, dshort, dev, coef, *came = after(
        gxb, dwide, dshort, dev, coef, *[train.received[0] for train in trains]
    )
    for train, first in zip(trains, came):
        train.received[0] = first
    halves_in = [v.reshape(1, 9 * m4 // 2, 128) for v in stride_train.finish()]
    dwide, dshort, dstride = run(
        "out_first",
        k_out_first,
        smem
        + flow("lead", dwide.reshape(2, m4 // 2, c4q), dshort.reshape(4, c3 // 4, c4q))
        + flow("all", *halves_in),
        [
            out("lead", (2, m4 // 2, c4q)),
            out("lead", (4, c3 // 4, c4q)),
            out("all", (2, 9 * m4 // 2, 128)),
        ],
        ahead=4,
    )
    mid_train.to_last()
    last_train.to_last()
    dstride, mid_train.received[0], last_train.received[0] = after(
        dstride, mid_train.received[0], last_train.received[0]
    )
    dnarrow, dexpand = unpack(
        "out_mid", *mid_train.finish(), [(1, c3, m4 // 4), (1, m3, c3 // 4)]
    )
    coef = lax.dynamic_slice_in_dim(coef, q * (m3 // 4), m3 // 4, 1)[:, :, None]
    mine, other = last_train.finish()
    dmix, dreduce = call(
        "out_last",
        k_out_last,
        smem + vm(mine, other, dev, coef),
        [sds((9, m3 // 4, m3)), sds((m3 // 4, c3))],
        [pltpu.VMEM((2,) + mine.shape, F32)],
    )

    def views_first(v, side):
        return jnp.transpose(v.reshape(side, side, VIEWS, v.shape[2]), (2, 0, 1, 3))

    small = call(
        "small_outputs",
        k_small_outputs,
        smem + vm(t1, t2, t3, t4, t5, t6[0], gxs[0]),
        [sds((2, m3 // 4))] * 2
        + [sds((1, c3 // 4))] * 2
        + [sds((2, m4 // 4))] * 2
        + [sds((2, c4q))] * 2,
        slack=4,
    )
    small[2], small[3] = small[2][0], small[3][0]
    return (
        views_first(out_b, hb // 2),
        views_first(out_s, hs // 2),
        views_first(gxb, hb),
        views_first(gxs, hs),
        dreduce.T,
        jnp.transpose(dmix.reshape(3, 3, m3 // 4, m3), (0, 1, 3, 2)),
        dexpand,
        dnarrow,
        dstride.reshape(3, 3, m4, m4 // 4),
        dwide.reshape(m4, c4q),
        dshort.reshape(c3, c4q),
        *small,
    )


def solution(mesh):
    act = P("img", None, None, "ch")
    flat, taps, vec = P(None, "ch"), P(None, None, None, "ch"), P("ch")
    in_specs = (act,) * 4 + (P(), flat, taps, flat, flat, taps, flat, flat)
    in_specs += (flat, flat, vec, vec, flat, flat, flat, flat)
    out_specs = (act,) * 4 + (flat, taps, flat, flat, taps, flat, flat)
    out_specs += (flat, flat, vec, vec, flat, flat, flat, flat)
    return jax.shard_map(
        functools.partial(per_device, mesh.shape["img"], mesh.shape["ch"]),
        mesh=mesh,
        in_specs=in_specs,
        out_specs=out_specs,
        check_vma=False,
    )
```

```python
import functools
import math

import jax
import jax.numpy as jnp
from jax import lax
from jax.experimental import pallas as pl
from jax.experimental.pallas import tpu as pltpu
from jax.sharding import PartitionSpec as P

EPS = 1e-05
G0 = 0.7978845608028654
G1 = G0 * 0.044715
F32 = jnp.float32
BF16 = jnp.bfloat16
VIEWS = 8

ANY = pl.BlockSpec(memory_space=pl.ANY)
HBM = pl.BlockSpec(memory_space=pltpu.HBM)
VMEM = pl.BlockSpec(memory_space=pltpu.VMEM)
SMEM = pl.BlockSpec(memory_space=pltpu.SMEM)


def sds(shape, dtype=F32):
    return jax.ShapeDtypeStruct(tuple(shape), dtype)


class Flow:
    WHOLE = ("w", "w4", "all", "chip", "w_in", "w_ahead", "w_back")

    def __init__(self, kind, base=0, shape=None, which=0):
        self.kind, self.base, self.shape, self.which = kind, base, shape, which

    def keys(self, geo, shape):
        parts = (0, 1)
        if self.kind in ("big", "big_px"):
            parts = (0,)
        if self.kind in ("small", "small_px"):
            parts = (1,)
        if self.kind not in ("lead",) + self.WHOLE:
            return [(part, n) for part in parts for n in range(len(geo.groups[part]))]
        if self.kind == "lead":
            return list(range(shape[0]))
        return [None]

    def buffer(self, geo, shapes, dtype):
        if self.kind == "x":
            return pltpu.VMEM((4, geo.rows, shapes[0][1]), dtype)
        if self.kind == "w":
            return pltpu.VMEM(self.shape, dtype)
        if self.kind in ("chip", "w4"):
            return pltpu.VMEM(self.shape, dtype)
        c = shapes[0][-1]
        if self.kind.startswith("w_"):
            return pltpu.VMEM({"w_in": (4, c, c), "w_ahead": (3, c, 3 * c), "w_back": (9, c, c)}[self.kind], dtype)
        return pltpu.VMEM(tuple(shapes[0]), dtype)

    def pairs(self, geo, q, hbm, buf, key):
        if self.kind == "w":
            rows, n = buf.shape[0], buf.shape[1] // 4
            found = []
            for p in range(4):
                for b in range(n // 128):
                    at = pl.ds(pl.multiple_of((q ^ p) * n + 128 * b, 128), 128)
                    found.append((hbm[p].at[pl.ds(self.base + rows * b, rows)], buf.at[:, at]))
            return found
        if self.kind.startswith("w_"):
            c = buf.shape[1]
            n = c // 4
            found = []
            for p in range(4):
                at = pl.ds(pl.multiple_of((q ^ p) * n, n), n)
                for t in range(4 if self.kind == "w_in" else 9):
                    src = hbm[p].at[pl.ds(self.base + n * t, n)]
                    if self.kind == "w_ahead":
                        found.append((src, buf.at[t // 3, at, pl.ds(t % 3 * c, c)]))
                    else:
                        found.append((src, buf.at[t, at]))
            return found
        if self.kind == "chip":
            return [(hbm[0].at[(q >> 1) ^ self.which, pl.ds(self.base, buf.shape[0])], buf)]
        if self.kind == "w4":
            n = buf.shape[1] // 4
            found = []
            for chip in range(2):
                for other in range(2):
                    at = pl.multiple_of((2 * chip + ((q & 1) ^ other)) * n, n)
                    found.append((hbm[other].at[chip], buf.at[:, pl.ds(at, n)]))
            return found
        if key is None:
            return [(hbm[0], buf)]
        if self.kind == "lead":
            return [(hbm[0].at[key], buf.at[key])]
        part, group = key
        i, end = geo.groups[part][group]
        pix, npx, row, nrows = geo.step(part, i)
        npx, nrows, first = npx * (end - i), nrows * (end - i), pix - geo.parts[part][1]
        if self.kind == "px":
            at = pl.ds(pix, npx)
        elif self.kind == "rows":
            at = pl.ds(row, nrows)
        elif self.kind in ("big_px", "small_px"):
            at = pl.ds(first, npx)
        elif self.kind == "x":
            local = pl.ds(first * VIEWS, nrows)
            return [
                (hbm[4 * part + p].at[local], buf.at[q ^ p, pl.ds(row, nrows)]) for p in range(4)
            ]
        else:
            at = pl.ds(i, end - i)
            return [(hbm[0].at[:, :, at], buf.at[:, :, at])]
        return [(hbm[0].at[at], buf.at[at])]


class Moves:
    def __init__(self, geo, q, ahead):
        self.geo, self.q, self.flows, self.kept, self.ahead = geo, q, [], [], ahead

    def add(self, flow, hbm, buf, sem, inward):
        self.flows.append((flow, hbm, buf, sem, inward))

    def copies(self, entry, key):
        flow, hbm, buf, sem, inward = entry
        if flow.kind in flow.WHOLE:
            at = 0
        elif flow.kind == "lead":
            at = key
        elif flow.kind in ("px", "rows", "x"):
            at = (0, len(self.geo.groups[0]))[key[0]] + key[1]
        else:
            at = key[1]
        pairs = flow.pairs(self.geo, self.q, hbm, buf, key)
        return [
            pltpu.make_async_copy(*((a, b) if inward else (b, a)), sem.at[n, at])
            for n, (a, b) in enumerate(pairs)
        ]

    def entries(self, inward, key):
        for entry in self.flows:
            flow = entry[0]
            if entry[4] != inward:
                continue
            if key is None:
                fits = flow.kind in flow.WHOLE
            elif isinstance(key, int):
                fits = flow.kind == "lead" and key < entry[1][0].shape[0]
            else:
                kinds = ("px", "rows", "x") + (("big", "big_px"), ("small", "small_px"))[key[0]]
                fits = flow.kind in kinds
            if fits:
                yield entry

    def start(self, inward, key):
        for entry in self.entries(inward, key):
            for c in self.copies(entry, key):
                c.start()

    def wait(self, inward, key):
        for entry in self.entries(inward, key):
            for c in self.copies(entry, key):
                c.wait()

    def begin(self, hold):
        self.order = [(part, n) for part in range(2) for n in range(len(self.geo.groups[part]))]
        if hold:
            self.start(True, None)
            return
        self.start(True, self.order[0])
        self.start(True, None)
        for key in self.order[1 : self.ahead]:
            self.start(True, key)
        for n in range(self.ahead):
            self.start_lead(n)
        streams = any(e[4] and e[0].kind not in ("lead",) + Flow.WHOLE for e in self.flows)
        if not streams:
            for c in self.kept:
                c.start()

    def start_steps(self):
        for key in self.order:
            self.start(True, key)

    def start_lead(self, n):
        for entry in self.flows:
            if entry[4] and entry[0].kind == "lead" and n < entry[1][0].shape[0]:
                for c in self.copies(entry, n):
                    c.start()

    def ready(self):
        self.wait(True, None)

    def arrive(self, *key):
        if len(key) == 1:
            self.wait(True, key[0])
            self.start_lead(key[0] + self.ahead)
            return
        self.wait(True, key)
        at = self.order.index(key)
        if at + self.ahead < len(self.order):
            self.start(True, self.order[at + self.ahead])
        streams = any(e[4] and e[0].kind not in ("lead",) + Flow.WHOLE for e in self.flows)
        if at == 0 and streams:
            for c in self.kept:
                c.start()

    def leave(self, *key):
        self.start(False, key if len(key) > 1 else key[0])

    def send(self, *refs):
        for entry in self.entries(False, None):
            if any(entry[2] is r for r in refs):
                for c in self.copies(entry, None):
                    c.start()

    def finish(self):
        for entry in self.flows:
            if not entry[4]:
                shape = entry[1][0].shape
                for key in entry[0].keys(self.geo, shape):
                    for c in self.copies(entry, key):
                        c.wait()
        for c in self.kept:
            c.wait()


class Keep:
    kind = "keep"

    def __init__(self, source):
        self.source = source


def fast(shape, dtype=F32):
    return pltpu.VMEM(tuple(shape), dtype)


def scoped_bytes(v):
    return math.prod(v.shape) * jnp.dtype(v.dtype).itemsize


def in_hbm(v):
    return pltpu.with_memory_space_constraint(v, pltpu.HBM)


def call(name, kernel, ins, outs, scratch=(), cost=None, order=False, geo=None, slack=14, ahead=3, hold=False, staying=0):
    if order:
        inner, n_in, n_out = kernel, len(ins), len(outs)

        def kernel(*refs):
            rest = refs[n_in:]
            return inner(*refs[:n_in], *rest[n_out:], *rest[:n_out])

    outs = [o if isinstance(o, tuple) else (o, VMEM) for o in outs]
    arrays, specs, moved = [], [], []
    for a, spec in ins:
        group = a if isinstance(a, list) else [a]
        flow = isinstance(spec, Flow)
        arrays += [in_hbm(v) for v in group] if flow else group
        specs += [HBM if flow else spec] * len(group)
        moved.append((spec if flow else None, len(group), [v.shape for v in group], group[0].dtype))
    out_shapes, out_specs = [], []
    for shape, spec in outs:
        flow = isinstance(spec, (Flow, Keep))
        out_shapes.append(pltpu.HBM(shape.shape, shape.dtype) if flow else shape)
        out_specs.append(HBM if flow else spec)
        moved.append((spec if flow else None, 1, [shape.shape], shape.dtype))
    extra = []
    for flow, _, shapes, dtype in moved:
        if isinstance(flow, Keep):
            extra += [pltpu.SemaphoreType.DMA((1,))]
        elif flow:
            keys = len(flow.keys(geo, shapes[0]))
            copies = {"x": 4, "w": 4, "w4": 4, "w_in": 16, "w_ahead": 36, "w_back": 36}.get(flow.kind, 1)
            if flow.kind == "w":
                copies = flow.shape[1] // 128
            extra += [flow.buffer(geo, shapes, dtype), pltpu.SemaphoreType.DMA((copies, keys))]
    body = kernel
    if extra:

        def body(*refs):
            n_io = sum(n for _, n, _, _ in moved)
            given, own, rest = list(refs[:n_io]), refs[n_io : n_io + len(scratch)], refs[n_io + len(scratch) :]
            rest = list(rest)
            moves = Moves(geo, given[0][0], ahead)
            args = []
            for n, (flow, count, _, _) in enumerate(moved):
                group, given = given[:count], given[count:]
                if not flow:
                    args += group
                    continue
                if isinstance(flow, Keep):
                    moves.kept.append(pltpu.make_async_copy(args[flow.source], group[0], rest[0].at[0]))
                    rest = rest[1:]
                    continue
                buf, sem = rest[:2]
                rest = rest[2:]
                moves.add(flow, group, buf, sem, n < len(ins))
                args.append(buf)
            moves.begin(hold)
            kernel(moves, *args, *own)
            moves.finish()

    scratch = list(scratch)
    def held(v):
        pinned = "vmem" in str(getattr(v, "memory_space", "")).lower()
        return 0 if pinned else scoped_bytes(v)

    need = sum(held(jax.typeof(a)) for a, spec in zip(arrays, specs) if spec is VMEM)
    need += sum(held(o) for o, spec in zip(out_shapes, out_specs) if spec is VMEM)
    need += sum(
        scoped_bytes(v)
        for v in scratch + extra
        if getattr(v, "memory_space", None) == pltpu.VMEM
    )
    need -= staying
    result = pl.pallas_call(
        body,
        out_shape=out_shapes,
        in_specs=specs,
        out_specs=out_specs,
        scratch_shapes=scratch + extra,
        compiler_params=pltpu.CompilerParams(vmem_limit_bytes=need + need // 16 + (slack << 20)),
        cost_estimate=cost,
        name=name,
    )(*arrays)
    return list(result)


def vm(*arrays):
    return [(a, VMEM) for a in arrays]


def nn(a, b):
    return lax.dot_general(a, b, (((1,), (0,)), ((), ())), preferred_element_type=F32)


def nt(a, b):
    return lax.dot_general(a, b, (((1,), (1,)), ((), ())), preferred_element_type=F32)


def tn(a, b):
    return lax.dot_general(a, b, (((0,), (0,)), ((), ())), preferred_element_type=F32)


def gelu(t):
    half = 0.5 * t
    return half + half * jnp.tanh(t * (G0 + G1 * (t * t)))


def gelu_both(t):
    sq = t * t
    half = 0.5 * t
    th = jnp.tanh(t * (G0 + G1 * sq))
    return half + half * th, 0.5 + 0.5 * th + half * (1.0 - th * th) * (G0 + (3.0 * G1) * sq)


def gelu_slope(t):
    sq = t * t
    th = jnp.tanh(t * (G0 + G1 * sq))
    return 0.5 * (1.0 + th) + (0.5 * t) * (1.0 - th * th) * (G0 + (3.0 * G1) * sq)


def live_rows(count, chans):
    return (lax.broadcasted_iota(jnp.int32, (VIEWS, chans), 0) < count).astype(F32)


def rows_sum(v):
    return jnp.sum(v, axis=0, keepdims=True)


def merged(sa, sb, na, nb):
    total = na + nb
    mean = (na * sa[0:1] + nb * sb[0:1]) / total
    diff = sb[0:1] - sa[0:1]
    square = sa[1:2] + sb[1:2] + diff * diff * (na * nb / total)
    return mean, lax.rsqrt(square / total + EPS)


def as_rows(v):
    return v.reshape(v.shape[0] * v.shape[1], v.shape[2])


def as_pix_rows(v):
    return v.reshape(v.shape[0] * v.shape[1], VIEWS, v.shape[3])


def as_pix(v):
    return v.reshape(v.shape[0] // VIEWS, VIEWS, v.shape[1])


class Geo:
    def __init__(self, hb, hs):
        self.hb, self.hs = hb, hs
        self.pb, self.ps = hb * hb, hs * hs
        self.px = self.pb + self.ps
        self.rows = self.px * VIEWS
        self.qb, self.qs = self.pb // 4, self.ps // 4
        self.px4 = self.qb + self.qs
        self.rows4 = self.px4 * VIEWS
        self.parts = ((hb, 0), (hs, self.pb))
        self.groups = [self.cuts(hb // 2, 1), self.cuts(hs // 2, 2)]
        self.spans = [[list(range(n))[: n // 2], list(range(n))[n // 2 :]] for n in map(len, self.groups)]
        self.bands = [[(0, hb // 2), (hb // 2, hb)], [(0, hs)]]

    @staticmethod
    def cuts(steps, first):
        at = sorted({0, steps} | set(range(first, steps, 2)))
        return list(zip(at[:-1], at[1:]))

    @staticmethod
    def aligned(n):
        return n if isinstance(n, int) else pl.multiple_of(n, 16)

    def step(self, part, i):
        side, start = self.parts[part]
        npx = 2 * side
        return start + i * npx, npx, self.aligned((start + i * npx) * VIEWS), npx * VIEWS

    def staged(self, io, before, product, carries):
        out = []
        for part in range(2):
            carry = carries[part]
            for span in self.spans[part]:
                lo, hi = self.groups[part][span[0]][0], self.groups[part][span[-1]][1]
                for n in span:
                    io.arrive(part, n)
                pix, npx, row, nrows = self.step(part, lo)
                if before:

                    def early(i, c, part=part):
                        before(part, i, *self.step(part, i))
                        return c

                    lax.fori_loop(lo, hi, early, 0)
                carry = product(part, pix, npx * (hi - lo), row, nrows * (hi - lo), carry)
                for n in span:
                    io.leave(part, n)
            out.append(carry)
        return out

    def loop(self, body, carries, arrive=None, leave=None):
        out = []
        for part in range(2):

            def run(i, carry, part=part):
                for n, (lo, hi) in enumerate(self.groups[part]):
                    if arrive:
                        pl.when(i == lo)(functools.partial(arrive.arrive, part, n))
                carry = body(part, i, *self.step(part, i), carry)
                for n, (lo, hi) in enumerate(self.groups[part]):
                    if leave:
                        pl.when(i == hi - 1)(functools.partial(leave.leave, part, n))
                return carry

            out.append(lax.fori_loop(0, self.groups[part][-1][1], run, carries[part]))
        return out


def finish_stats(geo, ref, sums, lives, count, out, quarter=None):
    mean = (rows_sum(sums[0] * lives[0]) + rows_sum(sums[1] * lives[1])) / count

    def body(part, i, pix, npx, row, nrows, carry):
        dev = ref[pl.ds(pix, npx)] - mean
        return carry + jnp.sum(dev * dev, axis=0)

    zero = jnp.zeros(sums[0].shape, F32)
    sq = geo.loop(body, [zero, zero])
    out[0:1] = mean
    out[1:2] = rows_sum(sq[0] * lives[0]) + rows_sum(sq[1] * lives[1])


def block_stats(geo, value, lives, count):
    big, small = value[: geo.qb], value[geo.qb :]
    mean = (
        rows_sum(jnp.sum(big, axis=0) * lives[0]) + rows_sum(jnp.sum(small, axis=0) * lives[1])
    ) / count
    db, ds = big - mean, small - mean
    square = rows_sum(jnp.sum(db * db, axis=0) * lives[0]) + rows_sum(
        jnp.sum(ds * ds, axis=0) * lives[1]
    )
    return mean, square


def k_reduce(geo, io, me, nf, xs, wt, pre, stats):
    io.ready()
    chans = wt.shape[1]
    lives = [live_rows(me[1], chans), live_rows(me[2], chans)]

    def product(part, pix, npx, row, nrows, carry):
        acc = None
        for j in range(4):
            d = nt(xs[j, row : row + nrows, :], wt[j])
            acc = d if acc is None else acc + d
        z = as_pix(acc)
        pre[pix : pix + npx] = z
        return carry + jnp.sum(z, axis=0)

    zero = jnp.zeros((VIEWS, chans), F32)
    sums = geo.staged(io, None, product, [zero, zero])
    finish_stats(geo, pre, sums, lives, nf[0], stats)


def k_counts(ni, sizes, counts, me, nf3, cnt3, nf4, cnt4):
    img = lax.axis_index("img")
    levels = ni.bit_length() - 1
    me[0] = lax.axis_index("ch").astype(jnp.int32)
    me[1] = counts[img, 0]
    me[2] = counts[img, 1]
    me[3] = img
    for (big, small), nf, cnt in zip(sizes, (nf3, nf4), (cnt3, cnt4)):

        def group(shift, index):
            def add(i, total):
                at = index * (1 << shift) + i
                return total + counts[at, 0] * big + counts[at, 1] * small

            return lax.fori_loop(0, 1 << shift, add, jnp.int32(0)).astype(F32)

        nf[0] = group(0, img)
        for m in range(2):
            nf[1 + m] = group(levels - 1, (img >> (levels - 1)) ^ m)
        row, k = 0, 0
        while k < levels - 1:
            bits = 2 if k == 0 else 1
            for m in range(8):
                cnt[row + m] = group(k, (img >> k) ^ m) if m < 1 << bits else jnp.float32(0.0)
            row, k = row + 8, k + bits


def k_pack_params(gm3, sm3, go3, so3, gm4, sm4, go4, so4, out, rows):
    rows[...] = jnp.zeros(rows.shape, F32)
    rows[0:2, 0:64] = gm3[...]
    rows[2:4, 0:64] = sm3[...]
    for b in range(2):
        lanes = slice(128 * b, 128 * b + 128)
        rows[4 + b : 5 + b] = go3[:, lanes]
        rows[6 + b : 7 + b] = so3[:, lanes]
    rows[8:10] = gm4[...]
    rows[10:12] = sm4[...]
    for n in range(2):
        for b in range(4):
            lanes = slice(128 * b, 128 * b + 128)
            rows[12 + 4 * n + b : 13 + 4 * n + b] = go4[n : n + 1, lanes]
            rows[20 + 4 * n + b : 21 + 4 * n + b] = so4[n : n + 1, lanes]
    v = rows[...]
    high = v.astype(BF16)
    rest = v - high.astype(F32)
    mid = rest.astype(BF16)
    low = (rest - mid.astype(F32)).astype(BF16)
    out[0:32, 0:128] = high
    out[0:32, 128:256] = mid
    out[32:64, 0:128] = low
    out[32:64, 128:256] = jnp.zeros_like(low)


def k_unpack_params(base, me, p0, p1, p2, p3, gs1, gs2, gs3, gs4, gs5, gs6, buf, sem):
    copies = [
        pltpu.make_async_copy(p.at[pl.ds(base, 64)], buf.at[n], sem.at[n])
        for n, p in enumerate((p0, p1, p2, p3))
    ]
    for c in copies:
        c.start()
    for c in copies:
        c.wait()
    rows = []
    for n in range(4):
        v = buf[n].astype(F32)
        rows.append(v[0:32, 0:128] + v[0:32, 128:256] + v[32:64, 0:128])
    odd = me[0] & 1
    for chip in range(2):
        mine, other = rows[2 * chip][:, 0:64], rows[2 * chip + 1][:, 0:64]
        both = jnp.where(
            odd == 0,
            jnp.concatenate([mine, other], axis=1),
            jnp.concatenate([other, mine], axis=1),
        )
        at = pl.ds(pl.multiple_of(((me[0] >> 1) ^ chip) * 128, 128), 128)
        for n, gs in enumerate((gs1, gs2)):
            gs[0:1, at] = both[n : n + 1]
            gs[1:2, at] = both[2 + n : 3 + n]
    for p, v in enumerate(rows):
        for b in range(2):
            at = pl.ds(pl.multiple_of((me[0] ^ p) * 256 + 128 * b, 128), 128)
            gs3[0:1, at] = v[4 + b : 5 + b]
            gs3[1:2, at] = v[6 + b : 7 + b]
        at = pl.ds(pl.multiple_of((me[0] ^ p) * 128, 128), 128)
        for n, gs in enumerate((gs4, gs5)):
            gs[0:1, at] = v[8 + n : 9 + n]
            gs[1:2, at] = v[10 + n : 11 + n]
    for chip in range(2):
        v = rows[2 * chip]
        for n in range(2):
            for b in range(4):
                lanes = slice(128 * b, 128 * b + 128)
                gs6[chip, 2 * n : 2 * n + 1, lanes] = v[12 + 4 * n + b : 13 + 4 * n + b]
                gs6[chip, 2 * n + 1 : 2 * n + 2, lanes] = v[20 + 4 * n + b : 21 + 4 * n + b]


def k_merge(first, n, cnt, *refs):
    arrays, out = refs[:n], refs[n]
    for at in range(0, out.shape[-2], 2):
        mean_at, sq_at = (..., slice(at, at + 1), slice(None)), (..., slice(at + 1, at + 2), slice(None))
        groups = [(cnt[first + m], a[mean_at], a[sq_at]) for m, a in enumerate(arrays)]
        while len(groups) > 1:
            pairs = []
            for (na, ma, qa), (nb, mb, qb) in zip(groups[::2], groups[1::2]):
                total = na + nb
                diff = mb - ma
                pairs.append(
                    (total, (na * ma + nb * mb) / total, qa + qb + diff * diff * (na * nb / total))
                )
            groups = pairs
        out[mean_at], out[sq_at] = groups[0][1], groups[0][2]


def k_add(n, *refs):
    values = [r[...] for r in refs[:n]]
    while len(values) > 1:
        values = [a + b for a, b in zip(values[::2], values[1::2])]
    refs[n][...] = values[0]


def side_shift(v, by):
    zero = jnp.zeros((v.shape[0], 1) + v.shape[2:], v.dtype)
    if by > 0:
        return jnp.concatenate([zero, v[:, :-1]], axis=1)
    return jnp.concatenate([v[:, 1:], zero], axis=1)


def store_shifted(buf, row, nrows, side, v, order):
    img = v.reshape(2, side, VIEWS, v.shape[-1])
    chans = v.shape[-1]
    forms = [side_shift(img, 1), img, side_shift(img, -1)]
    for lane, k in enumerate(order):
        flat = forms[k].reshape(nrows, chans).astype(BF16)
        buf[pl.ds(row, nrows), lane * chans : (lane + 1) * chans] = flat


def put_phases(ref, i, v):
    for k in range(4):
        ref[k // 2, k % 2, i] = v[k // 2, :, k % 2]


def get_phases(ref, i):
    rows = [jnp.stack([ref[r, 0, i], ref[r, 1, i]], axis=1) for r in range(2)]
    return jnp.stack(rows)


def zero_edges(buf, edge):
    total = buf.shape[0]
    buf[0:edge, :] = jnp.zeros((edge, buf.shape[1]), BF16)
    buf[total - edge : total, :] = jnp.zeros((edge, buf.shape[1]), BF16)


def k_mix(geo, io, me, nf, pre1, sa, sb, gs, w, pre2, wb, ws, stats, dev, center):
    chans = pre1.shape[-1]
    lives = [live_rows(me[1], chans), live_rows(me[2], chans)]
    mean, inv = merged(sa[...], sb[...], nf[1], nf[2])
    scale, shift = gs[0:1] * inv, gs[1:2]
    bufs = (wb, ws)
    for part, (side, _) in enumerate(geo.parts):
        zero_edges(bufs[part], side * VIEWS)

    def act(part, i, pix, npx, row, nrows, carry):
        a = gelu((pre1[pl.ds(pix, npx)] - mean) * scale + shift)
        own = (pre1[pl.ds(pix, npx), :, lanes] - center[:, lanes]) * lives[part][:, 0:128]
        dev[pl.ds(row, nrows), :] = as_rows(own).astype(BF16)
        side = geo.parts[part][0]
        at = pl.multiple_of(side * VIEWS + i * nrows, 16)
        store_shifted(bufs[part], at, nrows, side, a, (0, 1, 2))
        return carry

    lanes, _ = own_block(me)
    center[...] = mean
    geo.loop(act, [0, 0], io)
    io.send(wb, ws, dev)
    io.ready()

    sums = [jnp.zeros((VIEWS, chans), F32)] * 2
    for part, (side, start) in enumerate(geo.parts):
        for lo, hi in geo.bands[part]:
            acc = None
            for r in range(3):
                at = (lo + r) * side * VIEWS
                d = nt(bufs[part][at : at + (hi - lo) * side * VIEWS, :], w[r])
                acc = d if acc is None else acc + d
            z = as_pix(acc)
            pre2[start + lo * side : start + hi * side] = z
            sums[part] = sums[part] + jnp.sum(z, axis=0)
    finish_stats(geo, pre2, sums, lives, nf[0], stats)


def k_expand(geo, io, me, nf, pre2, sa, sb, gs, w, pre3, act2, stats):
    chans = w.shape[1]
    lives = [live_rows(me[1], chans), live_rows(me[2], chans)]
    mean, inv = merged(sa[...], sb[...], nf[1], nf[2])
    scale, shift = gs[0:1] * inv, gs[1:2]

    def before(part, i, pix, npx, row, nrows):
        a = as_rows(gelu((pre2[pl.ds(pix, npx)] - mean) * scale + shift)).astype(BF16)
        act2[pl.ds(row, nrows), :] = a

    def product(part, pix, npx, row, nrows, carry):
        total = []
        for j in range(4):
            at = slice(256 * j, 256 * j + 256)
            z = as_pix(nn(act2[row : row + nrows, :], w[:, at]))
            pre3[pix : pix + npx, :, at] = z
            total.append(jnp.sum(z, axis=0))
        return carry + jnp.concatenate(total, axis=1)

    io.ready()
    zero = jnp.zeros((VIEWS, chans), F32)
    sums = geo.staged(io, before, product, [zero, zero])
    finish_stats(geo, pre3, sums, lives, nf[0], stats)


def k_narrow(geo, io, me, nf, pre3, xs, sa, sb, gs, w, pre4b, pre4s, mid, mids, stats, dev3, slope3, mid_even):
    chans = w.shape[1]
    lives = [live_rows(me[1], chans), live_rows(me[2], chans)]
    mean, inv = merged(sa[...], sb[...], nf[1], nf[2])
    scale, shift = gs[0:1] * inv, gs[1:2]
    pre4 = (pre4b, pre4s)

    def body(part, i, pix, npx, row, nrows, carry):
        side = geo.parts[part][0]
        half = side // 2
        for j in range(4):
            at = slice(256 * j, 256 * j + 256)
            dev = pre3[pl.ds(pix, npx), :, at] - mean[:, at]
            x = as_pix(xs[j, pl.ds(row, nrows), :].astype(F32))
            a, slope = gelu_both(dev * scale[:, at] + shift[:, at] + x)
            mid[pl.ds(row, nrows), at] = as_rows(a).astype(BF16)
            dev3[pl.ds(row, nrows), at] = as_rows(dev).astype(BF16)
            slope3[pl.ds(row, nrows), at] = as_rows(slope).astype(BF16)
            even = a.reshape(2, half, 2, VIEWS, 256)[0, :, 0]
            mid_even[pl.ds((0, geo.qb)[part] + half * i, half), :, at] = even
        z = nn(mid[pl.ds(row, nrows), :], w[...])
        put_phases(pre4[part], i, z.reshape(2, half, 2, VIEWS, chans))
        return carry + jnp.sum(as_pix(z), axis=0)

    io.ready()
    zero = jnp.zeros((VIEWS, chans), F32)
    sums = geo.loop(body, [zero, zero], io, io)
    mean4 = (rows_sum(sums[0] * lives[0]) + rows_sum(sums[1] * lives[1])) / nf[0]
    mids[...] = as_rows(mid_even[...]).astype(BF16)
    io.send(mids)
    sq = []
    for part in range(2):

        def dev2(i, carry, part=part):
            for k in range(4):
                d = pre4[part][k // 2, k % 2, i] - mean4
                carry = carry + jnp.sum(d * d, axis=0)
            return carry

        sq.append(lax.fori_loop(0, geo.parts[part][0] // 2, dev2, zero))
    stats[0:1] = mean4
    stats[1:2] = rows_sum(sq[0] * lives[0]) + rows_sum(sq[1] * lives[1])


def k_short(geo, io, me, nf, mids, w0, w1, side, stats):
    io.ready()
    chans = w0.shape[1]
    lives = [live_rows(me[1], chans), live_rows(me[2], chans)]
    for j, w in enumerate((w0, w1)):
        z = as_pix(nn(mids[...], w[...]))
        side[j] = z
        io.leave(j)
        mean, square = block_stats(geo, z, lives, nf[0])
        stats[j] = jnp.concatenate([mean, square], axis=0)


def k_stride(geo, io, me, nf, n4, pre4b, pre4s, sa, sb, gs, w, pre5, cols, stats, sb_act, ss_act):
    chans = pre4b.shape[-1]
    lives = [live_rows(me[1], chans), live_rows(me[2], chans)]
    mean, inv = merged(sa[...], sb[...], n4[1], n4[2])
    scale, shift = gs[0:1] * inv, gs[1:2]
    srcs, dsts = (pre4b, pre4s), (sb_act, ss_act)

    def act(part, i, pix, npx, row, nrows, carry):
        for k in range(4):
            at = (k // 2, k % 2, i)
            dsts[part][at] = gelu((srcs[part][at] - mean) * scale + shift)
        return carry

    geo.loop(act, [0, 0], io)
    for r in range(3):
        for c in range(3):
            flats = []
            for part in range(2):
                half = geo.parts[part][0] // 2
                v = dsts[part][(r + 1) % 2, (c + 1) % 2]
                if c == 0:
                    v = side_shift(v, 1)
                if r == 0:
                    v = jnp.concatenate([jnp.zeros((1,) + v.shape[1:], F32), v[:-1]], axis=0)
                flats.append(v.reshape(half * half * VIEWS, chans))
            t = 3 * r + c
            cols[t] = jnp.concatenate(flats, axis=0).astype(BF16)
            io.leave(t)
    io.ready()
    acc = None
    for t in range(9):
        d = nn(cols[t], w[t * chans : (t + 1) * chans, :])
        acc = d if acc is None else acc + d
    z = as_pix(acc)
    pre5[...] = z
    m5, s5 = block_stats(geo, z, lives, nf[0])
    stats[0:1] = m5
    stats[1:2] = s5


def k_widen(geo, io, me, nf, pre5, sa, sb, gs, w0, w1, st_side, pre6, act5, stats):
    chans = w0.shape[1]
    lives = [live_rows(me[1], chans), live_rows(me[2], chans)]
    mean, inv = merged(sa[...], sb[...], nf[1], nf[2])
    scale, shift = gs[0:1] * inv, gs[1:2]
    act5[...] = as_rows(gelu((pre5[...] - mean) * scale + shift)).astype(BF16)
    io.ready()
    for j, w in enumerate((w0, w1)):
        z = as_pix(nn(act5[...], w[...]))
        pre6[j] = z
        io.leave(j)
        m6, s6 = block_stats(geo, z, lives, nf[0])
        stats[j] = jnp.concatenate([m6, s6, st_side[j]], axis=0)


def k_total(geo, io, me, nf, pre6, side, sa, sb, gs, cb0, cb1, cs0, cs1, out_b, out_s, dt, sums, cot):
    chans = pre6.shape[-1]
    lives = [live_rows(me[1], chans), live_rows(me[2], chans)]
    cots = ((cb0, cb1), (cs0, cs1))
    spans = ((0, geo.qb), (geo.qb, geo.px4))
    outs = (out_b, out_s)
    io.ready()
    for j in range(2):
        io.arrive(j)
        a, b, g = sa[j], sb[j], gs[j]
        m6, r6 = merged(a[0:2], b[0:2], nf[1], nf[2])
        ms, rs = merged(a[2:4], b[2:4], nf[1], nf[2])
        k6, ks = g[0:1] * r6, g[2:3] * rs
        off = g[1:2] + g[3:4]
        acc = [jnp.zeros((VIEWS, chans), F32)] * 3
        for part, (lo, hi) in enumerate(spans):
            half = geo.parts[part][0] // 2
            cot[lo:hi] = as_pix(cots[part][j][...].astype(F32))

            def row(i, carry, part=part, lo=lo, half=half):
                at = pl.ds(lo + i * half, half)
                d6 = pre6[j, at] - m6
                dd = side[j, at] - ms
                value, slope = gelu_both(d6 * k6 + (dd * ks + off))
                if j == 0:
                    outs[part][pl.ds(i * half, half)] = value * lives[part]
                grad = slope * (cot[at] * lives[part])
                dt[j, at] = grad
                terms = [jnp.sum(v, axis=0) for v in (grad, grad * d6, grad * dd)]
                return [s + t for s, t in zip(carry, terms)]

            acc = lax.fori_loop(0, half, row, acc)
        io.leave(j)
        if j == 0:
            io.send(out_b, out_s)
        sums[j] = jnp.concatenate(
            [rows_sum(acc[0]), rows_sum(acc[1]) * r6, rows_sum(acc[2]) * rs], axis=0
        )


def back_coefs(lives, s1, s2, inv, gain, count):
    c1 = gain * inv
    c2 = [live * (c1 * s1 / count) for live in lives]
    c3 = [live * (c1 * inv * s2 / count) for live in lives]
    return c1, c2, c3


def k_back_wide(geo, io, me, nf, dt, pre6, side, sa, sb, gs, ga, gb, w0, w1, part5, dz6, dzs, tot):
    chans = pre6.shape[-1]
    lives = [live_rows(me[1], chans), live_rows(me[2], chans)]
    total = nf[1] + nf[2]
    spans = ((0, geo.qb), (geo.qb, geo.px4))
    acc = None
    io.ready()
    for j, w in enumerate((w0, w1)):
        io.arrive(j)
        a, b, g = sa[j], sb[j], gs[j]
        s = ga[j] + gb[j]
        tot[j] = s
        m6, r6 = merged(a[0:2], b[0:2], nf[1], nf[2])
        ms, rs = merged(a[2:4], b[2:4], nf[1], nf[2])
        k1, k2, k3 = back_coefs(lives, s[0:1], s[1:2], r6, g[0:1], total)
        h1, h2, h3 = back_coefs(lives, s[0:1], s[2:3], rs, g[2:3], total)
        main, short = [], []
        for part, (lo, hi) in enumerate(spans):
            grad = dt[j, lo:hi]
            main.append(grad * k1 - k2[part] - (pre6[j, lo:hi] - m6) * k3[part])
            short.append(grad * h1 - h2[part] - (side[j, lo:hi] - ms) * h3[part])
        z6 = as_rows(jnp.concatenate(main, axis=0)).astype(BF16)
        dzs[j] = as_rows(jnp.concatenate(short, axis=0)).astype(BF16)
        io.leave(j)
        if j == 0:
            dz6[...] = z6
        d = nt(z6, w[...])
        acc = d if acc is None else acc + d
    part5[...] = as_pix(acc)


def k_back_act5(nf, mine, other, pre5, sa5, sb5, gs5, dt5, sums5):
    m5, r5 = merged(sa5[...], sb5[...], nf[1], nf[2])
    dev = pre5[...] - m5
    grad = gelu_slope(dev * (gs5[0:1] * r5) + gs5[1:2]) * (mine[...] + other[...])
    dt5[...] = grad
    sums5[0:1] = rows_sum(jnp.sum(grad, axis=0))
    sums5[1:2] = rows_sum(jnp.sum(grad * dev, axis=0)) * r5


def k_back_short(io, me, dzs, w0, w1, dms):
    io.ready()
    acc = None
    for j, w in enumerate((w0, w1)):
        d = nt(dzs[j], w[...])
        acc = d if acc is None else acc + d
    dms[...] = as_pix(acc).astype(BF16)


def k_back_stride(geo, io, me, nf, dt5, pre5, sa5, sb5, gs5, ga, gb, pre4b, pre4s, sa4, sb4, gs4, n4, w, dt4b, dt4s, dz5, sums4, tot, shifts):
    chans = pre5.shape[-1]
    lives = [live_rows(me[1], chans), live_rows(me[2], chans)]
    s = ga[...] + gb[...]
    tot[...] = s
    m5, r5 = merged(sa5[...], sb5[...], nf[1], nf[2])
    c1, c2, c3 = back_coefs(lives, s[0:1], s[1:2], r5, gs5[0:1], nf[1] + nf[2])
    spans = ((0, geo.qb), (geo.qb, geo.px4))
    imgs = []
    for part, (lo, hi) in enumerate(spans):
        half = geo.parts[part][0] // 2
        z = dt5[lo:hi] * c1 - c2[part] - (pre5[lo:hi] - m5) * c3[part]
        imgs.append(z.reshape(half, half, VIEWS, chans))

    def flat(moved):
        return jnp.concatenate([v.reshape(-1, chans) for v in moved], axis=0).astype(BF16)

    def up(v):
        return jnp.concatenate([v[1:], jnp.zeros((1,) + v.shape[1:], F32)], axis=0)

    shifts[0] = flat(imgs)
    dz5[...] = shifts[0]
    shifts[1] = flat([side_shift(v, -1) for v in imgs])
    shifts[2] = flat([up(v) for v in imgs])
    shifts[3] = flat([up(side_shift(v, -1)) for v in imgs])
    m4, r4 = merged(sa4[...], sb4[...], n4[1], n4[2])
    scale, off = gs4[0:1] * r4, gs4[1:2]
    io.ready()
    plan = {
        (0, 0): ((0, 4),),
        (0, 1): ((0, 5), (1, 3)),
        (1, 0): ((0, 7), (2, 1)),
        (1, 1): ((0, 8), (1, 6), (2, 2), (3, 0)),
    }
    t1, t2 = jnp.zeros((VIEWS, chans), F32), jnp.zeros((VIEWS, chans), F32)
    for (rp, cp), terms in plan.items():
        acc = None
        for k, t in terms:
            d = nt(shifts[k], w[t * chans : (t + 1) * chans, :])
            acc = d if acc is None else acc + d
        for part, (lo, hi) in enumerate(spans):
            half = geo.parts[part][0] // 2
            d = acc[lo * VIEWS : hi * VIEWS].reshape(half, half, VIEWS, chans)
            dev = (pre4b, pre4s)[part][rp, cp] - m4
            grad = gelu_slope(dev * scale + off) * d
            (dt4b, dt4s)[part][rp, cp] = grad
            t1 = t1 + jnp.sum(grad, axis=(0, 1))
            t2 = t2 + jnp.sum(grad * dev, axis=(0, 1))
    io.send(dt4b, dt4s)
    sums4[0:1] = rows_sum(t1)
    sums4[1:2] = rows_sum(t2) * r4


def k_back_narrow(geo, io, me, nf, dt4b, dt4s, pre4b, pre4s, sa4, sb4, gs4, ga, gb, dev3, slope3, sa3, sb3, dms, dmo, w, dt3, dz4, sums3, tot):
    chans = w.shape[1]
    wide = w.shape[0]
    lives = [live_rows(me[1], chans), live_rows(me[2], chans)]
    s = ga[...] + gb[...]
    tot[...] = s
    m4, r4 = merged(sa4[...], sb4[...], nf[1], nf[2])
    c1, c2, c3 = back_coefs(lives, s[0:1], s[1:2], r4, gs4[0:1], nf[1] + nf[2])
    _, r3 = merged(sa3[...], sb3[...], nf[1], nf[2])
    dts, pres = (dt4b, dt4s), (pre4b, pre4s)

    def body(part, i, pix, npx, row, nrows, carry):
        half = geo.parts[part][0] // 2
        dev4 = get_phases(pres[part], i) - m4
        z = get_phases(dts[part], i) * c1 - c2[part] - dev4 * c3[part]
        z = z.reshape(nrows, chans).astype(BF16)
        dz4[pl.ds(row, nrows), :] = z
        at = pl.ds((0, geo.qb)[part] + half * i, half)
        t1, t2 = [], []
        for j in range(4):
            at_j = slice(256 * j, 256 * j + 256)
            d = nt(z, w[at_j, :]).reshape(2, half, 2, VIEWS, 256)
            even = d[0, :, 0] + (dms[at, :, at_j].astype(F32) + dmo[at, :, at_j].astype(F32))
            top = jnp.stack([even, d[0, :, 1]], axis=1)
            d = jnp.concatenate([as_pix_rows(top), as_pix_rows(d[1])], axis=0)
            dev = as_pix(dev3[pl.ds(row, nrows), at_j].astype(F32))
            grad = as_pix(slope3[pl.ds(row, nrows), at_j].astype(F32)) * d
            dt3[pl.ds(row, nrows), at_j] = as_rows(grad).astype(BF16)
            t1.append(jnp.sum(grad, axis=0))
            t2.append(jnp.sum(grad * dev, axis=0))
        return carry[0] + jnp.concatenate(t1, axis=1), carry[1] + jnp.concatenate(t2, axis=1)

    io.ready()
    zero = jnp.zeros((VIEWS, wide), F32)
    (a1, a2), (b1, b2) = geo.loop(body, [(zero, zero), (zero, zero)], io, io)
    sums3[0:1] = rows_sum(a1 + b1)
    sums3[1:2] = rows_sum(a2 + b2) * r3


def k_back_expand(geo, io, me, nf, dt3, dev3, sa3, sb3, gs3, ga, gb, pre2, sa2, sb2, gs2, w, dt2, dz3, dt3q, sums2, tot, zbuf_b, zbuf_s):
    wide, chans = w.shape[1], w.shape[0]
    lives = [live_rows(me[1], wide), live_rows(me[2], wide)]
    s = ga[...] + gb[...]
    tot[...] = s
    _, r3 = merged(sa3[...], sb3[...], nf[1], nf[2])
    c1, c2, c3 = back_coefs(lives, s[0:1], s[1:2], r3, gs3[0:1], nf[1] + nf[2])
    m2, r2 = merged(sa2[...], sb2[...], nf[1], nf[2])
    scale, off = gs2[0:1] * r2, gs2[1:2]
    mine = pl.ds(pl.multiple_of(me[0] * 256, 256), 256)

    def body(part, i, pix, npx, row, nrows, carry):
        zbuf = (zbuf_b, zbuf_s)[part]
        dt3q[pl.ds(row, nrows), :] = dt3[pl.ds(row, nrows), mine]
        for j in range(4):
            at = slice(256 * j, 256 * j + 256)
            z = (
                as_pix(dt3[pl.ds(row, nrows), at].astype(F32)) * c1[:, at]
                - c2[part][:, at]
                - as_pix(dev3[pl.ds(row, nrows), at].astype(F32)) * c3[part][:, at]
            )
            zbuf[:, at] = as_rows(z).astype(BF16)
        dz3[pl.ds(row, nrows), :] = zbuf[:, mine]
        d = as_pix(nt(zbuf[...], w[...]))
        dev = pre2[pl.ds(pix, npx)] - m2
        grad = gelu_slope(dev * scale + off) * d
        dt2[pl.ds(pix, npx)] = grad
        return carry[0] + jnp.sum(grad, axis=0), carry[1] + jnp.sum(grad * dev, axis=0)

    io.ready()
    zero = jnp.zeros((VIEWS, chans), F32)
    (a1, a2), (b1, b2) = geo.loop(body, [(zero, zero), (zero, zero)], io, io)
    sums2[0:1] = rows_sum(a1 + b1)
    sums2[1:2] = rows_sum(a2 + b2) * r2


def k_back_mix(geo, io, me, nf, dt2, pre2, sa2, sb2, gs2, ga, gb, pre1, sa1, sb1, gs1, w, dt1, dz2, sums1, tot, dt1q, zb, zs):
    chans = pre2.shape[-1]
    lives = [live_rows(me[1], chans), live_rows(me[2], chans)]
    s = ga[...] + gb[...]
    tot[...] = s
    m2, r2 = merged(sa2[...], sb2[...], nf[1], nf[2])
    c1, c2, c3 = back_coefs(lives, s[0:1], s[1:2], r2, gs2[0:1], nf[1] + nf[2])
    m1, r1 = merged(sa1[...], sb1[...], nf[1], nf[2])
    scale, off = gs1[0:1] * r1, gs1[1:2]
    bufs = (zb, zs)
    for part, (side, _) in enumerate(geo.parts):
        zero_edges(bufs[part], side * VIEWS)

    def back(part, i, pix, npx, row, nrows, carry):
        z = dt2[pl.ds(pix, npx)] * c1 - c2[part] - (pre2[pl.ds(pix, npx)] - m2) * c3[part]
        dz2[pl.ds(row, nrows), :] = as_rows(z).astype(BF16)
        side = geo.parts[part][0]
        at = pl.multiple_of(side * VIEWS + i * nrows, 16)
        store_shifted(bufs[part], at, nrows, side, z, (2, 1, 0))
        return carry

    lanes, _ = own_block(me)
    geo.loop(back, [0, 0], io)
    io.send(dz2)
    io.ready()

    for part, (side, start) in enumerate(geo.parts):
        for lo, hi in geo.bands[part]:
            acc = None
            for r in range(3):
                at = (lo + 2 - r) * side * VIEWS
                taps = w[3 * r : 3 * r + 3].reshape(3 * chans, chans)
                d = nn(bufs[part][at : at + (hi - lo) * side * VIEWS, :], taps)
                acc = d if acc is None else acc + d
            dt1[start + lo * side : start + hi * side] = as_pix(acc)

    def finish(part, i, pix, npx, row, nrows, carry):
        dev = pre1[pl.ds(pix, npx)] - m1
        grad = gelu_slope(dev * scale + off) * dt1[pl.ds(pix, npx)]
        dt1[pl.ds(pix, npx)] = grad
        dt1q[pl.ds(row, nrows), :] = as_rows(dt1[pl.ds(pix, npx), :, lanes]).astype(BF16)
        return carry[0] + jnp.sum(grad, axis=0), carry[1] + jnp.sum(grad * dev, axis=0)

    zero = jnp.zeros((VIEWS, chans), F32)
    (a1, a2), (b1, b2) = geo.loop(finish, [(zero, zero), (zero, zero)], None, io)
    sums1[0:1] = rows_sum(a1 + b1)
    sums1[1:2] = rows_sum(a2 + b2) * r1


def k_back_reduce(geo, io, me, nf, dt1, pre1, sa1, sb1, gs1, ga, gb, dt3q, wt, gxb, gxs, tot, coef):
    chans = pre1.shape[-1]
    lives = [live_rows(me[1], chans), live_rows(me[2], chans)]
    s = ga[...] + gb[...]
    tot[...] = s
    m1, r1 = merged(sa1[...], sb1[...], nf[1], nf[2])
    c1, c2, c3 = back_coefs(lives, s[0:1], s[1:2], r1, gs1[0:1], nf[1] + nf[2])
    io.ready()
    total = nf[1] + nf[2]
    coef[0:1] = c1
    coef[1:2] = c1 * s[0:1] / total
    coef[2:3] = c1 * r1 * s[1:2] / total

    def body(part, i, pix, npx, row, nrows, carry):
        z = dt1[pl.ds(pix, npx)] * c1 - c2[part] - (pre1[pl.ds(pix, npx)] - m1) * c3[part]
        z = as_rows(z).astype(BF16)
        g = as_pix(nn(z, wt[me[0]])) + as_pix(dt3q[pl.ds(row, nrows), :].astype(F32))
        (gxb, gxs)[part][pl.ds(pix - (0, geo.pb)[part], npx)] = g
        return carry

    geo.loop(body, [0, 0], io, io)


def k_dw_wide(act5, dz6, mids, dzs, dwide, dshort):
    dwide[...] = tn(act5[...], dz6[...]).astype(BF16)
    dshort[...] = tn(mids[...], dzs[0]).astype(BF16)


def lane_blocks(v):
    return [v[:, 128 * b : 128 * b + 128] for b in range(v.shape[1] // 128)]


def put_halves(me, full, keep, send):
    bit = me[3] & 1
    keep[...] = full[bit].astype(BF16)
    send[...] = full[1 - bit].astype(BF16)


def k_dw_stride(io, me, cols, dz5, keep, send, full):
    mine = pl.ds(pl.multiple_of(me[0] * 128, 128), 128)
    z = dz5[:, mine]
    rows = full.shape[1]
    for t in range(9):
        io.arrive(t)
        dw = tn(cols[t], z)
        lo = 0
        while lo < 512:
            half, at = divmod(t * 512 + lo, rows)
            n = min(512 - lo, rows - at)
            full[half, at : at + n] = dw[lo : lo + n]
            lo += n
    put_halves(me, full, keep, send)


def k_dw_mid(me, mid, dz4, act2, dz3, keep, send, full):
    mine = pl.ds(pl.multiple_of(me[0] * 128, 128), 128)
    blocks = [tn(mid[...], dz4[:, mine])] + lane_blocks(tn(act2[...], dz3[...]))
    full[...] = jnp.concatenate(blocks, axis=0).reshape(full.shape)
    put_halves(me, full, keep, send)


def own_block(me):
    lanes = pl.ds(pl.multiple_of((me[0] >> 1) * 128, 128), 128)
    return lanes, pl.ds(pl.multiple_of((me[0] & 1) * 64, 64), 64)


def k_dev_products(geo, io, me, devq, xs, out, part):
    lives = [live_rows(me[1], 256), live_rows(me[2], 256)]
    _, mine = own_block(me)
    io.ready()

    def body(step, i, pix, npx, row, nrows, carry):
        return [
            carry[j] + jnp.sum(as_pix(xs[j, pl.ds(row, nrows), :].astype(F32)), axis=0) for j in range(4)
        ]

    zero = [jnp.zeros((VIEWS, 256), F32)] * 4
    big, small = geo.loop(body, [zero, zero], io)
    sums = [jnp.broadcast_to(rows_sum(b * lives[0] + s * lives[1]), (8, 256)) for b, s in zip(big, small)]
    for j in range(4):
        part[...] = tn(devq[...], xs[j])
        out[:, 256 * j : 256 * j + 256] = jnp.concatenate([part[mine, :], sums[j]], axis=0).astype(BF16)


def k_dw_last(geo, io, me, wb, ws, dz2, xs, dt1q, keep, send, full, part, flat):
    lanes, mine = own_block(me)
    io.ready()
    io.start_steps()
    nb, ns = geo.pb * VIEWS, geo.ps * VIEWS
    at = 0
    for r in range(3):
        ob, os = r * geo.hb * VIEWS, r * geo.hs * VIEWS
        full[...] = tn(dz2[0:nb, lanes], wb[ob : ob + nb, :]) + tn(
            dz2[nb : nb + ns, lanes], ws[os : os + ns, :]
        )
        for block in lane_blocks(full[mine, :]):
            flat[at : at + 64] = block
            at += 64
    geo.loop(lambda step, i, pix, npx, row, nrows, carry: carry, [0, 0], io)
    for j in range(4):
        part[:, 256 * j : 256 * j + 256] = tn(dt1q[...], xs[j])
    flat[at:] = jnp.concatenate(lane_blocks(part[mine, :]), axis=0)
    half = keep.shape[0]
    bit = me[3] & 1
    keep[...] = flat[pl.ds(pl.multiple_of(bit * half, 8), half)].astype(BF16)
    send[...] = flat[pl.ds(pl.multiple_of((1 - bit) * half, 8), half)].astype(BF16)


def k_out_first(io, me, wide, short, a, b, dwide, dshort, dstride):
    bit = me[3] & 1
    for n in range(4):
        io.arrive(n)
        if n < 2:
            dwide[n] = wide[n].astype(F32)
        dshort[n] = short[n].astype(F32)
        io.leave(n)
    io.ready()
    dstride[bit] = a[0].astype(F32)
    dstride[1 - bit] = b[0].astype(F32)
    io.send(dstride)


def k_small_outputs(me, t1, t2, t3, t4, t5, t6, late, gm3, sm3, go3, so3, gm4, sm4, go4, so4):
    lanes, _ = own_block(me)
    half = me[0] & 1
    for n, t in enumerate((t1, t2)):
        block = t[:, lanes]
        mine = jnp.where(half == 0, block[:, 0:64], block[:, 64:128])
        gm3[n : n + 1] = mine[1:2]
        sm3[n : n + 1] = mine[0:1]
    wide = pl.ds(pl.multiple_of(me[0] * 256, 256), 256)
    go3[...] = t3[1:2, wide]
    so3[...] = t3[0:1, wide]
    mid = pl.ds(pl.multiple_of(me[0] * 128, 128), 128)
    for n, t in enumerate((t4, t5)):
        gm4[n : n + 1] = t[1:2, mid]
        sm4[n : n + 1] = t[0:1, mid]
    go4[...] = t6[1:3]
    so4[0:1] = t6[0:1]
    so4[1:2] = t6[0:1]


def k_sum_split(shift, size, n_in, me, *refs):
    total = refs[n_in]
    acc = refs[0][...].astype(F32)
    for r in refs[1:n_in]:
        acc = acc + r[...].astype(F32)
    total[...] = acc
    where = (me[3] >> shift) & (size - 1)
    for m, out in enumerate(refs[n_in + 1 :]):
        out[...] = total[where ^ m].astype(BF16)


def k_sum(n_in, *refs):
    acc = refs[0][...].astype(F32)
    for r in refs[1:n_in]:
        acc = acc + r[...].astype(F32)
    refs[n_in][...] = acc.astype(BF16)


def k_join(shift, size, me, *refs):
    where = (me[3] >> shift) & (size - 1)
    for m in range(size):
        refs[size][where ^ m] = refs[m][...]


def k_unpack(plan, me, a, b, *refs):
    full = refs[-1]
    bit = me[3] & 1
    full[bit] = a[...].reshape(full.shape[1:]).astype(F32)
    full[1 - bit] = b[...].reshape(full.shape[1:]).astype(F32)
    flat = full[...].reshape(2 * full.shape[1], 128)
    at = 0
    for out, (lead, rows, cols) in zip(refs, plan):
        for t in range(lead):
            for block in range(cols // 128):
                v = flat[at : at + rows]
                lanes = slice(128 * block, 128 * block + 128)
                if lead > 1:
                    out[t, :, lanes] = v
                else:
                    out[:, lanes] = v
                at += rows


def k_out_last(me, a, b, dev, coef, dmix, dreduce, full):
    bit = me[3] & 1
    full[bit] = a[...].reshape(full.shape[1:]).astype(F32)
    full[1 - bit] = b[...].reshape(full.shape[1:]).astype(F32)
    flat = full[...].reshape(2 * full.shape[1], 128)
    at = 0
    for t in range(9):
        for block in range(2):
            dmix[t, :, 128 * block : 128 * block + 128] = flat[at : at + 64]
            at += 64
    fix = dev[64:65].astype(F32) * coef[1] + dev[0:64].astype(F32) * coef[2]
    for block in range(8):
        lanes = slice(128 * block, 128 * block + 128)
        dreduce[:, lanes] = flat[at : at + 64] * coef[0] - fix[:, lanes]
        at += 64


def per_device(
    ni,
    nc,
    x_big,
    x_small,
    cot_big,
    cot_small,
    counts,
    w_reduce,
    w_mix,
    w_expand,
    w_narrow,
    w_stride,
    w_widen,
    w_short,
    gain_mid3,
    shift_mid3,
    gain_out3,
    shift_out3,
    gain_mid4,
    shift_mid4,
    gain_out4,
    shift_out4,
):
    assert nc == 4 and ni >= 8 and x_big.shape[0] == VIEWS and x_small.shape[0] == VIEWS
    geo = Geo(x_big.shape[1], x_small.shape[1])
    img = lax.axis_index("img")
    q = lax.axis_index("ch").astype(jnp.int32)
    levels = ni.bit_length() - 1
    me, nf3, cnt3, nf4, cnt4 = call(
        "counts",
        functools.partial(k_counts, ni, ((geo.pb, geo.ps), (geo.qb, geo.qs))),
        [(counts, SMEM)],
        [(sds((4,), jnp.int32), SMEM)]
        + [(sds((n,)), SMEM) for n in (3, 8 * (levels - 2)) * 2],
        slack=1,
    )

    smem = [(me, SMEM)]

    def over_img(v, k):
        return lax.ppermute(v, "img", [(i, i ^ (1 << k)) for i in range(ni)])

    def over_ch(v, k):
        return lax.ppermute(v, "ch", [(i, i ^ k) for i in range(nc)])

    rounds, at = [], 0
    while at < levels:
        rounds.append((at, min(2, levels - at) if at == 0 else 1))
        at += rounds[-1][1]

    def peers(v, shift, bits):
        out = []
        for m in range(1, 1 << bits):
            out.append(lax.ppermute(v, "img", [(i, i ^ (m << shift)) for i in range(ni)]))
        return out

    def sync(v, combine, wait=(), free=()):
        wait, free = dict(wait), dict(free)
        freed = []
        for k, (shift, bits) in enumerate(rounds):
            if k in wait:
                v = lax.optimization_barrier((v,) + tuple(wait[k]))[0]
            others = peers(v, shift, bits)
            if k in free:
                held = lax.optimization_barrier(tuple(others) + tuple(free[k]))
                others = list(held[: len(others)])
                freed += held[len(others) :]
            if k == len(rounds) - 1:
                return (v, others[0]) + ((freed,) if free else ())
            v = combine(k, [v] + others)

    last = len(rounds) - 1

    def sync_stats(stats, cnt, wait=(), free=()):
        def combine(k, arrays):
            (v,) = call(
                "merge",
                functools.partial(k_merge, 8 * k, len(arrays)),
                [(cnt, SMEM)] + vm(*arrays),
                [sds(stats.shape)],
                slack=1,
            )
            return v

        return sync(stats, combine, wait, free)

    def sync_sums(sums, wait=(), free=()):
        def combine(k, arrays):
            (v,) = call("add", functools.partial(k_add, len(arrays)), vm(*arrays), [sds(sums.shape)], slack=1)
            return v

        return sync(sums, combine, wait, free)

    pairs = [(at, 1) for at in range(levels)]
    fours = [(0, 1)]
    while fours[-1][0] + fours[-1][1] < levels:
        done = fours[-1][0] + fours[-1][1]
        fours.append((done, min(2, levels - done)))

    def to_peers(parts, group):
        shift, bits = group
        out = []
        for m in range(1, 1 << bits):
            perm = [(i, i ^ (m << shift)) for i in range(ni)]
            out.append(lax.ppermute(parts[m if len(parts) > 1 else 0], "img", perm))
        return out

    def sum_split(name, arrays, group):
        shift, bits = group
        size = 1 << bits
        shape = arrays[0].shape
        view = (size, shape[0] // size) + shape[1:]
        return call(
            name,
            functools.partial(k_sum_split, shift, size, len(arrays)),
            smem + vm(*[a.reshape(view) for a in arrays]),
            [sds(view[1:], BF16)] * size,
            [pltpu.VMEM(view, F32)],
            order=True,
        )

    def join(name, parts, group):
        shift, bits = group
        size = 1 << bits
        (full,) = call(
            name,
            functools.partial(k_join, shift, size),
            smem + vm(*parts),
            [sds((size,) + parts[0].shape, BF16)],
        )
        return full.reshape((-1,) + parts[0].shape[1:])

    class Train:
        def __init__(self, name, groups, parts):
            self.name, self.groups, self.parts, self.at, self.summing = name, groups, parts, 0, True

        def sends(self):
            return self.parts[1:] if self.summing else self.parts

        def launch(self, sends):
            parts = self.parts[:1] + list(sends) if self.summing else list(sends)
            self.received = to_peers(parts, self.groups[self.at])

        def advance(self):
            name = "%s_%d" % (self.name, self.at)
            arrays = self.parts[:1] + self.received
            if self.summing and self.at + 1 < len(self.groups):
                self.at += 1
                self.parts = sum_split(name, arrays, self.groups[self.at])
            elif self.summing:
                self.summing = False
                self.parts = call(
                    name + "s",
                    functools.partial(k_sum, len(arrays)),
                    vm(*arrays),
                    [sds(arrays[0].shape, BF16)],
                    slack=2,
                )
            else:
                self.parts = [join(name + "j", arrays, self.groups[self.at])]
                self.at -= 1

        def to_last(self):
            while self.summing or self.at > 0:
                self.advance()
                self.launch(self.sends())

        def finish(self):
            self.to_last()
            return self.parts[0], self.received[0]

    def quarters(v):
        p1 = over_ch(v, 1)
        p2 = over_ch(v, 2)
        return [v, p1, p2, over_ch(p2, 1)]

    def after(marker, *arrays):
        return list(lax.optimization_barrier((marker,) + arrays))

    def sent(v):
        return [v, over_ch(v, 1), over_ch(v, 2)]

    def passed_on(g):
        return g + [over_ch(g[2], 1)]

    def rows_of(v):
        return jnp.transpose(v, (1, 2, 0, 3)).reshape(-1, v.shape[3])

    m3, c3 = 4 * w_reduce.shape[1], w_reduce.shape[0]
    m4, c4q = w_widen.shape
    first = [rows_of(x_small)]
    first.append(jnp.transpose(w_mix, (0, 1, 3, 2)).reshape(-1, m3))
    first += [w_reduce.T[:, j * m3 : (j + 1) * m3] for j in range(c3 // m3)]
    mix_at, reduce_at = first[0].shape[0], first[0].shape[0] + first[1].shape[0]
    held = (gain_mid3, shift_mid3, gain_out3[None], shift_out3[None], gain_mid4, shift_mid4, gain_out4, shift_out4)
    first += call(
        "pack_params",
        k_pack_params,
        vm(*held),
        [sds((64, 256), BF16)],
        [pltpu.VMEM((32, 128), F32)],
        slack=2,
    )
    params_at = sum(v.shape[0] for v in first[:-1])
    xb = quarters(rows_of(x_big))
    xb[1], me, *first = lax.optimization_barrier((xb[1], me, *first))
    smem = [(me, SMEM)]
    xsm = sent(jnp.concatenate(first))
    def blocks128(v):
        return [v[:, 128 * b : 128 * b + 128] for b in range(v.shape[1] // 128)]

    w_mid = jnp.concatenate(blocks128(w_expand) + blocks128(w_narrow))
    last_in = jnp.concatenate([w_short, w_widen, rows_of(cot_big), rows_of(cot_small)])
    wst = w_stride.reshape(-1, w_stride.shape[3])
    xb[3], xsm[2], w_mid, last_in, wst = after(xb[3], xsm[2], w_mid, last_in, wst)
    xsm = passed_on(xsm)
    gs1, gs2, gs3, gs4, gs5, gs6 = call(
        "unpack_params",
        functools.partial(k_unpack_params, params_at),
        smem + [(in_hbm(v), HBM) for v in xsm],
        [sds((2, n)) for n in (m3, m3, c3, m4, m4)] + [sds((2, 4, c4q))],
        [pltpu.VMEM((4, 64, 256), BF16), pltpu.SemaphoreType.DMA((4,))],
        slack=2,
    )

    chip_pairs = [[0, 2], [1, 3]]
    wst = lax.all_gather(wst, "ch", axis_index_groups=chip_pairs)
    last_in = lax.all_gather(last_in, "ch", axis_index_groups=chip_pairs)

    n3, n4 = [(nf3, SMEM)], [(nf4, SMEM)]

    def k(fn):
        return functools.partial(fn, geo)

    hb, hs = geo.hb, geo.hs
    sb4, ss4 = (2, 2, hb // 2, hb // 2, VIEWS, m4), (2, 2, hs // 2, hs // 2, VIEWS, m4)
    wb_shape, ws_shape = ((hb + 2) * hb * VIEWS, 3 * m3), ((hs + 2) * hs * VIEWS, 3 * m3)

    def flow(kind, *arrays):
        return [(a, Flow(kind)) for a in arrays]

    def out(kind, shape, dtype=F32):
        return (sds(shape, dtype), Flow(kind))

    x_all = [(xb + xsm, Flow("x"))]
    w_in, w_ahead, w_back = [
        [(xsm, Flow(kind, base))]
        for kind, base in (("w_in", reduce_at), ("w_ahead", mix_at), ("w_back", mix_at))
    ]
    run = functools.partial(call, geo=geo)
    px1, px3, px4 = (geo.px, VIEWS, m3), (geo.px, VIEWS, c3), (geo.px4, VIEWS, m4)

    pre1, st = run(
        "reduce",
        k(k_reduce),
        smem + n3 + x_all + w_in,
        [fast(px1), sds((2, m3))],
    )
    st, w_mid = after(st, w_mid)
    w_mid = sent(w_mid)
    a1, b1 = sync_stats(st, cnt3)
    pre2, winb, wins, st, devq, keep1 = run(
        "mix",
        k(k_mix),
        smem + n3 + vm(pre1, a1, b1, gs1) + w_ahead,
        [
            fast(px1),
            out("all", wb_shape, BF16),
            out("all", ws_shape, BF16),
            sds((2, m3)),
            out("all", (geo.rows, 128), BF16),
            (sds(px1), Keep(2)),
        ],
        [pltpu.VMEM((1, m3), F32)],
    )
    st, w_mid[2] = after(st, w_mid[2])
    w_mid = passed_on(w_mid)
    w_expand_all = [(w_mid, Flow("w", 0, (m3, c3)))]
    w_narrow_all = [(w_mid, Flow("w", m3 * (c3 // 4 // 128), (c3, m4)))]
    a2, b2 = sync_stats(st, cnt3)
    pre3, act2, st, keep2 = run(
        "expand",
        k(k_expand),
        smem + n3 + vm(pre2, a2, b2, gs2) + w_expand_all,
        [
            fast(px3),
            out("rows", (geo.rows, m3), BF16),
            sds((2, c3)),
            (sds(px1), Keep(2)),
        ],
    )
    a3, b3 = sync_stats(st, cnt3)
    pre4b, pre4s, mid, mids, st, dev3, slope3 = run(
        "narrow",
        k(k_narrow),
        smem + n3 + vm(pre3) + x_all + vm(a3, b3, gs3) + w_narrow_all,
        [
            out("big", sb4),
            out("small", ss4),
            out("rows", (geo.rows, c3), BF16),
            fast((geo.rows4, c3), BF16),
            sds((2, m4)),
            out("rows", (geo.rows, c3), BF16),
            out("rows", (geo.rows, c3), BF16),
        ],
        [pltpu.VMEM((geo.px4, VIEWS, c3), F32)],
        slack=6,
        staying=4 * math.prod(px3),
    )
    st, wst = after(st, wst)
    wst = [wst, over_ch(wst, 1)]
    a4, b4 = sync_stats(st, cnt3)
    w_stride_all = [(wst, Flow("w4", 0, (9 * m4, m4)))]
    pre5, cols, st = run(
        "stride",
        k(k_stride),
        smem
        + n4
        + n3
        + flow("big", pre4b)
        + flow("small", pre4s)
        + vm(a4, b4, gs4)
        + w_stride_all,
        [
            sds(px4),
            out("lead", (9, geo.rows4, m4), BF16),
            sds((2, m4)),
        ],
        [pltpu.VMEM(sb4, F32), pltpu.VMEM(ss4, F32)],
    )
    (dev,) = run(
        "dev_products",
        k(k_dev_products),
        smem + flow("all", devq) + x_all,
        [sds((m3 // 4 + 8, c3), BF16)],
        [pltpu.VMEM((128, c3 // 4), F32)],
        ahead=8,
    )
    a5, b5, (dev,) = sync_stats(st, cnt4, free={last: [dev]})
    a5, last_in, mids = after(a5, last_in, mids)
    at_w, at_b, at_s = c3, c3 + m4, c3 + m4 + geo.qb * VIEWS

    def from_chips(base, rows):
        return [(last_in, Flow("chip", base, (rows, c4q), j)) for j in range(2)]

    wsh, wwi = from_chips(0, c3), from_chips(at_w, m4)
    cots = from_chips(at_b, geo.qb * VIEWS) + from_chips(at_s, geo.qs * VIEWS)
    side, st_side = run(
        "short",
        k(k_short),
        smem + n4 + vm(mids) + wsh,
        [fast((2, geo.px4, VIEWS, c4q)), sds((2, 2, c4q))],
    )
    pre6, act5, st = run(
        "widen",
        k(k_widen),
        smem + n4 + vm(pre5, a5, b5, gs5) + wwi + vm(st_side),
        [
            fast((2, geo.px4, VIEWS, c4q)),
            sds((geo.rows4, m4), BF16),
            sds((2, 4, c4q)),
        ],
    )
    a6, b6 = sync_stats(st, cnt4)
    out_b, out_s, dt6, sums = run(
        "total",
        k(k_total),
        smem + n4 + vm(pre6, side, a6, b6, gs6) + cots,
        [
            out("all", (geo.qb, VIEWS, c4q)),
            out("all", (geo.qs, VIEWS, c4q)),
            fast((2, geo.px4, VIEWS, c4q)),
            sds((2, 3, c4q)),
        ],
        [pltpu.VMEM((geo.px4, VIEWS, c4q), F32)],
    )
    ga6, gb6 = sync_sums(sums)
    part5, dz6, dzs, t6 = run(
        "back_wide",
        k(k_back_wide),
        smem
        + n4
        + vm(dt6, pre6, side, a6, b6, gs6, ga6, gb6)
        + wwi,
        [
            sds(px4),
            sds((geo.rows4, c4q), BF16),
            sds((2, geo.rows4, c4q), BF16),
            sds((2, 3, c4q)),
        ],
    )
    other5 = over_ch(part5, 1)
    dt5, sums = call(
        "back_act5",
        k_back_act5,
        n4 + vm(part5, other5, pre5, a5, b5, gs5),
        [sds(px4), sds((2, m4))],
    )
    (dms,) = run(
        "back_short", k_back_short, smem + vm(dzs) + wsh, [sds((geo.px4, VIEWS, c3), BF16)]
    )
    dmo = over_ch(dms, 1)
    dwide, dshort = call(
        "dw_wide",
        k_dw_wide,
        vm(act5, dz6, mids, dzs),
        [sds((m4, c4q), BF16), sds((c3, c4q), BF16)],
    )
    ga5, gb5, (dwide, dshort) = sync_sums(sums, free={0: [dwide, dshort]})
    dt4b, dt4s, dz5, sums, t5 = run(
        "back_stride",
        k(k_back_stride),
        smem
        + n4
        + vm(dt5, pre5, a5, b5, gs5, ga5, gb5)
        + flow("all", pre4b, pre4s)
        + vm(a4, b4, gs4)
        + n3
        + w_stride_all,
        [fast(sb4), fast(ss4), sds((geo.rows4, m4), BF16), sds((2, m4)), sds((2, m4))],
        [pltpu.VMEM((4, geo.rows4, m4), BF16)],
    )

    def halves(rows):
        return [sds((rows // 2, 128), BF16)] * 2, pltpu.VMEM((2, rows // 2, 128), F32)

    outs, full = halves(9 * m4)
    parts = run("dw_stride", k_dw_stride, smem + flow("lead", cols) + vm(dz5), outs, [full])
    stride_train = Train("stride", pairs, parts)
    ga4, gb4, sends = sync_sums(sums, free={last: stride_train.sends()})
    stride_train.launch(sends)
    dt3, dz4, sums, t4 = run(
        "back_narrow",
        k(k_back_narrow),
        smem
        + n3
        + vm(dt4b, dt4s)
        + flow("big", pre4b)
        + flow("small", pre4s)
        + vm(a4, b4, gs4, ga4, gb4)
        + flow("rows", dev3, slope3)
        + vm(a3, b3, dms, dmo)
        + w_narrow_all,
        [
            fast((geo.rows, c3), BF16),
            out("rows", (geo.rows, m4), BF16),
            sds((2, c3)),
            sds((2, m4)),
        ],
    )
    came = stride_train.received
    stride_train.advance()
    ga3, gb3, sends = sync_sums(sums, wait={last: came}, free={last: stride_train.sends()})
    stride_train.launch(sends)
    dt2, dz3, dt3q, sums, t3 = run(
        "back_expand",
        k(k_back_expand),
        smem
        + n3
        + vm(dt3)
        + flow("rows", dev3)
        + vm(a3, b3, gs3, ga3, gb3)
        + flow("px", keep2)
        + vm(a2, b2, gs2)
        + w_expand_all,
        [
            fast(px1),
            out("rows", (geo.rows, c3 // 4), BF16),
            out("rows", (geo.rows, c3 // 4), BF16),
            sds((2, m3)),
            sds((2, c3)),
        ],
        [
            pltpu.VMEM((2 * hb * VIEWS, c3), BF16),
            pltpu.VMEM((2 * hs * VIEWS, c3), BF16),
        ],
    )
    came = stride_train.received
    stride_train.advance()
    outs, full = halves(c3 + (c3 // 4 // 128) * m3)
    parts = call("dw_mid", k_dw_mid, smem + vm(mid, dz4, act2, dz3), outs, [full])
    mid_train = Train("mid", pairs, parts)
    ga2, gb2, (mid_send, *sends) = sync_sums(
        sums, wait={last: came}, free={0: mid_train.sends(), last: stride_train.sends()}
    )
    mid_train.launch([mid_send])
    stride_train.launch(sends)
    dt1, dz2, sums, t2, dt1q = run(
        "back_mix",
        k(k_back_mix),
        smem
        + n3
        + vm(dt2)
        + flow("px", keep2)
        + vm(a2, b2, gs2, ga2, gb2)
        + flow("px", keep1)
        + vm(a1, b1, gs1)
        + w_back,
        [
            out("px", px1),
            out("all", (geo.rows, m3), BF16),
            sds((2, m3)),
            sds((2, m3)),
            out("rows", (geo.rows, 128), BF16),
        ],
        [pltpu.VMEM(wb_shape, BF16), pltpu.VMEM(ws_shape, BF16)],
    )
    came = stride_train.received + mid_train.received
    stride_train.advance()
    mid_train.advance()
    mix_rows = 9 * m3 // 128 * (m3 // 4)
    rows_last = mix_rows + c3 // 128 * (m3 // 4)
    outs, _ = halves(rows_last)
    parts = run(
        "dw_last",
        k(k_dw_last),
        smem + flow("all", winb, wins, dz2) + x_all + flow("all", dt1q),
        outs,
        [
            pltpu.VMEM((128, 3 * m3), F32),
            pltpu.VMEM((128, c3), F32),
            pltpu.VMEM((rows_last, 128), F32),
        ],
        ahead=8,
        hold=True,
    )
    last_train = Train("last", fours, parts)
    dwide, dshort, dev = lax.psum((dwide, dshort, dev), "img")
    wide = [dwide, dshort, dev]
    ga1, gb1, (last_send, mid_send, *sends) = sync_sums(
        sums,
        wait={last: came},
        free={last: last_train.sends() + mid_train.sends() + stride_train.sends()},
    )
    last_train.launch([last_send])
    mid_train.launch([mid_send])
    stride_train.launch(sends)
    dwide, dshort, dev = wide
    gxb, gxs, t1, coef = run(
        "back_reduce",
        k(k_back_reduce),
        smem
        + n3
        + flow("px", dt1, keep1)
        + vm(a1, b1, gs1, ga1, gb1)
        + flow("rows", dt3q)
        + w_in,
        [
            out("big_px", (geo.pb, VIEWS, c3 // 4)),
            out("small_px", (geo.ps, VIEWS, c3 // 4)),
            sds((2, m3)),
            sds((3, m3)),
        ],
    )
    def unpack(name, a, b, plan):
        shapes = [((lead,) if lead > 1 else ()) + (rows, cols) for lead, rows, cols in plan]
        return call(
            name,
            functools.partial(k_unpack, plan),
            smem + vm(a, b),
            [sds(shape) for shape in shapes],
            [pltpu.VMEM((2,) + a.shape, F32)],
        )

    trains = (last_train, mid_train, stride_train)
    gxb, dwide, dshort, dev, coef, *came = after(
        gxb, dwide, dshort, dev, coef, *[train.received[0] for train in trains]
    )
    for train, first in zip(trains, came):
        train.received[0] = first
    halves_in = [v.reshape(1, 9 * m4 // 2, 128) for v in stride_train.finish()]
    dwide, dshort, dstride = run(
        "out_first",
        k_out_first,
        smem
        + flow("lead", dwide.reshape(2, m4 // 2, c4q), dshort.reshape(4, c3 // 4, c4q))
        + flow("all", *halves_in),
        [
            out("lead", (2, m4 // 2, c4q)),
            out("lead", (4, c3 // 4, c4q)),
            out("all", (2, 9 * m4 // 2, 128)),
        ],
        ahead=4,
    )
    mid_train.to_last()
    last_train.to_last()
    dstride, mid_train.received[0], last_train.received[0] = after(
        dstride, mid_train.received[0], last_train.received[0]
    )
    dnarrow, dexpand = unpack(
        "out_mid", *mid_train.finish(), [(1, c3, m4 // 4), (1, m3, c3 // 4)]
    )
    coef = lax.dynamic_slice_in_dim(coef, q * (m3 // 4), m3 // 4, 1)[:, :, None]
    mine, other = last_train.finish()
    dmix, dreduce = call(
        "out_last",
        k_out_last,
        smem + vm(mine, other, dev, coef),
        [sds((9, m3 // 4, m3)), sds((m3 // 4, c3))],
        [pltpu.VMEM((2,) + mine.shape, F32)],
    )

    def views_first(v, side):
        return jnp.transpose(v.reshape(side, side, VIEWS, v.shape[2]), (2, 0, 1, 3))

    small = call(
        "small_outputs",
        k_small_outputs,
        smem + vm(t1, t2, t3, t4, t5, t6[0], gxs[0]),
        [sds((2, m3 // 4))] * 2
        + [sds((1, c3 // 4))] * 2
        + [sds((2, m4 // 4))] * 2
        + [sds((2, c4q))] * 2,
        slack=4,
    )
    small[2], small[3] = small[2][0], small[3][0]
    return (
        views_first(out_b, hb // 2),
        views_first(out_s, hs // 2),
        views_first(gxb, hb),
        views_first(gxs, hs),
        dreduce.T,
        jnp.transpose(dmix.reshape(3, 3, m3 // 4, m3), (0, 1, 3, 2)),
        dexpand,
        dnarrow,
        dstride.reshape(3, 3, m4, m4 // 4),
        dwide.reshape(m4, c4q),
        dshort.reshape(c3, c4q),
        *small,
    )


def solution(mesh):
    act = P("img", None, None, "ch")
    flat, taps, vec = P(None, "ch"), P(None, None, None, "ch"), P("ch")
    in_specs = (act,) * 4 + (P(), flat, taps, flat, flat, taps, flat, flat)
    in_specs += (flat, flat, vec, vec, flat, flat, flat, flat)
    out_specs = (act,) * 4 + (flat, taps, flat, flat, taps, flat, flat)
    out_specs += (flat, flat, vec, vec, flat, flat, flat, flat)
    return jax.shard_map(
        functools.partial(per_device, mesh.shape["img"], mesh.shape["ch"]),
        mesh=mesh,
        in_specs=in_specs,
        out_specs=out_specs,
        check_vma=False,
    )
```

```python
import functools
import math

import jax
import jax.numpy as jnp
from jax import lax
from jax.experimental import pallas as pl
from jax.experimental.pallas import tpu as pltpu
from jax.sharding import PartitionSpec as P

EPS = 1e-05
G0 = 0.7978845608028654
G1 = G0 * 0.044715
F32 = jnp.float32
BF16 = jnp.bfloat16
VIEWS = 8

ANY = pl.BlockSpec(memory_space=pl.ANY)
HBM = pl.BlockSpec(memory_space=pltpu.HBM)
VMEM = pl.BlockSpec(memory_space=pltpu.VMEM)
SMEM = pl.BlockSpec(memory_space=pltpu.SMEM)


def sds(shape, dtype=F32):
    return jax.ShapeDtypeStruct(tuple(shape), dtype)


class Flow:
    WHOLE = ("w", "w4", "all", "chip", "w_in", "w_ahead", "w_back")

    def __init__(self, kind, base=0, shape=None, which=0):
        self.kind, self.base, self.shape, self.which = kind, base, shape, which

    def keys(self, geo, shape):
        parts = (0, 1)
        if self.kind in ("big", "big_px"):
            parts = (0,)
        if self.kind in ("small", "small_px"):
            parts = (1,)
        if self.kind not in ("lead",) + self.WHOLE:
            return [(part, n) for part in parts for n in range(len(geo.groups[part]))]
        if self.kind == "lead":
            return list(range(shape[0]))
        return [None]

    def buffer(self, geo, shapes, dtype):
        if self.kind == "x":
            return pltpu.VMEM((4, geo.rows, shapes[0][1]), dtype)
        if self.kind == "w":
            return pltpu.VMEM(self.shape, dtype)
        if self.kind in ("chip", "w4"):
            return pltpu.VMEM(self.shape, dtype)
        c = shapes[0][-1]
        if self.kind.startswith("w_"):
            return pltpu.VMEM({"w_in": (4, c, c), "w_ahead": (3, c, 3 * c), "w_back": (9, c, c)}[self.kind], dtype)
        return pltpu.VMEM(tuple(shapes[0]), dtype)

    def pairs(self, geo, q, hbm, buf, key):
        if self.kind == "w":
            rows, n = buf.shape[0], buf.shape[1] // 4
            found = []
            for p in range(4):
                for b in range(n // 128):
                    at = pl.ds(pl.multiple_of((q ^ p) * n + 128 * b, 128), 128)
                    found.append((hbm[p].at[pl.ds(self.base + rows * b, rows)], buf.at[:, at]))
            return found
        if self.kind.startswith("w_"):
            c = buf.shape[1]
            n = c // 4
            found = []
            for p in range(4):
                at = pl.ds(pl.multiple_of((q ^ p) * n, n), n)
                for t in range(4 if self.kind == "w_in" else 9):
                    src = hbm[p].at[pl.ds(self.base + n * t, n)]
                    if self.kind == "w_ahead":
                        found.append((src, buf.at[t // 3, at, pl.ds(t % 3 * c, c)]))
                    else:
                        found.append((src, buf.at[t, at]))
            return found
        if self.kind == "chip":
            return [(hbm[0].at[(q >> 1) ^ self.which, pl.ds(self.base, buf.shape[0])], buf)]
        if self.kind == "w4":
            n = buf.shape[1] // 4
            found = []
            for chip in range(2):
                for other in range(2):
                    at = pl.multiple_of((2 * chip + ((q & 1) ^ other)) * n, n)
                    found.append((hbm[other].at[chip], buf.at[:, pl.ds(at, n)]))
            return found
        if key is None:
            return [(hbm[0], buf)]
        if self.kind == "lead":
            return [(hbm[0].at[key], buf.at[key])]
        part, group = key
        i, end = geo.groups[part][group]
        pix, npx, row, nrows = geo.step(part, i)
        npx, nrows, first = npx * (end - i), nrows * (end - i), pix - geo.parts[part][1]
        if self.kind == "px":
            at = pl.ds(pix, npx)
        elif self.kind == "rows":
            at = pl.ds(row, nrows)
        elif self.kind in ("big_px", "small_px"):
            at = pl.ds(first, npx)
        elif self.kind == "x":
            local = pl.ds(first * VIEWS, nrows)
            return [
                (hbm[4 * part + p].at[local], buf.at[q ^ p, pl.ds(row, nrows)]) for p in range(4)
            ]
        else:
            at = pl.ds(i, end - i)
            return [(hbm[0].at[:, :, at], buf.at[:, :, at])]
        return [(hbm[0].at[at], buf.at[at])]


class Moves:
    def __init__(self, geo, q, ahead):
        self.geo, self.q, self.flows, self.kept, self.ahead = geo, q, [], [], ahead

    def add(self, flow, hbm, buf, sem, inward):
        self.flows.append((flow, hbm, buf, sem, inward))

    def copies(self, entry, key):
        flow, hbm, buf, sem, inward = entry
        if flow.kind in flow.WHOLE:
            at = 0
        elif flow.kind == "lead":
            at = key
        elif flow.kind in ("px", "rows", "x"):
            at = (0, len(self.geo.groups[0]))[key[0]] + key[1]
        else:
            at = key[1]
        pairs = flow.pairs(self.geo, self.q, hbm, buf, key)
        return [
            pltpu.make_async_copy(*((a, b) if inward else (b, a)), sem.at[n, at])
            for n, (a, b) in enumerate(pairs)
        ]

    def entries(self, inward, key):
        for entry in self.flows:
            flow = entry[0]
            if entry[4] != inward:
                continue
            if key is None:
                fits = flow.kind in flow.WHOLE
            elif isinstance(key, int):
                fits = flow.kind == "lead" and key < entry[1][0].shape[0]
            else:
                kinds = ("px", "rows", "x") + (("big", "big_px"), ("small", "small_px"))[key[0]]
                fits = flow.kind in kinds
            if fits:
                yield entry

    def start(self, inward, key):
        for entry in self.entries(inward, key):
            for c in self.copies(entry, key):
                c.start()

    def wait(self, inward, key):
        for entry in self.entries(inward, key):
            for c in self.copies(entry, key):
                c.wait()

    def begin(self, hold):
        self.order = [(part, n) for part in range(2) for n in range(len(self.geo.groups[part]))]
        if hold:
            self.start(True, None)
            return
        self.start(True, self.order[0])
        self.start(True, None)
        for key in self.order[1 : self.ahead]:
            self.start(True, key)
        for n in range(self.ahead):
            self.start_lead(n)
        streams = any(e[4] and e[0].kind not in ("lead",) + Flow.WHOLE for e in self.flows)
        if not streams:
            for c in self.kept:
                c.start()

    def start_steps(self):
        for key in self.order:
            self.start(True, key)

    def start_lead(self, n):
        for entry in self.flows:
            if entry[4] and entry[0].kind == "lead" and n < entry[1][0].shape[0]:
                for c in self.copies(entry, n):
                    c.start()

    def ready(self):
        self.wait(True, None)

    def arrive(self, *key):
        if len(key) == 1:
            self.wait(True, key[0])
            self.start_lead(key[0] + self.ahead)
            return
        self.wait(True, key)
        at = self.order.index(key)
        if at + self.ahead < len(self.order):
            self.start(True, self.order[at + self.ahead])
        streams = any(e[4] and e[0].kind not in ("lead",) + Flow.WHOLE for e in self.flows)
        if at == 0 and streams:
            for c in self.kept:
                c.start()

    def leave(self, *key):
        self.start(False, key if len(key) > 1 else key[0])

    def send(self, *refs):
        for entry in self.entries(False, None):
            if any(entry[2] is r for r in refs):
                for c in self.copies(entry, None):
                    c.start()

    def finish(self):
        for entry in self.flows:
            if not entry[4]:
                shape = entry[1][0].shape
                for key in entry[0].keys(self.geo, shape):
                    for c in self.copies(entry, key):
                        c.wait()
        for c in self.kept:
            c.wait()


class Keep:
    kind = "keep"

    def __init__(self, source):
        self.source = source


def fast(shape, dtype=F32):
    return pltpu.VMEM(tuple(shape), dtype)


def scoped_bytes(v):
    return math.prod(v.shape) * jnp.dtype(v.dtype).itemsize


def in_hbm(v):
    return pltpu.with_memory_space_constraint(v, pltpu.HBM)


def call(name, kernel, ins, outs, scratch=(), cost=None, order=False, geo=None, slack=14, ahead=3, hold=False, staying=0):
    if order:
        inner, n_in, n_out = kernel, len(ins), len(outs)

        def kernel(*refs):
            rest = refs[n_in:]
            return inner(*refs[:n_in], *rest[n_out:], *rest[:n_out])

    outs = [o if isinstance(o, tuple) else (o, VMEM) for o in outs]
    arrays, specs, moved = [], [], []
    for a, spec in ins:
        group = a if isinstance(a, list) else [a]
        flow = isinstance(spec, Flow)
        arrays += [in_hbm(v) for v in group] if flow else group
        specs += [HBM if flow else spec] * len(group)
        moved.append((spec if flow else None, len(group), [v.shape for v in group], group[0].dtype))
    out_shapes, out_specs = [], []
    for shape, spec in outs:
        flow = isinstance(spec, (Flow, Keep))
        out_shapes.append(pltpu.HBM(shape.shape, shape.dtype) if flow else shape)
        out_specs.append(HBM if flow else spec)
        moved.append((spec if flow else None, 1, [shape.shape], shape.dtype))
    extra = []
    for flow, _, shapes, dtype in moved:
        if isinstance(flow, Keep):
            extra += [pltpu.SemaphoreType.DMA((1,))]
        elif flow:
            keys = len(flow.keys(geo, shapes[0]))
            copies = {"x": 4, "w": 4, "w4": 4, "w_in": 16, "w_ahead": 36, "w_back": 36}.get(flow.kind, 1)
            if flow.kind == "w":
                copies = flow.shape[1] // 128
            extra += [flow.buffer(geo, shapes, dtype), pltpu.SemaphoreType.DMA((copies, keys))]
    body = kernel
    if extra:

        def body(*refs):
            n_io = sum(n for _, n, _, _ in moved)
            given, own, rest = list(refs[:n_io]), refs[n_io : n_io + len(scratch)], refs[n_io + len(scratch) :]
            rest = list(rest)
            moves = Moves(geo, given[0][0], ahead)
            args = []
            for n, (flow, count, _, _) in enumerate(moved):
                group, given = given[:count], given[count:]
                if not flow:
                    args += group
                    continue
                if isinstance(flow, Keep):
                    moves.kept.append(pltpu.make_async_copy(args[flow.source], group[0], rest[0].at[0]))
                    rest = rest[1:]
                    continue
                buf, sem = rest[:2]
                rest = rest[2:]
                moves.add(flow, group, buf, sem, n < len(ins))
                args.append(buf)
            moves.begin(hold)
            kernel(moves, *args, *own)
            moves.finish()

    scratch = list(scratch)
    def held(v):
        pinned = "vmem" in str(getattr(v, "memory_space", "")).lower()
        return 0 if pinned else scoped_bytes(v)

    need = sum(held(jax.typeof(a)) for a, spec in zip(arrays, specs) if spec is VMEM)
    need += sum(held(o) for o, spec in zip(out_shapes, out_specs) if spec is VMEM)
    need += sum(
        scoped_bytes(v)
        for v in scratch + extra
        if getattr(v, "memory_space", None) == pltpu.VMEM
    )
    need -= staying
    result = pl.pallas_call(
        body,
        out_shape=out_shapes,
        in_specs=specs,
        out_specs=out_specs,
        scratch_shapes=scratch + extra,
        compiler_params=pltpu.CompilerParams(vmem_limit_bytes=need + need // 16 + (slack << 20)),
        cost_estimate=cost,
        name=name,
    )(*arrays)
    return list(result)


def vm(*arrays):
    return [(a, VMEM) for a in arrays]


def nn(a, b):
    return lax.dot_general(a, b, (((1,), (0,)), ((), ())), preferred_element_type=F32)


def nt(a, b):
    return lax.dot_general(a, b, (((1,), (1,)), ((), ())), preferred_element_type=F32)


def tn(a, b):
    return lax.dot_general(a, b, (((0,), (0,)), ((), ())), preferred_element_type=F32)


def gelu(t):
    half = 0.5 * t
    return half + half * jnp.tanh(t * (G0 + G1 * (t * t)))


def gelu_both(t):
    sq = t * t
    half = 0.5 * t
    th = jnp.tanh(t * (G0 + G1 * sq))
    return half + half * th, 0.5 + 0.5 * th + half * (1.0 - th * th) * (G0 + (3.0 * G1) * sq)


def gelu_slope(t):
    sq = t * t
    th = jnp.tanh(t * (G0 + G1 * sq))
    return 0.5 * (1.0 + th) + (0.5 * t) * (1.0 - th * th) * (G0 + (3.0 * G1) * sq)


def live_rows(count, chans):
    return (lax.broadcasted_iota(jnp.int32, (VIEWS, chans), 0) < count).astype(F32)


def rows_sum(v):
    return jnp.sum(v, axis=0, keepdims=True)


def merged(sa, sb, na, nb):
    total = na + nb
    mean = (na * sa[0:1] + nb * sb[0:1]) / total
    diff = sb[0:1] - sa[0:1]
    square = sa[1:2] + sb[1:2] + diff * diff * (na * nb / total)
    return mean, lax.rsqrt(square / total + EPS)


def as_rows(v):
    return v.reshape(v.shape[0] * v.shape[1], v.shape[2])


def as_pix_rows(v):
    return v.reshape(v.shape[0] * v.shape[1], VIEWS, v.shape[3])


def as_pix(v):
    return v.reshape(v.shape[0] // VIEWS, VIEWS, v.shape[1])


class Geo:
    def __init__(self, hb, hs):
        self.hb, self.hs = hb, hs
        self.pb, self.ps = hb * hb, hs * hs
        self.px = self.pb + self.ps
        self.rows = self.px * VIEWS
        self.qb, self.qs = self.pb // 4, self.ps // 4
        self.px4 = self.qb + self.qs
        self.rows4 = self.px4 * VIEWS
        self.parts = ((hb, 0), (hs, self.pb))
        self.groups = [self.cuts(hb // 2, 1), self.cuts(hs // 2, 2)]
        self.spans = [[list(range(n))[: n // 2], list(range(n))[n // 2 :]] for n in map(len, self.groups)]
        self.bands = [[(0, hb // 2), (hb // 2, hb)], [(0, hs)]]

    @staticmethod
    def cuts(steps, first):
        at = sorted({0, steps} | set(range(first, steps, 2)))
        return list(zip(at[:-1], at[1:]))

    @staticmethod
    def aligned(n):
        return n if isinstance(n, int) else pl.multiple_of(n, 16)

    def step(self, part, i):
        side, start = self.parts[part]
        npx = 2 * side
        return start + i * npx, npx, self.aligned((start + i * npx) * VIEWS), npx * VIEWS

    def staged(self, io, before, product, carries):
        out = []
        for part in range(2):
            carry = carries[part]
            for span in self.spans[part]:
                lo, hi = self.groups[part][span[0]][0], self.groups[part][span[-1]][1]
                for n in span:
                    io.arrive(part, n)
                pix, npx, row, nrows = self.step(part, lo)
                if before:

                    def early(i, c, part=part):
                        before(part, i, *self.step(part, i))
                        return c

                    lax.fori_loop(lo, hi, early, 0)
                carry = product(part, pix, npx * (hi - lo), row, nrows * (hi - lo), carry)
                for n in span:
                    io.leave(part, n)
            out.append(carry)
        return out

    def loop(self, body, carries, arrive=None, leave=None):
        out = []
        for part in range(2):

            def run(i, carry, part=part):
                for n, (lo, hi) in enumerate(self.groups[part]):
                    if arrive:
                        pl.when(i == lo)(functools.partial(arrive.arrive, part, n))
                carry = body(part, i, *self.step(part, i), carry)
                for n, (lo, hi) in enumerate(self.groups[part]):
                    if leave:
                        pl.when(i == hi - 1)(functools.partial(leave.leave, part, n))
                return carry

            out.append(lax.fori_loop(0, self.groups[part][-1][1], run, carries[part]))
        return out


def finish_stats(geo, ref, sums, lives, count, out, quarter=None):
    mean = (rows_sum(sums[0] * lives[0]) + rows_sum(sums[1] * lives[1])) / count

    def body(part, i, pix, npx, row, nrows, carry):
        dev = ref[pl.ds(pix, npx)] - mean
        return carry + jnp.sum(dev * dev, axis=0)

    zero = jnp.zeros(sums[0].shape, F32)
    sq = geo.loop(body, [zero, zero])
    out[0:1] = mean
    out[1:2] = rows_sum(sq[0] * lives[0]) + rows_sum(sq[1] * lives[1])


def block_stats(geo, value, lives, count):
    big, small = value[: geo.qb], value[geo.qb :]
    mean = (
        rows_sum(jnp.sum(big, axis=0) * lives[0]) + rows_sum(jnp.sum(small, axis=0) * lives[1])
    ) / count
    db, ds = big - mean, small - mean
    square = rows_sum(jnp.sum(db * db, axis=0) * lives[0]) + rows_sum(
        jnp.sum(ds * ds, axis=0) * lives[1]
    )
    return mean, square


def k_reduce(geo, io, me, nf, xs, wt, pre, stats):
    io.ready()
    chans = wt.shape[1]
    lives = [live_rows(me[1], chans), live_rows(me[2], chans)]

    def product(part, pix, npx, row, nrows, carry):
        acc = None
        for j in range(4):
            d = nt(xs[j, row : row + nrows, :], wt[j])
            acc = d if acc is None else acc + d
        z = as_pix(acc)
        pre[pix : pix + npx] = z
        return carry + jnp.sum(z, axis=0)

    zero = jnp.zeros((VIEWS, chans), F32)
    sums = geo.staged(io, None, product, [zero, zero])
    finish_stats(geo, pre, sums, lives, nf[0], stats)


def k_counts(ni, sizes, counts, me, nf3, cnt3, nf4, cnt4):
    img = lax.axis_index("img")
    levels = ni.bit_length() - 1
    me[0] = lax.axis_index("ch").astype(jnp.int32)
    me[1] = counts[img, 0]
    me[2] = counts[img, 1]
    me[3] = img
    for (big, small), nf, cnt in zip(sizes, (nf3, nf4), (cnt3, cnt4)):

        def group(shift, index):
            def add(i, total):
                at = index * (1 << shift) + i
                return total + counts[at, 0] * big + counts[at, 1] * small

            return lax.fori_loop(0, 1 << shift, add, jnp.int32(0)).astype(F32)

        nf[0] = group(0, img)
        for m in range(2):
            nf[1 + m] = group(levels - 1, (img >> (levels - 1)) ^ m)
        row, k = 0, 0
        while k < levels - 1:
            bits = 2 if k == 0 else 1
            for m in range(8):
                cnt[row + m] = group(k, (img >> k) ^ m) if m < 1 << bits else jnp.float32(0.0)
            row, k = row + 8, k + bits


def k_pack_params(gm3, sm3, go3, so3, gm4, sm4, go4, so4, out, rows):
    rows[...] = jnp.zeros(rows.shape, F32)
    rows[0:2, 0:64] = gm3[...]
    rows[2:4, 0:64] = sm3[...]
    for b in range(2):
        lanes = slice(128 * b, 128 * b + 128)
        rows[4 + b : 5 + b] = go3[:, lanes]
        rows[6 + b : 7 + b] = so3[:, lanes]
    rows[8:10] = gm4[...]
    rows[10:12] = sm4[...]
    for n in range(2):
        for b in range(4):
            lanes = slice(128 * b, 128 * b + 128)
            rows[12 + 4 * n + b : 13 + 4 * n + b] = go4[n : n + 1, lanes]
            rows[20 + 4 * n + b : 21 + 4 * n + b] = so4[n : n + 1, lanes]
    v = rows[...]
    high = v.astype(BF16)
    rest = v - high.astype(F32)
    mid = rest.astype(BF16)
    low = (rest - mid.astype(F32)).astype(BF16)
    out[0:32, 0:128] = high
    out[0:32, 128:256] = mid
    out[32:64, 0:128] = low
    out[32:64, 128:256] = jnp.zeros_like(low)


def k_unpack_params(base, me, p0, p1, p2, p3, gs1, gs2, gs3, gs4, gs5, gs6, buf, sem):
    copies = [
        pltpu.make_async_copy(p.at[pl.ds(base, 64)], buf.at[n], sem.at[n])
        for n, p in enumerate((p0, p1, p2, p3))
    ]
    for c in copies:
        c.start()
    for c in copies:
        c.wait()
    rows = []
    for n in range(4):
        v = buf[n].astype(F32)
        rows.append(v[0:32, 0:128] + v[0:32, 128:256] + v[32:64, 0:128])
    odd = me[0] & 1
    for chip in range(2):
        mine, other = rows[2 * chip][:, 0:64], rows[2 * chip + 1][:, 0:64]
        both = jnp.where(
            odd == 0,
            jnp.concatenate([mine, other], axis=1),
            jnp.concatenate([other, mine], axis=1),
        )
        at = pl.ds(pl.multiple_of(((me[0] >> 1) ^ chip) * 128, 128), 128)
        for n, gs in enumerate((gs1, gs2)):
            gs[0:1, at] = both[n : n + 1]
            gs[1:2, at] = both[2 + n : 3 + n]
    for p, v in enumerate(rows):
        for b in range(2):
            at = pl.ds(pl.multiple_of((me[0] ^ p) * 256 + 128 * b, 128), 128)
            gs3[0:1, at] = v[4 + b : 5 + b]
            gs3[1:2, at] = v[6 + b : 7 + b]
        at = pl.ds(pl.multiple_of((me[0] ^ p) * 128, 128), 128)
        for n, gs in enumerate((gs4, gs5)):
            gs[0:1, at] = v[8 + n : 9 + n]
            gs[1:2, at] = v[10 + n : 11 + n]
    for chip in range(2):
        v = rows[2 * chip]
        for n in range(2):
            for b in range(4):
                lanes = slice(128 * b, 128 * b + 128)
                gs6[chip, 2 * n : 2 * n + 1, lanes] = v[12 + 4 * n + b : 13 + 4 * n + b]
                gs6[chip, 2 * n + 1 : 2 * n + 2, lanes] = v[20 + 4 * n + b : 21 + 4 * n + b]


def k_merge(first, n, cnt, *refs):
    arrays, out = refs[:n], refs[n]
    for at in range(0, out.shape[-2], 2):
        mean_at, sq_at = (..., slice(at, at + 1), slice(None)), (..., slice(at + 1, at + 2), slice(None))
        groups = [(cnt[first + m], a[mean_at], a[sq_at]) for m, a in enumerate(arrays)]
        while len(groups) > 1:
            pairs = []
            for (na, ma, qa), (nb, mb, qb) in zip(groups[::2], groups[1::2]):
                total = na + nb
                diff = mb - ma
                pairs.append(
                    (total, (na * ma + nb * mb) / total, qa + qb + diff * diff * (na * nb / total))
                )
            groups = pairs
        out[mean_at], out[sq_at] = groups[0][1], groups[0][2]


def k_add(n, *refs):
    values = [r[...] for r in refs[:n]]
    while len(values) > 1:
        values = [a + b for a, b in zip(values[::2], values[1::2])]
    refs[n][...] = values[0]


def side_shift(v, by):
    zero = jnp.zeros((v.shape[0], 1) + v.shape[2:], v.dtype)
    if by > 0:
        return jnp.concatenate([zero, v[:, :-1]], axis=1)
    return jnp.concatenate([v[:, 1:], zero], axis=1)


def store_shifted(buf, row, nrows, side, v, order):
    img = v.reshape(2, side, VIEWS, v.shape[-1])
    chans = v.shape[-1]
    forms = [side_shift(img, 1), img, side_shift(img, -1)]
    for lane, k in enumerate(order):
        flat = forms[k].reshape(nrows, chans).astype(BF16)
        buf[pl.ds(row, nrows), lane * chans : (lane + 1) * chans] = flat


def put_phases(ref, i, v):
    for k in range(4):
        ref[k // 2, k % 2, i] = v[k // 2, :, k % 2]


def get_phases(ref, i):
    rows = [jnp.stack([ref[r, 0, i], ref[r, 1, i]], axis=1) for r in range(2)]
    return jnp.stack(rows)


def zero_edges(buf, edge):
    total = buf.shape[0]
    buf[0:edge, :] = jnp.zeros((edge, buf.shape[1]), BF16)
    buf[total - edge : total, :] = jnp.zeros((edge, buf.shape[1]), BF16)


def k_mix(geo, io, me, nf, pre1, sa, sb, gs, w, pre2, wb, ws, stats, dev, center):
    chans = pre1.shape[-1]
    lives = [live_rows(me[1], chans), live_rows(me[2], chans)]
    mean, inv = merged(sa[...], sb[...], nf[1], nf[2])
    scale, shift = gs[0:1] * inv, gs[1:2]
    bufs = (wb, ws)
    for part, (side, _) in enumerate(geo.parts):
        zero_edges(bufs[part], side * VIEWS)

    def act(part, i, pix, npx, row, nrows, carry):
        a = gelu((pre1[pl.ds(pix, npx)] - mean) * scale + shift)
        own = (pre1[pl.ds(pix, npx), :, lanes] - center[:, lanes]) * lives[part][:, 0:128]
        dev[pl.ds(row, nrows), :] = as_rows(own).astype(BF16)
        side = geo.parts[part][0]
        at = pl.multiple_of(side * VIEWS + i * nrows, 16)
        store_shifted(bufs[part], at, nrows, side, a, (0, 1, 2))
        return carry

    lanes, _ = own_block(me)
    center[...] = mean
    geo.loop(act, [0, 0], io)
    io.send(wb, ws, dev)
    io.ready()

    sums = [jnp.zeros((VIEWS, chans), F32)] * 2
    for part, (side, start) in enumerate(geo.parts):
        for lo, hi in geo.bands[part]:
            acc = None
            for r in range(3):
                at = (lo + r) * side * VIEWS
                d = nt(bufs[part][at : at + (hi - lo) * side * VIEWS, :], w[r])
                acc = d if acc is None else acc + d
            z = as_pix(acc)
            pre2[start + lo * side : start + hi * side] = z
            sums[part] = sums[part] + jnp.sum(z, axis=0)
    finish_stats(geo, pre2, sums, lives, nf[0], stats)


def k_expand(geo, io, me, nf, pre2, sa, sb, gs, w, pre3, act2, stats):
    chans = w.shape[1]
    lives = [live_rows(me[1], chans), live_rows(me[2], chans)]
    mean, inv = merged(sa[...], sb[...], nf[1], nf[2])
    scale, shift = gs[0:1] * inv, gs[1:2]

    def before(part, i, pix, npx, row, nrows):
        a = as_rows(gelu((pre2[pl.ds(pix, npx)] - mean) * scale + shift)).astype(BF16)
        act2[pl.ds(row, nrows), :] = a

    def product(part, pix, npx, row, nrows, carry):
        total = []
        for j in range(4):
            at = slice(256 * j, 256 * j + 256)
            z = as_pix(nn(act2[row : row + nrows, :], w[:, at]))
            pre3[pix : pix + npx, :, at] = z
            total.append(jnp.sum(z, axis=0))
        return carry + jnp.concatenate(total, axis=1)

    io.ready()
    zero = jnp.zeros((VIEWS, chans), F32)
    sums = geo.staged(io, before, product, [zero, zero])
    finish_stats(geo, pre3, sums, lives, nf[0], stats)


def k_narrow(geo, io, me, nf, pre3, xs, sa, sb, gs, w, pre4b, pre4s, mid, mids, stats, dev3, slope3, mid_even):
    chans = w.shape[1]
    lives = [live_rows(me[1], chans), live_rows(me[2], chans)]
    mean, inv = merged(sa[...], sb[...], nf[1], nf[2])
    scale, shift = gs[0:1] * inv, gs[1:2]
    pre4 = (pre4b, pre4s)

    def body(part, i, pix, npx, row, nrows, carry):
        side = geo.parts[part][0]
        half = side // 2
        for j in range(4):
            at = slice(256 * j, 256 * j + 256)
            dev = pre3[pl.ds(pix, npx), :, at] - mean[:, at]
            x = as_pix(xs[j, pl.ds(row, nrows), :].astype(F32))
            a, slope = gelu_both(dev * scale[:, at] + shift[:, at] + x)
            mid[pl.ds(row, nrows), at] = as_rows(a).astype(BF16)
            dev3[pl.ds(row, nrows), at] = as_rows(dev).astype(BF16)
            slope3[pl.ds(row, nrows), at] = as_rows(slope).astype(BF16)
            even = a.reshape(2, half, 2, VIEWS, 256)[0, :, 0]
            mid_even[pl.ds((0, geo.qb)[part] + half * i, half), :, at] = even
        z = nn(mid[pl.ds(row, nrows), :], w[...])
        put_phases(pre4[part], i, z.reshape(2, half, 2, VIEWS, chans))
        return carry + jnp.sum(as_pix(z), axis=0)

    io.ready()
    zero = jnp.zeros((VIEWS, chans), F32)
    sums = geo.loop(body, [zero, zero], io, io)
    mean4 = (rows_sum(sums[0] * lives[0]) + rows_sum(sums[1] * lives[1])) / nf[0]
    mids[...] = as_rows(mid_even[...]).astype(BF16)
    io.send(mids)
    sq = []
    for part in range(2):

        def dev2(i, carry, part=part):
            for k in range(4):
                d = pre4[part][k // 2, k % 2, i] - mean4
                carry = carry + jnp.sum(d * d, axis=0)
            return carry

        sq.append(lax.fori_loop(0, geo.parts[part][0] // 2, dev2, zero))
    stats[0:1] = mean4
    stats[1:2] = rows_sum(sq[0] * lives[0]) + rows_sum(sq[1] * lives[1])


def k_short(geo, io, me, nf, mids, w0, w1, side, stats):
    io.ready()
    chans = w0.shape[1]
    lives = [live_rows(me[1], chans), live_rows(me[2], chans)]
    for j, w in enumerate((w0, w1)):
        z = as_pix(nn(mids[...], w[...]))
        side[j] = z
        io.leave(j)
        mean, square = block_stats(geo, z, lives, nf[0])
        stats[j] = jnp.concatenate([mean, square], axis=0)


def k_stride(geo, io, me, nf, n4, pre4b, pre4s, sa, sb, gs, w, pre5, cols, stats, sb_act, ss_act):
    chans = pre4b.shape[-1]
    lives = [live_rows(me[1], chans), live_rows(me[2], chans)]
    mean, inv = merged(sa[...], sb[...], n4[1], n4[2])
    scale, shift = gs[0:1] * inv, gs[1:2]
    srcs, dsts = (pre4b, pre4s), (sb_act, ss_act)

    def act(part, i, pix, npx, row, nrows, carry):
        for k in range(4):
            at = (k // 2, k % 2, i)
            dsts[part][at] = gelu((srcs[part][at] - mean) * scale + shift)
        return carry

    geo.loop(act, [0, 0], io)
    for r in range(3):
        for c in range(3):
            flats = []
            for part in range(2):
                half = geo.parts[part][0] // 2
                v = dsts[part][(r + 1) % 2, (c + 1) % 2]
                if c == 0:
                    v = side_shift(v, 1)
                if r == 0:
                    v = jnp.concatenate([jnp.zeros((1,) + v.shape[1:], F32), v[:-1]], axis=0)
                flats.append(v.reshape(half * half * VIEWS, chans))
            t = 3 * r + c
            cols[t] = jnp.concatenate(flats, axis=0).astype(BF16)
            io.leave(t)
    io.ready()
    acc = None
    for t in range(9):
        d = nn(cols[t], w[t * chans : (t + 1) * chans, :])
        acc = d if acc is None else acc + d
    z = as_pix(acc)
    pre5[...] = z
    m5, s5 = block_stats(geo, z, lives, nf[0])
    stats[0:1] = m5
    stats[1:2] = s5


def k_widen(geo, io, me, nf, pre5, sa, sb, gs, w0, w1, st_side, pre6, act5, stats):
    chans = w0.shape[1]
    lives = [live_rows(me[1], chans), live_rows(me[2], chans)]
    mean, inv = merged(sa[...], sb[...], nf[1], nf[2])
    scale, shift = gs[0:1] * inv, gs[1:2]
    act5[...] = as_rows(gelu((pre5[...] - mean) * scale + shift)).astype(BF16)
    io.ready()
    for j, w in enumerate((w0, w1)):
        z = as_pix(nn(act5[...], w[...]))
        pre6[j] = z
        io.leave(j)
        m6, s6 = block_stats(geo, z, lives, nf[0])
        stats[j] = jnp.concatenate([m6, s6, st_side[j]], axis=0)


def k_total(geo, io, me, nf, pre6, side, sa, sb, gs, cb0, cb1, cs0, cs1, out_b, out_s, dt, sums, cot):
    chans = pre6.shape[-1]
    lives = [live_rows(me[1], chans), live_rows(me[2], chans)]
    cots = ((cb0, cb1), (cs0, cs1))
    spans = ((0, geo.qb), (geo.qb, geo.px4))
    outs = (out_b, out_s)
    io.ready()
    for j in range(2):
        io.arrive(j)
        a, b, g = sa[j], sb[j], gs[j]
        m6, r6 = merged(a[0:2], b[0:2], nf[1], nf[2])
        ms, rs = merged(a[2:4], b[2:4], nf[1], nf[2])
        k6, ks = g[0:1] * r6, g[2:3] * rs
        off = g[1:2] + g[3:4]
        acc = [jnp.zeros((VIEWS, chans), F32)] * 3
        for part, (lo, hi) in enumerate(spans):
            half = geo.parts[part][0] // 2
            cot[lo:hi] = as_pix(cots[part][j][...].astype(F32))[: hi - lo]

            def row(i, carry, part=part, lo=lo, half=half):
                at = pl.ds(lo + i * half, half)
                d6 = pre6[j, at] - m6
                dd = side[j, at] - ms
                value, slope = gelu_both(d6 * k6 + (dd * ks + off))
                if j == 0:
                    outs[part][pl.ds(i * half, half)] = value * lives[part]
                grad = slope * (cot[at] * lives[part])
                dt[j, at] = grad
                terms = [jnp.sum(v, axis=0) for v in (grad, grad * d6, grad * dd)]
                return [s + t for s, t in zip(carry, terms)]

            acc = lax.fori_loop(0, half, row, acc)
        io.leave(j)
        if j == 0:
            io.send(out_b, out_s)
        sums[j] = jnp.concatenate(
            [rows_sum(acc[0]), rows_sum(acc[1]) * r6, rows_sum(acc[2]) * rs], axis=0
        )


def back_coefs(lives, s1, s2, inv, gain, count):
    c1 = gain * inv
    c2 = [live * (c1 * s1 / count) for live in lives]
    c3 = [live * (c1 * inv * s2 / count) for live in lives]
    return c1, c2, c3


def k_back_wide(geo, io, me, nf, dt, pre6, side, sa, sb, gs, ga, gb, w0, w1, part5, dz6, dzs, tot):
    chans = pre6.shape[-1]
    lives = [live_rows(me[1], chans), live_rows(me[2], chans)]
    total = nf[1] + nf[2]
    spans = ((0, geo.qb), (geo.qb, geo.px4))
    acc = None
    io.ready()
    for j, w in enumerate((w0, w1)):
        io.arrive(j)
        a, b, g = sa[j], sb[j], gs[j]
        s = ga[j] + gb[j]
        tot[j] = s
        m6, r6 = merged(a[0:2], b[0:2], nf[1], nf[2])
        ms, rs = merged(a[2:4], b[2:4], nf[1], nf[2])
        k1, k2, k3 = back_coefs(lives, s[0:1], s[1:2], r6, g[0:1], total)
        h1, h2, h3 = back_coefs(lives, s[0:1], s[2:3], rs, g[2:3], total)
        main, short = [], []
        for part, (lo, hi) in enumerate(spans):
            grad = dt[j, lo:hi]
            main.append(grad * k1 - k2[part] - (pre6[j, lo:hi] - m6) * k3[part])
            short.append(grad * h1 - h2[part] - (side[j, lo:hi] - ms) * h3[part])
        z6 = as_rows(jnp.concatenate(main, axis=0)).astype(BF16)
        dzs[j] = as_rows(jnp.concatenate(short, axis=0)).astype(BF16)
        io.leave(j)
        if j == 0:
            dz6[...] = z6
        d = nt(z6, w[...])
        acc = d if acc is None else acc + d
    part5[...] = as_pix(acc)


def k_back_act5(nf, mine, other, pre5, sa5, sb5, gs5, dt5, sums5):
    m5, r5 = merged(sa5[...], sb5[...], nf[1], nf[2])
    dev = pre5[...] - m5
    grad = gelu_slope(dev * (gs5[0:1] * r5) + gs5[1:2]) * (mine[...] + other[...])
    dt5[...] = grad
    sums5[0:1] = rows_sum(jnp.sum(grad, axis=0))
    sums5[1:2] = rows_sum(jnp.sum(grad * dev, axis=0)) * r5


def k_back_short(io, me, dzs, w0, w1, dms):
    io.ready()
    acc = None
    for j, w in enumerate((w0, w1)):
        d = nt(dzs[j], w[...])
        acc = d if acc is None else acc + d
    dms[...] = as_pix(acc).astype(BF16)


def k_back_stride(geo, io, me, nf, dt5, pre5, sa5, sb5, gs5, ga, gb, pre4b, pre4s, sa4, sb4, gs4, n4, w, dt4b, dt4s, dz5, sums4, tot, shifts):
    chans = pre5.shape[-1]
    lives = [live_rows(me[1], chans), live_rows(me[2], chans)]
    s = ga[...] + gb[...]
    tot[...] = s
    m5, r5 = merged(sa5[...], sb5[...], nf[1], nf[2])
    c1, c2, c3 = back_coefs(lives, s[0:1], s[1:2], r5, gs5[0:1], nf[1] + nf[2])
    spans = ((0, geo.qb), (geo.qb, geo.px4))
    imgs = []
    for part, (lo, hi) in enumerate(spans):
        half = geo.parts[part][0] // 2
        z = dt5[lo:hi] * c1 - c2[part] - (pre5[lo:hi] - m5) * c3[part]
        imgs.append(z.reshape(half, half, VIEWS, chans))

    def flat(moved):
        return jnp.concatenate([v.reshape(-1, chans) for v in moved], axis=0).astype(BF16)

    def up(v):
        return jnp.concatenate([v[1:], jnp.zeros((1,) + v.shape[1:], F32)], axis=0)

    shifts[0] = flat(imgs)
    dz5[...] = shifts[0]
    shifts[1] = flat([side_shift(v, -1) for v in imgs])
    shifts[2] = flat([up(v) for v in imgs])
    shifts[3] = flat([up(side_shift(v, -1)) for v in imgs])
    m4, r4 = merged(sa4[...], sb4[...], n4[1], n4[2])
    scale, off = gs4[0:1] * r4, gs4[1:2]
    io.ready()
    plan = {
        (0, 0): ((0, 4),),
        (0, 1): ((0, 5), (1, 3)),
        (1, 0): ((0, 7), (2, 1)),
        (1, 1): ((0, 8), (1, 6), (2, 2), (3, 0)),
    }
    t1, t2 = jnp.zeros((VIEWS, chans), F32), jnp.zeros((VIEWS, chans), F32)
    for (rp, cp), terms in plan.items():
        acc = None
        for k, t in terms:
            d = nt(shifts[k], w[t * chans : (t + 1) * chans, :])
            acc = d if acc is None else acc + d
        for part, (lo, hi) in enumerate(spans):
            half = geo.parts[part][0] // 2
            d = acc[lo * VIEWS : hi * VIEWS].reshape(half, half, VIEWS, chans)
            dev = (pre4b, pre4s)[part][rp, cp] - m4
            grad = gelu_slope(dev * scale + off) * d
            (dt4b, dt4s)[part][rp, cp] = grad
            t1 = t1 + jnp.sum(grad, axis=(0, 1))
            t2 = t2 + jnp.sum(grad * dev, axis=(0, 1))
    io.send(dt4b, dt4s)
    sums4[0:1] = rows_sum(t1)
    sums4[1:2] = rows_sum(t2) * r4


def k_back_narrow(geo, io, me, nf, dt4b, dt4s, pre4b, pre4s, sa4, sb4, gs4, ga, gb, dev3, slope3, sa3, sb3, dms, dmo, w, dt3, dz4, sums3, tot):
    chans = w.shape[1]
    wide = w.shape[0]
    lives = [live_rows(me[1], chans), live_rows(me[2], chans)]
    s = ga[...] + gb[...]
    tot[...] = s
    m4, r4 = merged(sa4[...], sb4[...], nf[1], nf[2])
    c1, c2, c3 = back_coefs(lives, s[0:1], s[1:2], r4, gs4[0:1], nf[1] + nf[2])
    _, r3 = merged(sa3[...], sb3[...], nf[1], nf[2])
    dts, pres = (dt4b, dt4s), (pre4b, pre4s)

    def body(part, i, pix, npx, row, nrows, carry):
        half = geo.parts[part][0] // 2
        dev4 = get_phases(pres[part], i) - m4
        z = get_phases(dts[part], i) * c1 - c2[part] - dev4 * c3[part]
        z = z.reshape(nrows, chans).astype(BF16)
        dz4[pl.ds(row, nrows), :] = z
        at = pl.ds((0, geo.qb)[part] + half * i, half)
        t1, t2 = [], []
        for j in range(4):
            at_j = slice(256 * j, 256 * j + 256)
            d = nt(z, w[at_j, :]).reshape(2, half, 2, VIEWS, 256)
            even = d[0, :, 0] + (dms[at, :, at_j].astype(F32) + dmo[at, :, at_j].astype(F32))
            top = jnp.stack([even, d[0, :, 1]], axis=1)
            d = jnp.concatenate([as_pix_rows(top), as_pix_rows(d[1])], axis=0)
            dev = as_pix(dev3[pl.ds(row, nrows), at_j].astype(F32))
            grad = as_pix(slope3[pl.ds(row, nrows), at_j].astype(F32)) * d
            dt3[pl.ds(row, nrows), at_j] = as_rows(grad).astype(BF16)
            t1.append(jnp.sum(grad, axis=0))
            t2.append(jnp.sum(grad * dev, axis=0))
        return carry[0] + jnp.concatenate(t1, axis=1), carry[1] + jnp.concatenate(t2, axis=1)

    io.ready()
    zero = jnp.zeros((VIEWS, wide), F32)
    (a1, a2), (b1, b2) = geo.loop(body, [(zero, zero), (zero, zero)], io, io)
    sums3[0:1] = rows_sum(a1 + b1)
    sums3[1:2] = rows_sum(a2 + b2) * r3


def k_back_expand(geo, io, me, nf, dt3, dev3, sa3, sb3, gs3, ga, gb, pre2, sa2, sb2, gs2, w, dt2, dz3, dt3q, sums2, tot, zbuf_b, zbuf_s):
    wide, chans = w.shape[1], w.shape[0]
    lives = [live_rows(me[1], wide), live_rows(me[2], wide)]
    s = ga[...] + gb[...]
    tot[...] = s
    _, r3 = merged(sa3[...], sb3[...], nf[1], nf[2])
    c1, c2, c3 = back_coefs(lives, s[0:1], s[1:2], r3, gs3[0:1], nf[1] + nf[2])
    m2, r2 = merged(sa2[...], sb2[...], nf[1], nf[2])
    scale, off = gs2[0:1] * r2, gs2[1:2]
    mine = pl.ds(pl.multiple_of(me[0] * 256, 256), 256)

    def body(part, i, pix, npx, row, nrows, carry):
        zbuf = (zbuf_b, zbuf_s)[part]
        dt3q[pl.ds(row, nrows), :] = dt3[pl.ds(row, nrows), mine]
        for j in range(4):
            at = slice(256 * j, 256 * j + 256)
            z = (
                as_pix(dt3[pl.ds(row, nrows), at].astype(F32)) * c1[:, at]
                - c2[part][:, at]
                - as_pix(dev3[pl.ds(row, nrows), at].astype(F32)) * c3[part][:, at]
            )
            zbuf[:, at] = as_rows(z).astype(BF16)
        dz3[pl.ds(row, nrows), :] = zbuf[:, mine]
        d = as_pix(nt(zbuf[...], w[...]))
        dev = pre2[pl.ds(pix, npx)] - m2
        grad = gelu_slope(dev * scale + off) * d
        dt2[pl.ds(pix, npx)] = grad
        return carry[0] + jnp.sum(grad, axis=0), carry[1] + jnp.sum(grad * dev, axis=0)

    io.ready()
    zero = jnp.zeros((VIEWS, chans), F32)
    (a1, a2), (b1, b2) = geo.loop(body, [(zero, zero), (zero, zero)], io, io)
    sums2[0:1] = rows_sum(a1 + b1)
    sums2[1:2] = rows_sum(a2 + b2) * r2


def k_back_mix(geo, io, me, nf, dt2, pre2, sa2, sb2, gs2, ga, gb, pre1, sa1, sb1, gs1, w, dt1, dz2, sums1, tot, dt1q, zb, zs):
    chans = pre2.shape[-1]
    lives = [live_rows(me[1], chans), live_rows(me[2], chans)]
    s = ga[...] + gb[...]
    tot[...] = s
    m2, r2 = merged(sa2[...], sb2[...], nf[1], nf[2])
    c1, c2, c3 = back_coefs(lives, s[0:1], s[1:2], r2, gs2[0:1], nf[1] + nf[2])
    m1, r1 = merged(sa1[...], sb1[...], nf[1], nf[2])
    scale, off = gs1[0:1] * r1, gs1[1:2]
    bufs = (zb, zs)
    for part, (side, _) in enumerate(geo.parts):
        zero_edges(bufs[part], side * VIEWS)

    def back(part, i, pix, npx, row, nrows, carry):
        z = dt2[pl.ds(pix, npx)] * c1 - c2[part] - (pre2[pl.ds(pix, npx)] - m2) * c3[part]
        dz2[pl.ds(row, nrows), :] = as_rows(z).astype(BF16)
        side = geo.parts[part][0]
        at = pl.multiple_of(side * VIEWS + i * nrows, 16)
        store_shifted(bufs[part], at, nrows, side, z, (2, 1, 0))
        return carry

    lanes, _ = own_block(me)
    geo.loop(back, [0, 0], io)
    io.send(dz2)
    io.ready()

    for part, (side, start) in enumerate(geo.parts):
        for lo, hi in geo.bands[part]:
            acc = None
            for r in range(3):
                at = (lo + 2 - r) * side * VIEWS
                taps = w[3 * r : 3 * r + 3].reshape(3 * chans, chans)
                d = nn(bufs[part][at : at + (hi - lo) * side * VIEWS, :], taps)
                acc = d if acc is None else acc + d
            dt1[start + lo * side : start + hi * side] = as_pix(acc)

    def finish(part, i, pix, npx, row, nrows, carry):
        dev = pre1[pl.ds(pix, npx)] - m1
        grad = gelu_slope(dev * scale + off) * dt1[pl.ds(pix, npx)]
        dt1[pl.ds(pix, npx)] = grad
        dt1q[pl.ds(row, nrows), :] = as_rows(dt1[pl.ds(pix, npx), :, lanes]).astype(BF16)
        return carry[0] + jnp.sum(grad, axis=0), carry[1] + jnp.sum(grad * dev, axis=0)

    zero = jnp.zeros((VIEWS, chans), F32)
    (a1, a2), (b1, b2) = geo.loop(finish, [(zero, zero), (zero, zero)], None, io)
    sums1[0:1] = rows_sum(a1 + b1)
    sums1[1:2] = rows_sum(a2 + b2) * r1


def k_back_reduce(geo, io, me, nf, dt1, pre1, sa1, sb1, gs1, ga, gb, dt3q, wt, gxb, gxs, tot, coef):
    chans = pre1.shape[-1]
    lives = [live_rows(me[1], chans), live_rows(me[2], chans)]
    s = ga[...] + gb[...]
    tot[...] = s
    m1, r1 = merged(sa1[...], sb1[...], nf[1], nf[2])
    c1, c2, c3 = back_coefs(lives, s[0:1], s[1:2], r1, gs1[0:1], nf[1] + nf[2])
    io.ready()
    total = nf[1] + nf[2]
    coef[0:1] = c1
    coef[1:2] = c1 * s[0:1] / total
    coef[2:3] = c1 * r1 * s[1:2] / total

    def body(part, i, pix, npx, row, nrows, carry):
        z = dt1[pl.ds(pix, npx)] * c1 - c2[part] - (pre1[pl.ds(pix, npx)] - m1) * c3[part]
        z = as_rows(z).astype(BF16)
        g = as_pix(nn(z, wt[me[0]])) + as_pix(dt3q[pl.ds(row, nrows), :].astype(F32))
        (gxb, gxs)[part][pl.ds(pix - (0, geo.pb)[part], npx)] = g
        return carry

    geo.loop(body, [0, 0], io, io)


def k_dw_wide(act5, dz6, mids, dzs, dwide, dshort):
    dwide[...] = tn(act5[...], dz6[...]).astype(BF16)
    dshort[...] = tn(mids[...], dzs[0]).astype(BF16)


def lane_blocks(v):
    return [v[:, 128 * b : 128 * b + 128] for b in range(v.shape[1] // 128)]


def put_halves(me, full, keep, send):
    bit = me[3] & 1
    keep[...] = full[bit].astype(BF16)
    send[...] = full[1 - bit].astype(BF16)


def k_dw_stride(io, me, cols, dz5, keep, send, full):
    mine = pl.ds(pl.multiple_of(me[0] * 128, 128), 128)
    z = dz5[:, mine]
    rows = full.shape[1]
    for t in range(9):
        io.arrive(t)
        dw = tn(cols[t], z)
        lo = 0
        while lo < 512:
            half, at = divmod(t * 512 + lo, rows)
            n = min(512 - lo, rows - at)
            full[half, at : at + n] = dw[lo : lo + n]
            lo += n
    put_halves(me, full, keep, send)


def k_dw_mid(me, mid, dz4, act2, dz3, keep, send, full):
    mine = pl.ds(pl.multiple_of(me[0] * 128, 128), 128)
    blocks = [tn(mid[...], dz4[:, mine])] + lane_blocks(tn(act2[...], dz3[...]))
    full[...] = jnp.concatenate(blocks, axis=0).reshape(full.shape)
    put_halves(me, full, keep, send)


def own_block(me):
    lanes = pl.ds(pl.multiple_of((me[0] >> 1) * 128, 128), 128)
    return lanes, pl.ds(pl.multiple_of((me[0] & 1) * 64, 64), 64)


def k_dev_products(geo, io, me, devq, xs, out, part):
    lives = [live_rows(me[1], 256), live_rows(me[2], 256)]
    _, mine = own_block(me)
    io.ready()

    def body(step, i, pix, npx, row, nrows, carry):
        return [
            carry[j] + jnp.sum(as_pix(xs[j, pl.ds(row, nrows), :].astype(F32)), axis=0) for j in range(4)
        ]

    zero = [jnp.zeros((VIEWS, 256), F32)] * 4
    big, small = geo.loop(body, [zero, zero], io)
    sums = [jnp.broadcast_to(rows_sum(b * lives[0] + s * lives[1]), (16, 256)) for b, s in zip(big, small)]
    for j in range(4):
        part[...] = tn(devq[...], xs[j])
        out[:, 256 * j : 256 * j + 256] = jnp.concatenate([part[mine, :], sums[j]], axis=0).astype(BF16)


def k_dw_last(geo, io, me, wb, ws, dz2, xs, dt1q, keep, send, full, part, flat):
    lanes, mine = own_block(me)
    io.ready()
    io.start_steps()
    nb, ns = geo.pb * VIEWS, geo.ps * VIEWS
    at = 0
    for r in range(3):
        ob, os = r * geo.hb * VIEWS, r * geo.hs * VIEWS
        full[...] = tn(dz2[0:nb, lanes], wb[ob : ob + nb, :]) + tn(
            dz2[nb : nb + ns, lanes], ws[os : os + ns, :]
        )
        for block in lane_blocks(full[mine, :]):
            flat[at : at + 64] = block
            at += 64
    geo.loop(lambda step, i, pix, npx, row, nrows, carry: carry, [0, 0], io)
    for j in range(4):
        part[:, 256 * j : 256 * j + 256] = tn(dt1q[...], xs[j])
    flat[at:] = jnp.concatenate(lane_blocks(part[mine, :]), axis=0)
    half = keep.shape[0]
    bit = me[3] & 1
    keep[...] = flat[pl.ds(pl.multiple_of(bit * half, 8), half)].astype(BF16)
    send[...] = flat[pl.ds(pl.multiple_of((1 - bit) * half, 8), half)].astype(BF16)


def k_out_first(io, me, wide, short, a, b, dwide, dshort, dstride):
    bit = me[3] & 1
    for n in range(4):
        io.arrive(n)
        if n < 2:
            dwide[n] = wide[n].astype(F32)
        dshort[n] = short[n].astype(F32)
        io.leave(n)
    io.ready()
    dstride[bit] = a[0].astype(F32)
    dstride[1 - bit] = b[0].astype(F32)
    io.send(dstride)


def k_small_outputs(me, t1, t2, t3, t4, t5, t6, late, gm3, sm3, go3, so3, gm4, sm4, go4, so4):
    lanes, _ = own_block(me)
    half = me[0] & 1
    for n, t in enumerate((t1, t2)):
        block = t[:, lanes]
        mine = jnp.where(half == 0, block[:, 0:64], block[:, 64:128])
        gm3[n : n + 1] = mine[1:2]
        sm3[n : n + 1] = mine[0:1]
    wide = pl.ds(pl.multiple_of(me[0] * 256, 256), 256)
    go3[...] = t3[1:2, wide]
    so3[...] = t3[0:1, wide]
    mid = pl.ds(pl.multiple_of(me[0] * 128, 128), 128)
    for n, t in enumerate((t4, t5)):
        gm4[n : n + 1] = t[1:2, mid]
        sm4[n : n + 1] = t[0:1, mid]
    go4[...] = t6[1:3]
    so4[0:1] = t6[0:1]
    so4[1:2] = t6[0:1]


def k_sum_split(shift, size, n_in, me, *refs):
    total = refs[n_in]
    acc = refs[0][...].astype(F32)
    for r in refs[1:n_in]:
        acc = acc + r[...].astype(F32)
    total[...] = acc
    where = (me[3] >> shift) & (size - 1)
    for m, out in enumerate(refs[n_in + 1 :]):
        out[...] = total[where ^ m].astype(BF16)


def k_sum(n_in, *refs):
    acc = refs[0][...].astype(F32)
    for r in refs[1:n_in]:
        acc = acc + r[...].astype(F32)
    refs[n_in][...] = acc.astype(BF16)


def k_join(shift, size, me, *refs):
    where = (me[3] >> shift) & (size - 1)
    for m in range(size):
        refs[size][where ^ m] = refs[m][...]


def k_unpack(plan, me, a, b, *refs):
    full = refs[-1]
    bit = me[3] & 1
    full[bit] = a[...].reshape(full.shape[1:]).astype(F32)
    full[1 - bit] = b[...].reshape(full.shape[1:]).astype(F32)
    flat = full[...].reshape(2 * full.shape[1], 128)
    at = 0
    for out, (lead, rows, cols) in zip(refs, plan):
        for t in range(lead):
            for block in range(cols // 128):
                v = flat[at : at + rows]
                lanes = slice(128 * block, 128 * block + 128)
                if lead > 1:
                    out[t, :, lanes] = v
                else:
                    out[:, lanes] = v
                at += rows


def k_out_last(me, a, b, dev, coef, dmix, dreduce, full):
    bit = me[3] & 1
    full[bit] = a[...].reshape(full.shape[1:]).astype(F32)
    full[1 - bit] = b[...].reshape(full.shape[1:]).astype(F32)
    flat = full[...].reshape(2 * full.shape[1], 128)
    at = 0
    for t in range(9):
        for block in range(2):
            dmix[t, :, 128 * block : 128 * block + 128] = flat[at : at + 64]
            at += 64
    dev = dev[...].astype(F32)
    fix = dev[64:65] * coef[1] + dev[0:64] * coef[2]
    for block in range(8):
        lanes = slice(128 * block, 128 * block + 128)
        dreduce[:, lanes] = flat[at : at + 64] * coef[0] - fix[:, lanes]
        at += 64


def per_device(
    ni,
    nc,
    x_big,
    x_small,
    cot_big,
    cot_small,
    counts,
    w_reduce,
    w_mix,
    w_expand,
    w_narrow,
    w_stride,
    w_widen,
    w_short,
    gain_mid3,
    shift_mid3,
    gain_out3,
    shift_out3,
    gain_mid4,
    shift_mid4,
    gain_out4,
    shift_out4,
):
    assert nc == 4 and ni >= 8 and x_big.shape[0] == VIEWS and x_small.shape[0] == VIEWS
    geo = Geo(x_big.shape[1], x_small.shape[1])
    img = lax.axis_index("img")
    q = lax.axis_index("ch").astype(jnp.int32)
    levels = ni.bit_length() - 1
    me, nf3, cnt3, nf4, cnt4 = call(
        "counts",
        functools.partial(k_counts, ni, ((geo.pb, geo.ps), (geo.qb, geo.qs))),
        [(counts, SMEM)],
        [(sds((4,), jnp.int32), SMEM)]
        + [(sds((n,)), SMEM) for n in (3, 8 * (levels - 2)) * 2],
        slack=1,
    )

    smem = [(me, SMEM)]

    def over_img(v, k):
        return lax.ppermute(v, "img", [(i, i ^ (1 << k)) for i in range(ni)])

    def over_ch(v, k):
        return lax.ppermute(v, "ch", [(i, i ^ k) for i in range(nc)])

    rounds, at = [], 0
    while at < levels:
        rounds.append((at, min(2, levels - at) if at == 0 else 1))
        at += rounds[-1][1]

    def peers(v, shift, bits):
        out = []
        for m in range(1, 1 << bits):
            out.append(lax.ppermute(v, "img", [(i, i ^ (m << shift)) for i in range(ni)]))
        return out

    def sync(v, combine, wait=(), free=()):
        wait, free = dict(wait), dict(free)
        freed = []
        for k, (shift, bits) in enumerate(rounds):
            if k in wait:
                v = lax.optimization_barrier((v,) + tuple(wait[k]))[0]
            others = peers(v, shift, bits)
            if k in free:
                held = lax.optimization_barrier(tuple(others) + tuple(free[k]))
                others = list(held[: len(others)])
                freed += held[len(others) :]
            if k == len(rounds) - 1:
                return (v, others[0]) + ((freed,) if free else ())
            v = combine(k, [v] + others)

    last = len(rounds) - 1

    def sync_stats(stats, cnt, wait=(), free=()):
        def combine(k, arrays):
            (v,) = call(
                "merge",
                functools.partial(k_merge, 8 * k, len(arrays)),
                [(cnt, SMEM)] + vm(*arrays),
                [sds(stats.shape)],
                slack=1,
            )
            return v

        return sync(stats, combine, wait, free)

    def sync_sums(sums, wait=(), free=()):
        def combine(k, arrays):
            (v,) = call("add", functools.partial(k_add, len(arrays)), vm(*arrays), [sds(sums.shape)], slack=1)
            return v

        return sync(sums, combine, wait, free)

    pairs = [(at, 1) for at in range(levels)]
    fours = [(0, 1)]
    while fours[-1][0] + fours[-1][1] < levels:
        done = fours[-1][0] + fours[-1][1]
        fours.append((done, min(2, levels - done)))

    def to_peers(parts, group):
        shift, bits = group
        out = []
        for m in range(1, 1 << bits):
            perm = [(i, i ^ (m << shift)) for i in range(ni)]
            out.append(lax.ppermute(parts[m if len(parts) > 1 else 0], "img", perm))
        return out

    def sum_split(name, arrays, group):
        shift, bits = group
        size = 1 << bits
        shape = arrays[0].shape
        view = (size, shape[0] // size) + shape[1:]
        return call(
            name,
            functools.partial(k_sum_split, shift, size, len(arrays)),
            smem + vm(*[a.reshape(view) for a in arrays]),
            [sds(view[1:], BF16)] * size,
            [pltpu.VMEM(view, F32)],
            order=True,
        )

    def join(name, parts, group):
        shift, bits = group
        size = 1 << bits
        (full,) = call(
            name,
            functools.partial(k_join, shift, size),
            smem + vm(*parts),
            [sds((size,) + parts[0].shape, BF16)],
        )
        return full.reshape((-1,) + parts[0].shape[1:])

    class Train:
        def __init__(self, name, groups, parts):
            self.name, self.groups, self.parts, self.at, self.summing = name, groups, parts, 0, True

        def sends(self):
            return self.parts[1:] if self.summing else self.parts

        def launch(self, sends):
            parts = self.parts[:1] + list(sends) if self.summing else list(sends)
            self.received = to_peers(parts, self.groups[self.at])

        def advance(self):
            name = "%s_%d" % (self.name, self.at)
            arrays = self.parts[:1] + self.received
            if self.summing and self.at + 1 < len(self.groups):
                self.at += 1
                self.parts = sum_split(name, arrays, self.groups[self.at])
            elif self.summing:
                self.summing = False
                self.parts = call(
                    name + "s",
                    functools.partial(k_sum, len(arrays)),
                    vm(*arrays),
                    [sds(arrays[0].shape, BF16)],
                    slack=2,
                )
            else:
                self.parts = [join(name + "j", arrays, self.groups[self.at])]
                self.at -= 1

        def to_last(self):
            while self.summing or self.at > 0:
                self.advance()
                self.launch(self.sends())

        def finish(self):
            self.to_last()
            return self.parts[0], self.received[0]

    def quarters(v):
        p1 = over_ch(v, 1)
        p2 = over_ch(v, 2)
        return [v, p1, p2, over_ch(p2, 1)]

    def after(marker, *arrays):
        return list(lax.optimization_barrier((marker,) + arrays))

    def sent(v):
        return [v, over_ch(v, 1), over_ch(v, 2)]

    def passed_on(g):
        return g + [over_ch(g[2], 1)]

    def rows_of(v):
        return jnp.transpose(v, (1, 2, 0, 3)).reshape(-1, v.shape[3])

    m3, c3 = 4 * w_reduce.shape[1], w_reduce.shape[0]
    m4, c4q = w_widen.shape
    first = [rows_of(x_small)]
    first.append(jnp.transpose(w_mix, (0, 1, 3, 2)).reshape(-1, m3))
    first += [w_reduce.T[:, j * m3 : (j + 1) * m3] for j in range(c3 // m3)]
    mix_at, reduce_at = first[0].shape[0], first[0].shape[0] + first[1].shape[0]
    held = (gain_mid3, shift_mid3, gain_out3[None], shift_out3[None], gain_mid4, shift_mid4, gain_out4, shift_out4)
    first += call(
        "pack_params",
        k_pack_params,
        vm(*held),
        [sds((64, 256), BF16)],
        [pltpu.VMEM((32, 128), F32)],
        slack=2,
    )
    params_at = sum(v.shape[0] for v in first[:-1])
    xb = quarters(rows_of(x_big))
    xb[1], me, *first = lax.optimization_barrier((xb[1], me, *first))
    smem = [(me, SMEM)]
    xsm = sent(jnp.concatenate(first))
    def blocks128(v):
        return [v[:, 128 * b : 128 * b + 128] for b in range(v.shape[1] // 128)]

    w_mid = jnp.concatenate(blocks128(w_expand) + blocks128(w_narrow))
    def whole_tiles(v):
        return jnp.pad(v, ((0, -v.shape[0] % 16), (0, 0)))

    cots = [whole_tiles(rows_of(v)) for v in (cot_big, cot_small)]
    cot_rows = [v.shape[0] for v in cots]
    last_in = jnp.concatenate([w_short, w_widen] + cots)
    wst = w_stride.reshape(-1, w_stride.shape[3])
    xb[3], xsm[2], w_mid, last_in, wst = after(xb[3], xsm[2], w_mid, last_in, wst)
    xsm = passed_on(xsm)
    gs1, gs2, gs3, gs4, gs5, gs6 = call(
        "unpack_params",
        functools.partial(k_unpack_params, params_at),
        smem + [(in_hbm(v), HBM) for v in xsm],
        [sds((2, n)) for n in (m3, m3, c3, m4, m4)] + [sds((2, 4, c4q))],
        [pltpu.VMEM((4, 64, 256), BF16), pltpu.SemaphoreType.DMA((4,))],
        slack=2,
    )

    chip_pairs = [[0, 2], [1, 3]]
    wst = lax.all_gather(wst, "ch", axis_index_groups=chip_pairs)
    last_in = lax.all_gather(last_in, "ch", axis_index_groups=chip_pairs)

    n3, n4 = [(nf3, SMEM)], [(nf4, SMEM)]

    def k(fn):
        return functools.partial(fn, geo)

    hb, hs = geo.hb, geo.hs
    sb4, ss4 = (2, 2, hb // 2, hb // 2, VIEWS, m4), (2, 2, hs // 2, hs // 2, VIEWS, m4)
    wb_shape, ws_shape = ((hb + 2) * hb * VIEWS, 3 * m3), ((hs + 2) * hs * VIEWS, 3 * m3)

    def flow(kind, *arrays):
        return [(a, Flow(kind)) for a in arrays]

    def out(kind, shape, dtype=F32):
        return (sds(shape, dtype), Flow(kind))

    x_all = [(xb + xsm, Flow("x"))]
    w_in, w_ahead, w_back = [
        [(xsm, Flow(kind, base))]
        for kind, base in (("w_in", reduce_at), ("w_ahead", mix_at), ("w_back", mix_at))
    ]
    run = functools.partial(call, geo=geo)
    px1, px3, px4 = (geo.px, VIEWS, m3), (geo.px, VIEWS, c3), (geo.px4, VIEWS, m4)

    pre1, st = run(
        "reduce",
        k(k_reduce),
        smem + n3 + x_all + w_in,
        [fast(px1), sds((2, m3))],
    )
    st, w_mid = after(st, w_mid)
    w_mid = sent(w_mid)
    a1, b1 = sync_stats(st, cnt3)
    pre2, winb, wins, st, devq, keep1 = run(
        "mix",
        k(k_mix),
        smem + n3 + vm(pre1, a1, b1, gs1) + w_ahead,
        [
            fast(px1),
            out("all", wb_shape, BF16),
            out("all", ws_shape, BF16),
            sds((2, m3)),
            out("all", (geo.rows, 128), BF16),
            (sds(px1), Keep(2)),
        ],
        [pltpu.VMEM((1, m3), F32)],
    )
    st, w_mid[2] = after(st, w_mid[2])
    w_mid = passed_on(w_mid)
    w_expand_all = [(w_mid, Flow("w", 0, (m3, c3)))]
    w_narrow_all = [(w_mid, Flow("w", m3 * (c3 // 4 // 128), (c3, m4)))]
    a2, b2 = sync_stats(st, cnt3)
    pre3, act2, st, keep2 = run(
        "expand",
        k(k_expand),
        smem + n3 + vm(pre2, a2, b2, gs2) + w_expand_all,
        [
            fast(px3),
            out("rows", (geo.rows, m3), BF16),
            sds((2, c3)),
            (sds(px1), Keep(2)),
        ],
    )
    a3, b3 = sync_stats(st, cnt3)
    pre4b, pre4s, mid, mids, st, dev3, slope3 = run(
        "narrow",
        k(k_narrow),
        smem + n3 + vm(pre3) + x_all + vm(a3, b3, gs3) + w_narrow_all,
        [
            out("big", sb4),
            out("small", ss4),
            out("rows", (geo.rows, c3), BF16),
            fast((geo.rows4, c3), BF16),
            sds((2, m4)),
            out("rows", (geo.rows, c3), BF16),
            out("rows", (geo.rows, c3), BF16),
        ],
        [pltpu.VMEM((geo.px4, VIEWS, c3), F32)],
        slack=6,
        staying=4 * math.prod(px3),
    )
    st, wst = after(st, wst)
    wst = [wst, over_ch(wst, 1)]
    a4, b4 = sync_stats(st, cnt3)
    w_stride_all = [(wst, Flow("w4", 0, (9 * m4, m4)))]
    pre5, cols, st = run(
        "stride",
        k(k_stride),
        smem
        + n4
        + n3
        + flow("big", pre4b)
        + flow("small", pre4s)
        + vm(a4, b4, gs4)
        + w_stride_all,
        [
            sds(px4),
            out("lead", (9, geo.rows4, m4), BF16),
            sds((2, m4)),
        ],
        [pltpu.VMEM(sb4, F32), pltpu.VMEM(ss4, F32)],
    )
    (dev,) = run(
        "dev_products",
        k(k_dev_products),
        smem + flow("all", devq) + x_all,
        [sds((m3 // 4 + 16, c3), BF16)],
        [pltpu.VMEM((128, c3 // 4), F32)],
        ahead=8,
    )
    a5, b5, (dev,) = sync_stats(st, cnt4, free={last: [dev]})
    a5, last_in, mids = after(a5, last_in, mids)
    at_w, at_b, at_s = c3, c3 + m4, c3 + m4 + cot_rows[0]

    def from_chips(base, rows):
        return [(last_in, Flow("chip", base, (rows, c4q), j)) for j in range(2)]

    wsh, wwi = from_chips(0, c3), from_chips(at_w, m4)
    cots = from_chips(at_b, cot_rows[0]) + from_chips(at_s, cot_rows[1])
    side, st_side = run(
        "short",
        k(k_short),
        smem + n4 + vm(mids) + wsh,
        [fast((2, geo.px4, VIEWS, c4q)), sds((2, 2, c4q))],
    )
    pre6, act5, st = run(
        "widen",
        k(k_widen),
        smem + n4 + vm(pre5, a5, b5, gs5) + wwi + vm(st_side),
        [
            fast((2, geo.px4, VIEWS, c4q)),
            sds((geo.rows4, m4), BF16),
            sds((2, 4, c4q)),
        ],
    )
    a6, b6 = sync_stats(st, cnt4)
    out_b, out_s, dt6, sums = run(
        "total",
        k(k_total),
        smem + n4 + vm(pre6, side, a6, b6, gs6) + cots,
        [
            out("all", (geo.qb, VIEWS, c4q)),
            out("all", (geo.qs, VIEWS, c4q)),
            fast((2, geo.px4, VIEWS, c4q)),
            sds((2, 3, c4q)),
        ],
        [pltpu.VMEM((geo.px4, VIEWS, c4q), F32)],
    )
    ga6, gb6 = sync_sums(sums)
    part5, dz6, dzs, t6 = run(
        "back_wide",
        k(k_back_wide),
        smem
        + n4
        + vm(dt6, pre6, side, a6, b6, gs6, ga6, gb6)
        + wwi,
        [
            sds(px4),
            sds((geo.rows4, c4q), BF16),
            sds((2, geo.rows4, c4q), BF16),
            sds((2, 3, c4q)),
        ],
    )
    other5 = over_ch(part5, 1)
    dt5, sums = call(
        "back_act5",
        k_back_act5,
        n4 + vm(part5, other5, pre5, a5, b5, gs5),
        [sds(px4), sds((2, m4))],
    )
    (dms,) = run(
        "back_short", k_back_short, smem + vm(dzs) + wsh, [sds((geo.px4, VIEWS, c3), BF16)]
    )
    dmo = over_ch(dms, 1)
    dwide, dshort = call(
        "dw_wide",
        k_dw_wide,
        vm(act5, dz6, mids, dzs),
        [sds((m4, c4q), BF16), sds((c3, c4q), BF16)],
    )
    ga5, gb5, (dwide, dshort) = sync_sums(sums, free={0: [dwide, dshort]})
    dt4b, dt4s, dz5, sums, t5 = run(
        "back_stride",
        k(k_back_stride),
        smem
        + n4
        + vm(dt5, pre5, a5, b5, gs5, ga5, gb5)
        + flow("all", pre4b, pre4s)
        + vm(a4, b4, gs4)
        + n3
        + w_stride_all,
        [fast(sb4), fast(ss4), sds((geo.rows4, m4), BF16), sds((2, m4)), sds((2, m4))],
        [pltpu.VMEM((4, geo.rows4, m4), BF16)],
    )

    def halves(rows):
        return [sds((rows // 2, 128), BF16)] * 2, pltpu.VMEM((2, rows // 2, 128), F32)

    outs, full = halves(9 * m4)
    parts = run("dw_stride", k_dw_stride, smem + flow("lead", cols) + vm(dz5), outs, [full])
    stride_train = Train("stride", pairs, parts)
    ga4, gb4, sends = sync_sums(sums, free={last: stride_train.sends()})
    stride_train.launch(sends)
    dt3, dz4, sums, t4 = run(
        "back_narrow",
        k(k_back_narrow),
        smem
        + n3
        + vm(dt4b, dt4s)
        + flow("big", pre4b)
        + flow("small", pre4s)
        + vm(a4, b4, gs4, ga4, gb4)
        + flow("rows", dev3, slope3)
        + vm(a3, b3, dms, dmo)
        + w_narrow_all,
        [
            fast((geo.rows, c3), BF16),
            out("rows", (geo.rows, m4), BF16),
            sds((2, c3)),
            sds((2, m4)),
        ],
    )
    came = stride_train.received
    stride_train.advance()
    ga3, gb3, sends = sync_sums(sums, wait={last: came}, free={last: stride_train.sends()})
    stride_train.launch(sends)
    dt2, dz3, dt3q, sums, t3 = run(
        "back_expand",
        k(k_back_expand),
        smem
        + n3
        + vm(dt3)
        + flow("rows", dev3)
        + vm(a3, b3, gs3, ga3, gb3)
        + flow("px", keep2)
        + vm(a2, b2, gs2)
        + w_expand_all,
        [
            fast(px1),
            out("rows", (geo.rows, c3 // 4), BF16),
            out("rows", (geo.rows, c3 // 4), BF16),
            sds((2, m3)),
            sds((2, c3)),
        ],
        [
            pltpu.VMEM((2 * hb * VIEWS, c3), BF16),
            pltpu.VMEM((2 * hs * VIEWS, c3), BF16),
        ],
    )
    came = stride_train.received
    stride_train.advance()
    outs, full = halves(c3 + (c3 // 4 // 128) * m3)
    parts = call("dw_mid", k_dw_mid, smem + vm(mid, dz4, act2, dz3), outs, [full])
    mid_train = Train("mid", pairs, parts)
    ga2, gb2, (mid_send, *sends) = sync_sums(
        sums, wait={last: came}, free={0: mid_train.sends(), last: stride_train.sends()}
    )
    mid_train.launch([mid_send])
    stride_train.launch(sends)
    dt1, dz2, sums, t2, dt1q = run(
        "back_mix",
        k(k_back_mix),
        smem
        + n3
        + vm(dt2)
        + flow("px", keep2)
        + vm(a2, b2, gs2, ga2, gb2)
        + flow("px", keep1)
        + vm(a1, b1, gs1)
        + w_back,
        [
            out("px", px1),
            out("all", (geo.rows, m3), BF16),
            sds((2, m3)),
            sds((2, m3)),
            out("rows", (geo.rows, 128), BF16),
        ],
        [pltpu.VMEM(wb_shape, BF16), pltpu.VMEM(ws_shape, BF16)],
    )
    came = stride_train.received + mid_train.received
    stride_train.advance()
    mid_train.advance()
    mix_rows = 9 * m3 // 128 * (m3 // 4)
    rows_last = mix_rows + c3 // 128 * (m3 // 4)
    outs, _ = halves(rows_last)
    parts = run(
        "dw_last",
        k(k_dw_last),
        smem + flow("all", winb, wins, dz2) + x_all + flow("all", dt1q),
        outs,
        [
            pltpu.VMEM((128, 3 * m3), F32),
            pltpu.VMEM((128, c3), F32),
            pltpu.VMEM((rows_last, 128), F32),
        ],
        ahead=8,
        hold=True,
    )
    last_train = Train("last", fours, parts)
    dwide, dshort, dev = lax.psum((dwide, dshort, dev), "img")
    wide = [dwide, dshort, dev]
    ga1, gb1, (last_send, mid_send, *sends) = sync_sums(
        sums,
        wait={last: came},
        free={last: last_train.sends() + mid_train.sends() + stride_train.sends()},
    )
    last_train.launch([last_send])
    mid_train.launch([mid_send])
    stride_train.launch(sends)
    dwide, dshort, dev = wide
    gxb, gxs, t1, coef = run(
        "back_reduce",
        k(k_back_reduce),
        smem
        + n3
        + flow("px", dt1, keep1)
        + vm(a1, b1, gs1, ga1, gb1)
        + flow("rows", dt3q)
        + w_in,
        [
            out("big_px", (geo.pb, VIEWS, c3 // 4)),
            out("small_px", (geo.ps, VIEWS, c3 // 4)),
            sds((2, m3)),
            sds((3, m3)),
        ],
    )
    def unpack(name, a, b, plan):
        shapes = [((lead,) if lead > 1 else ()) + (rows, cols) for lead, rows, cols in plan]
        return call(
            name,
            functools.partial(k_unpack, plan),
            smem + vm(a, b),
            [sds(shape) for shape in shapes],
            [pltpu.VMEM((2,) + a.shape, F32)],
        )

    trains = (last_train, mid_train, stride_train)
    gxb, dwide, dshort, dev, coef, *came = after(
        gxb, dwide, dshort, dev, coef, *[train.received[0] for train in trains]
    )
    for train, first in zip(trains, came):
        train.received[0] = first
    halves_in = [v.reshape(1, 9 * m4 // 2, 128) for v in stride_train.finish()]
    dwide, dshort, dstride = run(
        "out_first",
        k_out_first,
        smem
        + flow("lead", dwide.reshape(2, m4 // 2, c4q), dshort.reshape(4, c3 // 4, c4q))
        + flow("all", *halves_in),
        [
            out("lead", (2, m4 // 2, c4q)),
            out("lead", (4, c3 // 4, c4q)),
            out("all", (2, 9 * m4 // 2, 128)),
        ],
        ahead=4,
    )
    mid_train.to_last()
    last_train.to_last()
    dstride, mid_train.received[0], last_train.received[0] = after(
        dstride, mid_train.received[0], last_train.received[0]
    )
    dnarrow, dexpand = unpack(
        "out_mid", *mid_train.finish(), [(1, c3, m4 // 4), (1, m3, c3 // 4)]
    )
    coef = lax.dynamic_slice_in_dim(coef, q * (m3 // 4), m3 // 4, 1)[:, :, None]
    mine, other = last_train.finish()
    dmix, dreduce = call(
        "out_last",
        k_out_last,
        smem + vm(mine, other, dev, coef),
        [sds((9, m3 // 4, m3)), sds((m3 // 4, c3))],
        [pltpu.VMEM((2,) + mine.shape, F32)],
    )

    def views_first(v, side):
        return jnp.transpose(v.reshape(side, side, VIEWS, v.shape[2]), (2, 0, 1, 3))

    small = call(
        "small_outputs",
        k_small_outputs,
        smem + vm(t1, t2, t3, t4, t5, t6[0], gxs[0]),
        [sds((2, m3 // 4))] * 2
        + [sds((1, c3 // 4))] * 2
        + [sds((2, m4 // 4))] * 2
        + [sds((2, c4q))] * 2,
        slack=4,
    )
    small[2], small[3] = small[2][0], small[3][0]
    return (
        views_first(out_b, hb // 2),
        views_first(out_s, hs // 2),
        views_first(gxb, hb),
        views_first(gxs, hs),
        dreduce.T,
        jnp.transpose(dmix.reshape(3, 3, m3 // 4, m3), (0, 1, 3, 2)),
        dexpand,
        dnarrow,
        dstride.reshape(3, 3, m4, m4 // 4),
        dwide.reshape(m4, c4q),
        dshort.reshape(c3, c4q),
        *small,
    )


def solution(mesh):
    act = P("img", None, None, "ch")
    flat, taps, vec = P(None, "ch"), P(None, None, None, "ch"), P("ch")
    in_specs = (act,) * 4 + (P(), flat, taps, flat, flat, taps, flat, flat)
    in_specs += (flat, flat, vec, vec, flat, flat, flat, flat)
    out_specs = (act,) * 4 + (flat, taps, flat, flat, taps, flat, flat)
    out_specs += (flat, flat, vec, vec, flat, flat, flat, flat)
    return jax.shard_map(
        functools.partial(per_device, mesh.shape["img"], mesh.shape["ch"]),
        mesh=mesh,
        in_specs=in_specs,
        out_specs=out_specs,
        check_vma=False,
    )
```

```python
import functools
import math

import jax
import jax.numpy as jnp
from jax import lax
from jax.experimental import pallas as pl
from jax.experimental.pallas import tpu as pltpu
from jax.sharding import PartitionSpec as P

EPS = 1e-05
G0 = 0.7978845608028654
G1 = G0 * 0.044715
F32 = jnp.float32
BF16 = jnp.bfloat16
VIEWS = 8

ANY = pl.BlockSpec(memory_space=pl.ANY)
HBM = pl.BlockSpec(memory_space=pltpu.HBM)
VMEM = pl.BlockSpec(memory_space=pltpu.VMEM)
SMEM = pl.BlockSpec(memory_space=pltpu.SMEM)


def sds(shape, dtype=F32):
    return jax.ShapeDtypeStruct(tuple(shape), dtype)


class Flow:
    WHOLE = ("w", "w4", "all", "chip", "w_in", "w_ahead", "w_back")

    def __init__(self, kind, base=0, shape=None, which=0):
        self.kind, self.base, self.shape, self.which = kind, base, shape, which

    def keys(self, geo, shape):
        parts = (0, 1)
        if self.kind in ("big", "big_px"):
            parts = (0,)
        if self.kind in ("small", "small_px"):
            parts = (1,)
        if self.kind not in ("lead",) + self.WHOLE:
            return [(part, n) for part in parts for n in range(len(geo.groups[part]))]
        if self.kind == "lead":
            return list(range(shape[0]))
        return [None]

    def buffer(self, geo, shapes, dtype):
        if self.kind == "x":
            return pltpu.VMEM((4, geo.rows, shapes[0][1]), dtype)
        if self.kind == "w":
            return pltpu.VMEM(self.shape, dtype)
        if self.kind in ("chip", "w4"):
            return pltpu.VMEM(self.shape, dtype)
        c = shapes[0][-1]
        if self.kind.startswith("w_"):
            return pltpu.VMEM({"w_in": (4, c, c), "w_ahead": (3, c, 3 * c), "w_back": (9, c, c)}[self.kind], dtype)
        return pltpu.VMEM(tuple(shapes[0]), dtype)

    def pairs(self, geo, q, hbm, buf, key):
        if self.kind == "w":
            rows, n = buf.shape[0], buf.shape[1] // 4
            found = []
            for p in range(4):
                for b in range(n // 128):
                    at = pl.ds(pl.multiple_of((q ^ p) * n + 128 * b, 128), 128)
                    found.append((hbm[p].at[pl.ds(self.base + rows * b, rows)], buf.at[:, at]))
            return found
        if self.kind.startswith("w_"):
            c = buf.shape[1]
            n = c // 4
            found = []
            for p in range(4):
                at = pl.ds(pl.multiple_of((q ^ p) * n, n), n)
                for t in range(4 if self.kind == "w_in" else 9):
                    src = hbm[p].at[pl.ds(self.base + n * t, n)]
                    if self.kind == "w_ahead":
                        found.append((src, buf.at[t // 3, at, pl.ds(t % 3 * c, c)]))
                    else:
                        found.append((src, buf.at[t, at]))
            return found
        if self.kind == "chip":
            return [(hbm[0].at[(q >> 1) ^ self.which, pl.ds(self.base, buf.shape[0])], buf)]
        if self.kind == "w4":
            n = buf.shape[1] // 4
            found = []
            for chip in range(2):
                for other in range(2):
                    at = pl.multiple_of((2 * chip + ((q & 1) ^ other)) * n, n)
                    found.append((hbm[other].at[chip], buf.at[:, pl.ds(at, n)]))
            return found
        if key is None:
            return [(hbm[0], buf)]
        if self.kind == "lead":
            return [(hbm[0].at[key], buf.at[key])]
        part, group = key
        i, end = geo.groups[part][group]
        pix, npx, row, nrows = geo.step(part, i)
        npx, nrows, first = npx * (end - i), nrows * (end - i), pix - geo.parts[part][1]
        if self.kind == "px":
            at = pl.ds(pix, npx)
        elif self.kind == "rows":
            at = pl.ds(row, nrows)
        elif self.kind in ("big_px", "small_px"):
            at = pl.ds(first, npx)
        elif self.kind == "x":
            local = pl.ds(first * VIEWS, nrows)
            return [
                (hbm[4 * part + p].at[local], buf.at[q ^ p, pl.ds(row, nrows)]) for p in range(4)
            ]
        else:
            at = pl.ds(i, end - i)
            return [(hbm[0].at[:, :, at], buf.at[:, :, at])]
        return [(hbm[0].at[at], buf.at[at])]


class Moves:
    def __init__(self, geo, q, ahead):
        self.geo, self.q, self.flows, self.kept, self.ahead = geo, q, [], [], ahead

    def add(self, flow, hbm, buf, sem, inward):
        self.flows.append((flow, hbm, buf, sem, inward))

    def copies(self, entry, key):
        flow, hbm, buf, sem, inward = entry
        if flow.kind in flow.WHOLE:
            at = 0
        elif flow.kind == "lead":
            at = key
        elif flow.kind in ("px", "rows", "x"):
            at = (0, len(self.geo.groups[0]))[key[0]] + key[1]
        else:
            at = key[1]
        pairs = flow.pairs(self.geo, self.q, hbm, buf, key)
        return [
            pltpu.make_async_copy(*((a, b) if inward else (b, a)), sem.at[n, at])
            for n, (a, b) in enumerate(pairs)
        ]

    def entries(self, inward, key):
        for entry in self.flows:
            flow = entry[0]
            if entry[4] != inward:
                continue
            if key is None:
                fits = flow.kind in flow.WHOLE
            elif isinstance(key, int):
                fits = flow.kind == "lead" and key < entry[1][0].shape[0]
            else:
                kinds = ("px", "rows", "x") + (("big", "big_px"), ("small", "small_px"))[key[0]]
                fits = flow.kind in kinds
            if fits:
                yield entry

    def start(self, inward, key):
        for entry in self.entries(inward, key):
            for c in self.copies(entry, key):
                c.start()

    def wait(self, inward, key):
        for entry in self.entries(inward, key):
            for c in self.copies(entry, key):
                c.wait()

    def begin(self, hold):
        self.order = [(part, n) for part in range(2) for n in range(len(self.geo.groups[part]))]
        if hold:
            self.start(True, None)
            return
        self.start(True, self.order[0])
        self.start(True, None)
        for key in self.order[1 : self.ahead]:
            self.start(True, key)
        for n in range(self.ahead):
            self.start_lead(n)
        streams = any(e[4] and e[0].kind not in ("lead",) + Flow.WHOLE for e in self.flows)
        if not streams:
            for c in self.kept:
                c.start()

    def start_steps(self):
        for key in self.order:
            self.start(True, key)

    def start_lead(self, n):
        for entry in self.flows:
            if entry[4] and entry[0].kind == "lead" and n < entry[1][0].shape[0]:
                for c in self.copies(entry, n):
                    c.start()

    def ready(self):
        self.wait(True, None)

    def arrive(self, *key):
        if len(key) == 1:
            self.wait(True, key[0])
            self.start_lead(key[0] + self.ahead)
            return
        self.wait(True, key)
        at = self.order.index(key)
        if at + self.ahead < len(self.order):
            self.start(True, self.order[at + self.ahead])
        streams = any(e[4] and e[0].kind not in ("lead",) + Flow.WHOLE for e in self.flows)
        if at == 0 and streams:
            for c in self.kept:
                c.start()

    def leave(self, *key):
        self.start(False, key if len(key) > 1 else key[0])

    def send(self, *refs):
        for entry in self.entries(False, None):
            if any(entry[2] is r for r in refs):
                for c in self.copies(entry, None):
                    c.start()

    def finish(self):
        for entry in self.flows:
            if not entry[4]:
                shape = entry[1][0].shape
                for key in entry[0].keys(self.geo, shape):
                    for c in self.copies(entry, key):
                        c.wait()
        for c in self.kept:
            c.wait()


class Keep:
    kind = "keep"

    def __init__(self, source):
        self.source = source


def fast(shape, dtype=F32):
    return pltpu.VMEM(tuple(shape), dtype)


def scoped_bytes(v):
    return math.prod(v.shape) * jnp.dtype(v.dtype).itemsize


def in_hbm(v):
    return pltpu.with_memory_space_constraint(v, pltpu.HBM)


def call(name, kernel, ins, outs, scratch=(), cost=None, order=False, geo=None, slack=14, ahead=3, hold=False, staying=0):
    if order:
        inner, n_in, n_out = kernel, len(ins), len(outs)

        def kernel(*refs):
            rest = refs[n_in:]
            return inner(*refs[:n_in], *rest[n_out:], *rest[:n_out])

    outs = [o if isinstance(o, tuple) else (o, VMEM) for o in outs]
    arrays, specs, moved = [], [], []
    for a, spec in ins:
        group = a if isinstance(a, list) else [a]
        flow = isinstance(spec, Flow)
        arrays += [in_hbm(v) for v in group] if flow else group
        specs += [HBM if flow else spec] * len(group)
        moved.append((spec if flow else None, len(group), [v.shape for v in group], group[0].dtype))
    out_shapes, out_specs = [], []
    for shape, spec in outs:
        flow = isinstance(spec, (Flow, Keep))
        out_shapes.append(pltpu.HBM(shape.shape, shape.dtype) if flow else shape)
        out_specs.append(HBM if flow else spec)
        moved.append((spec if flow else None, 1, [shape.shape], shape.dtype))
    extra = []
    for flow, _, shapes, dtype in moved:
        if isinstance(flow, Keep):
            extra += [pltpu.SemaphoreType.DMA((1,))]
        elif flow:
            keys = len(flow.keys(geo, shapes[0]))
            copies = {"x": 4, "w": 4, "w4": 4, "w_in": 16, "w_ahead": 36, "w_back": 36}.get(flow.kind, 1)
            if flow.kind == "w":
                copies = flow.shape[1] // 128
            extra += [flow.buffer(geo, shapes, dtype), pltpu.SemaphoreType.DMA((copies, keys))]
    body = kernel
    if extra:

        def body(*refs):
            n_io = sum(n for _, n, _, _ in moved)
            given, own, rest = list(refs[:n_io]), refs[n_io : n_io + len(scratch)], refs[n_io + len(scratch) :]
            rest = list(rest)
            moves = Moves(geo, given[0][0], ahead)
            args = []
            for n, (flow, count, _, _) in enumerate(moved):
                group, given = given[:count], given[count:]
                if not flow:
                    args += group
                    continue
                if isinstance(flow, Keep):
                    moves.kept.append(pltpu.make_async_copy(args[flow.source], group[0], rest[0].at[0]))
                    rest = rest[1:]
                    continue
                buf, sem = rest[:2]
                rest = rest[2:]
                moves.add(flow, group, buf, sem, n < len(ins))
                args.append(buf)
            moves.begin(hold)
            kernel(moves, *args, *own)
            moves.finish()

    scratch = list(scratch)
    def held(v):
        pinned = "vmem" in str(getattr(v, "memory_space", "")).lower()
        return 0 if pinned else scoped_bytes(v)

    need = sum(held(jax.typeof(a)) for a, spec in zip(arrays, specs) if spec is VMEM)
    need += sum(held(o) for o, spec in zip(out_shapes, out_specs) if spec is VMEM)
    need += sum(
        scoped_bytes(v)
        for v in scratch + extra
        if getattr(v, "memory_space", None) == pltpu.VMEM
    )
    need -= staying
    result = pl.pallas_call(
        body,
        out_shape=out_shapes,
        in_specs=specs,
        out_specs=out_specs,
        scratch_shapes=scratch + extra,
        compiler_params=pltpu.CompilerParams(vmem_limit_bytes=need + need // 16 + (slack << 20)),
        cost_estimate=cost,
        name=name,
    )(*arrays)
    return list(result)


def vm(*arrays):
    return [(a, VMEM) for a in arrays]


def nn(a, b):
    return lax.dot_general(a, b, (((1,), (0,)), ((), ())), preferred_element_type=F32)


def nt(a, b):
    return lax.dot_general(a, b, (((1,), (1,)), ((), ())), preferred_element_type=F32)


def tn(a, b):
    return lax.dot_general(a, b, (((0,), (0,)), ((), ())), preferred_element_type=F32)


def gelu(t):
    half = 0.5 * t
    return half + half * jnp.tanh(t * (G0 + G1 * (t * t)))


def gelu_both(t):
    sq = t * t
    half = 0.5 * t
    th = jnp.tanh(t * (G0 + G1 * sq))
    return half + half * th, 0.5 + 0.5 * th + half * (1.0 - th * th) * (G0 + (3.0 * G1) * sq)


def gelu_slope(t):
    sq = t * t
    th = jnp.tanh(t * (G0 + G1 * sq))
    return 0.5 * (1.0 + th) + (0.5 * t) * (1.0 - th * th) * (G0 + (3.0 * G1) * sq)


def live_rows(count, chans):
    return (lax.broadcasted_iota(jnp.int32, (VIEWS, chans), 0) < count).astype(F32)


def rows_sum(v):
    return jnp.sum(v, axis=0, keepdims=True)


def merged(sa, sb, na, nb):
    total = na + nb
    mean = (na * sa[0:1] + nb * sb[0:1]) / total
    diff = sb[0:1] - sa[0:1]
    square = sa[1:2] + sb[1:2] + diff * diff * (na * nb / total)
    return mean, lax.rsqrt(square / total + EPS)


def as_rows(v):
    return v.reshape(v.shape[0] * v.shape[1], v.shape[2])


def as_pix_rows(v):
    return v.reshape(v.shape[0] * v.shape[1], VIEWS, v.shape[3])


def as_pix(v):
    return v.reshape(v.shape[0] // VIEWS, VIEWS, v.shape[1])


class Geo:
    def __init__(self, hb, hs):
        self.hb, self.hs = hb, hs
        self.pb, self.ps = hb * hb, hs * hs
        self.px = self.pb + self.ps
        self.rows = self.px * VIEWS
        self.qb, self.qs = self.pb // 4, self.ps // 4
        self.px4 = self.qb + self.qs
        self.rows4 = self.px4 * VIEWS
        self.parts = ((hb, 0), (hs, self.pb))
        self.groups = [self.cuts(hb // 2, 1), self.cuts(hs // 2, 2)]
        self.spans = [[list(range(n))[: n // 2], list(range(n))[n // 2 :]] for n in map(len, self.groups)]
        self.bands = [[(0, hb // 2), (hb // 2, hb)], [(0, hs)]]

    @staticmethod
    def cuts(steps, first):
        at = sorted({0, steps} | set(range(first, steps, 2)))
        return list(zip(at[:-1], at[1:]))

    @staticmethod
    def aligned(n):
        return n if isinstance(n, int) else pl.multiple_of(n, 16)

    def step(self, part, i):
        side, start = self.parts[part]
        npx = 2 * side
        return start + i * npx, npx, self.aligned((start + i * npx) * VIEWS), npx * VIEWS

    def staged(self, io, before, product, carries):
        out = []
        for part in range(2):
            carry = carries[part]
            for span in self.spans[part]:
                lo, hi = self.groups[part][span[0]][0], self.groups[part][span[-1]][1]
                for n in span:
                    io.arrive(part, n)
                pix, npx, row, nrows = self.step(part, lo)
                if before:

                    def early(i, c, part=part):
                        before(part, i, *self.step(part, i))
                        return c

                    lax.fori_loop(lo, hi, early, 0)
                carry = product(part, pix, npx * (hi - lo), row, nrows * (hi - lo), carry)
                for n in span:
                    io.leave(part, n)
            out.append(carry)
        return out

    def loop(self, body, carries, arrive=None, leave=None):
        out = []
        for part in range(2):

            def run(i, carry, part=part):
                for n, (lo, hi) in enumerate(self.groups[part]):
                    if arrive:
                        pl.when(i == lo)(functools.partial(arrive.arrive, part, n))
                carry = body(part, i, *self.step(part, i), carry)
                for n, (lo, hi) in enumerate(self.groups[part]):
                    if leave:
                        pl.when(i == hi - 1)(functools.partial(leave.leave, part, n))
                return carry

            out.append(lax.fori_loop(0, self.groups[part][-1][1], run, carries[part]))
        return out


def finish_stats(geo, ref, sums, lives, count, out, quarter=None):
    mean = (rows_sum(sums[0] * lives[0]) + rows_sum(sums[1] * lives[1])) / count

    def body(part, i, pix, npx, row, nrows, carry):
        dev = ref[pl.ds(pix, npx)] - mean
        return carry + jnp.sum(dev * dev, axis=0)

    zero = jnp.zeros(sums[0].shape, F32)
    sq = geo.loop(body, [zero, zero])
    out[0:1] = mean
    out[1:2] = rows_sum(sq[0] * lives[0]) + rows_sum(sq[1] * lives[1])


def block_stats(geo, value, lives, count):
    big, small = value[: geo.qb], value[geo.qb :]
    mean = (
        rows_sum(jnp.sum(big, axis=0) * lives[0]) + rows_sum(jnp.sum(small, axis=0) * lives[1])
    ) / count
    db, ds = big - mean, small - mean
    square = rows_sum(jnp.sum(db * db, axis=0) * lives[0]) + rows_sum(
        jnp.sum(ds * ds, axis=0) * lives[1]
    )
    return mean, square


def k_reduce(geo, io, me, nf, xs, wt, pre, stats):
    io.ready()
    chans = wt.shape[1]
    lives = [live_rows(me[1], chans), live_rows(me[2], chans)]

    def product(part, pix, npx, row, nrows, carry):
        acc = None
        for j in range(4):
            d = nt(xs[j, row : row + nrows, :], wt[j])
            acc = d if acc is None else acc + d
        z = as_pix(acc)
        pre[pix : pix + npx] = z
        return carry + jnp.sum(z, axis=0)

    zero = jnp.zeros((VIEWS, chans), F32)
    sums = geo.staged(io, None, product, [zero, zero])
    finish_stats(geo, pre, sums, lives, nf[0], stats)


def k_counts(ni, sizes, counts, me, nf3, cnt3, nf4, cnt4):
    img = lax.axis_index("img")
    levels = ni.bit_length() - 1
    me[0] = lax.axis_index("ch").astype(jnp.int32)
    me[1] = counts[img, 0]
    me[2] = counts[img, 1]
    me[3] = img
    for (big, small), nf, cnt in zip(sizes, (nf3, nf4), (cnt3, cnt4)):

        def group(shift, index):
            def add(i, total):
                at = index * (1 << shift) + i
                return total + counts[at, 0] * big + counts[at, 1] * small

            return lax.fori_loop(0, 1 << shift, add, jnp.int32(0)).astype(F32)

        nf[0] = group(0, img)
        for m in range(2):
            nf[1 + m] = group(levels - 1, (img >> (levels - 1)) ^ m)
        row, k = 0, 0
        while k < levels - 1:
            bits = 2 if k == 0 else 1
            for m in range(8):
                cnt[row + m] = group(k, (img >> k) ^ m) if m < 1 << bits else jnp.float32(0.0)
            row, k = row + 8, k + bits


def k_pack_params(gm3, sm3, go3, so3, gm4, sm4, go4, so4, out, rows):
    rows[...] = jnp.zeros(rows.shape, F32)
    rows[0:2, 0:64] = gm3[...]
    rows[2:4, 0:64] = sm3[...]
    for b in range(2):
        lanes = slice(128 * b, 128 * b + 128)
        rows[4 + b : 5 + b] = go3[:, lanes]
        rows[6 + b : 7 + b] = so3[:, lanes]
    rows[8:10] = gm4[...]
    rows[10:12] = sm4[...]
    for n in range(2):
        for b in range(4):
            lanes = slice(128 * b, 128 * b + 128)
            rows[12 + 4 * n + b : 13 + 4 * n + b] = go4[n : n + 1, lanes]
            rows[20 + 4 * n + b : 21 + 4 * n + b] = so4[n : n + 1, lanes]
    v = rows[...]
    high = v.astype(BF16)
    rest = v - high.astype(F32)
    mid = rest.astype(BF16)
    low = (rest - mid.astype(F32)).astype(BF16)
    out[0:32, 0:128] = high
    out[0:32, 128:256] = mid
    out[32:64, 0:128] = low
    out[32:64, 128:256] = jnp.zeros_like(low)


def k_unpack_params(base, me, p0, p1, p2, p3, gs1, gs2, gs3, gs4, gs5, gs6, buf, sem):
    copies = [
        pltpu.make_async_copy(p.at[pl.ds(base, 64)], buf.at[n], sem.at[n])
        for n, p in enumerate((p0, p1, p2, p3))
    ]
    for c in copies:
        c.start()
    for c in copies:
        c.wait()
    rows = []
    for n in range(4):
        v = buf[n].astype(F32)
        rows.append(v[0:32, 0:128] + v[0:32, 128:256] + v[32:64, 0:128])
    odd = me[0] & 1
    for chip in range(2):
        mine, other = rows[2 * chip][:, 0:64], rows[2 * chip + 1][:, 0:64]
        both = jnp.where(
            odd == 0,
            jnp.concatenate([mine, other], axis=1),
            jnp.concatenate([other, mine], axis=1),
        )
        at = pl.ds(pl.multiple_of(((me[0] >> 1) ^ chip) * 128, 128), 128)
        for n, gs in enumerate((gs1, gs2)):
            gs[0:1, at] = both[n : n + 1]
            gs[1:2, at] = both[2 + n : 3 + n]
    for p, v in enumerate(rows):
        for b in range(2):
            at = pl.ds(pl.multiple_of((me[0] ^ p) * 256 + 128 * b, 128), 128)
            gs3[0:1, at] = v[4 + b : 5 + b]
            gs3[1:2, at] = v[6 + b : 7 + b]
        at = pl.ds(pl.multiple_of((me[0] ^ p) * 128, 128), 128)
        for n, gs in enumerate((gs4, gs5)):
            gs[0:1, at] = v[8 + n : 9 + n]
            gs[1:2, at] = v[10 + n : 11 + n]
    for chip in range(2):
        v = rows[2 * chip]
        for n in range(2):
            for b in range(4):
                lanes = slice(128 * b, 128 * b + 128)
                gs6[chip, 2 * n : 2 * n + 1, lanes] = v[12 + 4 * n + b : 13 + 4 * n + b]
                gs6[chip, 2 * n + 1 : 2 * n + 2, lanes] = v[20 + 4 * n + b : 21 + 4 * n + b]


def k_merge(first, n, cnt, *refs):
    arrays, out = refs[:n], refs[n]
    for at in range(0, out.shape[-2], 2):
        mean_at, sq_at = (..., slice(at, at + 1), slice(None)), (..., slice(at + 1, at + 2), slice(None))
        groups = [(cnt[first + m], a[mean_at], a[sq_at]) for m, a in enumerate(arrays)]
        while len(groups) > 1:
            pairs = []
            for (na, ma, qa), (nb, mb, qb) in zip(groups[::2], groups[1::2]):
                total = na + nb
                diff = mb - ma
                pairs.append(
                    (total, (na * ma + nb * mb) / total, qa + qb + diff * diff * (na * nb / total))
                )
            groups = pairs
        out[mean_at], out[sq_at] = groups[0][1], groups[0][2]


def k_add(n, *refs):
    values = [r[...] for r in refs[:n]]
    while len(values) > 1:
        values = [a + b for a, b in zip(values[::2], values[1::2])]
    refs[n][...] = values[0]


def side_shift(v, by):
    zero = jnp.zeros((v.shape[0], 1) + v.shape[2:], v.dtype)
    if by > 0:
        return jnp.concatenate([zero, v[:, :-1]], axis=1)
    return jnp.concatenate([v[:, 1:], zero], axis=1)


def store_shifted(buf, row, nrows, side, v, order):
    img = v.reshape(2, side, VIEWS, v.shape[-1])
    chans = v.shape[-1]
    forms = [side_shift(img, 1), img, side_shift(img, -1)]
    for lane, k in enumerate(order):
        flat = forms[k].reshape(nrows, chans).astype(BF16)
        buf[pl.ds(row, nrows), lane * chans : (lane + 1) * chans] = flat


def put_phases(ref, i, v):
    for k in range(4):
        ref[k // 2, k % 2, i] = v[k // 2, :, k % 2]


def get_phases(ref, i):
    rows = [jnp.stack([ref[r, 0, i], ref[r, 1, i]], axis=1) for r in range(2)]
    return jnp.stack(rows)


def zero_edges(buf, edge):
    total = buf.shape[0]
    buf[0:edge, :] = jnp.zeros((edge, buf.shape[1]), BF16)
    buf[total - edge : total, :] = jnp.zeros((edge, buf.shape[1]), BF16)


def k_mix(geo, io, me, nf, pre1, sa, sb, gs, w, pre2, wb, ws, stats, dev, center):
    chans = pre1.shape[-1]
    lives = [live_rows(me[1], chans), live_rows(me[2], chans)]
    mean, inv = merged(sa[...], sb[...], nf[1], nf[2])
    scale, shift = gs[0:1] * inv, gs[1:2]
    bufs = (wb, ws)
    for part, (side, _) in enumerate(geo.parts):
        zero_edges(bufs[part], side * VIEWS)

    def act(part, i, pix, npx, row, nrows, carry):
        a = gelu((pre1[pl.ds(pix, npx)] - mean) * scale + shift)
        own = (pre1[pl.ds(pix, npx), :, lanes] - center[:, lanes]) * lives[part][:, 0:128]
        dev[pl.ds(row, nrows), :] = as_rows(own).astype(BF16)
        side = geo.parts[part][0]
        at = pl.multiple_of(side * VIEWS + i * nrows, 16)
        store_shifted(bufs[part], at, nrows, side, a, (0, 1, 2))
        return carry

    lanes, _ = own_block(me)
    center[...] = mean
    geo.loop(act, [0, 0], io)
    io.send(wb, ws, dev)
    io.ready()

    sums = [jnp.zeros((VIEWS, chans), F32)] * 2
    for part, (side, start) in enumerate(geo.parts):
        for lo, hi in geo.bands[part]:
            acc = None
            for r in range(3):
                at = (lo + r) * side * VIEWS
                d = nt(bufs[part][at : at + (hi - lo) * side * VIEWS, :], w[r])
                acc = d if acc is None else acc + d
            z = as_pix(acc)
            pre2[start + lo * side : start + hi * side] = z
            sums[part] = sums[part] + jnp.sum(z, axis=0)
    finish_stats(geo, pre2, sums, lives, nf[0], stats)


def k_expand(geo, io, me, nf, pre2, sa, sb, gs, w, pre3, act2, stats):
    chans = w.shape[1]
    lives = [live_rows(me[1], chans), live_rows(me[2], chans)]
    mean, inv = merged(sa[...], sb[...], nf[1], nf[2])
    scale, shift = gs[0:1] * inv, gs[1:2]

    def before(part, i, pix, npx, row, nrows):
        a = as_rows(gelu((pre2[pl.ds(pix, npx)] - mean) * scale + shift)).astype(BF16)
        act2[pl.ds(row, nrows), :] = a

    def product(part, pix, npx, row, nrows, carry):
        total = []
        for j in range(4):
            at = slice(256 * j, 256 * j + 256)
            z = as_pix(nn(act2[row : row + nrows, :], w[:, at]))
            pre3[pix : pix + npx, :, at] = z
            total.append(jnp.sum(z, axis=0))
        return carry + jnp.concatenate(total, axis=1)

    io.ready()
    zero = jnp.zeros((VIEWS, chans), F32)
    sums = geo.staged(io, before, product, [zero, zero])
    finish_stats(geo, pre3, sums, lives, nf[0], stats)


def k_narrow(geo, io, me, nf, pre3, xs, sa, sb, gs, w, pre4b, pre4s, mid, mids, stats, dev3, slope3, mid_even):
    chans = w.shape[1]
    lives = [live_rows(me[1], chans), live_rows(me[2], chans)]
    mean, inv = merged(sa[...], sb[...], nf[1], nf[2])
    scale, shift = gs[0:1] * inv, gs[1:2]
    pre4 = (pre4b, pre4s)

    def body(part, i, pix, npx, row, nrows, carry):
        side = geo.parts[part][0]
        half = side // 2
        for j in range(4):
            at = slice(256 * j, 256 * j + 256)
            dev = pre3[pl.ds(pix, npx), :, at] - mean[:, at]
            x = as_pix(xs[j, pl.ds(row, nrows), :].astype(F32))
            a, slope = gelu_both(dev * scale[:, at] + shift[:, at] + x)
            mid[pl.ds(row, nrows), at] = as_rows(a).astype(BF16)
            dev3[pl.ds(row, nrows), at] = as_rows(dev).astype(BF16)
            slope3[pl.ds(row, nrows), at] = as_rows(slope).astype(BF16)
            even = a.reshape(2, half, 2, VIEWS, 256)[0, :, 0]
            mid_even[pl.ds((0, geo.qb)[part] + half * i, half), :, at] = even
        z = nn(mid[pl.ds(row, nrows), :], w[...])
        put_phases(pre4[part], i, z.reshape(2, half, 2, VIEWS, chans))
        return carry + jnp.sum(as_pix(z), axis=0)

    io.ready()
    zero = jnp.zeros((VIEWS, chans), F32)
    sums = geo.loop(body, [zero, zero], io, io)
    mean4 = (rows_sum(sums[0] * lives[0]) + rows_sum(sums[1] * lives[1])) / nf[0]
    mids[...] = as_rows(mid_even[...]).astype(BF16)
    io.send(mids)
    sq = []
    for part in range(2):

        def dev2(i, carry, part=part):
            for k in range(4):
                d = pre4[part][k // 2, k % 2, i] - mean4
                carry = carry + jnp.sum(d * d, axis=0)
            return carry

        sq.append(lax.fori_loop(0, geo.parts[part][0] // 2, dev2, zero))
    stats[0:1] = mean4
    stats[1:2] = rows_sum(sq[0] * lives[0]) + rows_sum(sq[1] * lives[1])


def k_short(geo, io, me, nf, mids, w0, w1, side, stats):
    io.ready()
    chans = w0.shape[1]
    lives = [live_rows(me[1], chans), live_rows(me[2], chans)]
    for j, w in enumerate((w0, w1)):
        z = as_pix(nn(mids[...], w[...]))
        side[j] = z
        io.leave(j)
        mean, square = block_stats(geo, z, lives, nf[0])
        stats[j] = jnp.concatenate([mean, square], axis=0)


def k_stride(geo, io, me, nf, n4, pre4b, pre4s, sa, sb, gs, w, pre5, cols, stats, sb_act, ss_act):
    chans = pre4b.shape[-1]
    lives = [live_rows(me[1], chans), live_rows(me[2], chans)]
    mean, inv = merged(sa[...], sb[...], n4[1], n4[2])
    scale, shift = gs[0:1] * inv, gs[1:2]
    srcs, dsts = (pre4b, pre4s), (sb_act, ss_act)

    def act(part, i, pix, npx, row, nrows, carry):
        for k in range(4):
            at = (k // 2, k % 2, i)
            dsts[part][at] = gelu((srcs[part][at] - mean) * scale + shift)
        return carry

    geo.loop(act, [0, 0], io)
    for r in range(3):
        for c in range(3):
            flats = []
            for part in range(2):
                half = geo.parts[part][0] // 2
                v = dsts[part][(r + 1) % 2, (c + 1) % 2]
                if c == 0:
                    v = side_shift(v, 1)
                if r == 0:
                    v = jnp.concatenate([jnp.zeros((1,) + v.shape[1:], F32), v[:-1]], axis=0)
                flats.append(v.reshape(half * half * VIEWS, chans))
            t = 3 * r + c
            cols[t] = jnp.concatenate(flats, axis=0).astype(BF16)
            io.leave(t)
    io.ready()
    acc = None
    for t in range(9):
        d = nn(cols[t], w[t * chans : (t + 1) * chans, :])
        acc = d if acc is None else acc + d
    z = as_pix(acc)
    pre5[...] = z
    m5, s5 = block_stats(geo, z, lives, nf[0])
    stats[0:1] = m5
    stats[1:2] = s5


def k_widen(geo, io, me, nf, pre5, sa, sb, gs, w0, w1, st_side, pre6, act5, stats):
    chans = w0.shape[1]
    lives = [live_rows(me[1], chans), live_rows(me[2], chans)]
    mean, inv = merged(sa[...], sb[...], nf[1], nf[2])
    scale, shift = gs[0:1] * inv, gs[1:2]
    act5[...] = as_rows(gelu((pre5[...] - mean) * scale + shift)).astype(BF16)
    io.ready()
    for j, w in enumerate((w0, w1)):
        z = as_pix(nn(act5[...], w[...]))
        pre6[j] = z
        io.leave(j)
        m6, s6 = block_stats(geo, z, lives, nf[0])
        stats[j] = jnp.concatenate([m6, s6, st_side[j]], axis=0)


def k_total(geo, io, me, nf, pre6, side, sa, sb, gs, cb0, cb1, cs0, cs1, out_b, out_s, dt, sums, cot):
    chans = pre6.shape[-1]
    lives = [live_rows(me[1], chans), live_rows(me[2], chans)]
    cots = ((cb0, cb1), (cs0, cs1))
    spans = ((0, geo.qb), (geo.qb, geo.px4))
    outs = (out_b, out_s)
    io.ready()
    for j in range(2):
        io.arrive(j)
        a, b, g = sa[j], sb[j], gs[j]
        m6, r6 = merged(a[0:2], b[0:2], nf[1], nf[2])
        ms, rs = merged(a[2:4], b[2:4], nf[1], nf[2])
        k6, ks = g[0:1] * r6, g[2:3] * rs
        off = g[1:2] + g[3:4]
        acc = [jnp.zeros((VIEWS, chans), F32)] * 3
        for part, (lo, hi) in enumerate(spans):
            half = geo.parts[part][0] // 2
            cot[lo:hi] = as_pix(cots[part][j][...].astype(F32))[: hi - lo]

            def row(i, carry, part=part, lo=lo, half=half):
                at = pl.ds(lo + i * half, half)
                d6 = pre6[j, at] - m6
                dd = side[j, at] - ms
                value, slope = gelu_both(d6 * k6 + (dd * ks + off))
                if j == 0:
                    outs[part][pl.ds(i * half, half)] = value * lives[part]
                grad = slope * (cot[at] * lives[part])
                dt[j, at] = grad
                terms = [jnp.sum(v, axis=0) for v in (grad, grad * d6, grad * dd)]
                return [s + t for s, t in zip(carry, terms)]

            acc = lax.fori_loop(0, half, row, acc)
        io.leave(j)
        if j == 0:
            io.send(out_b, out_s)
        sums[j] = jnp.concatenate(
            [rows_sum(acc[0]), rows_sum(acc[1]) * r6, rows_sum(acc[2]) * rs], axis=0
        )


def back_coefs(lives, s1, s2, inv, gain, count):
    c1 = gain * inv
    c2 = [live * (c1 * s1 / count) for live in lives]
    c3 = [live * (c1 * inv * s2 / count) for live in lives]
    return c1, c2, c3


def k_back_wide(geo, io, me, nf, dt, pre6, side, sa, sb, gs, ga, gb, w0, w1, part5, dz6, dzs, tot):
    chans = pre6.shape[-1]
    lives = [live_rows(me[1], chans), live_rows(me[2], chans)]
    total = nf[1] + nf[2]
    spans = ((0, geo.qb), (geo.qb, geo.px4))
    acc = None
    io.ready()
    for j, w in enumerate((w0, w1)):
        io.arrive(j)
        a, b, g = sa[j], sb[j], gs[j]
        s = ga[j] + gb[j]
        tot[j] = s
        m6, r6 = merged(a[0:2], b[0:2], nf[1], nf[2])
        ms, rs = merged(a[2:4], b[2:4], nf[1], nf[2])
        k1, k2, k3 = back_coefs(lives, s[0:1], s[1:2], r6, g[0:1], total)
        h1, h2, h3 = back_coefs(lives, s[0:1], s[2:3], rs, g[2:3], total)
        main, short = [], []
        for part, (lo, hi) in enumerate(spans):
            grad = dt[j, lo:hi]
            main.append(grad * k1 - k2[part] - (pre6[j, lo:hi] - m6) * k3[part])
            short.append(grad * h1 - h2[part] - (side[j, lo:hi] - ms) * h3[part])
        z6 = as_rows(jnp.concatenate(main, axis=0)).astype(BF16)
        dzs[j] = as_rows(jnp.concatenate(short, axis=0)).astype(BF16)
        io.leave(j)
        if j == 0:
            dz6[...] = z6
        d = nt(z6, w[...])
        acc = d if acc is None else acc + d
    part5[...] = as_pix(acc)


def k_back_act5(nf, mine, other, pre5, sa5, sb5, gs5, dt5, sums5):
    m5, r5 = merged(sa5[...], sb5[...], nf[1], nf[2])
    dev = pre5[...] - m5
    grad = gelu_slope(dev * (gs5[0:1] * r5) + gs5[1:2]) * (mine[...] + other[...])
    dt5[...] = grad
    sums5[0:1] = rows_sum(jnp.sum(grad, axis=0))
    sums5[1:2] = rows_sum(jnp.sum(grad * dev, axis=0)) * r5


def k_back_short(io, me, dzs, w0, w1, dms):
    io.ready()
    acc = None
    for j, w in enumerate((w0, w1)):
        d = nt(dzs[j], w[...])
        acc = d if acc is None else acc + d
    dms[...] = as_pix(acc).astype(BF16)


def k_back_stride(geo, io, me, nf, dt5, pre5, sa5, sb5, gs5, ga, gb, pre4b, pre4s, sa4, sb4, gs4, n4, w, dt4b, dt4s, dz5, sums4, tot, shifts):
    chans = pre5.shape[-1]
    lives = [live_rows(me[1], chans), live_rows(me[2], chans)]
    s = ga[...] + gb[...]
    tot[...] = s
    m5, r5 = merged(sa5[...], sb5[...], nf[1], nf[2])
    c1, c2, c3 = back_coefs(lives, s[0:1], s[1:2], r5, gs5[0:1], nf[1] + nf[2])
    spans = ((0, geo.qb), (geo.qb, geo.px4))
    imgs = []
    for part, (lo, hi) in enumerate(spans):
        half = geo.parts[part][0] // 2
        z = dt5[lo:hi] * c1 - c2[part] - (pre5[lo:hi] - m5) * c3[part]
        imgs.append(z.reshape(half, half, VIEWS, chans))

    def flat(moved):
        return jnp.concatenate([v.reshape(-1, chans) for v in moved], axis=0).astype(BF16)

    def up(v):
        return jnp.concatenate([v[1:], jnp.zeros((1,) + v.shape[1:], F32)], axis=0)

    shifts[0] = flat(imgs)
    dz5[...] = shifts[0]
    shifts[1] = flat([side_shift(v, -1) for v in imgs])
    shifts[2] = flat([up(v) for v in imgs])
    shifts[3] = flat([up(side_shift(v, -1)) for v in imgs])
    m4, r4 = merged(sa4[...], sb4[...], n4[1], n4[2])
    scale, off = gs4[0:1] * r4, gs4[1:2]
    io.ready()
    plan = {
        (0, 0): ((0, 4),),
        (0, 1): ((0, 5), (1, 3)),
        (1, 0): ((0, 7), (2, 1)),
        (1, 1): ((0, 8), (1, 6), (2, 2), (3, 0)),
    }
    t1, t2 = jnp.zeros((VIEWS, chans), F32), jnp.zeros((VIEWS, chans), F32)
    for (rp, cp), terms in plan.items():
        acc = None
        for k, t in terms:
            d = nt(shifts[k], w[t * chans : (t + 1) * chans, :])
            acc = d if acc is None else acc + d
        for part, (lo, hi) in enumerate(spans):
            half = geo.parts[part][0] // 2
            d = acc[lo * VIEWS : hi * VIEWS].reshape(half, half, VIEWS, chans)
            dev = (pre4b, pre4s)[part][rp, cp] - m4
            grad = gelu_slope(dev * scale + off) * d
            (dt4b, dt4s)[part][rp, cp] = grad
            t1 = t1 + jnp.sum(grad, axis=(0, 1))
            t2 = t2 + jnp.sum(grad * dev, axis=(0, 1))
    io.send(dt4b, dt4s)
    sums4[0:1] = rows_sum(t1)
    sums4[1:2] = rows_sum(t2) * r4


def k_back_narrow(geo, io, me, nf, dt4b, dt4s, pre4b, pre4s, sa4, sb4, gs4, ga, gb, dev3, slope3, sa3, sb3, dms, dmo, w, dt3, dz4, sums3, tot):
    chans = w.shape[1]
    wide = w.shape[0]
    lives = [live_rows(me[1], chans), live_rows(me[2], chans)]
    s = ga[...] + gb[...]
    tot[...] = s
    m4, r4 = merged(sa4[...], sb4[...], nf[1], nf[2])
    c1, c2, c3 = back_coefs(lives, s[0:1], s[1:2], r4, gs4[0:1], nf[1] + nf[2])
    _, r3 = merged(sa3[...], sb3[...], nf[1], nf[2])
    dts, pres = (dt4b, dt4s), (pre4b, pre4s)

    def body(part, i, pix, npx, row, nrows, carry):
        half = geo.parts[part][0] // 2
        dev4 = get_phases(pres[part], i) - m4
        z = get_phases(dts[part], i) * c1 - c2[part] - dev4 * c3[part]
        z = z.reshape(nrows, chans).astype(BF16)
        dz4[pl.ds(row, nrows), :] = z
        at = pl.ds((0, geo.qb)[part] + half * i, half)
        t1, t2 = [], []
        for j in range(4):
            at_j = slice(256 * j, 256 * j + 256)
            d = nt(z, w[at_j, :]).reshape(2, half, 2, VIEWS, 256)
            even = d[0, :, 0] + (dms[at, :, at_j].astype(F32) + dmo[at, :, at_j].astype(F32))
            top = jnp.stack([even, d[0, :, 1]], axis=1)
            d = jnp.concatenate([as_pix_rows(top), as_pix_rows(d[1])], axis=0)
            dev = as_pix(dev3[pl.ds(row, nrows), at_j].astype(F32))
            grad = as_pix(slope3[pl.ds(row, nrows), at_j].astype(F32)) * d
            dt3[pl.ds(row, nrows), at_j] = as_rows(grad).astype(BF16)
            t1.append(jnp.sum(grad, axis=0))
            t2.append(jnp.sum(grad * dev, axis=0))
        return carry[0] + jnp.concatenate(t1, axis=1), carry[1] + jnp.concatenate(t2, axis=1)

    io.ready()
    zero = jnp.zeros((VIEWS, wide), F32)
    (a1, a2), (b1, b2) = geo.loop(body, [(zero, zero), (zero, zero)], io, io)
    sums3[0:1] = rows_sum(a1 + b1)
    sums3[1:2] = rows_sum(a2 + b2) * r3


def k_back_expand(geo, io, me, nf, dt3, dev3, sa3, sb3, gs3, ga, gb, pre2, sa2, sb2, gs2, w, dt2, dz3, dt3q, sums2, tot, zbuf_b, zbuf_s):
    wide, chans = w.shape[1], w.shape[0]
    lives = [live_rows(me[1], wide), live_rows(me[2], wide)]
    s = ga[...] + gb[...]
    tot[...] = s
    _, r3 = merged(sa3[...], sb3[...], nf[1], nf[2])
    c1, c2, c3 = back_coefs(lives, s[0:1], s[1:2], r3, gs3[0:1], nf[1] + nf[2])
    m2, r2 = merged(sa2[...], sb2[...], nf[1], nf[2])
    scale, off = gs2[0:1] * r2, gs2[1:2]
    mine = pl.ds(pl.multiple_of(me[0] * 256, 256), 256)

    def body(part, i, pix, npx, row, nrows, carry):
        zbuf = (zbuf_b, zbuf_s)[part]
        dt3q[pl.ds(row, nrows), :] = dt3[pl.ds(row, nrows), mine]
        for j in range(4):
            at = slice(256 * j, 256 * j + 256)
            z = (
                as_pix(dt3[pl.ds(row, nrows), at].astype(F32)) * c1[:, at]
                - c2[part][:, at]
                - as_pix(dev3[pl.ds(row, nrows), at].astype(F32)) * c3[part][:, at]
            )
            zbuf[:, at] = as_rows(z).astype(BF16)
        dz3[pl.ds(row, nrows), :] = zbuf[:, mine]
        d = as_pix(nt(zbuf[...], w[...]))
        dev = pre2[pl.ds(pix, npx)] - m2
        grad = gelu_slope(dev * scale + off) * d
        dt2[pl.ds(pix, npx)] = grad
        return carry[0] + jnp.sum(grad, axis=0), carry[1] + jnp.sum(grad * dev, axis=0)

    io.ready()
    zero = jnp.zeros((VIEWS, chans), F32)
    (a1, a2), (b1, b2) = geo.loop(body, [(zero, zero), (zero, zero)], io, io)
    sums2[0:1] = rows_sum(a1 + b1)
    sums2[1:2] = rows_sum(a2 + b2) * r2


def k_back_mix(geo, io, me, nf, dt2, pre2, sa2, sb2, gs2, ga, gb, pre1, sa1, sb1, gs1, w, dt1, dz2, sums1, tot, dt1q, zb, zs):
    chans = pre2.shape[-1]
    lives = [live_rows(me[1], chans), live_rows(me[2], chans)]
    s = ga[...] + gb[...]
    tot[...] = s
    m2, r2 = merged(sa2[...], sb2[...], nf[1], nf[2])
    c1, c2, c3 = back_coefs(lives, s[0:1], s[1:2], r2, gs2[0:1], nf[1] + nf[2])
    m1, r1 = merged(sa1[...], sb1[...], nf[1], nf[2])
    scale, off = gs1[0:1] * r1, gs1[1:2]
    bufs = (zb, zs)
    for part, (side, _) in enumerate(geo.parts):
        zero_edges(bufs[part], side * VIEWS)

    def back(part, i, pix, npx, row, nrows, carry):
        z = dt2[pl.ds(pix, npx)] * c1 - c2[part] - (pre2[pl.ds(pix, npx)] - m2) * c3[part]
        dz2[pl.ds(row, nrows), :] = as_rows(z).astype(BF16)
        side = geo.parts[part][0]
        at = pl.multiple_of(side * VIEWS + i * nrows, 16)
        store_shifted(bufs[part], at, nrows, side, z, (2, 1, 0))
        return carry

    lanes, _ = own_block(me)
    geo.loop(back, [0, 0], io)
    io.send(dz2)
    io.ready()

    for part, (side, start) in enumerate(geo.parts):
        for lo, hi in geo.bands[part]:
            acc = None
            for r in range(3):
                at = (lo + 2 - r) * side * VIEWS
                taps = w[3 * r : 3 * r + 3].reshape(3 * chans, chans)
                d = nn(bufs[part][at : at + (hi - lo) * side * VIEWS, :], taps)
                acc = d if acc is None else acc + d
            dt1[start + lo * side : start + hi * side] = as_pix(acc)

    def finish(part, i, pix, npx, row, nrows, carry):
        dev = pre1[pl.ds(pix, npx)] - m1
        grad = gelu_slope(dev * scale + off) * dt1[pl.ds(pix, npx)]
        dt1[pl.ds(pix, npx)] = grad
        dt1q[pl.ds(row, nrows), :] = as_rows(dt1[pl.ds(pix, npx), :, lanes]).astype(BF16)
        return carry[0] + jnp.sum(grad, axis=0), carry[1] + jnp.sum(grad * dev, axis=0)

    zero = jnp.zeros((VIEWS, chans), F32)
    (a1, a2), (b1, b2) = geo.loop(finish, [(zero, zero), (zero, zero)], None, io)
    sums1[0:1] = rows_sum(a1 + b1)
    sums1[1:2] = rows_sum(a2 + b2) * r1


def k_back_reduce(geo, io, me, nf, dt1, pre1, sa1, sb1, gs1, ga, gb, dt3q, wt, gxb, gxs, tot, coef):
    chans = pre1.shape[-1]
    lives = [live_rows(me[1], chans), live_rows(me[2], chans)]
    s = ga[...] + gb[...]
    tot[...] = s
    m1, r1 = merged(sa1[...], sb1[...], nf[1], nf[2])
    c1, c2, c3 = back_coefs(lives, s[0:1], s[1:2], r1, gs1[0:1], nf[1] + nf[2])
    io.ready()
    total = nf[1] + nf[2]
    coef[0:1] = c1
    coef[1:2] = c1 * s[0:1] / total
    coef[2:3] = c1 * r1 * s[1:2] / total

    def body(part, i, pix, npx, row, nrows, carry):
        z = dt1[pl.ds(pix, npx)] * c1 - c2[part] - (pre1[pl.ds(pix, npx)] - m1) * c3[part]
        z = as_rows(z).astype(BF16)
        g = as_pix(nn(z, wt[me[0]])) + as_pix(dt3q[pl.ds(row, nrows), :].astype(F32))
        (gxb, gxs)[part][pl.ds(pix - (0, geo.pb)[part], npx)] = g
        return carry

    geo.loop(body, [0, 0], io, io)


def k_dw_wide(act5, dz6, mids, dzs, dwide, dshort):
    dwide[...] = tn(act5[...], dz6[...]).astype(BF16)
    dshort[...] = tn(mids[...], dzs[0]).astype(BF16)


def lane_blocks(v):
    return [v[:, 128 * b : 128 * b + 128] for b in range(v.shape[1] // 128)]


def put_halves(me, full, keep, send):
    bit = me[3] & 1
    keep[...] = full[bit].astype(BF16)
    send[...] = full[1 - bit].astype(BF16)


def k_dw_stride(io, me, cols, dz5, keep, send, full):
    mine = pl.ds(pl.multiple_of(me[0] * 128, 128), 128)
    z = dz5[:, mine]
    rows = full.shape[1]
    for t in range(9):
        io.arrive(t)
        dw = tn(cols[t], z)
        lo = 0
        while lo < 512:
            half, at = divmod(t * 512 + lo, rows)
            n = min(512 - lo, rows - at)
            full[half, at : at + n] = dw[lo : lo + n]
            lo += n
    put_halves(me, full, keep, send)


def k_dw_mid(me, mid, dz4, act2, dz3, keep, send, full):
    mine = pl.ds(pl.multiple_of(me[0] * 128, 128), 128)
    blocks = [tn(mid[...], dz4[:, mine])] + lane_blocks(tn(act2[...], dz3[...]))
    full[...] = jnp.concatenate(blocks, axis=0).reshape(full.shape)
    put_halves(me, full, keep, send)


def own_block(me):
    lanes = pl.ds(pl.multiple_of((me[0] >> 1) * 128, 128), 128)
    return lanes, pl.ds(pl.multiple_of((me[0] & 1) * 64, 64), 64)


def k_dev_products(geo, io, me, devq, xs, out, part):
    lives = [live_rows(me[1], 256), live_rows(me[2], 256)]
    _, mine = own_block(me)
    io.ready()

    def body(step, i, pix, npx, row, nrows, carry):
        return [
            carry[j] + jnp.sum(as_pix(xs[j, pl.ds(row, nrows), :].astype(F32)), axis=0) for j in range(4)
        ]

    zero = [jnp.zeros((VIEWS, 256), F32)] * 4
    big, small = geo.loop(body, [zero, zero], io)
    sums = [jnp.broadcast_to(rows_sum(b * lives[0] + s * lives[1]), (16, 256)) for b, s in zip(big, small)]
    for j in range(4):
        part[...] = tn(devq[...], xs[j])
        out[:, 256 * j : 256 * j + 256] = jnp.concatenate([part[mine, :], sums[j]], axis=0).astype(BF16)


def k_dw_last(geo, io, me, wb, ws, dz2, xs, dt1q, keep, send, full, part, flat):
    lanes, mine = own_block(me)
    io.ready()
    io.start_steps()
    nb, ns = geo.pb * VIEWS, geo.ps * VIEWS
    at = 0
    for r in range(3):
        ob, os = r * geo.hb * VIEWS, r * geo.hs * VIEWS
        full[...] = tn(dz2[0:nb, lanes], wb[ob : ob + nb, :]) + tn(
            dz2[nb : nb + ns, lanes], ws[os : os + ns, :]
        )
        for block in lane_blocks(full[mine, :]):
            flat[at : at + 64] = block
            at += 64
    geo.loop(lambda step, i, pix, npx, row, nrows, carry: carry, [0, 0], io)
    for j in range(4):
        part[:, 256 * j : 256 * j + 256] = tn(dt1q[...], xs[j])
    flat[at:] = jnp.concatenate(lane_blocks(part[mine, :]), axis=0)
    half = keep.shape[0]
    bit = me[3] & 1
    keep[...] = flat[pl.ds(pl.multiple_of(bit * half, 8), half)].astype(BF16)
    send[...] = flat[pl.ds(pl.multiple_of((1 - bit) * half, 8), half)].astype(BF16)


def k_out_first(io, me, wide, short, a, b, dwide, dshort, dstride):
    bit = me[3] & 1
    for n in range(4):
        io.arrive(n)
        if n < 2:
            dwide[n] = wide[n].astype(F32)
        dshort[n] = short[n].astype(F32)
        io.leave(n)
    io.ready()
    dstride[bit] = a[0].astype(F32)
    dstride[1 - bit] = b[0].astype(F32)
    io.send(dstride)


def k_small_outputs(me, t1, t2, t3, t4, t5, t6, late, gm3, sm3, go3, so3, gm4, sm4, go4, so4):
    lanes, _ = own_block(me)
    half = me[0] & 1
    for n, t in enumerate((t1, t2)):
        block = t[:, lanes]
        mine = jnp.where(half == 0, block[:, 0:64], block[:, 64:128])
        gm3[n : n + 1] = mine[1:2]
        sm3[n : n + 1] = mine[0:1]
    wide = pl.ds(pl.multiple_of(me[0] * 256, 256), 256)
    go3[...] = t3[1:2, wide]
    so3[...] = t3[0:1, wide]
    mid = pl.ds(pl.multiple_of(me[0] * 128, 128), 128)
    for n, t in enumerate((t4, t5)):
        gm4[n : n + 1] = t[1:2, mid]
        sm4[n : n + 1] = t[0:1, mid]
    go4[...] = t6[1:3]
    so4[0:1] = t6[0:1]
    so4[1:2] = t6[0:1]


def k_sum_split(shift, size, n_in, me, *refs):
    total = refs[n_in]
    acc = refs[0][...].astype(F32)
    for r in refs[1:n_in]:
        acc = acc + r[...].astype(F32)
    total[...] = acc
    where = (me[3] >> shift) & (size - 1)
    for m, out in enumerate(refs[n_in + 1 :]):
        out[...] = total[where ^ m].astype(BF16)


def k_sum(n_in, *refs):
    acc = refs[0][...].astype(F32)
    for r in refs[1:n_in]:
        acc = acc + r[...].astype(F32)
    refs[n_in][...] = acc.astype(BF16)


def k_join(shift, size, me, *refs):
    where = (me[3] >> shift) & (size - 1)
    for m in range(size):
        refs[size][where ^ m] = refs[m][...]


def k_unpack(plan, me, a, b, *refs):
    full = refs[-1]
    bit = me[3] & 1
    full[bit] = a[...].reshape(full.shape[1:]).astype(F32)
    full[1 - bit] = b[...].reshape(full.shape[1:]).astype(F32)
    flat = full[...].reshape(2 * full.shape[1], 128)
    at = 0
    for out, (lead, rows, cols) in zip(refs, plan):
        for t in range(lead):
            for block in range(cols // 128):
                v = flat[at : at + rows]
                lanes = slice(128 * block, 128 * block + 128)
                if lead > 1:
                    out[t, :, lanes] = v
                else:
                    out[:, lanes] = v
                at += rows


def k_out_last(me, a, b, dev, coef, dmix, dreduce, full):
    bit = me[3] & 1
    full[bit] = a[...].reshape(full.shape[1:]).astype(F32)
    full[1 - bit] = b[...].reshape(full.shape[1:]).astype(F32)
    flat = full[...].reshape(2 * full.shape[1], 128)
    at = 0
    for t in range(9):
        for block in range(2):
            dmix[t, :, 128 * block : 128 * block + 128] = flat[at : at + 64]
            at += 64
    dev = dev[...].astype(F32)
    fix = dev[64:65] * coef[1] + dev[0:64] * coef[2]
    for block in range(8):
        lanes = slice(128 * block, 128 * block + 128)
        dreduce[:, lanes] = flat[at : at + 64] * coef[0] - fix[:, lanes]
        at += 64


def per_device(
    ni,
    nc,
    x_big,
    x_small,
    cot_big,
    cot_small,
    counts,
    w_reduce,
    w_mix,
    w_expand,
    w_narrow,
    w_stride,
    w_widen,
    w_short,
    gain_mid3,
    shift_mid3,
    gain_out3,
    shift_out3,
    gain_mid4,
    shift_mid4,
    gain_out4,
    shift_out4,
):
    assert nc == 4 and ni >= 8 and x_big.shape[0] == VIEWS and x_small.shape[0] == VIEWS
    geo = Geo(x_big.shape[1], x_small.shape[1])
    img = lax.axis_index("img")
    q = lax.axis_index("ch").astype(jnp.int32)
    levels = ni.bit_length() - 1
    me, nf3, cnt3, nf4, cnt4 = call(
        "counts",
        functools.partial(k_counts, ni, ((geo.pb, geo.ps), (geo.qb, geo.qs))),
        [(counts, SMEM)],
        [(sds((4,), jnp.int32), SMEM)]
        + [(sds((n,)), SMEM) for n in (3, 8 * (levels - 2)) * 2],
        slack=1,
    )

    smem = [(me, SMEM)]

    def over_img(v, k):
        return lax.ppermute(v, "img", [(i, i ^ (1 << k)) for i in range(ni)])

    def over_ch(v, k):
        return lax.ppermute(v, "ch", [(i, i ^ k) for i in range(nc)])

    rounds, at = [], 0
    while at < levels:
        rounds.append((at, min(2, levels - at) if at == 0 else 1))
        at += rounds[-1][1]

    def peers(v, shift, bits):
        out = []
        for m in range(1, 1 << bits):
            out.append(lax.ppermute(v, "img", [(i, i ^ (m << shift)) for i in range(ni)]))
        return out

    def sync(v, combine, wait=(), free=()):
        wait, free = dict(wait), dict(free)
        freed = []
        for k, (shift, bits) in enumerate(rounds):
            if k in wait:
                v = lax.optimization_barrier((v,) + tuple(wait[k]))[0]
            others = peers(v, shift, bits)
            if k in free:
                held = lax.optimization_barrier(tuple(others) + tuple(free[k]))
                others = list(held[: len(others)])
                freed += held[len(others) :]
            if k == len(rounds) - 1:
                return (v, others[0]) + ((freed,) if free else ())
            v = combine(k, [v] + others)

    last = len(rounds) - 1

    def sync_stats(stats, cnt, wait=(), free=()):
        def combine(k, arrays):
            (v,) = call(
                "merge",
                functools.partial(k_merge, 8 * k, len(arrays)),
                [(cnt, SMEM)] + vm(*arrays),
                [sds(stats.shape)],
                slack=1,
            )
            return v

        return sync(stats, combine, wait, free)

    def sync_sums(sums, wait=(), free=()):
        def combine(k, arrays):
            (v,) = call("add", functools.partial(k_add, len(arrays)), vm(*arrays), [sds(sums.shape)], slack=1)
            return v

        return sync(sums, combine, wait, free)

    pairs = [(at, 1) for at in range(levels)]
    fours = [(0, 1)]
    while fours[-1][0] + fours[-1][1] < levels:
        done = fours[-1][0] + fours[-1][1]
        fours.append((done, min(2, levels - done)))

    def to_peers(parts, group):
        shift, bits = group
        out = []
        for m in range(1, 1 << bits):
            perm = [(i, i ^ (m << shift)) for i in range(ni)]
            out.append(lax.ppermute(parts[m if len(parts) > 1 else 0], "img", perm))
        return out

    def sum_split(name, arrays, group):
        shift, bits = group
        size = 1 << bits
        shape = arrays[0].shape
        view = (size, shape[0] // size) + shape[1:]
        return call(
            name,
            functools.partial(k_sum_split, shift, size, len(arrays)),
            smem + vm(*[a.reshape(view) for a in arrays]),
            [sds(view[1:], BF16)] * size,
            [pltpu.VMEM(view, F32)],
            order=True,
        )

    def join(name, parts, group):
        shift, bits = group
        size = 1 << bits
        (full,) = call(
            name,
            functools.partial(k_join, shift, size),
            smem + vm(*parts),
            [sds((size,) + parts[0].shape, BF16)],
        )
        return full.reshape((-1,) + parts[0].shape[1:])

    class Train:
        def __init__(self, name, groups, parts):
            self.name, self.groups, self.parts, self.at, self.summing = name, groups, parts, 0, True

        def sends(self):
            return self.parts[1:] if self.summing else self.parts

        def launch(self, sends):
            parts = self.parts[:1] + list(sends) if self.summing else list(sends)
            self.received = to_peers(parts, self.groups[self.at])

        def advance(self):
            name = "%s_%d" % (self.name, self.at)
            arrays = self.parts[:1] + self.received
            if self.summing and self.at + 1 < len(self.groups):
                self.at += 1
                self.parts = sum_split(name, arrays, self.groups[self.at])
            elif self.summing:
                self.summing = False
                self.parts = call(
                    name + "s",
                    functools.partial(k_sum, len(arrays)),
                    vm(*arrays),
                    [sds(arrays[0].shape, BF16)],
                    slack=2,
                )
            else:
                self.parts = [join(name + "j", arrays, self.groups[self.at])]
                self.at -= 1

        def to_last(self):
            while self.summing or self.at > 0:
                self.advance()
                self.launch(self.sends())

        def finish(self):
            self.to_last()
            return self.parts[0], self.received[0]

    def quarters(v):
        p1 = over_ch(v, 1)
        p2 = over_ch(v, 2)
        return [v, p1, p2, over_ch(p2, 1)]

    def after(marker, *arrays):
        return list(lax.optimization_barrier((marker,) + arrays))

    def sent(v):
        return [v, over_ch(v, 1), over_ch(v, 2)]

    def passed_on(g):
        return g + [over_ch(g[2], 1)]

    def rows_of(v):
        return jnp.transpose(v, (1, 2, 0, 3)).reshape(-1, v.shape[3])

    m3, c3 = 4 * w_reduce.shape[1], w_reduce.shape[0]
    m4, c4q = w_widen.shape
    first = [rows_of(x_small)]
    first.append(jnp.transpose(w_mix, (0, 1, 3, 2)).reshape(-1, m3))
    first += [w_reduce.T[:, j * m3 : (j + 1) * m3] for j in range(c3 // m3)]
    mix_at, reduce_at = first[0].shape[0], first[0].shape[0] + first[1].shape[0]
    held = (gain_mid3, shift_mid3, gain_out3[None], shift_out3[None], gain_mid4, shift_mid4, gain_out4, shift_out4)
    first += call(
        "pack_params",
        k_pack_params,
        vm(*held),
        [sds((64, 256), BF16)],
        [pltpu.VMEM((32, 128), F32)],
        slack=2,
    )
    params_at = sum(v.shape[0] for v in first[:-1])
    xb = quarters(rows_of(x_big))
    xb[1], me, *first = lax.optimization_barrier((xb[1], me, *first))
    smem = [(me, SMEM)]
    xsm = sent(jnp.concatenate(first))
    def blocks128(v):
        return [v[:, 128 * b : 128 * b + 128] for b in range(v.shape[1] // 128)]

    w_mid = jnp.concatenate(blocks128(w_expand) + blocks128(w_narrow))
    def whole_tiles(v):
        return jnp.pad(v, ((0, -v.shape[0] % 16), (0, 0)))

    cots = [whole_tiles(rows_of(v)) for v in (cot_big, cot_small)]
    cot_rows = [v.shape[0] for v in cots]
    last_in = jnp.concatenate([w_short, w_widen] + cots)
    wst = w_stride.reshape(-1, w_stride.shape[3])
    xb[3], xsm[2], w_mid, last_in, wst = after(xb[3], xsm[2], w_mid, last_in, wst)
    xsm = passed_on(xsm)
    gs1, gs2, gs3, gs4, gs5, gs6 = call(
        "unpack_params",
        functools.partial(k_unpack_params, params_at),
        smem + [(in_hbm(v), HBM) for v in xsm],
        [sds((2, n)) for n in (m3, m3, c3, m4, m4)] + [sds((2, 4, c4q))],
        [pltpu.VMEM((4, 64, 256), BF16), pltpu.SemaphoreType.DMA((4,))],
        slack=2,
    )

    chip_pairs = [[0, 2], [1, 3]]
    wst = lax.all_gather(wst, "ch", axis_index_groups=chip_pairs)
    last_in = lax.all_gather(last_in, "ch", axis_index_groups=chip_pairs)

    n3, n4 = [(nf3, SMEM)], [(nf4, SMEM)]

    def k(fn):
        return functools.partial(fn, geo)

    hb, hs = geo.hb, geo.hs
    sb4, ss4 = (2, 2, hb // 2, hb // 2, VIEWS, m4), (2, 2, hs // 2, hs // 2, VIEWS, m4)
    wb_shape, ws_shape = ((hb + 2) * hb * VIEWS, 3 * m3), ((hs + 2) * hs * VIEWS, 3 * m3)

    def flow(kind, *arrays):
        return [(a, Flow(kind)) for a in arrays]

    def out(kind, shape, dtype=F32):
        return (sds(shape, dtype), Flow(kind))

    x_all = [(xb + xsm, Flow("x"))]
    w_in, w_ahead, w_back = [
        [(xsm, Flow(kind, base))]
        for kind, base in (("w_in", reduce_at), ("w_ahead", mix_at), ("w_back", mix_at))
    ]
    run = functools.partial(call, geo=geo)
    px1, px3, px4 = (geo.px, VIEWS, m3), (geo.px, VIEWS, c3), (geo.px4, VIEWS, m4)

    pre1, st = run(
        "reduce",
        k(k_reduce),
        smem + n3 + x_all + w_in,
        [fast(px1), sds((2, m3))],
    )
    st, w_mid = after(st, w_mid)
    w_mid = sent(w_mid)
    a1, b1 = sync_stats(st, cnt3)
    pre2, winb, wins, st, devq, keep1 = run(
        "mix",
        k(k_mix),
        smem + n3 + vm(pre1, a1, b1, gs1) + w_ahead,
        [
            fast(px1),
            out("all", wb_shape, BF16),
            out("all", ws_shape, BF16),
            sds((2, m3)),
            out("all", (geo.rows, 128), BF16),
            (sds(px1), Keep(2)),
        ],
        [pltpu.VMEM((1, m3), F32)],
    )
    st, w_mid[2] = after(st, w_mid[2])
    w_mid = passed_on(w_mid)
    w_expand_all = [(w_mid, Flow("w", 0, (m3, c3)))]
    w_narrow_all = [(w_mid, Flow("w", m3 * (c3 // 4 // 128), (c3, m4)))]
    a2, b2 = sync_stats(st, cnt3)
    pre3, act2, st, keep2 = run(
        "expand",
        k(k_expand),
        smem + n3 + vm(pre2, a2, b2, gs2) + w_expand_all,
        [
            fast(px3),
            out("rows", (geo.rows, m3), BF16),
            sds((2, c3)),
            (sds(px1), Keep(2)),
        ],
    )
    a3, b3 = sync_stats(st, cnt3)
    pre4b, pre4s, mid, mids, st, dev3, slope3 = run(
        "narrow",
        k(k_narrow),
        smem + n3 + vm(pre3) + x_all + vm(a3, b3, gs3) + w_narrow_all,
        [
            out("big", sb4),
            out("small", ss4),
            out("rows", (geo.rows, c3), BF16),
            fast((geo.rows4, c3), BF16),
            sds((2, m4)),
            out("rows", (geo.rows, c3), BF16),
            out("rows", (geo.rows, c3), BF16),
        ],
        [pltpu.VMEM((geo.px4, VIEWS, c3), F32)],
        slack=6,
        staying=4 * math.prod(px3),
    )
    st, wst = after(st, wst)
    wst = [wst, over_ch(wst, 1)]
    a4, b4 = sync_stats(st, cnt3)
    w_stride_all = [(wst, Flow("w4", 0, (9 * m4, m4)))]
    pre5, cols, st = run(
        "stride",
        k(k_stride),
        smem
        + n4
        + n3
        + flow("big", pre4b)
        + flow("small", pre4s)
        + vm(a4, b4, gs4)
        + w_stride_all,
        [
            sds(px4),
            out("lead", (9, geo.rows4, m4), BF16),
            sds((2, m4)),
        ],
        [pltpu.VMEM(sb4, F32), pltpu.VMEM(ss4, F32)],
    )
    (dev,) = run(
        "dev_products",
        k(k_dev_products),
        smem + flow("all", devq) + x_all,
        [sds((m3 // 4 + 16, c3), BF16)],
        [pltpu.VMEM((128, c3 // 4), F32)],
        ahead=8,
    )
    a5, b5, (dev,) = sync_stats(st, cnt4, free={last: [dev]})
    a5, last_in, mids = after(a5, last_in, mids)
    at_w, at_b, at_s = c3, c3 + m4, c3 + m4 + cot_rows[0]

    def from_chips(base, rows):
        return [(last_in, Flow("chip", base, (rows, c4q), j)) for j in range(2)]

    wsh, wwi = from_chips(0, c3), from_chips(at_w, m4)
    cots = from_chips(at_b, cot_rows[0]) + from_chips(at_s, cot_rows[1])
    side, st_side = run(
        "short",
        k(k_short),
        smem + n4 + vm(mids) + wsh,
        [fast((2, geo.px4, VIEWS, c4q)), sds((2, 2, c4q))],
    )
    pre6, act5, st = run(
        "widen",
        k(k_widen),
        smem + n4 + vm(pre5, a5, b5, gs5) + wwi + vm(st_side),
        [
            fast((2, geo.px4, VIEWS, c4q)),
            sds((geo.rows4, m4), BF16),
            sds((2, 4, c4q)),
        ],
    )
    a6, b6 = sync_stats(st, cnt4)
    out_b, out_s, dt6, sums = run(
        "total",
        k(k_total),
        smem + n4 + vm(pre6, side, a6, b6, gs6) + cots,
        [
            out("all", (geo.qb, VIEWS, c4q)),
            out("all", (geo.qs, VIEWS, c4q)),
            fast((2, geo.px4, VIEWS, c4q)),
            sds((2, 3, c4q)),
        ],
        [pltpu.VMEM((geo.px4, VIEWS, c4q), F32)],
    )
    ga6, gb6 = sync_sums(sums)
    part5, dz6, dzs, t6 = run(
        "back_wide",
        k(k_back_wide),
        smem
        + n4
        + vm(dt6, pre6, side, a6, b6, gs6, ga6, gb6)
        + wwi,
        [
            sds(px4),
            sds((geo.rows4, c4q), BF16),
            sds((2, geo.rows4, c4q), BF16),
            sds((2, 3, c4q)),
        ],
    )
    other5 = over_ch(part5, 1)
    dt5, sums = call(
        "back_act5",
        k_back_act5,
        n4 + vm(part5, other5, pre5, a5, b5, gs5),
        [sds(px4), sds((2, m4))],
    )
    (dms,) = run(
        "back_short", k_back_short, smem + vm(dzs) + wsh, [sds((geo.px4, VIEWS, c3), BF16)]
    )
    dmo = over_ch(dms, 1)
    dwide, dshort = call(
        "dw_wide",
        k_dw_wide,
        vm(act5, dz6, mids, dzs),
        [sds((m4, c4q), BF16), sds((c3, c4q), BF16)],
    )
    ga5, gb5, (dwide, dshort) = sync_sums(sums, free={0: [dwide, dshort]})
    dt4b, dt4s, dz5, sums, t5 = run(
        "back_stride",
        k(k_back_stride),
        smem
        + n4
        + vm(dt5, pre5, a5, b5, gs5, ga5, gb5)
        + flow("all", pre4b, pre4s)
        + vm(a4, b4, gs4)
        + n3
        + w_stride_all,
        [fast(sb4), fast(ss4), sds((geo.rows4, m4), BF16), sds((2, m4)), sds((2, m4))],
        [pltpu.VMEM((4, geo.rows4, m4), BF16)],
    )

    def halves(rows):
        return [sds((rows // 2, 128), BF16)] * 2, pltpu.VMEM((2, rows // 2, 128), F32)

    outs, full = halves(9 * m4)
    parts = run("dw_stride", k_dw_stride, smem + flow("lead", cols) + vm(dz5), outs, [full])
    stride_train = Train("stride", pairs, parts)
    ga4, gb4, sends = sync_sums(sums, free={last: stride_train.sends()})
    stride_train.launch(sends)
    dt3, dz4, sums, t4 = run(
        "back_narrow",
        k(k_back_narrow),
        smem
        + n3
        + vm(dt4b, dt4s)
        + flow("big", pre4b)
        + flow("small", pre4s)
        + vm(a4, b4, gs4, ga4, gb4)
        + flow("rows", dev3, slope3)
        + vm(a3, b3, dms, dmo)
        + w_narrow_all,
        [
            fast((geo.rows, c3), BF16),
            out("rows", (geo.rows, m4), BF16),
            sds((2, c3)),
            sds((2, m4)),
        ],
    )
    came = stride_train.received
    stride_train.advance()
    ga3, gb3, sends = sync_sums(sums, wait={last: came}, free={last: stride_train.sends()})
    stride_train.launch(sends)
    dt2, dz3, dt3q, sums, t3 = run(
        "back_expand",
        k(k_back_expand),
        smem
        + n3
        + vm(dt3)
        + flow("rows", dev3)
        + vm(a3, b3, gs3, ga3, gb3)
        + flow("px", keep2)
        + vm(a2, b2, gs2)
        + w_expand_all,
        [
            fast(px1),
            out("rows", (geo.rows, c3 // 4), BF16),
            out("rows", (geo.rows, c3 // 4), BF16),
            sds((2, m3)),
            sds((2, c3)),
        ],
        [
            pltpu.VMEM((2 * hb * VIEWS, c3), BF16),
            pltpu.VMEM((2 * hs * VIEWS, c3), BF16),
        ],
    )
    came = stride_train.received
    stride_train.advance()
    outs, full = halves(c3 + (c3 // 4 // 128) * m3)
    parts = call("dw_mid", k_dw_mid, smem + vm(mid, dz4, act2, dz3), outs, [full])
    mid_train = Train("mid", pairs, parts)
    ga2, gb2, (mid_send, *sends) = sync_sums(
        sums, wait={last: came}, free={0: mid_train.sends(), last: stride_train.sends()}
    )
    mid_train.launch([mid_send])
    stride_train.launch(sends)
    dt1, dz2, sums, t2, dt1q = run(
        "back_mix",
        k(k_back_mix),
        smem
        + n3
        + vm(dt2)
        + flow("px", keep2)
        + vm(a2, b2, gs2, ga2, gb2)
        + flow("px", keep1)
        + vm(a1, b1, gs1)
        + w_back,
        [
            out("px", px1),
            out("all", (geo.rows, m3), BF16),
            sds((2, m3)),
            sds((2, m3)),
            out("rows", (geo.rows, 128), BF16),
        ],
        [pltpu.VMEM(wb_shape, BF16), pltpu.VMEM(ws_shape, BF16)],
        ahead=8,
    )
    came = stride_train.received + mid_train.received
    stride_train.advance()
    mid_train.advance()
    mix_rows = 9 * m3 // 128 * (m3 // 4)
    rows_last = mix_rows + c3 // 128 * (m3 // 4)
    outs, _ = halves(rows_last)
    parts = run(
        "dw_last",
        k(k_dw_last),
        smem + flow("all", winb, wins, dz2) + x_all + flow("all", dt1q),
        outs,
        [
            pltpu.VMEM((128, 3 * m3), F32),
            pltpu.VMEM((128, c3), F32),
            pltpu.VMEM((rows_last, 128), F32),
        ],
        ahead=8,
        hold=True,
    )
    last_train = Train("last", fours, parts)
    dwide, dshort, dev = lax.psum((dwide, dshort, dev), "img")
    wide = [dwide, dshort, dev]
    ga1, gb1, (last_send, mid_send, *sends) = sync_sums(
        sums,
        wait={last: came},
        free={last: last_train.sends() + mid_train.sends() + stride_train.sends()},
    )
    last_train.launch([last_send])
    mid_train.launch([mid_send])
    stride_train.launch(sends)
    dwide, dshort, dev = wide
    gxb, gxs, t1, coef = run(
        "back_reduce",
        k(k_back_reduce),
        smem
        + n3
        + flow("px", dt1, keep1)
        + vm(a1, b1, gs1, ga1, gb1)
        + flow("rows", dt3q)
        + w_in,
        [
            out("big_px", (geo.pb, VIEWS, c3 // 4)),
            out("small_px", (geo.ps, VIEWS, c3 // 4)),
            sds((2, m3)),
            sds((3, m3)),
        ],
    )
    def unpack(name, a, b, plan):
        shapes = [((lead,) if lead > 1 else ()) + (rows, cols) for lead, rows, cols in plan]
        return call(
            name,
            functools.partial(k_unpack, plan),
            smem + vm(a, b),
            [sds(shape) for shape in shapes],
            [pltpu.VMEM((2,) + a.shape, F32)],
        )

    trains = (last_train, mid_train, stride_train)
    gxb, dwide, dshort, dev, coef, *came = after(
        gxb, dwide, dshort, dev, coef, *[train.received[0] for train in trains]
    )
    for train, first in zip(trains, came):
        train.received[0] = first
    halves_in = [v.reshape(1, 9 * m4 // 2, 128) for v in stride_train.finish()]
    dwide, dshort, dstride = run(
        "out_first",
        k_out_first,
        smem
        + flow("lead", dwide.reshape(2, m4 // 2, c4q), dshort.reshape(4, c3 // 4, c4q))
        + flow("all", *halves_in),
        [
            out("lead", (2, m4 // 2, c4q)),
            out("lead", (4, c3 // 4, c4q)),
            out("all", (2, 9 * m4 // 2, 128)),
        ],
        ahead=4,
    )
    mid_train.to_last()
    last_train.to_last()
    dstride, mid_train.received[0], last_train.received[0] = after(
        dstride, mid_train.received[0], last_train.received[0]
    )
    dnarrow, dexpand = unpack(
        "out_mid", *mid_train.finish(), [(1, c3, m4 // 4), (1, m3, c3 // 4)]
    )
    coef = lax.dynamic_slice_in_dim(coef, q * (m3 // 4), m3 // 4, 1)[:, :, None]
    mine, other = last_train.finish()
    dmix, dreduce = call(
        "out_last",
        k_out_last,
        smem + vm(mine, other, dev, coef),
        [sds((9, m3 // 4, m3)), sds((m3 // 4, c3))],
        [pltpu.VMEM((2,) + mine.shape, F32)],
    )

    def views_first(v, side):
        return jnp.transpose(v.reshape(side, side, VIEWS, v.shape[2]), (2, 0, 1, 3))

    small = call(
        "small_outputs",
        k_small_outputs,
        smem + vm(t1, t2, t3, t4, t5, t6[0], gxs[0]),
        [sds((2, m3 // 4))] * 2
        + [sds((1, c3 // 4))] * 2
        + [sds((2, m4 // 4))] * 2
        + [sds((2, c4q))] * 2,
        slack=4,
    )
    small[2], small[3] = small[2][0], small[3][0]
    return (
        views_first(out_b, hb // 2),
        views_first(out_s, hs // 2),
        views_first(gxb, hb),
        views_first(gxs, hs),
        dreduce.T,
        jnp.transpose(dmix.reshape(3, 3, m3 // 4, m3), (0, 1, 3, 2)),
        dexpand,
        dnarrow,
        dstride.reshape(3, 3, m4, m4 // 4),
        dwide.reshape(m4, c4q),
        dshort.reshape(c3, c4q),
        *small,
    )


def solution(mesh):
    act = P("img", None, None, "ch")
    flat, taps, vec = P(None, "ch"), P(None, None, None, "ch"), P("ch")
    in_specs = (act,) * 4 + (P(), flat, taps, flat, flat, taps, flat, flat)
    in_specs += (flat, flat, vec, vec, flat, flat, flat, flat)
    out_specs = (act,) * 4 + (flat, taps, flat, flat, taps, flat, flat)
    out_specs += (flat, flat, vec, vec, flat, flat, flat, flat)
    return jax.shard_map(
        functools.partial(per_device, mesh.shape["img"], mesh.shape["ch"]),
        mesh=mesh,
        in_specs=in_specs,
        out_specs=out_specs,
        check_vma=False,
    )
```
